32 devices in a mesh: tile: 8 (over z, x), rot: 4 (over y, core).
Axes of the slice: x: 2, y: 2, z: 4, core: 2. Of those that a mesh axis runs over, the one named last changes fastest.
Arguments:
- tomogram: bfloat16 [256, 5120], P('tile'), may hold values from -12 to 12
- templates: bfloat16 [16, 110592], P('rot', 'tile'), may hold values from -6 to 6
- valid: int32 [256, 80], P('tile'), may hold values from 0 to 1, as said below
- quats: float32 [4, 4096], replicated, may hold values from -1 to 1, as said below
- rot_index: int32 [16], P('rot'), may hold values from 0 to 4095
Outputs:
- best: float32 [256, 5120], P('tile', 'rot')
- evidence: float32 [256, 5120], P('tile', 'rot')
- moments: float32 [4, 256, 5120], P(None, 'tile', 'rot')
The draws below stay inside these ranges and needn't reach their ends.
Inputs may be any that keep to these rules, and one draw needn't show every extreme that they name: `valid`: 1 marks a column (x, y) of voxels inside the lamella. `quats`: each column is a unit quaternion with a non-negative first component.
All inputs are finite; a program needn't handle non-finite values.
Results may differ from the reference program's by a relative error of at most 0.0003.
Values may be sent and summed in bfloat16 or wider, within the bound.
No kernel may reach another device: no remote copies, remote signals or barrier semaphores. Data moves between devices by JAX's collectives and lax.ppermute only.
A program may use at most 128 MiB of HBM per device.

```python
import math
import jax
import jax.numpy as jnp
from jax import lax

TEMPL = 48
HALF = 24
NY = 80
Z = 64
NQ = 4096
ROTS = 16
NX = 256


def template_bank(key):
    shape_bank = (ROTS, TEMPL ** 3)
    base = jnp.clip(jax.random.normal(jax.random.fold_in(key, 11), shape_bank, jnp.float32), -4.5, 4.5)
    return base


def draw_templates(key, part):
    return template_bank(key).astype(jnp.bfloat16)


def draw_tomogram(key, part):
    column_scale = jnp.exp(jax.random.uniform(jax.random.fold_in(key, 21), (NX, NY, 1), jnp.float32, math.log(0.3), math.log(3.0)))
    volume = jnp.clip(jax.random.normal(jax.random.fold_in(key, 23), (NX, NY, Z), jnp.float32), -4.0, 4.0) * column_scale
    return volume.reshape(NX, NY * Z).astype(jnp.bfloat16)


def draw_valid(key, part):
    threshold = NX + 2 * jnp.arange(NX, dtype=jnp.int32)[:, None]
    numbers = jax.random.randint(jax.random.fold_in(key, 31), (NX, NY), 0, 4 * NX)
    return (numbers < threshold).astype(jnp.int32)


def draw_quats(key, part):
    raw_quats = jax.random.normal(jax.random.fold_in(key, 41), (4, NQ), jnp.float32)
    unit_quats = raw_quats / jnp.sqrt(jnp.sum(raw_quats * raw_quats, axis=0, keepdims=True))
    return unit_quats.at[0].set(jnp.abs(unit_quats[0]))


def touch_ends(array, own_key, smallest, largest):
    place = [jax.random.randint(jax.random.fold_in(own_key, axis), (), 0, length) for axis, length in enumerate(array.shape)]
    longest = array.shape.index(max(array.shape))
    neighbour = place[:longest] + [(place[longest] + 1) % array.shape[longest]] + place[longest + 1:]
    return array.at[tuple(place)].set(smallest).at[tuple(neighbour)].set(largest)


def setup_inputs(seed: int = 0) -> dict:
    splits = jax.random.split(jax.random.key(seed), 6)
    return {
        "tomogram": draw_tomogram(jax.random.fold_in(splits[5], 71), 0),
        "templates": draw_templates(jax.random.fold_in(splits[5], 71), 0),
        "valid": draw_valid(jax.random.fold_in(splits[5], 71), 0),
        "quats": draw_quats(jax.random.fold_in(splits[5], 71), 0),
        "rot_index": touch_ends(jax.random.randint(splits[4], (ROTS,), 0, NQ), jax.random.fold_in(splits[4], 1), 0, NQ - 1).astype(jnp.int32),
    }


EPSILON = 1e-06

def unit_templates(templates):
    bank_float = templates.astype(jnp.float32)
    centred = bank_float - lax.optimization_barrier(jnp.mean(bank_float, axis=1, keepdims=True))
    spread = jnp.sqrt(lax.optimization_barrier(jnp.mean(centred * centred, axis=1, keepdims=True)) + EPSILON)
    return centred / (spread * jnp.float32(TEMPL) ** 1.5)

def correlate(slab_vol, kernel):
    padded_shape = (NX + TEMPL, NY + TEMPL, Z + TEMPL)
    padded = jnp.pad(slab_vol, HALF)
    kernel_pad = jnp.zeros(padded_shape, slab_vol.dtype).at[:TEMPL, :TEMPL, :TEMPL].set(kernel)
    spectrum = jnp.fft.rfftn(padded) * jnp.conj(jnp.fft.rfftn(kernel_pad))
    circular = jnp.fft.irfftn(spectrum, s=padded_shape)
    return circular[:NX, :NY, :Z].astype(slab_vol.dtype)

def reference(tomogram, templates, valid, quats, rot_index):
    slab_vol = tomogram.astype(jnp.float32).reshape(NX, NY, Z)
    kernels = unit_templates(templates).reshape(ROTS, TEMPL, TEMPL, TEMPL)
    inside = valid.astype(jnp.float32)[:, :, None]
    voxel_count = jnp.sum(inside) * Z

    def statistics(kernel):
        correlation = correlate(slab_vol, kernel)
        average = jnp.sum(inside * correlation) / voxel_count
        deviation = correlation - average
        spread = jnp.sqrt(jnp.sum(inside * deviation * deviation) / voxel_count + EPSILON)
        return (average, spread)
    averages, spreads = lax.map(statistics, kernels)
    orient = quats[:, rot_index].T

    def accumulate(state_in, rot_item):
        highest, exp_total, moment = state_in
        kernel, average, spread, quaternion = rot_item
        scores = (correlate(slab_vol, kernel) - average) / spread
        new_high = jnp.maximum(highest, scores)
        rescale = jnp.exp(highest - new_high)
        weight = jnp.exp(scores - new_high)
        exp_total = exp_total * rescale + weight
        moment = moment * rescale[None] + weight[None] * quaternion[:, None, None, None]
        return ((new_high, exp_total, moment), None)
    start_state = (jnp.full((NX, NY, Z), -jnp.inf, jnp.float32), jnp.zeros((NX, NY, Z), jnp.float32), jnp.zeros((4, NX, NY, Z), jnp.float32))
    (highest, exp_total, moment), _ = lax.scan(accumulate, start_state, (kernels, averages, spreads, orient))
    best = (inside * highest).reshape(NX, NY * Z)
    evidence = (inside * (highest + jnp.log(exp_total))).reshape(NX, NY * Z)
    moments = (inside[None] * moment / exp_total[None]).reshape(4, NX, NY * Z)
    return (best, evidence, moments)
```

```python
import math

import jax
import jax.numpy as jnp
from jax import lax
from jax.sharding import PartitionSpec as P

TEMPL = 48
HALF = 24


EPSILON = 1e-06
TWO_PI = 2.0 * math.pi


def padded(block, sides, width):
    for axis, dim in sides:
        count = lax.axis_size(axis)
        forward = [(i, i + 1) for i in range(count - 1)]
        backward = [(target, source) for source, target in forward]
        low = lax.ppermute(
            lax.slice_in_dim(block, block.shape[dim] - width, None, axis=dim), axis, forward
        )
        high = lax.ppermute(lax.slice_in_dim(block, 0, width, axis=dim), axis, backward)
        block = jnp.concatenate([low, block, high], axis=dim)
    return block


def twiddle(count_in, shift_in, count_out, shift_out, length, direction, factor):
    row_idx = (jnp.arange(count_in, dtype=jnp.int32) + shift_in)[:, None]
    col_idx = (jnp.arange(count_out, dtype=jnp.int32) + shift_out)[None, :]
    phase_idx = jnp.remainder(row_idx * col_idx, length).astype(jnp.float32)
    angles = phase_idx * jnp.float32(direction * TWO_PI / length)
    real_part = jnp.cos(angles) * factor
    imag_part = jnp.sin(angles) * factor
    upper_half = jnp.stack([real_part, imag_part], axis=1)
    lower_half = jnp.stack([-imag_part, real_part], axis=1)
    return jnp.stack([upper_half, lower_half], axis=0)


def product(formula, left_arr, right_arr):
    return jnp.einsum(
        formula,
        left_arr,
        right_arr,
        precision=lax.Precision.HIGH,
        preferred_element_type=jnp.float32,
    )


def forward(volume, shift, direction, lengths):
    size_x, size_y, size_z = volume.shape
    table_z = twiddle(size_z, shift, lengths[2], 0, lengths[2], direction, 1.0)[0]
    spectrum = product("xyz,zdk->dxyk", volume, table_z)
    spectrum = product(
        "cxyz,cydk->dxkz",
        spectrum,
        twiddle(size_y, shift, lengths[1], 0, lengths[1], direction, 1.0),
    )
    return product(
        "cxyz,cxdk->dkyz",
        spectrum,
        twiddle(size_x, shift, lengths[0], 0, lengths[0], direction, 1.0),
    )


def inverse(spectrum, out_x, out_y, out_z, lengths):
    spectrum = product(
        "cxyz,cxdk->dkyz",
        spectrum,
        twiddle(lengths[0], 0, out_x, HALF, lengths[0], 1, 1.0 / lengths[0]),
    )
    spectrum = product(
        "cxyz,cydk->dxkz",
        spectrum,
        twiddle(lengths[1], 0, out_y, 0, lengths[1], 1, 1.0 / lengths[1]),
    )
    real_table = twiddle(lengths[2], 0, out_z, 0, lengths[2], 1, 1.0 / lengths[2])[:, :, 0]
    return product("cxyz,czk->xyk", spectrum, real_table)


def multiply(first_arr, other_arr):
    return jnp.stack(
        [
            first_arr[0] * other_arr[0] - first_arr[1] * other_arr[1],
            first_arr[0] * other_arr[1] + first_arr[1] * other_arr[0],
        ]
    )


def ring_gather(block, axis):
    count = lax.axis_size(axis)
    if count > 16:
        return lax.all_gather(block, axis, axis=0, tiled=True)
    order = list(range(0, count, 2)) + list(range(count - 1, 0, -2))
    place = [order.index(i) for i in range(count)]
    right = [(order[i], order[(i + 1) % count]) for i in range(count)]
    left = [(target, source) for source, target in right]
    me = lax.axis_index(axis)
    my_place = jnp.array(place, jnp.int32)[me]
    order_arr = jnp.array(order, jnp.int32)
    gathered = jnp.zeros((count,) + block.shape, block.dtype)
    gathered = lax.dynamic_update_index_in_dim(gathered, block, me, 0)
    from_left, from_right = block, block
    for step in range(1, count // 2 + 1):
        from_left = lax.ppermute(from_left, axis, right)
        owner = order_arr[jnp.remainder(my_place - step + count, count)]
        gathered = lax.dynamic_update_index_in_dim(gathered, from_left, owner, 0)
        if step < count - step:
            from_right = lax.ppermute(from_right, axis, left)
            owner = order_arr[jnp.remainder(my_place + step, count)]
            gathered = lax.dynamic_update_index_in_dim(gathered, from_right, owner, 0)
    return gathered.reshape((-1,) + block.shape[1:])


def merge(first, other):
    n_a, s_a, q_a = first
    n_b, s_b, q_b = other
    mean_a = s_a / jnp.maximum(n_a, 1.0)
    mean_b = s_b / jnp.maximum(n_b, 1.0)
    total = n_a + n_b
    gap = mean_b - mean_a
    between = gap * gap * (n_a * n_b / jnp.maximum(total, 1.0))
    return total, s_a + s_b, (q_a + q_b) + between


def butterfly(state, axis):
    count = lax.axis_size(axis)
    step = 1
    while step < count:
        swap = [(i, i ^ step) for i in range(count)]
        other = lax.ppermute(jnp.stack(state), axis, swap)
        state = merge(state, (other[0], other[1], other[2]))
        step *= 2
    return state


def exchange(mine, axis):
    count = lax.axis_size(axis)
    me = lax.axis_index(axis)
    parts = [lax.dynamic_index_in_dim(mine, me, 0, keepdims=False)]
    for step in range(1, count):
        swap = [(i, i ^ step) for i in range(count)]
        piece = lax.dynamic_index_in_dim(mine, me ^ step, 0, keepdims=False)
        parts.append(lax.ppermute(piece, axis, swap))
    return parts


def local(tomogram, templates, valid, quats, rot_index):
    x_cells, voxels = tomogram.shape
    y_cells = valid.shape[1]
    z_cells = voxels // y_cells
    lengths = (x_cells + TEMPL, y_cells + HALF, z_cells + HALF)
    groups = lax.axis_size("rot")
    share_len = voxels // groups
    offset = lax.axis_index("rot") * share_len
    rots = templates.shape[0]
    widened = padded(tomogram, (("tile", 0),), HALF)
    banks = [ring_gather(templates[r], "tile") for r in range(rots)]
    one_hot = (rot_index[:, None] == jnp.arange(quats.shape[1], dtype=jnp.int32)[None, :]).astype(
        jnp.float32
    )
    orient = jnp.einsum("rq,kq->rk", one_hot, quats, precision=lax.Precision.HIGHEST)
    slab_spectrum = forward(
        widened.astype(jnp.float32).reshape(x_cells + TEMPL, y_cells, z_cells), 0, -1, lengths
    )
    inside = jnp.repeat(valid.astype(jnp.float32), z_cells, axis=1)
    count = jnp.sum(valid.astype(jnp.float32)) * z_cells

    pieces, sums, squares = [], [], []
    for r in range(rots):
        bank = banks[r].astype(jnp.float32)
        centred = bank - jnp.mean(bank)
        tmpl_spread = jnp.sqrt(jnp.mean(centred * centred) + EPSILON)
        unit = centred / (tmpl_spread * jnp.float32(TEMPL) ** 1.5)
        tmpl_spectrum = forward(unit.reshape(TEMPL, TEMPL, TEMPL), -HALF, 1, lengths)
        corr = inverse(multiply(slab_spectrum, tmpl_spectrum), x_cells, y_cells, z_cells, lengths)
        corr = corr.reshape(x_cells, voxels)
        total = jnp.sum(corr * inside)
        gap = corr - total / jnp.maximum(count, 1.0)
        sums.append(total)
        squares.append(jnp.sum(inside * gap * gap))
        pieces.append(exchange(jnp.stack(jnp.split(corr, groups, axis=1)), "rot"))

    state = (jnp.broadcast_to(count, (rots,)), jnp.stack(sums), jnp.stack(squares))
    state = butterfly(state, "tile")
    average = state[1] / state[0]
    spread = jnp.sqrt(state[2] / state[0] + EPSILON)
    packed = jnp.concatenate([average[:, None], spread[:, None], orient], axis=1)
    peers = exchange(jnp.broadcast_to(packed[None], (groups,) + packed.shape), "rot")

    scores, weights = [], []
    for g in range(groups):
        for r in range(rots):
            scores.append((pieces[r][g] - peers[g][r, 0]) / peers[g][r, 1])
            weights.append(peers[g][r, 2:])
    highest = scores[0]
    for item in scores[1:]:
        highest = jnp.maximum(highest, item)
    exps = [jnp.exp(item - highest) for item in scores]
    exp_total = sum(exps[1:], exps[0])
    moment = jnp.stack([sum(e * w[k] for e, w in zip(exps, weights)) for k in range(4)])
    inside_part = lax.dynamic_slice_in_dim(inside, offset, share_len, 1)
    best = inside_part * highest
    evidence = inside_part * (highest + jnp.log(exp_total))
    moments = inside_part[None] * moment / exp_total[None]
    return (best, evidence, moments)


def solution(mesh):
    placed = (P("tile", None), P("rot", "tile"), P("tile", None), P(), P("rot"))
    return jax.shard_map(
        local,
        mesh=mesh,
        in_specs=placed,
        out_specs=(P("tile", "rot"), P("tile", "rot"), P(None, "tile", "rot")),
        check_vma=False,
    )
```

```python
import functools
import math

import jax
import jax.numpy as jnp
import ml_dtypes
import numpy as np
from jax import lax
from jax.experimental import pallas as pl
from jax.experimental.pallas import tpu as pltpu
from jax.sharding import PartitionSpec as P

TEMPL = 48
HALF = 24
EPSILON = 1e-06
LANES = 128
SPLIT = 64
VMEM_LIMIT = 48 * 1024 * 1024
F32 = jnp.float32
BF16 = jnp.bfloat16


def two_parts(table):
    high = table.astype(ml_dtypes.bfloat16)
    low = (table - high.astype(np.float64)).astype(ml_dtypes.bfloat16)
    return high, low


def row_table(out_idx, in_idx, length, sign, factor):
    theta = 2.0 * math.pi / length * np.outer(out_idx, in_idx)
    full = np.concatenate([np.cos(theta), sign * np.sin(theta)], axis=0) * factor
    high, low = two_parts(full)
    return np.concatenate([high, high, low], axis=1)


def depth_table(in_idx, length, sign, factor):
    freq = np.arange(length // 2) + 0.5
    theta = 2.0 * math.pi / length * np.outer(in_idx, freq)
    out = np.zeros((len(in_idx), LANES))
    out[:, : length // 2] = np.cos(theta) * factor
    out[:, SPLIT : SPLIT + length // 2] = sign * np.sin(theta) * factor
    return out


def make_tables(x_cells, y_cells, z_cells):
    n_x, n_y, n_z = x_cells + TEMPL, y_cells + HALF, z_cells + HALF
    k_x, k_y = np.arange(n_x), np.arange(n_y)
    tables = {}
    slab = np.zeros((2 * z_cells, 4 * LANES), ml_dtypes.bfloat16)
    high, low = two_parts(depth_table(np.arange(z_cells), n_z, -1.0, 1.0))
    for j in range(2):
        rows = slice(j * z_cells, (j + 1) * z_cells)
        slab[rows, 2 * j * LANES : (2 * j + 1) * LANES] = high
        slab[rows, (2 * j + 1) * LANES : (2 * j + 2) * LANES] = low
    tables["slab_z"] = slab
    tables["slab_y"] = row_table(k_y, np.arange(y_cells), n_y, -1.0, 1.0)
    tables["slab_x"] = row_table(k_x, np.arange(n_x), n_x, -1.0, 1.0)
    high, low = two_parts(depth_table(np.arange(TEMPL) - HALF, n_z, 1.0, 1.0))
    tmpl = np.zeros((8, 2 * LANES, 2 * LANES), ml_dtypes.bfloat16)
    for j in range(8):
        start = TEMPL * j - (LANES if j >= 4 else 0)
        tmpl[j, start : start + TEMPL, :LANES] = high
        tmpl[j, start : start + TEMPL, LANES:] = low
    tables["tmpl_z"] = tmpl
    ones = (high.astype(np.float64) + low.astype(np.float64)).sum(axis=0)
    tables["ones_z"] = np.broadcast_to(ones.astype(np.float32)[None], (8, LANES)).copy()
    tables["tmpl_y"] = row_table(k_y, np.arange(TEMPL) - HALF, n_y, 1.0, 1.0)
    tables["tmpl_x"] = row_table(k_x, np.arange(TEMPL), n_x, 1.0, 1.0)
    tables["back_x"] = row_table(np.arange(x_cells), k_x, n_x, 1.0, 1.0 / n_x)
    tables["back_y"] = row_table(np.arange(y_cells), k_y, n_y, 1.0, 1.0 / n_y)
    back = depth_table(np.arange(z_cells), n_z, -1.0, 2.0 / n_z).T
    high, low = two_parts(back)
    back_z = np.zeros((2 * LANES, 2 * LANES), ml_dtypes.bfloat16)
    for j in range(2):
        rows = slice(j * LANES, (j + 1) * LANES)
        back_z[rows, j * z_cells : (j + 1) * z_cells] = high
        back_z[rows, LANES + j * z_cells : LANES + (j + 1) * z_cells] = low
    tables["back_z"] = back_z
    return tables


def split_rows(value):
    high = value.astype(BF16)
    if value.shape[0] % 16 == 0:
        low = (value - high.astype(F32)).astype(BF16)
        return jnp.concatenate([high, low, high], axis=0)
    high = high.astype(F32)
    return jnp.concatenate([high, value - high, high], axis=0).astype(BF16)


def swap(value):
    parts = [
        pltpu.roll(value[:, s : s + LANES], SPLIT, 1) for s in range(0, value.shape[1], LANES)
    ]
    return jnp.concatenate(parts, axis=1)


def lane_sign(width):
    lane = lax.broadcasted_iota(jnp.int32, (8, width), 1) % LANES
    return jnp.where(lane < SPLIT, -1.0, 1.0)[:1]


def complex_rows(table, value, sign):
    out = jnp.dot(table, split_rows(value), preferred_element_type=F32)
    half = out.shape[0] // 2
    return out[:half] + sign * swap(out[half:])


def pick(ref, first, count, stride):
    return jnp.concatenate(
        [ref[pl.ds(first + i, count, stride=stride), :] for i in range(2)], axis=1
    )


def store_pair(ref, first, step, value):
    rows = value.shape[0]
    for i in range(2):
        start = pl.multiple_of(first + i * step, 8)
        ref[pl.ds(start, rows), :] = value[:, i * LANES : (i + 1) * LANES]


def loop(count, unroll, body):
    def several(i, carry):
        for u in range(unroll):
            body(i * unroll + u)
        return carry

    assert count % unroll == 0
    lax.fori_loop(0, count // unroll, several, 0)


def slab_kernel(dims, slab_ref, z_ref, y_ref, x_ref, same_ref, cross_ref, depth_buf, rows_buf):
    x_cells, y_cells, z_cells = dims
    n_x, n_y = x_cells + TEMPL, y_cells + HALF
    sign = lane_sign(2 * LANES)

    def depth_step(q):
        lanes = pl.multiple_of(q * LANES, LANES)
        block = slab_ref[:, pl.ds(lanes, LANES)]
        out = jnp.dot(block, z_ref[...], preferred_element_type=F32)
        for j in range(2):
            part = out[:, 2 * j * LANES : (2 * j + 1) * LANES]
            part = part + out[:, (2 * j + 1) * LANES : (2 * j + 2) * LANES]
            start = pl.multiple_of((2 * q + j) * n_x, 8)
            depth_buf[pl.ds(start, n_x), :] = part

    loop(y_cells // 2, 4, depth_step)

    def y_step(i):
        value = pick(depth_buf, 2 * i, y_cells, n_x)
        store_pair(rows_buf, 2 * i * n_y, n_y, complex_rows(y_ref[...], value, sign))

    loop(n_x // 2, 4, y_step)

    def x_step(i):
        value = pick(rows_buf, 2 * i, n_x, n_y)
        spec = complex_rows(x_ref[...], value, sign)
        turned = swap(spec)
        real_lane = sign < 0
        same_ref[i] = jnp.where(real_lane, spec, turned)
        cross_ref[i] = jnp.where(real_lane, -turned, spec)

    loop(n_y // 2, 4, x_step)


def slab_spectrum(widened, dims, tables):
    x_cells, y_cells, z_cells = dims
    n_x, n_y = x_cells + TEMPL, y_cells + HALF
    shape = jax.ShapeDtypeStruct((n_y // 2, n_x, 2 * LANES), F32)
    vmem = pl.BlockSpec(memory_space=pltpu.VMEM)
    return pl.pallas_call(
        functools.partial(slab_kernel, dims),
        out_shape=(shape, shape),
        in_specs=[vmem] * 4,
        out_specs=(vmem, vmem),
        scratch_shapes=[
            pltpu.VMEM((y_cells * n_x, LANES), F32),
            pltpu.VMEM((n_x * n_y, LANES), F32),
        ],
        compiler_params=pltpu.CompilerParams(vmem_limit_bytes=VMEM_LIMIT),
        name="slab_spectrum",
    )(widened, tables["slab_z"], tables["slab_y"], tables["slab_x"])


def corr_kernel(
    dims, place_ref, tmpl_ref, mask_ref, same_hbm, cross_hbm,
    z_ref, ones_ref, y_ref, x_ref, bx_ref, by_ref, bz_ref,
    mine_ref, side_ref, far_ref, stat_ref,
    same_ref, cross_ref, depth_buf, rows_buf, back_buf, vol_buf, sems,
):
    x_cells, y_cells, z_cells = dims
    n_x, n_y = x_cells + TEMPL, y_cells + HALF
    copies = [
        pltpu.make_async_copy(same_hbm, same_ref, sems.at[0]),
        pltpu.make_async_copy(cross_hbm, cross_ref, sems.at[1]),
    ]
    for copy in copies:
        copy.start()
    sign = lane_sign(2 * LANES)

    tmpl = tmpl_ref[0].astype(F32)
    inv_size = 1.0 / TEMPL**3
    mean = jnp.sum(tmpl) * inv_size
    centred = tmpl - mean
    var = jnp.sum(centred * centred) * inv_size
    scale = 1.0 / (jnp.sqrt(jnp.full((1, LANES), var + EPSILON, F32)) * TEMPL**1.5)
    shift = ones_ref[:1] * mean

    wide = 8 * TEMPL
    block = jnp.concatenate(
        [tmpl_ref[0, :, g * wide : (g + 1) * wide] for g in range(TEMPL // 8)], axis=0
    )
    for j in range(8):
        window = block[:, : 2 * LANES] if j < 4 else block[:, LANES:]
        out = jnp.dot(window, z_ref[j], preferred_element_type=F32)
        part = (out[:, :LANES] + out[:, LANES:] - shift) * scale
        for g in range(TEMPL // 8):
            start = (8 * g + j) * TEMPL
            depth_buf[start : start + TEMPL, :] = part[g * TEMPL : (g + 1) * TEMPL]

    def y_step(i):
        value = pick(depth_buf, 2 * i, TEMPL, TEMPL)
        store_pair(rows_buf, 2 * i * n_y, n_y, complex_rows(y_ref[...], value, sign))

    loop(TEMPL // 2, 4, y_step)
    for copy in copies:
        copy.wait()

    def x_step(i):
        value = pick(rows_buf, 2 * i, TEMPL, n_y)
        spec = complex_rows(x_ref[...], value, sign)
        prod = spec * same_ref[i] + swap(spec) * cross_ref[i]
        store_pair(back_buf, 2 * i * x_cells, x_cells, complex_rows(bx_ref[...], prod, sign))

    loop(n_y // 2, 4, x_step)

    def back_step(i):
        value = pick(back_buf, 2 * i, n_y, x_cells)
        store_pair(vol_buf, 2 * i * y_cells, y_cells, complex_rows(by_ref[...], value, sign))

    loop(x_cells // 2, 4, back_step)

    share = y_cells // 8
    me = place_ref[0]
    total = jnp.zeros((x_cells, LANES), F32)
    number = jnp.zeros((x_cells, LANES), F32)
    targets = [mine_ref, side_ref, far_ref.at[0], far_ref.at[1]]
    for p, target in enumerate(targets):
        first = (me ^ p) * share
        for i in range(share):
            value = pick(vol_buf, 2 * (first + i), x_cells, y_cells)
            high = value.astype(BF16)
            low = (value - high.astype(F32)).astype(BF16)
            out = jnp.dot(jnp.concatenate([high, low], axis=0), bz_ref[...], preferred_element_type=F32)
            corr = out[:x_cells, :LANES] + out[:x_cells, LANES:] + out[x_cells:, :LANES]
            target[:, i * LANES : (i + 1) * LANES] = corr
            mask = mask_ref[first + i]
            total = total + corr * mask
            number = number + mask
    number_sum = jnp.sum(number)
    total_sum = jnp.sum(total)
    local_mean = jnp.full((1, LANES), total_sum, F32) / jnp.maximum(number_sum, 1.0)
    square = jnp.zeros((x_cells, LANES), F32)
    for p, target in enumerate(targets):
        first = (me ^ p) * share
        for i in range(share):
            gap = target[:, i * LANES : (i + 1) * LANES] - local_mean
            square = square + gap * gap * mask_ref[first + i]
    row = lax.broadcasted_iota(jnp.int32, (8, LANES), 0)
    stat_ref[...] = jnp.where(row == 0, number_sum, jnp.where(row == 1, total_sum, jnp.sum(square)))


def correlate(place, bank, rot, mask, same, cross, dims, tables):
    x_cells, y_cells, z_cells = dims
    n_x, n_y = x_cells + TEMPL, y_cells + HALF
    width = y_cells * z_cells // 4
    vmem = pl.BlockSpec(memory_space=pltpu.VMEM)
    anyspace = pl.BlockSpec(memory_space=pl.ANY)
    return pl.pallas_call(
        functools.partial(corr_kernel, dims),
        grid=(1,),
        out_shape=(
            jax.ShapeDtypeStruct((x_cells, width), F32),
            jax.ShapeDtypeStruct((x_cells, width), F32),
            jax.ShapeDtypeStruct((2, x_cells, width), F32),
            jax.ShapeDtypeStruct((8, LANES), F32),
        ),
        in_specs=[
            pl.BlockSpec(memory_space=pltpu.SMEM),
            pl.BlockSpec((1, TEMPL, TEMPL * TEMPL), lambda i: (rot, 0, 0)),
            vmem, anyspace, anyspace, vmem, vmem, vmem, vmem, vmem, vmem, vmem,
        ],
        out_specs=(vmem,) * 4,
        scratch_shapes=[
            pltpu.VMEM((n_y // 2, n_x, 2 * LANES), F32),
            pltpu.VMEM((n_y // 2, n_x, 2 * LANES), F32),
            pltpu.VMEM((TEMPL * TEMPL, LANES), F32),
            pltpu.VMEM((TEMPL * n_y, LANES), F32),
            pltpu.VMEM((n_y * x_cells, LANES), F32),
            pltpu.VMEM((x_cells * y_cells, LANES), F32),
            pltpu.SemaphoreType.DMA((2,)),
        ],
        compiler_params=pltpu.CompilerParams(vmem_limit_bytes=VMEM_LIMIT),
        name="correlate",
    )(
        place, bank, mask, same, cross,
        tables["tmpl_z"], tables["ones_z"], tables["tmpl_y"], tables["tmpl_x"],
        tables["back_x"], tables["back_y"], tables["back_z"],
    )


def score_kernel(groups, rots, coef_ref, mask_ref, *refs):
    pieces = refs[: len(refs) - 3]
    best_ref, evid_ref, mom_ref = refs[len(refs) - 3 :]

    def step(i):
        lanes = pl.ds(pl.multiple_of(i * LANES, LANES), LANES)
        for top in range(0, best_ref.shape[0], 8):
            rows = slice(top, top + 8)
            mask = mask_ref[i, rows]
            scores = []
            for k, piece in enumerate(pieces):
                scores.append((piece[rows, lanes] - coef_ref[k, 0]) * coef_ref[k, 1])
            high = functools.reduce(jnp.maximum, scores)
            total = jnp.zeros_like(high)
            moment = [jnp.zeros_like(high) for _ in range(4)]
            for k, score in enumerate(scores):
                weight = jnp.exp(score - high)
                total = total + weight
                for c in range(4):
                    moment[c] = moment[c] + weight * coef_ref[k, 2 + c]
            best_ref[rows, lanes] = mask * high
            evid_ref[rows, lanes] = mask * (high + jnp.log(total))
            share = mask / total
            for c in range(4):
                mom_ref[c, rows, lanes] = moment[c] * share

    loop(best_ref.shape[1] // LANES, 1, step)


def combine(coefs, mask, pieces):
    shape = pieces[0].shape
    vmem = pl.BlockSpec(memory_space=pltpu.VMEM)
    out = jax.ShapeDtypeStruct(shape, F32)
    return pl.pallas_call(
        functools.partial(score_kernel, 4, 4),
        out_shape=(out, out, jax.ShapeDtypeStruct((4,) + shape, F32)),
        in_specs=[pl.BlockSpec(memory_space=pltpu.SMEM)] + [vmem] * (1 + len(pieces)),
        out_specs=(vmem,) * 3,
        compiler_params=pltpu.CompilerParams(vmem_limit_bytes=VMEM_LIMIT),
        name="combine",
    )(coefs, mask, *pieces)


def padded(block, axis, width):
    count = lax.axis_size(axis)
    forward = [(i, i + 1) for i in range(count - 1)]
    backward = [(target, source) for source, target in forward]
    low = lax.ppermute(block[block.shape[0] - width :], axis, forward)
    high = lax.ppermute(block[:width], axis, backward)
    return jnp.concatenate([low, block, high], axis=0)


def local(tomogram, templates, valid, quats, rot_index):
    x_cells, voxels = tomogram.shape
    y_cells = valid.shape[1]
    z_cells = voxels // y_cells
    dims = (x_cells, y_cells, z_cells)
    tables = {name: jnp.asarray(table) for name, table in make_tables(*dims).items()}
    groups = lax.axis_size("rot")
    tiles = lax.axis_size("tile")
    me = lax.axis_index("rot")
    rots = templates.shape[0]

    widened = padded(tomogram, "tile", HALF)
    gathered = lax.all_gather(templates, "tile", axis=0)
    bank = jnp.transpose(gathered, (1, 0, 2)).reshape(rots, TEMPL, TEMPL * TEMPL)
    one_hot = (rot_index[:, None] == jnp.arange(quats.shape[1], dtype=jnp.int32)[None, :]).astype(F32)
    orient = jnp.einsum("rq,kq->rk", one_hot, quats, precision=lax.Precision.HIGHEST)
    place = jnp.reshape(me, (1,)).astype(jnp.int32)
    inside = jnp.repeat(valid.astype(F32), z_cells, axis=1)
    mask = jnp.transpose(inside.reshape(x_cells, voxels // LANES, LANES), (1, 0, 2))
    share_blocks = voxels // LANES // groups
    mask_part = lax.dynamic_slice_in_dim(mask, me * share_blocks, share_blocks, 0)

    same, cross = slab_spectrum(widened, dims, tables)
    far_swap = [(i, i ^ 2) for i in range(groups)]
    side_swap = [(i, i ^ 1) for i in range(groups)]
    pieces, stats = [], []
    for r in range(rots):
        mine, side, far, stat = correlate(place, bank, r, mask, same, cross, dims, tables)
        stats.append(stat[:3, 0])
        from_far = lax.ppermute(far, "rot", far_swap)
        from_side = lax.ppermute(jnp.stack([side, from_far[1]]), "rot", side_swap)
        pieces.append((mine, from_side[0], from_far[0], from_side[1]))

    packed = jnp.concatenate([jnp.stack(stats), orient], axis=1).reshape(1, rots * 7)
    packed = jnp.pad(packed, ((0, 0), (0, LANES - rots * 7)))
    everyone = lax.all_gather(packed, ("rot", "tile"), axis=0, tiled=True)
    everyone = everyone[:, : rots * 7].reshape(groups, tiles, rots, 7)
    number, total, square = everyone[..., 0], everyone[..., 1], everyone[..., 2]
    count = jnp.sum(number, axis=1)
    average = jnp.sum(total, axis=1) / count
    gap = total / jnp.maximum(number, 1.0) - average[:, None]
    spread = jnp.sqrt(jnp.sum(square + number * gap * gap, axis=1) / count + EPSILON)
    coefs = jnp.concatenate(
        [average[..., None], 1.0 / spread[..., None], everyone[:, 0, :, 3:]], axis=-1
    )
    order = jnp.arange(groups, dtype=jnp.int32) ^ me
    coefs = coefs[order].reshape(groups * rots, 6)
    flat = [pieces[r][p] for p in range(groups) for r in range(rots)]
    return combine(coefs, mask_part, flat)


def solution(mesh):
    placed = (P("tile", None), P("rot", "tile"), P("tile", None), P(), P("rot"))
    return jax.shard_map(
        local,
        mesh=mesh,
        in_specs=placed,
        out_specs=(P("tile", "rot"), P("tile", "rot"), P(None, "tile", "rot")),
        check_vma=False,
    )
```

```python
import functools
import math

import jax
import jax.numpy as jnp
import ml_dtypes
import numpy as np
from jax import lax
from jax.experimental import pallas as pl
from jax.experimental.pallas import tpu as pltpu
from jax.sharding import PartitionSpec as P

TEMPL = 48
HALF = 24
EPSILON = 1e-06
LANES = 128
SPLIT = 64
VMEM_LIMIT = 48 * 1024 * 1024
F32 = jnp.float32
BF16 = jnp.bfloat16


def two_parts(table):
    high = table.astype(ml_dtypes.bfloat16)
    low = (table - high.astype(np.float64)).astype(ml_dtypes.bfloat16)
    return high, low


def row_table(out_idx, in_idx, length, sign, factor, wide):
    theta = 2.0 * math.pi / length * np.outer(out_idx, in_idx)
    pad = np.zeros((-len(out_idx) % 8, len(in_idx)))
    full = np.concatenate([np.cos(theta), pad, sign * np.sin(theta), pad], axis=0) * factor
    high, low = two_parts(full)
    if wide:
        return np.concatenate([high, high, low], axis=1)
    zeros = np.zeros_like(low)
    return np.concatenate(
        [np.concatenate([high, high], axis=1), np.concatenate([low, zeros], axis=1)], axis=0
    )


def depth_table(in_idx, length, sign, factor):
    freq = np.arange(length // 2) + 0.5
    theta = 2.0 * math.pi / length * np.outer(in_idx, freq)
    out = np.zeros((len(in_idx), LANES))
    out[:, : length // 2] = np.cos(theta) * factor
    out[:, SPLIT : SPLIT + length // 2] = sign * np.sin(theta) * factor
    return out


def half_odd(count):
    return np.arange(count // 2) + 0.5


def make_tables(x_cells, y_cells, z_cells):
    n_x, n_y, n_z = x_cells + TEMPL, y_cells + HALF, z_cells + HALF
    k_x, k_y = half_odd(n_x), half_odd(n_y)
    both_x = np.concatenate([k_x, -k_x])
    both_y = np.stack([k_y, -k_y], axis=1).reshape(-1)
    mid_x, mid_y = (x_cells - 1) / 2, (y_cells - 1) / 2
    tables = {}
    slab = np.zeros((2 * z_cells, 4 * LANES), ml_dtypes.bfloat16)
    high, low = two_parts(depth_table(np.arange(z_cells), n_z, -1.0, 1.0))
    for j in range(2):
        rows = slice(j * z_cells, (j + 1) * z_cells)
        slab[rows, 2 * j * LANES : (2 * j + 1) * LANES] = high
        slab[rows, (2 * j + 1) * LANES : (2 * j + 2) * LANES] = low
    tables["slab_z"] = slab
    tables["slab_y"] = row_table(k_y, np.arange(y_cells), n_y, -1.0, 1.0, True)
    tables["slab_x"] = row_table(k_x, np.arange(n_x), n_x, -1.0, 1.0, True)
    high, low = two_parts(depth_table(np.arange(TEMPL) - HALF, n_z, 1.0, 1.0))
    tmpl = np.zeros((8, 2 * LANES, 2 * LANES), ml_dtypes.bfloat16)
    for j in range(8):
        start = TEMPL * j - (LANES if j >= 4 else 0)
        tmpl[j, start : start + TEMPL, :LANES] = high
        tmpl[j, start : start + TEMPL, LANES:] = low
    tables["tmpl_z"] = tmpl
    ones = (high.astype(np.float64) + low.astype(np.float64)).sum(axis=0)
    tables["ones_z"] = np.broadcast_to(ones.astype(np.float32)[None], (8, LANES)).copy()
    tables["tmpl_y"] = row_table(k_y, np.arange(TEMPL) - HALF + mid_y, n_y, 1.0, 1.0, True)
    tables["tmpl_x"] = row_table(k_x, np.arange(TEMPL) + mid_x, n_x, 1.0, 1.0, True)
    tables["back_x"] = row_table(half_odd(x_cells), both_x, n_x, 1.0, 1.0 / n_x, False)
    tables["back_y"] = row_table(half_odd(y_cells), both_y, n_y, 1.0, 1.0 / n_y, False)
    back = depth_table(np.arange(z_cells), n_z, -1.0, 2.0 / n_z).T
    high, low = two_parts(back)
    back_z = np.zeros((2 * LANES, 2 * LANES), ml_dtypes.bfloat16)
    for j in range(2):
        rows = slice(j * LANES, (j + 1) * LANES)
        back_z[rows, j * z_cells : (j + 1) * z_cells] = high
        back_z[rows, LANES + j * z_cells : LANES + (j + 1) * z_cells] = low
    tables["back_z"] = back_z
    return tables


def split_rows(value, wide):
    high = value.astype(BF16)
    if value.shape[0] % 16 == 0:
        low = (value - high.astype(F32)).astype(BF16)
        return jnp.concatenate([high, low, high] if wide else [high, low], axis=0)
    high = high.astype(F32)
    low = value - high
    return jnp.concatenate([high, low, high] if wide else [high, low], axis=0).astype(BF16)


def swap(value):
    parts = [
        pltpu.roll(value[:, s : s + LANES], SPLIT, 1) for s in range(0, value.shape[1], LANES)
    ]
    return jnp.concatenate(parts, axis=1)


def lane_sign(width):
    lane = lax.broadcasted_iota(jnp.int32, (8, width), 1) % LANES
    return jnp.where(lane < SPLIT, -1.0, 1.0)[:1]


def pair_rows(table, value, wide):
    out = jnp.dot(table, split_rows(value, wide), preferred_element_type=F32)
    if not wide:
        half = out.shape[0] // 2
        out = out[:half] + out[half:]
    half = out.shape[0] // 2
    turned = swap(out[half:]) * lane_sign(out.shape[1])
    return out[:half] + turned, out[:half] - turned


def pick(ref, firsts, count, stride):
    return jnp.concatenate([ref[pl.ds(f, count, stride=stride), :] for f in firsts], axis=1)


def store(ref, start, value):
    ref[pl.ds(pl.multiple_of(start, 8), value.shape[0]), :] = value


def lane_block(value, i):
    return value[:, i * LANES : (i + 1) * LANES]


def loop(count, body):
    def one(i, carry):
        body(i)
        return carry

    lax.fori_loop(0, count, one, 0)


GROUP = 8


def slab_kernel(dims, slab_ref, z_ref, y_ref, x_ref, same_ref, cross_ref, depth_buf, rows_buf):
    x_cells, y_cells, z_cells = dims
    n_x, n_y = x_cells + TEMPL, y_cells + HALF
    half_y = n_y // 2
    pad_y = half_y + -half_y % 8

    def depth_step(i):
        block = jnp.concatenate(
            [slab_ref[:, pl.ds(pl.multiple_of((4 * i + u) * LANES, LANES), LANES)] for u in range(4)],
            axis=0,
        )
        out = jnp.dot(block, z_ref[...], preferred_element_type=F32)
        for u in range(4):
            part = out[u * n_x : (u + 1) * n_x]
            for j in range(2):
                store(
                    depth_buf, (8 * i + 2 * u + j) * n_x,
                    lane_block(part, 2 * j) + lane_block(part, 2 * j + 1),
                )

    loop(y_cells // 8, depth_step)

    def y_step(i):
        value = pick(depth_buf, [GROUP * i + u for u in range(GROUP)], y_cells, n_x)
        plus, minus = pair_rows(y_ref[...], value, True)
        for u in range(GROUP):
            start = (GROUP * i + u) * 2 * pad_y
            store(rows_buf, start, lane_block(plus, u))
            store(rows_buf, start + pad_y, lane_block(minus, u))

    loop(n_x // GROUP, y_step)

    def x_step(i):
        firsts = [GROUP // 2 * i + u // 2 + u % 2 * pad_y for u in range(GROUP)]
        value = pick(rows_buf, firsts, n_x, 2 * pad_y)
        plus, minus = pair_rows(x_ref[...], value, True)
        spec = jnp.concatenate([plus, minus], axis=0)
        turned = swap(spec)
        real_lane = lane_sign(GROUP * LANES) < 0
        same_ref[i] = jnp.where(real_lane, spec, turned)
        cross_ref[i] = jnp.where(real_lane, -turned, spec)

    loop(n_y // GROUP, x_step)


def slab_spectrum(widened, dims, tables):
    x_cells, y_cells, z_cells = dims
    n_x, n_y = x_cells + TEMPL, y_cells + HALF
    pad_y = n_y // 2 + -(n_y // 2) % 8
    shape = jax.ShapeDtypeStruct((n_y // GROUP, n_x, GROUP * LANES), F32)
    vmem = pl.BlockSpec(memory_space=pltpu.VMEM)
    return pl.pallas_call(
        functools.partial(slab_kernel, dims),
        out_shape=(shape, shape),
        in_specs=[vmem] * 4,
        out_specs=(vmem, vmem),
        scratch_shapes=[
            pltpu.VMEM((y_cells * n_x, LANES), F32),
            pltpu.VMEM((n_x * 2 * pad_y, LANES), F32),
        ],
        compiler_params=pltpu.CompilerParams(vmem_limit_bytes=VMEM_LIMIT),
        cost_estimate=pl.CostEstimate(flops=10**10, bytes_accessed=10**7, transcendentals=0),
        name="slab_spectrum",
    )(widened, tables["slab_z"], tables["slab_y"], tables["slab_x"])


def corr_kernel(
    dims, place_ref, tmpl_ref, mask_ref, same_hbm, cross_hbm,
    z_ref, ones_ref, y_ref, x_ref, bx_ref, by_ref, bz_ref,
    mine_ref, side_ref, far_ref, stat_ref,
    same_ref, cross_ref, depth_buf, rows_buf, back_buf, vol_buf, sems,
):
    x_cells, y_cells, z_cells = dims
    n_x, n_y = x_cells + TEMPL, y_cells + HALF
    half_y = n_y // 2
    pad_y = half_y + -half_y % 8
    copies = [
        pltpu.make_async_copy(same_hbm, same_ref, sems.at[0]),
        pltpu.make_async_copy(cross_hbm, cross_ref, sems.at[1]),
    ]
    for copy in copies:
        copy.start()

    tmpl = tmpl_ref[0].astype(F32)
    inv_size = 1.0 / TEMPL**3
    mean = jnp.sum(tmpl) * inv_size
    centred = tmpl - mean
    var = jnp.sum(centred * centred) * inv_size
    scale = 1.0 / (jnp.sqrt(jnp.full((1, LANES), var + EPSILON, F32)) * TEMPL**1.5)
    shift = ones_ref[:1] * mean

    wide = 8 * TEMPL
    block = jnp.concatenate(
        [tmpl_ref[0, :, g * wide : (g + 1) * wide] for g in range(TEMPL // 8)], axis=0
    )
    for j in range(8):
        window = block[:, : 2 * LANES] if j < 4 else block[:, LANES:]
        out = jnp.dot(window, z_ref[j], preferred_element_type=F32)
        part = (out[:, :LANES] + out[:, LANES:] - shift) * scale
        for g in range(TEMPL // 8):
            start = (8 * g + j) * TEMPL
            depth_buf[start : start + TEMPL, :] = part[g * TEMPL : (g + 1) * TEMPL]

    def y_step(i):
        value = pick(depth_buf, [GROUP * i + u for u in range(GROUP)], TEMPL, TEMPL)
        plus, minus = pair_rows(y_ref[...], value, True)
        for u in range(GROUP):
            start = (GROUP * i + u) * 2 * pad_y
            store(rows_buf, start, lane_block(plus, u))
            store(rows_buf, start + pad_y, lane_block(minus, u))

    loop(TEMPL // GROUP, y_step)
    for copy in copies:
        copy.wait()

    def x_step(i):
        firsts = [GROUP // 2 * i + u // 2 + u % 2 * pad_y for u in range(GROUP)]
        value = pick(rows_buf, firsts, TEMPL, 2 * pad_y)
        plus, minus = pair_rows(x_ref[...], value, True)
        spec = jnp.concatenate([plus, minus], axis=0)
        prod = spec * same_ref[i] + swap(spec) * cross_ref[i]
        plus, minus = pair_rows(bx_ref[...], prod, False)
        for u in range(GROUP):
            start = (GROUP * i + u) * x_cells
            store(back_buf, start, lane_block(plus, u))
            store(back_buf, start + x_cells // 2, lane_block(minus, u))

    loop(n_y // GROUP, x_step)

    def back_step(i):
        value = pick(back_buf, [GROUP * i + u for u in range(GROUP)], n_y, x_cells)
        plus, minus = pair_rows(by_ref[...], value, False)
        for u in range(GROUP):
            row = GROUP * i + u
            x = jnp.where(row < x_cells // 2, row + x_cells // 2, x_cells - 1 - row)
            store(vol_buf, x * y_cells, lane_block(plus, u))
            store(vol_buf, x * y_cells + y_cells // 2, lane_block(minus, u))

    loop(x_cells // GROUP, back_step)

    share = y_cells // 8
    me = place_ref[0]
    total = jnp.zeros((x_cells, LANES), F32)
    number = jnp.zeros((x_cells, LANES), F32)
    targets = [mine_ref, side_ref, far_ref.at[0], far_ref.at[1]]
    for p, target in enumerate(targets):
        first = (me ^ p) * share
        values = []
        for i in range(share):
            firsts = []
            for j in range(2):
                y = 2 * (first + i) + j
                firsts.append(jnp.where(y < y_cells // 2, y_cells - 1 - y, y - y_cells // 2))
            values.append(pick(vol_buf, firsts, x_cells, y_cells))
        value = jnp.concatenate(values, axis=0)
        out = jnp.dot(split_rows(value, False), bz_ref[...], preferred_element_type=F32)
        rows = value.shape[0]
        full = out[:rows, :LANES] + out[:rows, LANES:] + out[rows:, :LANES]
        for i in range(share):
            corr = full[i * x_cells : (i + 1) * x_cells]
            target[:, i * LANES : (i + 1) * LANES] = corr
            mask = mask_ref[first + i]
            total = total + corr * mask
            number = number + mask
    number_sum = jnp.sum(number)
    total_sum = jnp.sum(total)
    local_mean = jnp.full((1, LANES), total_sum, F32) / jnp.maximum(number_sum, 1.0)
    square = jnp.zeros((x_cells, LANES), F32)
    for p, target in enumerate(targets):
        first = (me ^ p) * share
        for i in range(share):
            gap = target[:, i * LANES : (i + 1) * LANES] - local_mean
            square = square + gap * gap * mask_ref[first + i]
    row = lax.broadcasted_iota(jnp.int32, (8, LANES), 0)
    stat_ref[...] = jnp.where(row == 0, number_sum, jnp.where(row == 1, total_sum, jnp.sum(square)))


def correlate(place, bank, rot, mask, same, cross, dims, tables):
    x_cells, y_cells, z_cells = dims
    n_x, n_y = x_cells + TEMPL, y_cells + HALF
    pad_y = n_y // 2 + -(n_y // 2) % 8
    width = y_cells * z_cells // 4
    vmem = pl.BlockSpec(memory_space=pltpu.VMEM)
    anyspace = pl.BlockSpec(memory_space=pl.ANY)
    return pl.pallas_call(
        functools.partial(corr_kernel, dims),
        grid=(1,),
        out_shape=(
            jax.ShapeDtypeStruct((x_cells, width), F32),
            jax.ShapeDtypeStruct((x_cells, width), F32),
            jax.ShapeDtypeStruct((2, x_cells, width), F32),
            jax.ShapeDtypeStruct((8, LANES), F32),
        ),
        in_specs=[
            pl.BlockSpec(memory_space=pltpu.SMEM),
            pl.BlockSpec((1, TEMPL, TEMPL * TEMPL), lambda i: (rot, 0, 0)),
            vmem, anyspace, anyspace, vmem, vmem, vmem, vmem, vmem, vmem, vmem,
        ],
        out_specs=(vmem,) * 4,
        scratch_shapes=[
            pltpu.VMEM((n_y // GROUP, n_x, GROUP * LANES), F32),
            pltpu.VMEM((n_y // GROUP, n_x, GROUP * LANES), F32),
            pltpu.VMEM((TEMPL * TEMPL, LANES), F32),
            pltpu.VMEM((TEMPL * 2 * pad_y, LANES), F32),
            pltpu.VMEM((n_y * x_cells, LANES), F32),
            pltpu.VMEM((x_cells * y_cells, LANES), F32),
            pltpu.SemaphoreType.DMA((2,)),
        ],
        compiler_params=pltpu.CompilerParams(vmem_limit_bytes=VMEM_LIMIT),
        cost_estimate=pl.CostEstimate(flops=15 * 10**9, bytes_accessed=10**7, transcendentals=0),
        name="correlate",
    )(
        place, bank, mask, same, cross,
        tables["tmpl_z"], tables["ones_z"], tables["tmpl_y"], tables["tmpl_x"],
        tables["back_x"], tables["back_y"], tables["back_z"],
    )


def score_kernel(coef_ref, mask_ref, *refs):
    pieces = refs[: len(refs) - 3]
    best_ref, evid_ref, mom_ref = refs[len(refs) - 3 :]

    def step(i):
        lanes = pl.ds(pl.multiple_of(i * LANES, LANES), LANES)
        for top in range(0, best_ref.shape[0], 8):
            rows = slice(top, top + 8)
            mask = mask_ref[i, rows]
            scores = []
            for k, piece in enumerate(pieces):
                scores.append((piece[rows, lanes] - coef_ref[k, 0]) * coef_ref[k, 1])
            high = functools.reduce(jnp.maximum, scores)
            total = jnp.zeros_like(high)
            moment = [jnp.zeros_like(high) for _ in range(4)]
            for k, score in enumerate(scores):
                weight = jnp.exp(score - high)
                total = total + weight
                for c in range(4):
                    moment[c] = moment[c] + weight * coef_ref[k, 2 + c]
            best_ref[rows, lanes] = mask * high
            evid_ref[rows, lanes] = mask * (high + jnp.log(total))
            share = mask / total
            for c in range(4):
                mom_ref[c, rows, lanes] = moment[c] * share

    loop(best_ref.shape[1] // LANES, step)


def combine(coefs, mask, pieces):
    shape = pieces[0].shape
    vmem = pl.BlockSpec(memory_space=pltpu.VMEM)
    out = jax.ShapeDtypeStruct(shape, F32)
    return pl.pallas_call(
        score_kernel,
        out_shape=(out, out, jax.ShapeDtypeStruct((4,) + shape, F32)),
        in_specs=[pl.BlockSpec(memory_space=pltpu.SMEM)] + [vmem] * (1 + len(pieces)),
        out_specs=(vmem,) * 3,
        compiler_params=pltpu.CompilerParams(vmem_limit_bytes=VMEM_LIMIT),
        name="combine",
    )(coefs, mask, *pieces)


def doubling_gather(block, axis):
    count = lax.axis_size(axis)
    me = lax.axis_index(axis)
    steps = [1 << i for i in reversed(range(count.bit_length() - 1))]
    block = block[None]
    for step in steps:
        other = lax.ppermute(block, axis, [(i, i ^ step) for i in range(count)])
        upper = (me & step) != 0
        pair = [jnp.where(upper, other, block), jnp.where(upper, block, other)]
        block = jnp.stack(pair, axis=1).reshape((-1,) + block.shape[1:])
    return block


def merge(first, other):
    mean_a = first[1] / jnp.maximum(first[0], 1.0)
    mean_b = other[1] / jnp.maximum(other[0], 1.0)
    number = first[0] + other[0]
    gap = mean_b - mean_a
    between = gap * gap * (first[0] * other[0] / jnp.maximum(number, 1.0))
    return jnp.stack([number, first[1] + other[1], (first[2] + other[2]) + between])


def padded(block, axis, width):
    count = lax.axis_size(axis)
    forward = [(i, i + 1) for i in range(count - 1)]
    backward = [(target, source) for source, target in forward]
    low = lax.ppermute(block[block.shape[0] - width :], axis, forward)
    high = lax.ppermute(block[:width], axis, backward)
    return jnp.concatenate([low, block, high], axis=0)


def local(tomogram, templates, valid, quats, rot_index):
    x_cells, voxels = tomogram.shape
    y_cells = valid.shape[1]
    z_cells = voxels // y_cells
    dims = (x_cells, y_cells, z_cells)
    tables = {name: jnp.asarray(table) for name, table in make_tables(*dims).items()}
    groups = lax.axis_size("rot")
    tiles = lax.axis_size("tile")
    me = lax.axis_index("rot")
    rots = templates.shape[0]

    widened = padded(tomogram, "tile", HALF)
    gathered = doubling_gather(templates, "tile")
    bank = jnp.transpose(gathered, (1, 0, 2)).reshape(rots, TEMPL, TEMPL * TEMPL)
    one_hot = (rot_index[:, None] == jnp.arange(quats.shape[1], dtype=jnp.int32)[None, :]).astype(F32)
    orient = jnp.einsum("rq,kq->rk", one_hot, quats, precision=lax.Precision.HIGHEST)
    place = jnp.reshape(me, (1,)).astype(jnp.int32)
    inside = jnp.repeat(valid.astype(F32), z_cells, axis=1)
    mask = jnp.transpose(inside.reshape(x_cells, voxels // LANES, LANES), (1, 0, 2))
    share_blocks = voxels // LANES // groups
    mask_part = lax.dynamic_slice_in_dim(mask, me * share_blocks, share_blocks, 0)

    same, cross = slab_spectrum(widened, dims, tables)
    far_swap = [(i, i ^ 2) for i in range(groups)]
    side_swap = [(i, i ^ 1) for i in range(groups)]
    mines, sides, fars, from_sides, stats = [], [], [], [], []
    for r in range(rots):
        if r >= 2:
            place, fars[r - 2] = lax.optimization_barrier((place, fars[r - 2]))
        if r >= 3:
            place, from_sides[r - 3] = lax.optimization_barrier((place, from_sides[r - 3]))
        mine, side, far, stat = correlate(place, bank, r, mask, same, cross, dims, tables)
        if r >= 1 and r < rots - 1:
            both = jnp.stack([sides[r - 1], fars[r - 1][1]])
        mines.append(mine)
        sides.append(side)
        stats.append(stat[:3, 0])
        fars.append(lax.ppermute(far, "rot", far_swap))
        if r >= 1 and r < rots - 1:
            from_sides.append(lax.ppermute(both, "rot", side_swap))
    state = jnp.stack(stats, axis=1)
    state, fars[rots - 2], from_sides[rots - 3] = lax.optimization_barrier(
        (state, fars[rots - 2], from_sides[rots - 3])
    )
    step = 1
    while step < tiles:
        swap_pairs = [(i, i ^ step) for i in range(tiles)]
        state = merge(state, lax.ppermute(state, "tile", swap_pairs))
        step *= 2
    average = state[1] / state[0]
    inverse = 1.0 / jnp.sqrt(state[2] / state[0] + EPSILON)
    coefs = jnp.concatenate([average[:, None], inverse[:, None], orient], axis=1)[None]
    from_far = lax.ppermute(coefs, "rot", far_swap)
    coefs = jnp.concatenate([coefs, from_far], axis=0)
    from_side = lax.ppermute(coefs, "rot", side_swap)
    coefs = jnp.stack([coefs[0], from_side[0], coefs[1], from_side[1]])
    last = [part for r in range(rots - 2, rots) for part in (sides[r], fars[r][1])]
    last = lax.ppermute(jnp.stack(last), "rot", side_swap)
    from_sides += [last[:2], last[2:]]
    flat = mines + [f[0] for f in from_sides] + [f[0] for f in fars] + [f[1] for f in from_sides]
    return combine(coefs.reshape(groups * rots, 6), mask_part, flat)


def solution(mesh):
    placed = (P("tile", None), P("rot", "tile"), P("tile", None), P(), P("rot"))
    return jax.shard_map(
        local,
        mesh=mesh,
        in_specs=placed,
        out_specs=(P("tile", "rot"), P("tile", "rot"), P(None, "tile", "rot")),
        check_vma=False,
    )
```

```python
import functools
import math

import jax
import jax.numpy as jnp
import ml_dtypes
import numpy as np
from jax import lax
from jax.experimental import pallas as pl
from jax.experimental.pallas import tpu as pltpu
from jax.sharding import PartitionSpec as P

TEMPL = 48
HALF = 24
EPSILON = 1e-06
LANES = 128
SPLIT = 64
VMEM_LIMIT = 48 * 1024 * 1024
F32 = jnp.float32
BF16 = jnp.bfloat16


def two_parts(table):
    high = table.astype(ml_dtypes.bfloat16)
    low = (table - high.astype(np.float64)).astype(ml_dtypes.bfloat16)
    return high, low


def row_table(out_idx, in_idx, length, sign, factor, wide):
    theta = 2.0 * math.pi / length * np.outer(out_idx, in_idx)
    pad = np.zeros((-len(out_idx) % 8, len(in_idx)))
    full = np.concatenate([np.cos(theta), pad, sign * np.sin(theta), pad], axis=0) * factor
    high, low = two_parts(full)
    if wide:
        return np.concatenate([high, high, low], axis=1)
    zeros = np.zeros_like(low)
    return np.concatenate(
        [np.concatenate([high, high], axis=1), np.concatenate([low, zeros], axis=1)], axis=0
    )


def depth_table(in_idx, length, sign, factor):
    freq = np.arange(length // 2) + 0.5
    theta = 2.0 * math.pi / length * np.outer(in_idx, freq)
    out = np.zeros((len(in_idx), LANES))
    out[:, : length // 2] = np.cos(theta) * factor
    out[:, SPLIT : SPLIT + length // 2] = sign * np.sin(theta) * factor
    return out


def half_odd(count):
    return np.arange(count // 2) + 0.5


def make_tables(x_cells, y_cells, z_cells):
    n_x, n_y, n_z = x_cells + TEMPL, y_cells + HALF, z_cells + HALF
    k_x, k_y = half_odd(n_x), half_odd(n_y)
    both_x = np.concatenate([k_x, -k_x])
    both_y = np.stack([k_y, -k_y], axis=1).reshape(-1)
    mid_x, mid_y = (x_cells - 1) / 2, (y_cells - 1) / 2
    tables = {}
    slab = np.zeros((2 * z_cells, 4 * LANES), ml_dtypes.bfloat16)
    high, low = two_parts(depth_table(np.arange(z_cells), n_z, -1.0, 1.0))
    for j in range(2):
        rows = slice(j * z_cells, (j + 1) * z_cells)
        slab[rows, 2 * j * LANES : (2 * j + 1) * LANES] = high
        slab[rows, (2 * j + 1) * LANES : (2 * j + 2) * LANES] = low
    tables["slab_z"] = slab
    tables["slab_y"] = row_table(k_y, np.arange(y_cells), n_y, -1.0, 1.0, True)
    own = np.arange(HALF, HALF + x_cells)
    halo = np.concatenate([np.arange(HALF), np.arange(HALF + x_cells, n_x)])
    tables["slab_x"] = row_table(k_x, np.concatenate([own, halo]), n_x, -1.0, 1.0, True)
    high, low = two_parts(depth_table(np.arange(TEMPL) - HALF, n_z, 1.0, 1.0))
    tmpl = np.zeros((8, 2 * LANES, 2 * LANES), ml_dtypes.bfloat16)
    for j in range(8):
        start = TEMPL * j - (LANES if j >= 4 else 0)
        tmpl[j, start : start + TEMPL, :LANES] = high
        tmpl[j, start : start + TEMPL, LANES:] = low
    tables["tmpl_z"] = tmpl
    ones = (high.astype(np.float64) + low.astype(np.float64)).sum(axis=0)
    tables["ones_z"] = np.broadcast_to(ones.astype(np.float32)[None], (8, LANES)).copy()
    tables["tmpl_y"] = row_table(k_y, np.arange(TEMPL) - HALF + mid_y, n_y, 1.0, 1.0, True)
    tables["tmpl_x"] = row_table(k_x, np.arange(TEMPL) + mid_x, n_x, 1.0, 1.0, True)
    tables["back_x"] = row_table(half_odd(x_cells), both_x, n_x, 1.0, 1.0 / n_x, False)
    tables["back_y"] = row_table(half_odd(y_cells), both_y, n_y, 1.0, 1.0 / n_y, False)
    back = depth_table(np.arange(z_cells), n_z, -1.0, 2.0 / n_z).T
    high, low = two_parts(back)
    back_z = np.zeros((2 * LANES, 2 * LANES), ml_dtypes.bfloat16)
    for j in range(2):
        rows = slice(j * LANES, (j + 1) * LANES)
        back_z[rows, j * z_cells : (j + 1) * z_cells] = high
        back_z[rows, LANES + j * z_cells : LANES + (j + 1) * z_cells] = low
    tables["back_z"] = back_z
    return tables


def split_rows(value, wide):
    high = value.astype(BF16)
    if value.shape[0] % 16 == 0:
        low = (value - high.astype(F32)).astype(BF16)
        return jnp.concatenate([high, low, high] if wide else [high, low], axis=0)
    high = high.astype(F32)
    low = value - high
    return jnp.concatenate([high, low, high] if wide else [high, low], axis=0).astype(BF16)


def swap(value):
    parts = [
        pltpu.roll(value[:, s : s + LANES], SPLIT, 1) for s in range(0, value.shape[1], LANES)
    ]
    return jnp.concatenate(parts, axis=1)


def lane_sign(width):
    lane = lax.broadcasted_iota(jnp.int32, (8, width), 1) % LANES
    return jnp.where(lane < SPLIT, -1.0, 1.0)[:1]


def pair_rows(table, value, wide):
    return pair_dot(table, split_rows(value, wide), wide)


def pair_dot(table, parts, wide):
    out = jnp.dot(table, parts, preferred_element_type=F32)
    if not wide:
        half = out.shape[0] // 2
        out = out[:half] + out[half:]
    half = out.shape[0] // 2
    turned = swap(out[half:]) * lane_sign(out.shape[1])
    return out[:half] + turned, out[:half] - turned


def pick(ref, firsts, count, stride):
    return jnp.concatenate([ref[pl.ds(f, count, stride=stride), :] for f in firsts], axis=1)


def store(ref, start, value):
    ref[pl.ds(pl.multiple_of(start, 8), value.shape[0]), :] = value


def lane_block(value, i):
    return value[:, i * LANES : (i + 1) * LANES]


def loop(count, body):
    def one(i, carry):
        body(i)
        return carry

    lax.fori_loop(0, count, one, 0)


GROUP = 8


def slab_rows_kernel(dims, *refs):
    slab_refs, (z_ref, y_ref, rows_ref, depth_buf) = refs[:-4], refs[-4:]
    x_cells, y_cells, z_cells = dims
    count = sum(ref.shape[0] for ref in slab_refs)
    n_y = y_cells + HALF
    pad_y = n_y // 2 + -(n_y // 2) % 8
    many = 4

    def depth_step(i):
        top = 0
        for ref in slab_refs:
            size = ref.shape[0]
            lanes = [pl.ds(pl.multiple_of((many * i + u) * LANES, LANES), LANES) for u in range(many)]
            block = jnp.concatenate([ref[:, l].astype(F32) for l in lanes], axis=0).astype(BF16)
            out = jnp.dot(block, z_ref[...], preferred_element_type=F32)
            for u in range(many):
                part = out[u * size : (u + 1) * size]
                for j in range(2):
                    store(
                        depth_buf, (2 * many * i + 2 * u + j) * count + top,
                        lane_block(part, 2 * j) + lane_block(part, 2 * j + 1),
                    )
            top += size

    loop(y_cells // (2 * many), depth_step)

    def y_step(i):
        value = pick(depth_buf, [GROUP * i + u for u in range(GROUP)], y_cells, count)
        plus, minus = pair_rows(y_ref[...], value, True)
        for u in range(GROUP):
            start = (GROUP * i + u) * 2 * pad_y
            store(rows_ref, start, lane_block(plus, u))
            store(rows_ref, start + pad_y, lane_block(minus, u))

    loop(count // GROUP, y_step)


def slab_rows(blocks, dims, tables, name):
    x_cells, y_cells, z_cells = dims
    count = sum(block.shape[0] for block in blocks)
    n_y = y_cells + HALF
    pad_y = n_y // 2 + -(n_y // 2) % 8
    vmem = pl.BlockSpec(memory_space=pltpu.VMEM)
    return pl.pallas_call(
        functools.partial(slab_rows_kernel, dims),
        out_shape=jax.ShapeDtypeStruct((count * 2 * pad_y, LANES), F32),
        in_specs=[vmem] * (2 + len(blocks)),
        out_specs=vmem,
        scratch_shapes=[pltpu.VMEM((y_cells * count, LANES), F32)],
        compiler_params=pltpu.CompilerParams(vmem_limit_bytes=VMEM_LIMIT),
        cost_estimate=pl.CostEstimate(flops=count * 10**8, bytes_accessed=10**6, transcendentals=0),
        name=name,
    )(*blocks, tables["slab_z"], tables["slab_y"])


def slab_x_kernel(dims, own_ref, halo_ref, x_ref, spec_ref):
    x_cells, y_cells, z_cells = dims
    n_y = y_cells + HALF
    pad_y = n_y // 2 + -(n_y // 2) % 8

    def x_step(i):
        firsts = [GROUP // 2 * i + u // 2 + u % 2 * pad_y for u in range(GROUP)]
        value = jnp.concatenate(
            [
                pick(own_ref, firsts, x_cells, 2 * pad_y),
                pick(halo_ref, firsts, TEMPL, 2 * pad_y),
            ],
            axis=0,
        )
        plus, minus = pair_rows(x_ref[...], value, True)
        spec = jnp.concatenate([plus, minus], axis=0)
        turned = swap(spec)
        real_lane = lane_sign(GROUP * LANES) < 0
        spec_ref[i, 0] = jnp.where(real_lane, spec, turned)
        spec_ref[i, 1] = jnp.where(real_lane, -turned, spec)

    loop(n_y // GROUP, x_step)


def slab_x(own, halo, dims, tables):
    x_cells, y_cells, z_cells = dims
    n_x, n_y = x_cells + TEMPL, y_cells + HALF
    vmem = pl.BlockSpec(memory_space=pltpu.VMEM)
    return pl.pallas_call(
        functools.partial(slab_x_kernel, dims),
        out_shape=jax.ShapeDtypeStruct((n_y // GROUP, 2, n_x, GROUP * LANES), F32),
        in_specs=[vmem] * 3,
        out_specs=vmem,
        compiler_params=pltpu.CompilerParams(vmem_limit_bytes=VMEM_LIMIT),
        cost_estimate=pl.CostEstimate(flops=5 * 10**9, bytes_accessed=10**6, transcendentals=0),
        name="slab_x",
    )(own, halo, tables["slab_x"])


def corr_kernel(
    dims, rot, place_ref, tmpl_ref, mask_ref, spec_hbm,
    z_ref, ones_ref, y_ref, x_ref, bx_ref, by_ref, bz_ref,
    mine_ref, side_ref, far_ref, stat_ref,
    spec_ref, depth_buf, rows_buf, first_buf, second_buf, back_buf, vol_buf, sem,
):
    x_cells, y_cells, z_cells = dims
    n_x, n_y = x_cells + TEMPL, y_cells + HALF
    half_y = n_y // 2
    pad_y = half_y + -half_y % 8
    copy = pltpu.make_async_copy(spec_hbm, spec_ref, sem)
    copy.start()

    each = TEMPL // 8
    rows = slice(rot * each, (rot + 1) * each)
    tmpl = jnp.concatenate([tmpl_ref[t, rows, :] for t in range(8)], axis=0)
    inv_size = 1.0 / TEMPL**3
    mean = jnp.sum(tmpl) * inv_size
    centred = tmpl - mean
    var = jnp.sum(centred * centred) * inv_size
    scale = 1.0 / (jnp.sqrt(jnp.full((1, LANES), var + EPSILON, F32)) * TEMPL**1.5)
    shift = ones_ref[:1] * mean

    wide = 8 * TEMPL
    narrow = tmpl.astype(BF16)
    block = jnp.concatenate(
        [narrow[:, g * wide : (g + 1) * wide] for g in range(TEMPL // 8)], axis=0
    )
    for j in range(8):
        window = block[:, : 2 * LANES] if j < 4 else block[:, LANES:]
        out = jnp.dot(window, z_ref[j], preferred_element_type=F32)
        part = (out[:, :LANES] + out[:, LANES:] - shift) * scale
        for g in range(TEMPL // 8):
            start = (8 * g + j) * TEMPL
            depth_buf[start : start + TEMPL, :] = part[g * TEMPL : (g + 1) * TEMPL]

    def y_step(i):
        for i in (2 * i, 2 * i + 1):
            value = pick(depth_buf, [GROUP * i + u for u in range(GROUP)], TEMPL, TEMPL)
            plus, minus = pair_rows(y_ref[...], value, True)
            for u in range(GROUP):
                start = (GROUP * i + u) * 2 * pad_y
                store(rows_buf, start, lane_block(plus, u))
                store(rows_buf, start + pad_y, lane_block(minus, u))

    loop(TEMPL // GROUP // 2, y_step)
    copy.wait()

    def gather_rows(i):
        firsts = [GROUP // 2 * i + u // 2 + u % 2 * pad_y for u in range(GROUP)]
        first_buf[...] = split_rows(pick(rows_buf, firsts, TEMPL, 2 * pad_y), True)

    def multiply(i):
        plus, minus = pair_dot(x_ref[...], first_buf[...], True)
        spec = jnp.concatenate([plus, minus], axis=0)
        prod = spec * spec_ref[i, 0] + swap(spec) * spec_ref[i, 1]
        second_buf[...] = split_rows(prod, False)

    def back_x(i):
        plus, minus = pair_dot(bx_ref[...], second_buf[...], False)
        for u in range(GROUP):
            start = (GROUP * i + u) * x_cells
            store(back_buf, start, lane_block(plus, u))
            store(back_buf, start + x_cells // 2, lane_block(minus, u))

    steps = n_y // GROUP
    gather_rows(0)
    multiply(0)
    gather_rows(1)

    def pipelined(i):
        back_x(i)
        multiply(i + 1)
        gather_rows(i + 2)

    loop(steps - 2, pipelined)
    back_x(steps - 2)
    multiply(steps - 1)
    back_x(steps - 1)

    def back_step(i):
        for i in (2 * i, 2 * i + 1):
            value = pick(back_buf, [GROUP * i + u for u in range(GROUP)], n_y, x_cells)
            plus, minus = pair_rows(by_ref[...], value, False)
            for u in range(GROUP):
                row = GROUP * i + u
                x = jnp.where(row < x_cells // 2, row + x_cells // 2, x_cells - 1 - row)
                store(vol_buf, x * y_cells, lane_block(plus, u))
                store(vol_buf, x * y_cells + y_cells // 2, lane_block(minus, u))

    loop(x_cells // GROUP // 2, back_step)

    share = y_cells // 8
    me = place_ref[0]
    total = jnp.zeros((x_cells, LANES), F32)
    number = jnp.zeros((x_cells, LANES), F32)
    targets = [mine_ref, side_ref, far_ref.at[0], far_ref.at[1]]
    for p, target in enumerate(targets):
        first = (me ^ p) * share
        values = []
        for i in range(share):
            firsts = []
            for j in range(2):
                y = 2 * (first + i) + j
                firsts.append(jnp.where(y < y_cells // 2, y_cells - 1 - y, y - y_cells // 2))
            values.append(pick(vol_buf, firsts, x_cells, y_cells))
        value = jnp.concatenate(values, axis=0)
        out = jnp.dot(split_rows(value, False), bz_ref[...], preferred_element_type=F32)
        rows = value.shape[0]
        full = out[:rows, :LANES] + out[:rows, LANES:] + out[rows:, :LANES]
        for i in range(share):
            corr = full[i * x_cells : (i + 1) * x_cells]
            target[:, i * LANES : (i + 1) * LANES] = corr
            mask = mask_ref[first + i]
            total = total + corr * mask
            number = number + mask
    number_sum = jnp.sum(number)
    total_sum = jnp.sum(total)
    local_mean = jnp.full((1, LANES), total_sum, F32) / jnp.maximum(number_sum, 1.0)
    square = jnp.zeros((x_cells, LANES), F32)
    for p, target in enumerate(targets):
        first = (me ^ p) * share
        for i in range(share):
            gap = target[:, i * LANES : (i + 1) * LANES] - local_mean
            square = square + gap * gap * mask_ref[first + i]
    row = lax.broadcasted_iota(jnp.int32, (8, LANES), 0)
    stat_ref[...] = jnp.where(row == 0, number_sum, jnp.where(row == 1, total_sum, jnp.sum(square)))


def correlate(place, bank, rot, mask, spec, dims, tables):
    x_cells, y_cells, z_cells = dims
    n_x, n_y = x_cells + TEMPL, y_cells + HALF
    pad_y = n_y // 2 + -(n_y // 2) % 8
    width = y_cells * z_cells // 4
    vmem = pl.BlockSpec(memory_space=pltpu.VMEM)
    return pl.pallas_call(
        functools.partial(corr_kernel, dims, rot),
        out_shape=(
            jax.ShapeDtypeStruct((x_cells, width), F32),
            jax.ShapeDtypeStruct((x_cells, width), F32),
            jax.ShapeDtypeStruct((2, x_cells, width), F32),
            jax.ShapeDtypeStruct((8, LANES), F32),
        ),
        in_specs=[pl.BlockSpec(memory_space=pltpu.SMEM), vmem, vmem]
        + [pl.BlockSpec(memory_space=pl.ANY)] + [vmem] * 7,
        out_specs=(vmem,) * 4,
        scratch_shapes=[
            pltpu.VMEM(spec.shape, F32),
            pltpu.VMEM((TEMPL * TEMPL, LANES), F32),
            pltpu.VMEM((TEMPL * 2 * pad_y, LANES), F32),
            pltpu.VMEM((3 * TEMPL, GROUP * LANES), BF16),
            pltpu.VMEM((2 * n_x, GROUP * LANES), BF16),
            pltpu.VMEM((n_y * x_cells, LANES), F32),
            pltpu.VMEM((x_cells * y_cells, LANES), F32),
            pltpu.SemaphoreType.DMA,
        ],
        compiler_params=pltpu.CompilerParams(vmem_limit_bytes=VMEM_LIMIT),
        cost_estimate=pl.CostEstimate(flops=15 * 10**9, bytes_accessed=10**7, transcendentals=0),
        name="correlate",
    )(
        place, bank, mask, spec,
        tables["tmpl_z"], tables["ones_z"], tables["tmpl_y"], tables["tmpl_x"],
        tables["back_x"], tables["back_y"], tables["back_z"],
    )


def score_kernel(coef_ref, mask_ref, *refs):
    pieces = refs[: len(refs) - 3]
    best_ref, evid_ref, mom_ref = refs[len(refs) - 3 :]

    def step(i):
        lanes = pl.ds(pl.multiple_of(i * LANES, LANES), LANES)
        for top in range(0, best_ref.shape[0], 8):
            rows = slice(top, top + 8)
            mask = mask_ref[i, rows]
            scores = []
            for k, piece in enumerate(pieces):
                scores.append((piece[rows, lanes] - coef_ref[k, 0]) * coef_ref[k, 1])
            high = functools.reduce(jnp.maximum, scores)
            total = jnp.zeros_like(high)
            moment = [jnp.zeros_like(high) for _ in range(4)]
            for k, score in enumerate(scores):
                weight = jnp.exp(score - high)
                total = total + weight
                for c in range(4):
                    moment[c] = moment[c] + weight * coef_ref[k, 2 + c]
            best_ref[rows, lanes] = mask * high
            evid_ref[rows, lanes] = mask * (high + jnp.log(total))
            share = mask / total
            for c in range(4):
                mom_ref[c, rows, lanes] = moment[c] * share

    loop(best_ref.shape[1] // LANES, step)


def combine(coefs, mask, pieces):
    shape = pieces[0].shape
    vmem = pl.BlockSpec(memory_space=pltpu.VMEM)
    out = jax.ShapeDtypeStruct(shape, F32)
    return pl.pallas_call(
        score_kernel,
        out_shape=(out, out, jax.ShapeDtypeStruct((4,) + shape, F32)),
        in_specs=[pl.BlockSpec(memory_space=pltpu.SMEM)] + [vmem] * (1 + len(pieces)),
        out_specs=(vmem,) * 3,
        compiler_params=pltpu.CompilerParams(vmem_limit_bytes=VMEM_LIMIT),
        name="combine",
    )(coefs, mask, *pieces)


def gather_steps(count):
    return [1 << i for i in reversed(range(count.bit_length() - 1))]


def gather_step(block, axis, step):
    count = lax.axis_size(axis)
    other = lax.ppermute(block, axis, [(i, i ^ step) for i in range(count)])
    upper = (lax.axis_index(axis) & step) != 0
    pair = [jnp.where(upper, other, block), jnp.where(upper, block, other)]
    return jnp.stack(pair, axis=1).reshape((-1,) + block.shape[1:])


def merge(first, other):
    mean_a = first[1] / jnp.maximum(first[0], 1.0)
    mean_b = other[1] / jnp.maximum(other[0], 1.0)
    number = first[0] + other[0]
    gap = mean_b - mean_a
    between = gap * gap * (first[0] * other[0] / jnp.maximum(number, 1.0))
    return jnp.stack([number, first[1] + other[1], (first[2] + other[2]) + between])


def halos(block, axis, width):
    count = lax.axis_size(axis)
    forward = [(i, i + 1) for i in range(count - 1)]
    backward = [(target, source) for source, target in forward]
    low = lax.ppermute(block[block.shape[0] - width :], axis, forward)
    high = lax.ppermute(block[:width], axis, backward)
    return low, high


def local(tomogram, templates, valid, quats, rot_index):
    x_cells, voxels = tomogram.shape
    y_cells = valid.shape[1]
    z_cells = voxels // y_cells
    dims = (x_cells, y_cells, z_cells)
    tables = {name: jnp.asarray(table) for name, table in make_tables(*dims).items()}
    groups = lax.axis_size("rot")
    tiles = lax.axis_size("tile")
    me = lax.axis_index("rot")
    rots = templates.shape[0]

    low, high = halos(tomogram, "tile", HALF)
    row = TEMPL * TEMPL
    chunk = templates.shape[1]
    whole_rows = chunk % row == 0
    block = templates.reshape(rots * chunk // row, row) if whole_rows else templates
    block = block[None]
    steps = gather_steps(tiles)
    for step in steps[:-1]:
        block = gather_step(block, "tile", step)
    one_hot = (rot_index[:, None] == jnp.arange(quats.shape[1], dtype=jnp.int32)[None, :]).astype(F32)
    orient = jnp.einsum("rq,kq->rk", one_hot, quats, precision=lax.Precision.HIGHEST)
    place = jnp.reshape(me, (1,)).astype(jnp.int32)
    inside = jnp.repeat(valid.astype(F32), z_cells, axis=1)
    mask = jnp.transpose(inside.reshape(x_cells, voxels // LANES, LANES), (1, 0, 2))
    share_blocks = voxels // LANES // groups
    mask_part = lax.dynamic_slice_in_dim(mask, me * share_blocks, share_blocks, 0)

    own = slab_rows([tomogram], dims, tables, "slab_own")
    halo = slab_rows([low, high], dims, tables, "slab_halo")
    spec = slab_x(own, halo, dims, tables)
    block = gather_step(block, "tile", steps[-1])
    if not whole_rows:
        block = jnp.transpose(block, (1, 0, 2)).reshape(rots, 8, TEMPL // 8, row)
        block = jnp.transpose(block, (1, 0, 2, 3))
    bank = block.reshape(8, rots * (TEMPL // 8), row).astype(F32)
    far_swap = [(i, i ^ 2) for i in range(groups)]
    side_swap = [(i, i ^ 1) for i in range(groups)]
    mines, sides, fars, from_sides, stats = [], [], [], [], []
    for r in range(rots):
        if r >= 2:
            place, fars[r - 2] = lax.optimization_barrier((place, fars[r - 2]))
        if r >= 3:
            place, from_sides[r - 3] = lax.optimization_barrier((place, from_sides[r - 3]))
        mine, side, far, stat = correlate(place, bank, r, mask, spec, dims, tables)
        if r >= 1:
            stat, fars[r - 1] = lax.optimization_barrier((stat, fars[r - 1]))
        if r >= 1 and r < rots - 1:
            both = jnp.stack([sides[r - 1], fars[r - 1][1]])
        mines.append(mine)
        sides.append(side)
        stats.append(stat[:3, 0])
        fars.append(lax.ppermute(far, "rot", far_swap))
        if r >= 1 and r < rots - 1:
            from_sides.append(lax.ppermute(both, "rot", side_swap))
    state = jnp.stack(stats, axis=1)
    state, fars[rots - 2], from_sides[rots - 3] = lax.optimization_barrier(
        (state, fars[rots - 2], from_sides[rots - 3])
    )
    step = 1
    while step < tiles:
        swap_pairs = [(i, i ^ step) for i in range(tiles)]
        state = merge(state, lax.ppermute(state, "tile", swap_pairs))
        step *= 2
    average = state[1] / state[0]
    inverse = 1.0 / jnp.sqrt(state[2] / state[0] + EPSILON)
    coefs = jnp.concatenate([average[:, None], inverse[:, None], orient], axis=1)[None]
    from_far = lax.ppermute(coefs, "rot", far_swap)
    coefs = jnp.concatenate([coefs, from_far], axis=0)
    from_side = lax.ppermute(coefs, "rot", side_swap)
    coefs = jnp.stack([coefs[0], from_side[0], coefs[1], from_side[1]])
    last = [part for r in range(rots - 2, rots) for part in (sides[r], fars[r][1])]
    last = lax.ppermute(jnp.stack(last), "rot", side_swap)
    from_sides += [last[:2], last[2:]]
    flat = mines + [f[0] for f in from_sides] + [f[0] for f in fars] + [f[1] for f in from_sides]
    return combine(coefs.reshape(groups * rots, 6), mask_part, flat)


def solution(mesh):
    placed = (P("tile", None), P("rot", "tile"), P("tile", None), P(), P("rot"))
    return jax.shard_map(
        local,
        mesh=mesh,
        in_specs=placed,
        out_specs=(P("tile", "rot"), P("tile", "rot"), P(None, "tile", "rot")),
        check_vma=False,
    )
```

```python
import functools
import math

import jax
import jax.numpy as jnp
import ml_dtypes
import numpy as np
from jax import lax
from jax.experimental import pallas as pl
from jax.experimental.pallas import tpu as pltpu
from jax.sharding import PartitionSpec as P

TEMPL = 48
HALF = 24
EPSILON = 1e-06
LANES = 128
SPLIT = 64
F32 = jnp.float32
BF16 = jnp.bfloat16


def two_parts(table):
    high = table.astype(ml_dtypes.bfloat16)
    low = (table - high.astype(np.float64)).astype(ml_dtypes.bfloat16)
    return high, low


def row_table(out_idx, in_idx, length, sign, factor, wide):
    theta = 2.0 * math.pi / length * np.outer(out_idx, in_idx)
    pad = np.zeros((-len(out_idx) % 8, len(in_idx)))
    full = np.concatenate([np.cos(theta), pad, sign * np.sin(theta), pad], axis=0) * factor
    high, low = two_parts(full)
    if wide:
        return np.concatenate([high, high, low], axis=1)
    zeros = np.zeros_like(low)
    return np.concatenate(
        [np.concatenate([high, high], axis=1), np.concatenate([low, zeros], axis=1)], axis=0
    )


def depth_table(in_idx, length, sign, factor):
    freq = np.arange(length // 2) + 0.5
    theta = 2.0 * math.pi / length * np.outer(in_idx, freq)
    out = np.zeros((len(in_idx), LANES))
    out[:, : length // 2] = np.cos(theta) * factor
    out[:, SPLIT : SPLIT + length // 2] = sign * np.sin(theta) * factor
    return out


def half_odd(count):
    return np.arange(count // 2) + 0.5


def make_tables(x_cells, y_cells, z_cells):
    n_x, n_y, n_z = x_cells + TEMPL, y_cells + HALF, z_cells + HALF
    k_x, k_y = half_odd(n_x), half_odd(n_y)
    both_x = np.concatenate([k_x, -k_x])
    both_y = np.stack([k_y, -k_y], axis=1).reshape(-1)
    mid_x, mid_y = (x_cells - 1) / 2, (y_cells - 1) / 2
    tables = {}
    slab = np.zeros((2 * z_cells, 4 * LANES), ml_dtypes.bfloat16)
    high, low = two_parts(depth_table(np.arange(z_cells), n_z, -1.0, 1.0))
    for j in range(2):
        rows = slice(j * z_cells, (j + 1) * z_cells)
        slab[rows, 2 * j * LANES : (2 * j + 1) * LANES] = high
        slab[rows, (2 * j + 1) * LANES : (2 * j + 2) * LANES] = low
    tables["slab_z"] = slab
    tables["slab_y"] = row_table(k_y, np.arange(y_cells), n_y, -1.0, 1.0, True)
    own = np.arange(HALF, HALF + x_cells)
    halo = np.concatenate([np.arange(HALF), np.arange(HALF + x_cells, n_x)])
    tables["slab_x"] = row_table(k_x, np.concatenate([own, halo]), n_x, -1.0, 1.0, True)
    high, low = two_parts(depth_table(np.arange(TEMPL) - HALF, n_z, 1.0, 1.0))
    tmpl = np.zeros((8, 2 * LANES, 2 * LANES), ml_dtypes.bfloat16)
    for j in range(8):
        start = TEMPL * j - (LANES if j >= 4 else 0)
        tmpl[j, start : start + TEMPL, :LANES] = high
        tmpl[j, start : start + TEMPL, LANES:] = low
    tables["tmpl_z"] = tmpl
    ones = (high.astype(np.float64) + low.astype(np.float64)).sum(axis=0)
    tables["ones_z"] = np.broadcast_to(ones.astype(np.float32)[None], (8, LANES)).copy()
    tables["tmpl_y"] = row_table(k_y, np.arange(TEMPL) - HALF + mid_y, n_y, 1.0, 1.0, True)
    tables["tmpl_x"] = row_table(k_x, np.arange(TEMPL) + mid_x, n_x, 1.0, 1.0, True)
    tables["back_x"] = row_table(half_odd(x_cells), both_x, n_x, 1.0, 1.0 / n_x, False)
    tables["back_y"] = row_table(half_odd(y_cells), both_y, n_y, 1.0, 1.0 / n_y, False)
    back = depth_table(np.arange(z_cells), n_z, -1.0, 2.0 / n_z).T
    high, low = two_parts(back)
    back_z = np.zeros((2 * LANES, 2 * LANES), ml_dtypes.bfloat16)
    for j in range(2):
        rows = slice(j * LANES, (j + 1) * LANES)
        back_z[rows, j * z_cells : (j + 1) * z_cells] = high
        back_z[rows, LANES + j * z_cells : LANES + (j + 1) * z_cells] = low
    tables["back_z"] = back_z
    return tables


def split_rows(value, wide):
    high = value.astype(BF16)
    if value.shape[0] % 16 == 0:
        low = (value - high.astype(F32)).astype(BF16)
        return jnp.concatenate([high, low, high] if wide else [high, low], axis=0)
    high = high.astype(F32)
    low = value - high
    return jnp.concatenate([high, low, high] if wide else [high, low], axis=0).astype(BF16)


def swap(value):
    parts = [
        pltpu.roll(value[:, s : s + LANES], SPLIT, 1) for s in range(0, value.shape[1], LANES)
    ]
    return jnp.concatenate(parts, axis=1)


def lane_sign(width):
    lane = lax.broadcasted_iota(jnp.int32, (8, width), 1) % LANES
    return jnp.where(lane < SPLIT, -1.0, 1.0)[:1]


def pair_rows(table, value, wide):
    return pair_dot(table, split_rows(value, wide), wide)


def pair_dot(table, parts, wide):
    out = jnp.dot(table, parts, preferred_element_type=F32)
    if not wide:
        half = out.shape[0] // 2
        out = out[:half] + out[half:]
    half = out.shape[0] // 2
    turned = swap(out[half:]) * lane_sign(out.shape[1])
    return out[:half] + turned, out[:half] - turned


def pick(ref, firsts, count, stride):
    return jnp.concatenate([ref[pl.ds(f, count, stride=stride), :] for f in firsts], axis=1)


def store(ref, start, value):
    ref[pl.ds(pl.multiple_of(start, 8), value.shape[0]), :] = value


def lane_block(value, i):
    return value[:, i * LANES : (i + 1) * LANES]


def loop(count, body):
    def one(i, carry):
        body(i)
        return carry

    lax.fori_loop(0, count, one, 0)


GROUP = 8


def pipeline(steps, stages, width):
    blocks = -(-steps // width)
    depth = len(stages)

    def turn(t, static):
        for s in reversed(range(depth)):
            if static and not 0 <= t - s < blocks:
                continue
            for slot in range(width):
                step = (t - s) * width + slot
                if not static or step < steps:
                    stages[s](step, slot)

    full = steps // width
    first, last = depth - 1, max(full, depth - 1)
    for t in range(first):
        turn(t, True)
    if last - first >= 2:
        loop(last - first, lambda i: turn(i + first, False))
    else:
        last = first
    for t in range(last, blocks + depth - 1):
        turn(t, True)


def slab_rows_kernel(dims, row_slices, *refs):
    parts = len(row_slices)
    slab_refs, refs = refs[:parts], refs[parts:]
    if parts == 1:
        valid_ref, z_ref, y_ref, rows_ref, mask_ref, depth_buf, parts_buf = refs
    else:
        z_ref, y_ref, rows_ref, depth_buf, parts_buf = refs
    x_cells, y_cells, z_cells = dims
    count = sum(stop - start for start, stop in row_slices)
    n_y = y_cells + HALF
    pad_y = n_y // 2 + -(n_y // 2) % 8
    many = 4

    if parts == 1:
        valid = valid_ref[...].astype(F32)
        low_lane = lax.broadcasted_iota(jnp.int32, (x_cells, LANES), 1) < z_cells
        for q in range(y_cells // 2):
            mask_ref[q] = jnp.where(low_lane, valid[:, 2 * q : 2 * q + 1], valid[:, 2 * q + 1 : 2 * q + 2])

    def depth_step(i):
        top = 0
        for ref, (start, stop) in zip(slab_refs, row_slices):
            size = stop - start
            lanes = [pl.ds(pl.multiple_of((many * i + u) * LANES, LANES), LANES) for u in range(many)]
            block = jnp.concatenate([ref[:, l].astype(F32)[start:stop] for l in lanes], axis=0)
            out = jnp.dot(block.astype(BF16), z_ref[...], preferred_element_type=F32)
            for u in range(many):
                part = out[u * size : (u + 1) * size]
                for j in range(2):
                    store(
                        depth_buf, (2 * many * i + 2 * u + j) * count + top,
                        lane_block(part, 2 * j) + lane_block(part, 2 * j + 1),
                    )
            top += size

    loop(y_cells // (2 * many), depth_step)

    def gather_rows(i, slot):
        value = pick(depth_buf, [GROUP * i + u for u in range(GROUP)], y_cells, count)
        parts_buf[slot] = split_rows(value, True)

    def y_step(i, slot):
        plus, minus = pair_dot(y_ref[...], parts_buf[slot], True)
        for u in range(GROUP):
            start = (GROUP * i + u) * 2 * pad_y
            store(rows_ref, start, lane_block(plus, u))
            store(rows_ref, start + pad_y, lane_block(minus, u))

    pipeline(count // GROUP, [gather_rows, y_step], 2)


def slab_rows(blocks, row_slices, valid, dims, tables, name):
    x_cells, y_cells, z_cells = dims
    count = sum(stop - start for start, stop in row_slices)
    n_y = y_cells + HALF
    pad_y = n_y // 2 + -(n_y // 2) % 8
    vmem = pl.BlockSpec(memory_space=pltpu.VMEM)
    out_shape = [jax.ShapeDtypeStruct((count * 2 * pad_y, LANES), F32)]
    if valid is not None:
        blocks = blocks + [valid]
        out_shape.append(jax.ShapeDtypeStruct((y_cells // 2, x_cells, LANES), F32))
    return pl.pallas_call(
        functools.partial(slab_rows_kernel, dims, row_slices),
        out_shape=tuple(out_shape),
        in_specs=[vmem] * (2 + len(blocks)),
        out_specs=(vmem,) * len(out_shape),
        scratch_shapes=[
            pltpu.VMEM((y_cells * count, LANES), F32),
            pltpu.VMEM((2, 3 * y_cells, GROUP * LANES), BF16),
        ],
        compiler_params=pltpu.CompilerParams(vmem_limit_bytes=20 * 1024 * 1024),
        cost_estimate=pl.CostEstimate(flops=count * 10**8, bytes_accessed=10**6, transcendentals=0),
        name=name,
    )(*blocks, tables["slab_z"], tables["slab_y"])


def slab_x_kernel(dims, own_ref, halo_ref, x_ref, out_hbm, spec_buf, parts_buf, sems):
    x_cells, y_cells, z_cells = dims
    n_y = y_cells + HALF
    pad_y = n_y // 2 + -(n_y // 2) % 8
    steps = n_y // GROUP

    def send(i):
        return pltpu.make_async_copy(spec_buf.at[i], out_hbm.at[i], sems.at[i])

    def gather_rows(i, slot):
        firsts = [GROUP // 2 * i + u // 2 + u % 2 * pad_y for u in range(GROUP)]
        value = jnp.concatenate(
            [
                pick(own_ref, firsts, x_cells, 2 * pad_y),
                pick(halo_ref, firsts, TEMPL, 2 * pad_y),
            ],
            axis=0,
        )
        parts_buf[slot] = split_rows(value, True)

    def x_step(i, slot):
        plus, minus = pair_dot(x_ref[...], parts_buf[slot], True)
        spec = jnp.concatenate([plus, minus], axis=0)
        turned = swap(spec)
        real_lane = lane_sign(GROUP * LANES) < 0
        spec_buf[i, 0] = jnp.where(real_lane, spec, turned)
        spec_buf[i, 1] = jnp.where(real_lane, -turned, spec)
        send(i).start()

    pipeline(steps, [gather_rows, x_step], 2)
    loop(steps, lambda i: send(i).wait())


def slab_x(own, halo, dims, tables):
    x_cells, y_cells, z_cells = dims
    n_x, n_y = x_cells + TEMPL, y_cells + HALF
    steps = n_y // GROUP
    vmem = pl.BlockSpec(memory_space=pltpu.VMEM)
    shape = (steps, 2, n_x, GROUP * LANES)
    return pl.pallas_call(
        functools.partial(slab_x_kernel, dims),
        out_shape=jax.ShapeDtypeStruct(shape, F32),
        in_specs=[vmem] * 3,
        out_specs=pl.BlockSpec(memory_space=pl.ANY),
        scratch_shapes=[
            pltpu.VMEM(shape, F32),
            pltpu.VMEM((2, 3 * n_x, GROUP * LANES), BF16),
            pltpu.SemaphoreType.DMA((steps,)),
        ],
        compiler_params=pltpu.CompilerParams(vmem_limit_bytes=24 * 1024 * 1024),
        cost_estimate=pl.CostEstimate(flops=5 * 10**9, bytes_accessed=10**6, transcendentals=0),
        name="slab_x",
    )(own, halo, tables["slab_x"])


def corr_kernel(
    dims, rot, place_ref, tmpl_ref, mask_ref, spec_hbm,
    z_ref, ones_ref, y_ref, x_ref, bx_ref, by_ref, bz_ref,
    mine_ref, side_ref, far_ref, stat_ref,
    spec_ref, depth_buf, rows_buf, first_buf, second_buf, third_buf, back_buf, vol_buf, sem,
):
    x_cells, y_cells, z_cells = dims
    n_x, n_y = x_cells + TEMPL, y_cells + HALF
    half_y = n_y // 2
    pad_y = half_y + -half_y % 8
    copy = pltpu.make_async_copy(spec_hbm, spec_ref, sem)
    copy.start()

    each = TEMPL // 8
    rows = slice(rot * each, (rot + 1) * each)
    tmpl = jnp.concatenate([tmpl_ref[t, rows, :] for t in range(8)], axis=0)
    inv_size = 1.0 / TEMPL**3
    mean = jnp.sum(tmpl) * inv_size
    centred = tmpl - mean
    var = jnp.sum(centred * centred) * inv_size
    scale = 1.0 / (jnp.sqrt(jnp.full((1, LANES), var + EPSILON, F32)) * TEMPL**1.5)
    shift = ones_ref[:1] * mean

    wide = 8 * TEMPL
    narrow = tmpl.astype(BF16)
    block = jnp.concatenate(
        [narrow[:, g * wide : (g + 1) * wide] for g in range(TEMPL // 8)], axis=0
    )
    for j in range(8):
        window = block[:, : 2 * LANES] if j < 4 else block[:, LANES:]
        out = jnp.dot(window, z_ref[j], preferred_element_type=F32)
        part = out[:, :LANES] + out[:, LANES:] - shift
        for g in range(TEMPL // 8):
            start = (8 * g + j) * TEMPL
            depth_buf[start : start + TEMPL, :] = part[g * TEMPL : (g + 1) * TEMPL]

    def gather_a(i, slot):
        value = pick(depth_buf, [GROUP * i + u for u in range(GROUP)], TEMPL, TEMPL)
        first_buf[slot] = split_rows(value, True)

    def y_step(i, slot):
        plus, minus = pair_dot(y_ref[...], first_buf[slot], True)
        for u in range(GROUP):
            start = (GROUP * i + u) * 2 * pad_y
            store(rows_buf, start, lane_block(plus, u))
            store(rows_buf, start + pad_y, lane_block(minus, u))

    pipeline(TEMPL // GROUP, [gather_a, y_step], 2)
    copy.wait()

    def gather_ky(i, slot):
        firsts = [GROUP // 2 * i + u // 2 + u % 2 * pad_y for u in range(GROUP)]
        first_buf[slot] = split_rows(pick(rows_buf, firsts, TEMPL, 2 * pad_y), True)

    def multiply(i, slot):
        plus, minus = pair_dot(x_ref[...], first_buf[slot], True)
        spec = jnp.concatenate([plus, minus], axis=0)
        prod = spec * spec_ref[i, 0] + swap(spec) * spec_ref[i, 1]
        second_buf[slot] = split_rows(prod, False)

    def back_x(i, slot):
        plus, minus = pair_dot(bx_ref[...], second_buf[slot], False)
        for u in range(GROUP):
            start = (GROUP * i + u) * x_cells
            store(back_buf, start, lane_block(plus, u))
            store(back_buf, start + x_cells // 2, lane_block(minus, u))

    pipeline(n_y // GROUP, [gather_ky, multiply, back_x], 2)

    def gather_x(i, slot):
        value = pick(back_buf, [GROUP * i + u for u in range(GROUP)], n_y, x_cells)
        third_buf[slot] = split_rows(value, False)

    def back_y(i, slot):
        plus, minus = pair_dot(by_ref[...], third_buf[slot], False)
        for u in range(GROUP):
            row = GROUP * i + u
            x = jnp.where(row < x_cells // 2, row + x_cells // 2, x_cells - 1 - row)
            store(vol_buf, x * y_cells, lane_block(plus, u))
            store(vol_buf, x * y_cells + y_cells // 2, lane_block(minus, u))

    pipeline(x_cells // GROUP, [gather_x, back_y], 2)

    share = y_cells // 8
    me = place_ref[0]
    total = jnp.zeros((x_cells, LANES), F32)
    number = jnp.zeros((x_cells, LANES), F32)
    targets = [mine_ref, side_ref, far_ref.at[0], far_ref.at[1]]
    for p, target in enumerate(targets):
        first = (me ^ p) * share
        values = []
        for i in range(share):
            firsts = []
            for j in range(2):
                y = 2 * (first + i) + j
                firsts.append(jnp.where(y < y_cells // 2, y_cells - 1 - y, y - y_cells // 2))
            values.append(pick(vol_buf, firsts, x_cells, y_cells))
        value = jnp.concatenate(values, axis=0)
        out = jnp.dot(split_rows(value, False), bz_ref[...], preferred_element_type=F32)
        rows = value.shape[0]
        full = out[:rows, :LANES] + out[:rows, LANES:] + out[rows:, :LANES]
        for i in range(share):
            corr = full[i * x_cells : (i + 1) * x_cells] * scale
            target[:, i * LANES : (i + 1) * LANES] = corr
            mask = mask_ref[first + i]
            total = total + corr * mask
            number = number + mask
    number_sum = jnp.sum(number)
    total_sum = jnp.sum(total)
    local_mean = jnp.full((1, LANES), total_sum, F32) / jnp.maximum(number_sum, 1.0)
    square = jnp.zeros((x_cells, LANES), F32)
    for p, target in enumerate(targets):
        first = (me ^ p) * share
        for i in range(share):
            gap = target[:, i * LANES : (i + 1) * LANES] - local_mean
            square = square + gap * gap * mask_ref[first + i]
    row = lax.broadcasted_iota(jnp.int32, (8, LANES), 0)
    stat_ref[...] = jnp.where(row == 0, number_sum, jnp.where(row == 1, total_sum, jnp.sum(square)))


def correlate(place, bank, rot, mask, spec, dims, tables):
    x_cells, y_cells, z_cells = dims
    n_x, n_y = x_cells + TEMPL, y_cells + HALF
    pad_y = n_y // 2 + -(n_y // 2) % 8
    width = y_cells * z_cells // 4
    vmem = pl.BlockSpec(memory_space=pltpu.VMEM)
    return pl.pallas_call(
        functools.partial(corr_kernel, dims, rot),
        out_shape=(
            jax.ShapeDtypeStruct((x_cells, width), F32),
            jax.ShapeDtypeStruct((x_cells, width), F32),
            jax.ShapeDtypeStruct((2, x_cells, width), F32),
            jax.ShapeDtypeStruct((8, LANES), F32),
        ),
        in_specs=[pl.BlockSpec(memory_space=pltpu.SMEM), vmem, vmem]
        + [pl.BlockSpec(memory_space=pl.ANY)] + [vmem] * 7,
        out_specs=(vmem,) * 4,
        scratch_shapes=[
            pltpu.VMEM(spec.shape, F32),
            pltpu.VMEM((TEMPL * TEMPL, LANES), F32),
            pltpu.VMEM((TEMPL * 2 * pad_y, LANES), F32),
            pltpu.VMEM((2, 3 * TEMPL, GROUP * LANES), BF16),
            pltpu.VMEM((2, 2 * n_x, GROUP * LANES), BF16),
            pltpu.VMEM((2, 2 * n_y, GROUP * LANES), BF16),
            pltpu.VMEM((n_y * x_cells, LANES), F32),
            pltpu.VMEM((x_cells * y_cells, LANES), F32),
            pltpu.SemaphoreType.DMA,
        ],
        compiler_params=pltpu.CompilerParams(vmem_limit_bytes=32 * 1024 * 1024),
        cost_estimate=pl.CostEstimate(flops=15 * 10**9, bytes_accessed=10**7, transcendentals=0),
        name="correlate",
    )(
        place, bank, mask, spec,
        tables["tmpl_z"], tables["ones_z"], tables["tmpl_y"], tables["tmpl_x"],
        tables["back_x"], tables["back_y"], tables["back_z"],
    )


def score_kernel(place_ref, coef_ref, mask_ref, *refs):
    pieces = refs[: len(refs) - 3]
    best_ref, evid_ref, mom_ref = refs[len(refs) - 3 :]

    blocks = best_ref.shape[1] // LANES

    def step(i):
        lanes = pl.ds(pl.multiple_of(i * LANES, LANES), LANES)
        for top in range(0, best_ref.shape[0], 8):
            rows = slice(top, top + 8)
            mask = mask_ref[place_ref[0] * blocks + i, rows]
            scores = []
            for k, piece in enumerate(pieces):
                scores.append((piece[rows, lanes] - coef_ref[k, 0]) * coef_ref[k, 1])
            high = functools.reduce(jnp.maximum, scores)
            total = jnp.zeros_like(high)
            moment = [jnp.zeros_like(high) for _ in range(4)]
            for k, score in enumerate(scores):
                weight = jnp.exp(score - high)
                total = total + weight
                for c in range(4):
                    moment[c] = moment[c] + weight * coef_ref[k, 2 + c]
            best_ref[rows, lanes] = mask * high
            evid_ref[rows, lanes] = mask * (high + jnp.log(total))
            share = mask / total
            for c in range(4):
                mom_ref[c, rows, lanes] = moment[c] * share

    loop(blocks, step)


def combine(place, coefs, mask, pieces):
    shape = pieces[0].shape
    vmem = pl.BlockSpec(memory_space=pltpu.VMEM)
    out = jax.ShapeDtypeStruct(shape, F32)
    return pl.pallas_call(
        score_kernel,
        out_shape=(out, out, jax.ShapeDtypeStruct((4,) + shape, F32)),
        in_specs=[pl.BlockSpec(memory_space=pltpu.SMEM)] * 2 + [vmem] * (1 + len(pieces)),
        out_specs=(vmem,) * 3,
        compiler_params=pltpu.CompilerParams(vmem_limit_bytes=16 * 1024 * 1024),
        name="combine",
    )(place, coefs, mask, *pieces)


def gather_steps(count):
    return [1 << i for i in reversed(range(count.bit_length() - 1))]


def gather_step(block, axis, step):
    count = lax.axis_size(axis)
    other = lax.ppermute(block, axis, [(i, i ^ step) for i in range(count)])
    upper = (lax.axis_index(axis) & step) != 0
    pair = [jnp.where(upper, other, block), jnp.where(upper, block, other)]
    return jnp.stack(pair, axis=1).reshape((-1,) + block.shape[1:])


def merge(parts):
    number, total, square = parts[:, 0], parts[:, 1], parts[:, 2]
    all_number = jnp.sum(number, axis=0)
    all_total = jnp.sum(total, axis=0)
    gap = total / jnp.maximum(number, 1.0) - all_total / jnp.maximum(all_number, 1.0)
    return jnp.stack([all_number, all_total, jnp.sum(square + number * gap * gap, axis=0)])


def exchange_all(block, axis, low, high):
    count = lax.axis_size(axis)
    parts = [block]
    for step in range(low, high, low):
        parts.append(lax.ppermute(block, axis, [(i, i ^ step) for i in range(count)]))
    return jnp.stack(parts)


def neighbours(block, axis):
    count = lax.axis_size(axis)
    forward = [(i, i + 1) for i in range(count - 1)]
    backward = [(target, source) for source, target in forward]
    return lax.ppermute(block, axis, forward), lax.ppermute(block, axis, backward)


def local(tomogram, templates, valid, quats, rot_index):
    x_cells, voxels = tomogram.shape
    y_cells = valid.shape[1]
    z_cells = voxels // y_cells
    dims = (x_cells, y_cells, z_cells)
    tables = {name: jnp.asarray(table) for name, table in make_tables(*dims).items()}
    groups = lax.axis_size("rot")
    tiles = lax.axis_size("tile")
    me = lax.axis_index("rot")
    rots = templates.shape[0]

    row = TEMPL * TEMPL
    chunk = templates.shape[1]
    whole_rows = chunk % row == 0
    block = templates.reshape(rots * chunk // row, row) if whole_rows else templates
    block = block[None]
    steps = gather_steps(tiles)
    block = gather_step(block, "tile", steps[0])
    low, high = neighbours(tomogram, "tile")
    for step in steps[1:-1]:
        block = gather_step(block, "tile", step)
    one_hot = (rot_index[:, None] == jnp.arange(quats.shape[1], dtype=jnp.int32)[None, :]).astype(F32)
    orient = jnp.einsum("rq,kq->rk", one_hot, quats, precision=lax.Precision.HIGHEST)
    place = me_place = jnp.reshape(me, (1,)).astype(jnp.int32)
    own, mask = slab_rows([tomogram], [(0, x_cells)], valid, dims, tables, "slab_own")
    (halo,) = slab_rows(
        [low, high], [(x_cells - HALF, x_cells), (0, HALF)], None, dims, tables, "slab_halo"
    )
    spec = slab_x(own, halo, dims, tables)
    block = gather_step(block, "tile", steps[-1])
    if not whole_rows:
        block = jnp.transpose(block, (1, 0, 2)).reshape(rots, 8, TEMPL // 8, row)
        block = jnp.transpose(block, (1, 0, 2, 3))
    bank = block.reshape(8, rots * (TEMPL // 8), row).astype(F32)
    far_swap = [(i, i ^ 2) for i in range(groups)]
    side_swap = [(i, i ^ 1) for i in range(groups)]
    mines, sides, fars, from_sides, stats = [], [], [], [], []
    for r in range(rots):
        if r >= 2:
            place, fars[r - 2] = lax.optimization_barrier((place, fars[r - 2]))
        if r >= 3:
            place, from_sides[r - 3] = lax.optimization_barrier((place, from_sides[r - 3]))
        mine, side, far, stat = correlate(place, bank, r, mask, spec, dims, tables)
        if r >= 1:
            stat, fars[r - 1] = lax.optimization_barrier((stat, fars[r - 1]))
        if r >= 1 and r < rots - 1:
            both = jnp.stack([sides[r - 1], fars[r - 1][1]])
        mines.append(mine)
        sides.append(side)
        stats.append(stat[:3, 0])
        fars.append(lax.ppermute(far, "rot", far_swap))
        if r >= 1 and r < rots - 1:
            from_sides.append(lax.ppermute(both, "rot", side_swap))
    state = jnp.stack(stats, axis=1)
    state, fars[rots - 2], from_sides[rots - 3] = lax.optimization_barrier(
        (state, fars[rots - 2], from_sides[rots - 3])
    )
    step = 1
    while step < tiles:
        following = min(step * 8, tiles)
        state = merge(exchange_all(state, "tile", step, following))
        step = following
    average = state[1] / state[0]
    inverse = 1.0 / jnp.sqrt(state[2] / state[0] + EPSILON)
    coefs = jnp.concatenate([average[:, None], inverse[:, None], orient], axis=1)
    coefs = exchange_all(coefs, "rot", 1, groups)
    last = [part for r in range(rots - 2, rots) for part in (sides[r], fars[r][1])]
    last = lax.ppermute(jnp.stack(last), "rot", side_swap)
    from_sides += [last[:2], last[2:]]
    flat = mines + [f[0] for f in from_sides] + [f[0] for f in fars] + [f[1] for f in from_sides]
    return combine(me_place, coefs.reshape(groups * rots, 6), mask, flat)


def solution(mesh):
    placed = (P("tile", None), P("rot", "tile"), P("tile", None), P(), P("rot"))
    return jax.shard_map(
        local,
        mesh=mesh,
        in_specs=placed,
        out_specs=(P("tile", "rot"), P("tile", "rot"), P(None, "tile", "rot")),
        check_vma=False,
    )
```

```python
import functools
import math

import jax
import jax.numpy as jnp
import ml_dtypes
import numpy as np
from jax import lax
from jax.experimental import pallas as pl
from jax.experimental.pallas import tpu as pltpu
from jax.sharding import PartitionSpec as P

TEMPL = 48
HALF = 24
EPSILON = 1e-06
LANES = 128
SPLIT = 64
F32 = jnp.float32
BF16 = jnp.bfloat16


def two_parts(table):
    high = table.astype(ml_dtypes.bfloat16)
    low = (table - high.astype(np.float64)).astype(ml_dtypes.bfloat16)
    return high, low


def row_table(out_idx, in_idx, length, sign, factor, wide):
    theta = 2.0 * math.pi / length * np.outer(out_idx, in_idx)
    pad = np.zeros((-len(out_idx) % 8, len(in_idx)))
    full = np.concatenate([np.cos(theta), pad, sign * np.sin(theta), pad], axis=0) * factor
    high, low = two_parts(full)
    if wide:
        return np.concatenate([high, high, low], axis=1)
    zeros = np.zeros_like(low)
    return np.concatenate(
        [np.concatenate([high, high], axis=1), np.concatenate([low, zeros], axis=1)], axis=0
    )


def depth_table(in_idx, length, sign, factor):
    freq = np.arange(length // 2) + 0.5
    theta = 2.0 * math.pi / length * np.outer(in_idx, freq)
    out = np.zeros((len(in_idx), LANES))
    out[:, : length // 2] = np.cos(theta) * factor
    out[:, SPLIT : SPLIT + length // 2] = sign * np.sin(theta) * factor
    return out


def half_odd(count):
    return np.arange(count // 2) + 0.5


def make_tables(x_cells, y_cells, z_cells):
    n_x, n_y, n_z = x_cells + TEMPL, y_cells + HALF, z_cells + HALF
    k_x, k_y = half_odd(n_x), half_odd(n_y)
    both_x = np.concatenate([k_x, -k_x])
    both_y = np.stack([k_y, -k_y], axis=1).reshape(-1)
    mid_x, mid_y = (x_cells - 1) / 2, (y_cells - 1) / 2
    tables = {}
    slab = np.zeros((2 * z_cells, 4 * LANES), ml_dtypes.bfloat16)
    high, low = two_parts(depth_table(np.arange(z_cells), n_z, -1.0, 1.0))
    for j in range(2):
        rows = slice(j * z_cells, (j + 1) * z_cells)
        slab[rows, 2 * j * LANES : (2 * j + 1) * LANES] = high
        slab[rows, (2 * j + 1) * LANES : (2 * j + 2) * LANES] = low
    tables["slab_z"] = slab
    tables["slab_y"] = row_table(k_y, np.arange(y_cells), n_y, -1.0, 1.0, True)
    own = np.arange(HALF, HALF + x_cells)
    halo = np.concatenate([np.arange(HALF), np.arange(HALF + x_cells, n_x)])
    tables["slab_x"] = row_table(k_x, np.concatenate([own, halo]), n_x, -1.0, 1.0, True)
    high, low = two_parts(depth_table(np.arange(TEMPL) - HALF, n_z, 1.0, 1.0))
    tmpl = np.zeros((8, 2 * LANES, 2 * LANES), ml_dtypes.bfloat16)
    for j in range(8):
        start = TEMPL * j - (LANES if j >= 4 else 0)
        tmpl[j, start : start + TEMPL, :LANES] = high
        tmpl[j, start : start + TEMPL, LANES:] = low
    tables["tmpl_z"] = tmpl
    ones = (high.astype(np.float64) + low.astype(np.float64)).sum(axis=0)
    tables["ones_z"] = np.broadcast_to(ones.astype(np.float32)[None], (8, LANES)).copy()
    tables["tmpl_y"] = row_table(k_y, np.arange(TEMPL) - HALF + mid_y, n_y, 1.0, 1.0, True)
    tables["tmpl_x"] = row_table(k_x, np.arange(TEMPL) + mid_x, n_x, 1.0, 1.0, True)
    tables["back_x"] = row_table(half_odd(x_cells), both_x, n_x, 1.0, 1.0 / n_x, False)
    tables["back_y"] = row_table(half_odd(y_cells), both_y, n_y, 1.0, 1.0 / n_y, False)
    back = depth_table(np.arange(z_cells), n_z, -1.0, 2.0 / n_z).T
    high, low = two_parts(back)
    back_z = np.zeros((2 * LANES, 2 * LANES), ml_dtypes.bfloat16)
    for j in range(2):
        rows = slice(j * LANES, (j + 1) * LANES)
        back_z[rows, j * z_cells : (j + 1) * z_cells] = high
        back_z[rows, LANES + j * z_cells : LANES + (j + 1) * z_cells] = low
    tables["back_z"] = back_z
    return tables


def split_rows(value, wide):
    high = value.astype(BF16)
    if value.shape[0] % 16 == 0:
        low = (value - high.astype(F32)).astype(BF16)
        return jnp.concatenate([high, low, high] if wide else [high, low], axis=0)
    high = high.astype(F32)
    low = value - high
    return jnp.concatenate([high, low, high] if wide else [high, low], axis=0).astype(BF16)


def swap(value):
    parts = [
        pltpu.roll(value[:, s : s + LANES], SPLIT, 1) for s in range(0, value.shape[1], LANES)
    ]
    return jnp.concatenate(parts, axis=1)


def lane_sign(width):
    lane = lax.broadcasted_iota(jnp.int32, (8, width), 1) % LANES
    return jnp.where(lane < SPLIT, -1.0, 1.0)[:1]


def pair_rows(table, value, wide):
    return pair_dot(table, split_rows(value, wide), wide)


def pair_dot(table, parts, wide):
    out = jnp.dot(table, parts, preferred_element_type=F32)
    if not wide:
        half = out.shape[0] // 2
        out = out[:half] + out[half:]
    half = out.shape[0] // 2
    turned = swap(out[half:]) * lane_sign(out.shape[1])
    return out[:half] + turned, out[:half] - turned


def pick(ref, firsts, count, stride):
    return jnp.concatenate([ref[pl.ds(f, count, stride=stride), :] for f in firsts], axis=1)


def store(ref, start, value):
    ref[pl.ds(start, value.shape[0]), :] = value


def odd(rows):
    return rows + 1


def lane_block(value, i):
    return value[:, i * LANES : (i + 1) * LANES]


def loop(count, body):
    def one(i, carry):
        body(i)
        return carry

    lax.fori_loop(0, count, one, 0)


GROUP = 8


def pipeline(steps, stages, width):
    blocks = -(-steps // width)
    depth = len(stages)

    def turn(t, static):
        for s in reversed(range(depth)):
            if static and not 0 <= t - s < blocks:
                continue
            for slot in range(width):
                step = (t - s) * width + slot
                if not static or step < steps:
                    stages[s](step, slot)

    full = steps // width
    first, last = depth - 1, max(full, depth - 1)
    for t in range(first):
        turn(t, True)
    if last - first >= 2:
        loop(last - first, lambda i: turn(i + first, False))
    else:
        last = first
    for t in range(last, blocks + depth - 1):
        turn(t, True)


def slab_rows_kernel(dims, row_slices, *refs):
    parts = len(row_slices)
    if parts == 1:
        ins, (rows_ref, mask_ref), scratch = refs[:4], refs[4:6], refs[6:]
        depth_buf, parts_buf, slab_buf, valid_ref, z_ref, y_ref, sems = scratch
        slab_refs = [slab_buf]
        copies = [
            pltpu.make_async_copy(source, target, sems.at[i])
            for i, (source, target) in enumerate(zip(ins, (slab_buf, valid_ref, z_ref, y_ref)))
        ]
        for copy in copies:
            copy.start()
        for copy in copies:
            copy.wait()
    else:
        slab_refs, (z_ref, y_ref, rows_ref, depth_buf, parts_buf) = refs[:parts], refs[parts:]
    x_cells, y_cells, z_cells = dims
    count = sum(stop - start for start, stop in row_slices)
    n_y = y_cells + HALF
    pad_y = n_y // 2 + -(n_y // 2) % 8
    many = 4

    if parts == 1:
        valid = valid_ref[...].astype(F32)
        low_lane = lax.broadcasted_iota(jnp.int32, (x_cells, LANES), 1) < z_cells
        for q in range(y_cells // 2):
            mask_ref[q] = jnp.where(low_lane, valid[:, 2 * q : 2 * q + 1], valid[:, 2 * q + 1 : 2 * q + 2])

    def depth_step(i):
        top = 0
        for ref, (start, stop) in zip(slab_refs, row_slices):
            size = stop - start
            lanes = [pl.ds(pl.multiple_of((many * i + u) * LANES, LANES), LANES) for u in range(many)]
            block = jnp.concatenate([ref[:, l].astype(F32)[start:stop] for l in lanes], axis=0)
            out = jnp.dot(block.astype(BF16), z_ref[...], preferred_element_type=F32)
            for u in range(many):
                part = out[u * size : (u + 1) * size]
                for j in range(2):
                    store(
                        depth_buf, (2 * many * i + 2 * u + j) * odd(count) + top,
                        lane_block(part, 2 * j) + lane_block(part, 2 * j + 1),
                    )
            top += size

    loop(y_cells // (2 * many), depth_step)

    def gather_rows(i, slot):
        value = pick(depth_buf, [GROUP * i + u for u in range(GROUP)], y_cells, odd(count))
        parts_buf[slot] = split_rows(value, True)

    def y_step(i, slot):
        plus, minus = pair_dot(y_ref[...], parts_buf[slot], True)
        for u in range(GROUP):
            start = (GROUP * i + u) * odd(2 * pad_y)
            store(rows_ref, start, lane_block(plus, u))
            store(rows_ref, start + pad_y, lane_block(minus, u))

    pipeline(count // GROUP, [gather_rows, y_step], 2)


def slab_rows(blocks, row_slices, valid, dims, tables, name):
    x_cells, y_cells, z_cells = dims
    count = sum(stop - start for start, stop in row_slices)
    n_y = y_cells + HALF
    pad_y = n_y // 2 + -(n_y // 2) % 8
    vmem = pl.BlockSpec(memory_space=pltpu.VMEM)
    out_shape = [jax.ShapeDtypeStruct((count * odd(2 * pad_y), LANES), F32)]
    scratch = [
        pltpu.VMEM((y_cells * odd(count), LANES), F32),
        pltpu.VMEM((2, 3 * y_cells, GROUP * LANES), BF16),
    ]
    slab_z, slab_y = tables["slab_z"], tables["slab_y"]
    source = vmem
    if valid is not None:
        source = pl.BlockSpec(memory_space=pltpu.HBM)
        for array in (blocks[0], valid, slab_z, slab_y):
            scratch.append(pltpu.VMEM(array.shape, array.dtype))
        scratch.append(pltpu.SemaphoreType.DMA((4,)))
        blocks = blocks + [valid]
        out_shape.append(jax.ShapeDtypeStruct((y_cells // 2, x_cells, LANES), F32))
    return pl.pallas_call(
        functools.partial(slab_rows_kernel, dims, row_slices),
        out_shape=tuple(out_shape),
        in_specs=[source] * (2 + len(blocks)),
        out_specs=(vmem,) * len(out_shape),
        scratch_shapes=scratch,
        compiler_params=pltpu.CompilerParams(vmem_limit_bytes=20 * 1024 * 1024),
        cost_estimate=pl.CostEstimate(flops=count * 10**8, bytes_accessed=10**6, transcendentals=0),
        name=name,
    )(*blocks, slab_z, slab_y)


def slab_x_kernel(dims, own_ref, halo_ref, x_ref, spec_ref, parts_buf):
    x_cells, y_cells, z_cells = dims
    n_y = y_cells + HALF
    pad_y = n_y // 2 + -(n_y // 2) % 8

    def gather_rows(i, slot):
        firsts = [GROUP // 2 * i + u // 2 + u % 2 * pad_y for u in range(GROUP)]
        value = jnp.concatenate(
            [
                pick(own_ref, firsts, x_cells, odd(2 * pad_y)),
                pick(halo_ref, firsts, TEMPL, odd(2 * pad_y)),
            ],
            axis=0,
        )
        parts_buf[slot] = split_rows(value, True)

    def x_step(i, slot):
        plus, minus = pair_dot(x_ref[...], parts_buf[slot], True)
        spec = jnp.concatenate([plus, minus], axis=0)
        turned = swap(spec)
        real_lane = lane_sign(GROUP * LANES) < 0
        spec_ref[i, 0] = jnp.where(real_lane, spec, turned)
        spec_ref[i, 1] = jnp.where(real_lane, -turned, spec)

    pipeline(n_y // GROUP, [gather_rows, x_step], 2)


def slab_x(own, halo, dims, tables):
    x_cells, y_cells, z_cells = dims
    n_x, n_y = x_cells + TEMPL, y_cells + HALF
    steps = n_y // GROUP
    vmem = pl.BlockSpec(memory_space=pltpu.VMEM)
    shape = (steps, 2, n_x, GROUP * LANES)
    return pl.pallas_call(
        functools.partial(slab_x_kernel, dims),
        out_shape=jax.ShapeDtypeStruct(shape, F32),
        in_specs=[vmem] * 3,
        out_specs=vmem,
        scratch_shapes=[pltpu.VMEM((2, 3 * n_x, GROUP * LANES), BF16)],
        compiler_params=pltpu.CompilerParams(vmem_limit_bytes=20 * 1024 * 1024),
        cost_estimate=pl.CostEstimate(flops=5 * 10**9, bytes_accessed=10**6, transcendentals=0),
        name="slab_x",
    )(own, halo, tables["slab_x"])


def corr_kernel(
    dims, rot, place_ref, tmpl_ref, mask_ref, spec_ref,
    z_ref, ones_ref, y_ref, x_ref, bx_ref, by_ref, bz_ref,
    mine_ref, side_ref, far_ref, stat_ref,
    depth_buf, rows_buf, first_buf, second_buf, third_buf, back_buf, vol_buf,
):
    x_cells, y_cells, z_cells = dims
    n_x, n_y = x_cells + TEMPL, y_cells + HALF
    half_y = n_y // 2
    pad_y = half_y + -half_y % 8
    each = TEMPL // 8
    rows = slice(rot * each, (rot + 1) * each)
    tmpl = jnp.concatenate([tmpl_ref[t, rows, :] for t in range(8)], axis=0)
    inv_size = 1.0 / TEMPL**3
    mean = jnp.sum(tmpl) * inv_size
    centred = tmpl - mean
    var = jnp.sum(centred * centred) * inv_size
    scale = 1.0 / (jnp.sqrt(jnp.full((1, LANES), var + EPSILON, F32)) * TEMPL**1.5)
    shift = ones_ref[:1] * mean

    wide = 8 * TEMPL
    narrow = tmpl.astype(BF16)
    block = jnp.concatenate(
        [narrow[:, g * wide : (g + 1) * wide] for g in range(TEMPL // 8)], axis=0
    )
    for j in range(8):
        window = block[:, : 2 * LANES] if j < 4 else block[:, LANES:]
        out = jnp.dot(window, z_ref[j], preferred_element_type=F32)
        part = out[:, :LANES] + out[:, LANES:] - shift
        for g in range(TEMPL // 8):
            start = (8 * g + j) * odd(TEMPL)
            store(depth_buf, start, part[g * TEMPL : (g + 1) * TEMPL])

    def gather_a(i, slot):
        value = pick(depth_buf, [GROUP * i + u for u in range(GROUP)], TEMPL, odd(TEMPL))
        first_buf[slot] = split_rows(value, True)

    def y_step(i, slot):
        plus, minus = pair_dot(y_ref[...], first_buf[slot], True)
        for u in range(GROUP):
            start = (GROUP * i + u) * odd(2 * pad_y)
            store(rows_buf, start, lane_block(plus, u))
            store(rows_buf, start + pad_y, lane_block(minus, u))

    pipeline(TEMPL // GROUP, [gather_a, y_step], 2)

    def gather_ky(i, slot):
        firsts = [GROUP // 2 * i + u // 2 + u % 2 * pad_y for u in range(GROUP)]
        first_buf[slot] = split_rows(pick(rows_buf, firsts, TEMPL, odd(2 * pad_y)), True)

    def multiply(i, slot):
        plus, minus = pair_dot(x_ref[...], first_buf[slot], True)
        spec = jnp.concatenate([plus, minus], axis=0)
        prod = spec * spec_ref[i, 0] + swap(spec) * spec_ref[i, 1]
        second_buf[slot] = split_rows(prod, False)

    def back_x(i, slot):
        plus, minus = pair_dot(bx_ref[...], second_buf[slot], False)
        for u in range(GROUP):
            start = (GROUP * i + u) * odd(x_cells)
            store(back_buf, start, lane_block(plus, u))
            store(back_buf, start + x_cells // 2, lane_block(minus, u))

    pipeline(n_y // GROUP, [gather_ky, multiply, back_x], 2)

    def gather_x(i, slot):
        value = pick(back_buf, [GROUP * i + u for u in range(GROUP)], n_y, odd(x_cells))
        third_buf[slot] = split_rows(value, False)

    def back_y(i, slot):
        plus, minus = pair_dot(by_ref[...], third_buf[slot], False)
        for u in range(GROUP):
            row = GROUP * i + u
            x = jnp.where(row < x_cells // 2, row + x_cells // 2, x_cells - 1 - row)
            store(vol_buf, x * odd(y_cells), lane_block(plus, u))
            store(vol_buf, x * odd(y_cells) + y_cells // 2, lane_block(minus, u))

    pipeline(x_cells // GROUP, [gather_x, back_y], 2)

    share = y_cells // 8
    me = place_ref[0]
    total = jnp.zeros((x_cells, LANES), F32)
    number = jnp.zeros((x_cells, LANES), F32)
    targets = [mine_ref, side_ref, far_ref.at[0], far_ref.at[1]]
    for p, target in enumerate(targets):
        first = (me ^ p) * share
        values = []
        for i in range(share):
            firsts = []
            for j in range(2):
                y = 2 * (first + i) + j
                firsts.append(jnp.where(y < y_cells // 2, y_cells - 1 - y, y - y_cells // 2))
            values.append(pick(vol_buf, firsts, x_cells, odd(y_cells)))
        value = jnp.concatenate(values, axis=0)
        out = jnp.dot(split_rows(value, False), bz_ref[...], preferred_element_type=F32)
        rows = value.shape[0]
        full = out[:rows, :LANES] + out[:rows, LANES:] + out[rows:, :LANES]
        for i in range(share):
            corr = full[i * x_cells : (i + 1) * x_cells] * scale
            target[:, i * LANES : (i + 1) * LANES] = corr
            mask = mask_ref[first + i]
            total = total + corr * mask
            number = number + mask
    number_sum = jnp.sum(number)
    total_sum = jnp.sum(total)
    local_mean = jnp.full((1, LANES), total_sum, F32) / jnp.maximum(number_sum, 1.0)
    square = jnp.zeros((x_cells, LANES), F32)
    for p, target in enumerate(targets):
        first = (me ^ p) * share
        for i in range(share):
            gap = target[:, i * LANES : (i + 1) * LANES] - local_mean
            square = square + gap * gap * mask_ref[first + i]
    row = lax.broadcasted_iota(jnp.int32, (8, LANES), 0)
    stat_ref[...] = jnp.where(row == 0, number_sum, jnp.where(row == 1, total_sum, jnp.sum(square)))


def correlate(place, bank, rot, mask, spec, dims, tables):
    x_cells, y_cells, z_cells = dims
    n_x, n_y = x_cells + TEMPL, y_cells + HALF
    pad_y = n_y // 2 + -(n_y // 2) % 8
    width = y_cells * z_cells // 4
    vmem = pl.BlockSpec(memory_space=pltpu.VMEM)
    return pl.pallas_call(
        functools.partial(corr_kernel, dims, rot),
        out_shape=(
            jax.ShapeDtypeStruct((x_cells, width), F32),
            jax.ShapeDtypeStruct((x_cells, width), F32),
            jax.ShapeDtypeStruct((2, x_cells, width), F32),
            jax.ShapeDtypeStruct((8, LANES), F32),
        ),
        in_specs=[pl.BlockSpec(memory_space=pltpu.SMEM)] + [vmem] * 10,
        out_specs=(vmem,) * 4,
        scratch_shapes=[
            pltpu.VMEM((TEMPL * odd(TEMPL), LANES), F32),
            pltpu.VMEM((TEMPL * odd(2 * pad_y), LANES), F32),
            pltpu.VMEM((2, 3 * TEMPL, GROUP * LANES), BF16),
            pltpu.VMEM((2, 2 * n_x, GROUP * LANES), BF16),
            pltpu.VMEM((2, 2 * n_y, GROUP * LANES), BF16),
            pltpu.VMEM((n_y * odd(x_cells), LANES), F32),
            pltpu.VMEM((x_cells * odd(y_cells), LANES), F32),
        ],
        compiler_params=pltpu.CompilerParams(vmem_limit_bytes=24 * 1024 * 1024),
        cost_estimate=pl.CostEstimate(flops=15 * 10**9, bytes_accessed=10**7, transcendentals=0),
        name="correlate",
    )(
        place, bank, mask, spec,
        tables["tmpl_z"], tables["ones_z"], tables["tmpl_y"], tables["tmpl_x"],
        tables["back_x"], tables["back_y"], tables["back_z"],
    )


def score_kernel(place_ref, coef_ref, mask_ref, *refs):
    pieces = refs[: len(refs) - 3]
    best_ref, evid_ref, mom_ref = refs[len(refs) - 3 :]

    blocks = best_ref.shape[1] // LANES

    def step(i):
        lanes = pl.ds(pl.multiple_of(i * LANES, LANES), LANES)
        for top in range(0, best_ref.shape[0], 8):
            rows = slice(top, top + 8)
            mask = mask_ref[place_ref[0] * blocks + i, rows]
            scores = []
            for k, piece in enumerate(pieces):
                scores.append((piece[rows, lanes] - coef_ref[k, 0]) * coef_ref[k, 1])
            high = functools.reduce(jnp.maximum, scores)
            total = jnp.zeros_like(high)
            moment = [jnp.zeros_like(high) for _ in range(4)]
            for k, score in enumerate(scores):
                weight = jnp.exp(score - high)
                total = total + weight
                for c in range(4):
                    moment[c] = moment[c] + weight * coef_ref[k, 2 + c]
            best_ref[rows, lanes] = mask * high
            evid_ref[rows, lanes] = mask * (high + jnp.log(total))
            share = mask / total
            for c in range(4):
                mom_ref[c, rows, lanes] = moment[c] * share

    loop(blocks, step)


def combine(place, coefs, mask, pieces):
    shape = pieces[0].shape
    vmem = pl.BlockSpec(memory_space=pltpu.VMEM)
    out = jax.ShapeDtypeStruct(shape, F32)
    return pl.pallas_call(
        score_kernel,
        out_shape=(out, out, jax.ShapeDtypeStruct((4,) + shape, F32)),
        in_specs=[pl.BlockSpec(memory_space=pltpu.SMEM)] * 2 + [vmem] * (1 + len(pieces)),
        out_specs=(vmem,) * 3,
        compiler_params=pltpu.CompilerParams(vmem_limit_bytes=16 * 1024 * 1024),
        name="combine",
    )(place, coefs, mask, *pieces)


def gather_steps(count):
    return [1 << i for i in reversed(range(count.bit_length() - 1))]


def gather_step(block, axis, step):
    count = lax.axis_size(axis)
    other = lax.ppermute(block, axis, [(i, i ^ step) for i in range(count)])
    upper = (lax.axis_index(axis) & step) != 0
    pair = [jnp.where(upper, other, block), jnp.where(upper, block, other)]
    return jnp.stack(pair, axis=1).reshape((-1,) + block.shape[1:])


def merge(first, other):
    number_a, number_b = first[:1], other[:1]
    mean_a = first[1:2] / jnp.maximum(number_a, 1.0)
    mean_b = other[1:2] / jnp.maximum(number_b, 1.0)
    gap = mean_b - mean_a
    between = gap * gap * (number_a * number_b / jnp.maximum(number_a + number_b, 1.0))
    return first + other + jnp.where(jnp.arange(3)[:, None] == 2, between, 0.0)


def exchange_all(block, axis, low, high):
    count = lax.axis_size(axis)
    parts = [block]
    for step in range(low, high, low):
        parts.append(lax.ppermute(block, axis, [(i, i ^ step) for i in range(count)]))
    return jnp.stack(parts)


def neighbours(block, axis):
    count = lax.axis_size(axis)
    forward = [(i, i + 1) for i in range(count - 1)]
    backward = [(target, source) for source, target in forward]
    return lax.ppermute(block, axis, forward), lax.ppermute(block, axis, backward)


def local(tomogram, templates, valid, quats, rot_index):
    x_cells, voxels = tomogram.shape
    y_cells = valid.shape[1]
    z_cells = voxels // y_cells
    dims = (x_cells, y_cells, z_cells)
    tables = {name: jnp.asarray(table) for name, table in make_tables(*dims).items()}
    groups = lax.axis_size("rot")
    tiles = lax.axis_size("tile")
    me = lax.axis_index("rot")
    rots = templates.shape[0]

    row = TEMPL * TEMPL
    chunk = templates.shape[1]
    whole_rows = chunk % row == 0
    block = templates.reshape(rots * chunk // row, row) if whole_rows else templates
    block = block[None]
    steps = gather_steps(tiles)
    block = gather_step(block, "tile", steps[0])
    low, high = neighbours(tomogram, "tile")
    for step in steps[1:-1]:
        block = gather_step(block, "tile", step)
    one_hot = (rot_index[:, None] == jnp.arange(quats.shape[1], dtype=jnp.int32)[None, :]).astype(F32)
    orient = jnp.einsum("rq,kq->rk", one_hot, quats, precision=lax.Precision.HIGHEST)
    place = me_place = jnp.reshape(me, (1,)).astype(jnp.int32)
    own, mask = slab_rows([tomogram], [(0, x_cells)], valid, dims, tables, "slab_own")
    (halo,) = slab_rows(
        [low, high], [(x_cells - HALF, x_cells), (0, HALF)], None, dims, tables, "slab_halo"
    )
    spec = slab_x(own, halo, dims, tables)
    block = gather_step(block, "tile", steps[-1])
    if not whole_rows:
        block = jnp.transpose(block, (1, 0, 2)).reshape(rots, 8, TEMPL // 8, row)
        block = jnp.transpose(block, (1, 0, 2, 3))
    bank = block.reshape(8, rots * (TEMPL // 8), row).astype(F32)
    far_swap = [(i, i ^ 2) for i in range(groups)]
    side_swap = [(i, i ^ 1) for i in range(groups)]
    mines, sides, fars, from_sides, stats = [], [], [], [], []
    for r in range(rots):
        if r >= 2:
            place, fars[r - 2] = lax.optimization_barrier((place, fars[r - 2]))
        if r >= 3:
            place, from_sides[r - 3] = lax.optimization_barrier((place, from_sides[r - 3]))
        mine, side, far, stat = correlate(place, bank, r, mask, spec, dims, tables)
        if r >= 1:
            stat, fars[r - 1] = lax.optimization_barrier((stat, fars[r - 1]))
        if r >= 1 and r < rots - 1:
            both = jnp.stack([sides[r - 1], fars[r - 1][1]])
        mines.append(mine)
        sides.append(side)
        stats.append(stat[:3, 0])
        fars.append(lax.ppermute(far, "rot", far_swap))
        if r >= 1 and r < rots - 1:
            from_sides.append(lax.ppermute(both, "rot", side_swap))
    state = jnp.stack(stats, axis=1)
    state, fars[rots - 2], from_sides[rots - 3] = lax.optimization_barrier(
        (state, fars[rots - 2], from_sides[rots - 3])
    )
    step = 1
    while step < tiles:
        swap_pairs = [(i, i ^ step) for i in range(tiles)]
        state = merge(state, lax.ppermute(state, "tile", swap_pairs))
        step *= 2
    average = state[1] / state[0]
    inverse = 1.0 / jnp.sqrt(state[2] / state[0] + EPSILON)
    coefs = jnp.concatenate([average[:, None], inverse[:, None], orient], axis=1)
    coefs = exchange_all(coefs, "rot", 1, groups)
    last = [part for r in range(rots - 2, rots) for part in (sides[r], fars[r][1])]
    last = lax.ppermute(jnp.stack(last), "rot", side_swap)
    from_sides += [last[:2], last[2:]]
    flat = mines + [f[0] for f in from_sides] + [f[0] for f in fars] + [f[1] for f in from_sides]
    return combine(me_place, coefs.reshape(groups * rots, 6), mask, flat)


def solution(mesh):
    placed = (P("tile", None), P("rot", "tile"), P("tile", None), P(), P("rot"))
    return jax.shard_map(
        local,
        mesh=mesh,
        in_specs=placed,
        out_specs=(P("tile", "rot"), P("tile", "rot"), P(None, "tile", "rot")),
        check_vma=False,
    )
```

```python
import functools
import math

import jax
import jax.numpy as jnp
import ml_dtypes
import numpy as np
from jax import lax
from jax.experimental import pallas as pl
from jax.experimental.pallas import tpu as pltpu
from jax.sharding import PartitionSpec as P

TEMPL = 48
HALF = 24
EPSILON = 1e-06
LANES = 128
SPLIT = 64
F32 = jnp.float32
BF16 = jnp.bfloat16


def two_parts(table):
    high = table.astype(ml_dtypes.bfloat16)
    low = (table - high.astype(np.float64)).astype(ml_dtypes.bfloat16)
    return high, low


def row_table(out_idx, in_idx, length, sign, factor, wide):
    theta = 2.0 * math.pi / length * np.outer(out_idx, in_idx)
    pad = np.zeros((-len(out_idx) % 8, len(in_idx)))
    full = np.concatenate([np.cos(theta), pad, sign * np.sin(theta), pad], axis=0) * factor
    high, low = two_parts(full)
    if wide:
        return np.concatenate([high, high, low], axis=1)
    zeros = np.zeros_like(low)
    return np.concatenate(
        [np.concatenate([high, high], axis=1), np.concatenate([low, zeros], axis=1)], axis=0
    )


def depth_table(in_idx, length, sign, factor):
    freq = np.arange(length // 2) + 0.5
    theta = 2.0 * math.pi / length * np.outer(in_idx, freq)
    out = np.zeros((len(in_idx), LANES))
    out[:, : length // 2] = np.cos(theta) * factor
    out[:, SPLIT : SPLIT + length // 2] = sign * np.sin(theta) * factor
    return out


def half_odd(count):
    return np.arange(count // 2) + 0.5


def make_tables(x_cells, y_cells, z_cells):
    n_x, n_y, n_z = x_cells + TEMPL, y_cells + HALF, z_cells + HALF
    k_x, k_y = half_odd(n_x), half_odd(n_y)
    both_x = np.concatenate([k_x, -k_x])
    both_y = np.stack([k_y, -k_y], axis=1).reshape(-1)
    mid_x, mid_y = (x_cells - 1) / 2, (y_cells - 1) / 2
    tables = {}
    slab = np.zeros((2 * z_cells, 4 * LANES), ml_dtypes.bfloat16)
    high, low = two_parts(depth_table(np.arange(z_cells), n_z, -1.0, 1.0))
    for j in range(2):
        rows = slice(j * z_cells, (j + 1) * z_cells)
        slab[rows, 2 * j * LANES : (2 * j + 1) * LANES] = high
        slab[rows, (2 * j + 1) * LANES : (2 * j + 2) * LANES] = low
    slab_y = row_table(k_y, np.arange(y_cells), n_y, -1.0, 1.0, True)
    slab_y = np.pad(slab_y, ((0, 0), (0, slab.shape[1] - slab_y.shape[1])))
    tables["slab_rows"] = np.concatenate([slab, slab_y], axis=0)
    own = np.arange(HALF, HALF + x_cells)
    halo = np.concatenate([np.arange(HALF), np.arange(HALF + x_cells, n_x)])
    tables["slab_x"] = row_table(k_x, np.concatenate([own, halo]), n_x, -1.0, 1.0, True)
    high, low = two_parts(depth_table(np.arange(TEMPL) - HALF, n_z, 1.0, 1.0))
    tables["tmpl_z"] = np.concatenate([high, low], axis=1)
    ones = (high.astype(np.float64) + low.astype(np.float64)).sum(axis=0)
    tables["ones_z"] = np.broadcast_to(ones.astype(np.float32)[None], (8, LANES)).copy()
    tables["tmpl_y"] = row_table(k_y, np.arange(TEMPL) - HALF + mid_y, n_y, 1.0, 1.0, True)
    tables["tmpl_x"] = row_table(k_x, np.arange(TEMPL) + mid_x, n_x, 1.0, 1.0, True)
    tables["back_x"] = row_table(half_odd(x_cells), both_x, n_x, 1.0, 1.0 / n_x, False)
    tables["back_y"] = row_table(half_odd(y_cells), both_y, n_y, 1.0, 1.0 / n_y, False)
    back = depth_table(np.arange(z_cells), n_z, -1.0, 2.0 / n_z).T
    high, low = two_parts(back)
    back_z = np.zeros((2 * LANES, 2 * LANES), ml_dtypes.bfloat16)
    for j in range(2):
        rows = slice(j * LANES, (j + 1) * LANES)
        back_z[rows, j * z_cells : (j + 1) * z_cells] = high
        back_z[rows, LANES + j * z_cells : LANES + (j + 1) * z_cells] = low
    tables["back_z"] = back_z
    return tables


def split_rows(value, wide):
    high = value.astype(BF16)
    if value.shape[0] % 16 == 0:
        low = (value - high.astype(F32)).astype(BF16)
        return jnp.concatenate([high, low, high] if wide else [high, low], axis=0)
    high = high.astype(F32)
    low = value - high
    return jnp.concatenate([high, low, high] if wide else [high, low], axis=0).astype(BF16)


def swap(value):
    parts = [
        pltpu.roll(value[:, s : s + LANES], SPLIT, 1) for s in range(0, value.shape[1], LANES)
    ]
    return jnp.concatenate(parts, axis=1)


def lane_sign(width):
    lane = lax.broadcasted_iota(jnp.int32, (8, width), 1) % LANES
    return jnp.where(lane < SPLIT, -1.0, 1.0)[:1]


def pair_rows(table, value, wide):
    return pair_dot(table, split_rows(value, wide), wide)


def pair_dot(table, parts, wide):
    out = jnp.dot(table, parts, preferred_element_type=F32)
    if not wide:
        half = out.shape[0] // 2
        out = out[:half] + out[half:]
    half = out.shape[0] // 2
    turned = swap(out[half:]) * lane_sign(out.shape[1])
    return out[:half] + turned, out[:half] - turned


def pick(ref, firsts, count, stride):
    return jnp.concatenate([ref[pl.ds(f, count, stride=stride), :] for f in firsts], axis=1)


def store(ref, start, value):
    ref[pl.ds(start, value.shape[0]), :] = value


def odd(rows):
    return rows + 1


def lane_block(value, i):
    return value[:, i * LANES : (i + 1) * LANES]


def loop(count, body):
    def one(i, carry):
        body(i)
        return carry

    lax.fori_loop(0, count, one, 0)


GROUP = 8


def pipeline(steps, stages, width):
    blocks = -(-steps // width)
    depth = len(stages)

    def turn(t, static):
        for s in reversed(range(depth)):
            if static and not 0 <= t - s < blocks:
                continue
            for slot in range(width):
                step = (t - s) * width + slot
                if not static or step < steps:
                    stages[s](step, slot)

    full = steps // width
    first, last = depth - 1, max(full, depth - 1)
    for t in range(first):
        turn(t, True)
    if last - first >= 2:
        loop(last - first, lambda i: turn(i + first, False))
    else:
        last = first
    for t in range(last, blocks + depth - 1):
        turn(t, True)


def slab_rows_kernel(dims, place_ref, *refs):
    sources, (table_ref, rows_ref, depth_buf, parts_buf) = refs[:-4], refs[-4:]
    x_cells, y_cells, z_cells = dims
    half = x_cells // 2
    count = depth_buf.shape[0] // y_cells - 1
    n_y = y_cells + HALF
    pad_y = n_y // 2 + -(n_y // 2) % 8
    many = 4

    def read(lanes):
        if len(sources) == 1:
            return sources[0][:, lanes].astype(F32)
        first = (place_ref[0] & 1) == 0
        mine, other = ([ref[i, :, lanes].astype(F32) for i in range(2)] for ref in sources)
        low, high = (
            jnp.concatenate([jnp.where(first, m, o), jnp.where(first, o, m)], axis=0)
            for m, o in zip(mine, other)
        )
        return jnp.concatenate([low[x_cells - HALF :], high[:HALF]], axis=0)

    def depth_step(i):
        lanes = [pl.ds(pl.multiple_of((many * i + u) * LANES, LANES), LANES) for u in range(many)]
        block = jnp.concatenate([read(l) for l in lanes], axis=0).astype(BF16)
        out = jnp.dot(block, table_ref[: 2 * z_cells], preferred_element_type=F32)
        for u in range(many):
            part = out[u * count : (u + 1) * count]
            for j in range(2):
                store(
                    depth_buf, (2 * many * i + 2 * u + j) * odd(count),
                    lane_block(part, 2 * j) + lane_block(part, 2 * j + 1),
                )

    loop(y_cells // (2 * many), depth_step)

    def gather_rows(i, slot):
        value = pick(depth_buf, [GROUP * i + u for u in range(GROUP)], y_cells, odd(count))
        parts_buf[slot] = split_rows(value, True)

    def y_step(i, slot):
        plus, minus = pair_dot(table_ref[2 * z_cells :, : 3 * y_cells], parts_buf[slot], True)
        for u in range(GROUP):
            start = (GROUP * i + u) * odd(2 * pad_y)
            store(rows_ref, start, lane_block(plus, u))
            store(rows_ref, start + pad_y, lane_block(minus, u))

    pipeline(count // GROUP, [gather_rows, y_step], 2)


def slab_rows(place, blocks, count, dims, tables, name):
    x_cells, y_cells, z_cells = dims
    n_y = y_cells + HALF
    pad_y = n_y // 2 + -(n_y // 2) % 8
    vmem = pl.BlockSpec(memory_space=pltpu.VMEM)
    return pl.pallas_call(
        functools.partial(slab_rows_kernel, dims),
        out_shape=jax.ShapeDtypeStruct((count * odd(2 * pad_y), LANES), F32),
        in_specs=[pl.BlockSpec(memory_space=pltpu.SMEM)] + [vmem] * (1 + len(blocks)),
        out_specs=vmem,
        scratch_shapes=[
            pltpu.VMEM((y_cells * odd(count), LANES), F32),
            pltpu.VMEM((2, 3 * y_cells, GROUP * LANES), BF16),
        ],
        compiler_params=pltpu.CompilerParams(vmem_limit_bytes=20 * 1024 * 1024),
        cost_estimate=pl.CostEstimate(flops=count * 10**8, bytes_accessed=10**6, transcendentals=0),
        name=name,
    )(place, *blocks, tables["slab_rows"])


def slab_x_kernel(
    dims, own_ref, halo_ref, x_ref, valid_ref, tz_ref, spec_ref, mask_ref, z_ref, parts_buf
):
    x_cells, y_cells, z_cells = dims
    n_y = y_cells + HALF
    pad_y = n_y // 2 + -(n_y // 2) % 8

    def gather_rows(i, slot):
        firsts = [GROUP // 2 * i + u // 2 + u % 2 * pad_y for u in range(GROUP)]
        value = jnp.concatenate(
            [
                pick(own_ref, firsts, x_cells, odd(2 * pad_y)),
                pick(halo_ref, firsts, TEMPL, odd(2 * pad_y)),
            ],
            axis=0,
        )
        parts_buf[slot] = split_rows(value, True)

    def x_step(i, slot):
        plus, minus = pair_dot(x_ref[...], parts_buf[slot], True)
        spec = jnp.concatenate([plus, minus], axis=0)
        turned = swap(spec)
        real_lane = lane_sign(GROUP * LANES) < 0
        spec_ref[i, 0] = jnp.where(real_lane, spec, turned)
        spec_ref[i, 1] = jnp.where(real_lane, -turned, spec)

    pipeline(n_y // GROUP, [gather_rows, x_step], 2)

    valid = valid_ref[...].astype(F32)
    low_lane = lax.broadcasted_iota(jnp.int32, (x_cells, LANES), 1) < z_cells
    for q in range(y_cells // 2):
        mask_ref[q] = jnp.where(low_lane, valid[:, 2 * q : 2 * q + 1], valid[:, 2 * q + 1 : 2 * q + 2])
    z_ref[...] = jnp.zeros(z_ref.shape, BF16)
    for j in range(8):
        start = TEMPL * j - (LANES if j >= 4 else 0)
        z_ref[j, start : start + TEMPL, :] = tz_ref[...]


def slab_x(own, halo, valid, dims, tables):
    x_cells, y_cells, z_cells = dims
    n_x, n_y = x_cells + TEMPL, y_cells + HALF
    steps = n_y // GROUP
    vmem = pl.BlockSpec(memory_space=pltpu.VMEM)
    shape = (steps, 2, n_x, GROUP * LANES)
    return pl.pallas_call(
        functools.partial(slab_x_kernel, dims),
        out_shape=(
            jax.ShapeDtypeStruct(shape, F32),
            jax.ShapeDtypeStruct((y_cells // 2, x_cells, LANES), F32),
            jax.ShapeDtypeStruct((8, 2 * LANES, 2 * LANES), BF16),
        ),
        in_specs=[vmem] * 5,
        out_specs=(vmem,) * 3,
        scratch_shapes=[pltpu.VMEM((2, 3 * n_x, GROUP * LANES), BF16)],
        compiler_params=pltpu.CompilerParams(vmem_limit_bytes=20 * 1024 * 1024),
        cost_estimate=pl.CostEstimate(flops=5 * 10**9, bytes_accessed=10**6, transcendentals=0),
        name="slab_x",
    )(own, halo, tables["slab_x"], valid, tables["tmpl_z"])


def corr_kernel(
    dims, rot, place_ref, tmpl_ref, mask_ref, spec_ref,
    z_ref, ones_ref, y_ref, x_ref, bx_ref, by_ref, bz_ref,
    mine_ref, side_ref, far_ref, stat_ref,
    depth_buf, rows_buf, first_buf, second_buf, third_buf, back_buf, vol_buf,
):
    x_cells, y_cells, z_cells = dims
    n_x, n_y = x_cells + TEMPL, y_cells + HALF
    half_y = n_y // 2
    pad_y = half_y + -half_y % 8
    each = TEMPL // 8
    rows = slice(rot * each, (rot + 1) * each)
    tmpl = jnp.concatenate([tmpl_ref[t, rows, :] for t in range(8)], axis=0)
    inv_size = 1.0 / TEMPL**3
    mean = jnp.sum(tmpl) * inv_size
    centred = tmpl - mean
    var = jnp.sum(centred * centred) * inv_size
    scale = 1.0 / (jnp.sqrt(jnp.full((1, LANES), var + EPSILON, F32)) * TEMPL**1.5)
    shift = ones_ref[:1] * mean

    wide = 8 * TEMPL
    narrow = tmpl.astype(BF16)
    block = jnp.concatenate(
        [narrow[:, g * wide : (g + 1) * wide] for g in range(TEMPL // 8)], axis=0
    )
    for j in range(8):
        window = block[:, : 2 * LANES] if j < 4 else block[:, LANES:]
        out = jnp.dot(window, z_ref[j], preferred_element_type=F32)
        part = out[:, :LANES] + out[:, LANES:] - shift
        for g in range(TEMPL // 8):
            start = (8 * g + j) * odd(TEMPL)
            store(depth_buf, start, part[g * TEMPL : (g + 1) * TEMPL])

    def gather_a(i, slot):
        value = pick(depth_buf, [GROUP * i + u for u in range(GROUP)], TEMPL, odd(TEMPL))
        first_buf[slot] = split_rows(value, True)

    def y_step(i, slot):
        plus, minus = pair_dot(y_ref[...], first_buf[slot], True)
        for u in range(GROUP):
            start = (GROUP * i + u) * odd(2 * pad_y)
            store(rows_buf, start, lane_block(plus, u))
            store(rows_buf, start + pad_y, lane_block(minus, u))

    pipeline(TEMPL // GROUP, [gather_a, y_step], 2)

    def gather_ky(i, slot):
        firsts = [GROUP // 2 * i + u // 2 + u % 2 * pad_y for u in range(GROUP)]
        first_buf[slot] = split_rows(pick(rows_buf, firsts, TEMPL, odd(2 * pad_y)), True)

    def multiply(i, slot):
        plus, minus = pair_dot(x_ref[...], first_buf[slot], True)
        spec = jnp.concatenate([plus, minus], axis=0)
        prod = spec * spec_ref[i, 0] + swap(spec) * spec_ref[i, 1]
        second_buf[slot] = split_rows(prod, False)

    def back_x(i, slot):
        plus, minus = pair_dot(bx_ref[...], second_buf[slot], False)
        for u in range(GROUP):
            start = (GROUP * i + u) * odd(x_cells)
            store(back_buf, start, lane_block(plus, u))
            store(back_buf, start + x_cells // 2, lane_block(minus, u))

    pipeline(n_y // GROUP, [gather_ky, multiply, back_x], 2)

    def gather_x(i, slot):
        value = pick(back_buf, [GROUP * i + u for u in range(GROUP)], n_y, odd(x_cells))
        third_buf[slot] = split_rows(value, False)

    def back_y(i, slot):
        plus, minus = pair_dot(by_ref[...], third_buf[slot], False)
        for u in range(GROUP):
            row = GROUP * i + u
            x = jnp.where(row < x_cells // 2, row + x_cells // 2, x_cells - 1 - row)
            store(vol_buf, x * odd(y_cells), lane_block(plus, u))
            store(vol_buf, x * odd(y_cells) + y_cells // 2, lane_block(minus, u))

    pipeline(x_cells // GROUP, [gather_x, back_y], 2)

    share = y_cells // 8
    me = place_ref[0]
    total = jnp.zeros((x_cells, LANES), F32)
    number = jnp.zeros((x_cells, LANES), F32)
    targets = [mine_ref, side_ref, far_ref.at[0], far_ref.at[1]]
    for p, target in enumerate(targets):
        first = (me ^ p) * share
        values = []
        for i in range(share):
            firsts = []
            for j in range(2):
                y = 2 * (first + i) + j
                firsts.append(jnp.where(y < y_cells // 2, y_cells - 1 - y, y - y_cells // 2))
            values.append(pick(vol_buf, firsts, x_cells, odd(y_cells)))
        value = jnp.concatenate(values, axis=0)
        out = jnp.dot(split_rows(value, False), bz_ref[...], preferred_element_type=F32)
        rows = value.shape[0]
        full = out[:rows, :LANES] + out[:rows, LANES:] + out[rows:, :LANES]
        for i in range(share):
            corr = full[i * x_cells : (i + 1) * x_cells] * scale
            target[:, i * LANES : (i + 1) * LANES] = corr
            mask = mask_ref[first + i]
            total = total + corr * mask
            number = number + mask
    number_sum = jnp.sum(number)
    total_sum = jnp.sum(total)
    local_mean = jnp.full((1, LANES), total_sum, F32) / jnp.maximum(number_sum, 1.0)
    square = jnp.zeros((x_cells, LANES), F32)
    for p, target in enumerate(targets):
        first = (me ^ p) * share
        for i in range(share):
            gap = target[:, i * LANES : (i + 1) * LANES] - local_mean
            square = square + gap * gap * mask_ref[first + i]
    row = lax.broadcasted_iota(jnp.int32, (8, LANES), 0)
    stat_ref[...] = jnp.where(row == 0, number_sum, jnp.where(row == 1, total_sum, jnp.sum(square)))


def correlate(place, bank, rot, mask, spec, tmpl_z, dims, tables):
    x_cells, y_cells, z_cells = dims
    n_x, n_y = x_cells + TEMPL, y_cells + HALF
    pad_y = n_y // 2 + -(n_y // 2) % 8
    width = y_cells * z_cells // 4
    vmem = pl.BlockSpec(memory_space=pltpu.VMEM)
    return pl.pallas_call(
        functools.partial(corr_kernel, dims, rot),
        out_shape=(
            jax.ShapeDtypeStruct((x_cells, width), F32),
            jax.ShapeDtypeStruct((x_cells, width), F32),
            jax.ShapeDtypeStruct((2, x_cells, width), F32),
            jax.ShapeDtypeStruct((8, LANES), F32),
        ),
        in_specs=[pl.BlockSpec(memory_space=pltpu.SMEM)] + [vmem] * 10,
        out_specs=(vmem,) * 4,
        scratch_shapes=[
            pltpu.VMEM((TEMPL * odd(TEMPL), LANES), F32),
            pltpu.VMEM((TEMPL * odd(2 * pad_y), LANES), F32),
            pltpu.VMEM((2, 3 * TEMPL, GROUP * LANES), BF16),
            pltpu.VMEM((2, 2 * n_x, GROUP * LANES), BF16),
            pltpu.VMEM((2, 2 * n_y, GROUP * LANES), BF16),
            pltpu.VMEM((n_y * odd(x_cells), LANES), F32),
            pltpu.VMEM((x_cells * odd(y_cells), LANES), F32),
        ],
        compiler_params=pltpu.CompilerParams(vmem_limit_bytes=24 * 1024 * 1024),
        cost_estimate=pl.CostEstimate(flops=15 * 10**9, bytes_accessed=10**7, transcendentals=0),
        name="correlate",
    )(
        place, bank, mask, spec,
        tmpl_z, tables["ones_z"], tables["tmpl_y"], tables["tmpl_x"],
        tables["back_x"], tables["back_y"], tables["back_z"],
    )


def score_kernel(place_ref, coef_ref, mask_ref, *refs):
    pieces = refs[: len(refs) - 3]
    best_ref, evid_ref, mom_ref = refs[len(refs) - 3 :]

    blocks = best_ref.shape[1] // LANES

    def step(i):
        lanes = pl.ds(pl.multiple_of(i * LANES, LANES), LANES)
        for top in range(0, best_ref.shape[0], 8):
            rows = slice(top, top + 8)
            mask = mask_ref[place_ref[0] * blocks + i, rows]
            scores = []
            for k, piece in enumerate(pieces):
                scores.append((piece[rows, lanes] - coef_ref[k, 0]) * coef_ref[k, 1])
            high = functools.reduce(jnp.maximum, scores)
            total = jnp.zeros_like(high)
            moment = [jnp.zeros_like(high) for _ in range(4)]
            for k, score in enumerate(scores):
                weight = jnp.exp(score - high)
                total = total + weight
                for c in range(4):
                    moment[c] = moment[c] + weight * coef_ref[k, 2 + c]
            best_ref[rows, lanes] = mask * high
            evid_ref[rows, lanes] = mask * (high + jnp.log(total))
            share = mask / total
            for c in range(4):
                mom_ref[c, rows, lanes] = moment[c] * share

    loop(blocks, step)


def combine(place, coefs, mask, pieces):
    shape = pieces[0].shape
    vmem = pl.BlockSpec(memory_space=pltpu.VMEM)
    out = jax.ShapeDtypeStruct(shape, F32)
    return pl.pallas_call(
        score_kernel,
        out_shape=(out, out, jax.ShapeDtypeStruct((4,) + shape, F32)),
        in_specs=[pl.BlockSpec(memory_space=pltpu.SMEM)] * 2 + [vmem] * (1 + len(pieces)),
        out_specs=(vmem,) * 3,
        compiler_params=pltpu.CompilerParams(vmem_limit_bytes=16 * 1024 * 1024),
        name="combine",
    )(place, coefs, mask, *pieces)


def gather_steps(count):
    return [1 << i for i in reversed(range(count.bit_length() - 1))]


def gather_step(block, axis, step):
    count = lax.axis_size(axis)
    other = lax.ppermute(block, axis, [(i, i ^ step) for i in range(count)])
    upper = (lax.axis_index(axis) & step) != 0
    pair = [jnp.where(upper, other, block), jnp.where(upper, block, other)]
    return jnp.stack(pair, axis=1).reshape((-1,) + block.shape[1:])


def merge(first, other):
    number_a, number_b = first[:1], other[:1]
    mean_a = first[1:2] / jnp.maximum(number_a, 1.0)
    mean_b = other[1:2] / jnp.maximum(number_b, 1.0)
    gap = mean_b - mean_a
    between = gap * gap * (number_a * number_b / jnp.maximum(number_a + number_b, 1.0))
    return first + other + jnp.where(jnp.arange(3)[:, None] == 2, between, 0.0)


def exchange_all(block, axis, low, high):
    count = lax.axis_size(axis)
    parts = [block]
    for step in range(low, high, low):
        parts.append(lax.ppermute(block, axis, [(i, i ^ step) for i in range(count)]))
    return jnp.stack(parts)


def neighbours(block, axis):
    count = lax.axis_size(axis)
    forward = [(i, i + 1) for i in range(count - 1)]
    backward = [(target, source) for source, target in forward]
    return lax.ppermute(block, axis, forward), lax.ppermute(block, axis, backward)


def local(tomogram, templates, valid, quats, rot_index):
    x_cells, voxels = tomogram.shape
    y_cells = valid.shape[1]
    z_cells = voxels // y_cells
    dims = (x_cells, y_cells, z_cells)
    tables = {name: jnp.asarray(table) for name, table in make_tables(*dims).items()}
    groups = lax.axis_size("rot")
    tiles = lax.axis_size("tile")
    me = lax.axis_index("rot")
    rots = templates.shape[0]

    row = TEMPL * TEMPL
    chunk = templates.shape[1]
    whole_rows = chunk % row == 0
    block = templates.reshape(rots * chunk // row, row) if whole_rows else templates
    block = block[None]
    steps = gather_steps(tiles)
    block = gather_step(block, "tile", steps[0])
    half = x_cells // 2
    piece = lax.dynamic_slice_in_dim(tomogram, (me & 1) * half, half, 0)
    mine = jnp.stack(neighbours(piece, "tile"))
    side_swap = [(i, i ^ 1) for i in range(groups)]
    other = lax.ppermute(mine, "rot", side_swap)
    for step in steps[1:-1]:
        block = gather_step(block, "tile", step)
    one_hot = (rot_index[:, None] == jnp.arange(quats.shape[1], dtype=jnp.int32)[None, :]).astype(F32)
    orient = jnp.einsum("rq,kq->rk", one_hot, quats, precision=lax.Precision.HIGHEST)
    place = me_place = jnp.reshape(me, (1,)).astype(jnp.int32)
    own = slab_rows(place, [tomogram], x_cells, dims, tables, "slab_own")
    halo = slab_rows(place, [mine, other], TEMPL, dims, tables, "slab_halo")
    spec, mask, tmpl_z = slab_x(own, halo, valid, dims, tables)
    block = gather_step(block, "tile", steps[-1])
    if not whole_rows:
        block = jnp.transpose(block, (1, 0, 2)).reshape(rots, 8, TEMPL // 8, row)
        block = jnp.transpose(block, (1, 0, 2, 3))
    bank = block.reshape(8, rots * (TEMPL // 8), row).astype(F32)
    far_swap = [(i, i ^ 2) for i in range(groups)]
    mines, sides, fars, from_sides, stats = [], [], [], [], []
    for r in range(rots):
        if r >= 2:
            place, fars[r - 2] = lax.optimization_barrier((place, fars[r - 2]))
        if r >= 3:
            place, from_sides[r - 3] = lax.optimization_barrier((place, from_sides[r - 3]))
        mine, side, far, stat = correlate(place, bank, r, mask, spec, tmpl_z, dims, tables)
        if r >= 1:
            stat, fars[r - 1] = lax.optimization_barrier((stat, fars[r - 1]))
        if r >= 1 and r < rots - 1:
            both = jnp.stack([sides[r - 1], fars[r - 1][1]])
        mines.append(mine)
        sides.append(side)
        stats.append(stat[:3, 0])
        fars.append(lax.ppermute(far, "rot", far_swap))
        if r >= 1 and r < rots - 1:
            from_sides.append(lax.ppermute(both, "rot", side_swap))
    state = jnp.stack(stats, axis=1)
    state, fars[rots - 2], from_sides[rots - 3] = lax.optimization_barrier(
        (state, fars[rots - 2], from_sides[rots - 3])
    )
    last = jnp.stack([part for r in range(rots - 2, rots) for part in (sides[r], fars[r][1])])
    step = 1
    while step < tiles:
        partner = lax.ppermute(state, "tile", [(i, i ^ step) for i in range(tiles)])
        step *= 2
        if step == tiles:
            partner, last = lax.optimization_barrier((partner, last))
        state = merge(state, partner)
    average = state[1] / state[0]
    inverse = 1.0 / jnp.sqrt(state[2] / state[0] + EPSILON)
    coefs = jnp.concatenate([average[:, None], inverse[:, None], orient], axis=1)
    coefs = exchange_all(coefs, "rot", 1, groups)
    last = lax.ppermute(last, "rot", side_swap)
    from_sides += [last[:2], last[2:]]
    flat = mines + [f[0] for f in from_sides] + [f[0] for f in fars] + [f[1] for f in from_sides]
    return combine(me_place, coefs.reshape(groups * rots, 6), mask, flat)


def solution(mesh):
    placed = (P("tile", None), P("rot", "tile"), P("tile", None), P(), P("rot"))
    return jax.shard_map(
        local,
        mesh=mesh,
        in_specs=placed,
        out_specs=(P("tile", "rot"), P("tile", "rot"), P(None, "tile", "rot")),
        check_vma=False,
    )
```

```python
import functools
import math

import jax
import jax.numpy as jnp
import ml_dtypes
import numpy as np
from jax import lax
from jax.experimental import pallas as pl
from jax.experimental.pallas import tpu as pltpu
from jax.sharding import PartitionSpec as P

TEMPL = 48
HALF = 24
EPSILON = 1e-06
LANES = 128
SPLIT = 64
BLOCKS = 8
EACH = TEMPL // BLOCKS
CHUNKS = TEMPL * TEMPL // LANES
BLOCK_ROWS = EACH * CHUNKS + -EACH * CHUNKS % 16
HELD = (0, 4, 2, 6)
F32 = jnp.float32
BF16 = jnp.bfloat16


def two_parts(table):
    high = table.astype(ml_dtypes.bfloat16)
    low = (table - high.astype(np.float64)).astype(ml_dtypes.bfloat16)
    return high, low


def row_table(out_idx, in_idx, length, sign, factor, wide):
    theta = 2.0 * math.pi / length * np.outer(out_idx, in_idx)
    pad = np.zeros((-len(out_idx) % 8, len(in_idx)))
    full = np.concatenate([np.cos(theta), pad, sign * np.sin(theta), pad], axis=0) * factor
    high, low = two_parts(full)
    if wide:
        return np.concatenate([high, high, low], axis=1)
    zeros = np.zeros_like(low)
    return np.concatenate(
        [np.concatenate([high, high], axis=1), np.concatenate([low, zeros], axis=1)], axis=0
    )


def depth_table(in_idx, length, sign, factor):
    freq = np.arange(length // 2) + 0.5
    theta = 2.0 * math.pi / length * np.outer(in_idx, freq)
    out = np.zeros((len(in_idx), LANES))
    out[:, : length // 2] = np.cos(theta) * factor
    out[:, SPLIT : SPLIT + length // 2] = sign * np.sin(theta) * factor
    return out


def half_odd(count):
    return np.arange(count // 2) + 0.5


def make_tables(x_cells, y_cells, z_cells):
    n_x, n_y, n_z = x_cells + TEMPL, y_cells + HALF, z_cells + HALF
    k_x, k_y = half_odd(n_x), half_odd(n_y)
    both_x = np.concatenate([k_x, -k_x])
    both_y = np.stack([k_y, -k_y], axis=1).reshape(-1)
    mid_x, mid_y = (x_cells - 1) / 2, (y_cells - 1) / 2
    tables = {}
    slab = np.zeros((2 * z_cells, 4 * LANES), ml_dtypes.bfloat16)
    high, low = two_parts(depth_table(np.arange(z_cells), n_z, -1.0, 1.0))
    for j in range(2):
        rows = slice(j * z_cells, (j + 1) * z_cells)
        slab[rows, 2 * j * LANES : (2 * j + 1) * LANES] = high
        slab[rows, (2 * j + 1) * LANES : (2 * j + 2) * LANES] = low
    slab_y = row_table(k_y, np.arange(y_cells), n_y, -1.0, 1.0, True)
    slab_y = np.pad(slab_y, ((0, 0), (0, slab.shape[1] - slab_y.shape[1])))
    tables["slab_rows"] = np.concatenate([slab, slab_y], axis=0)
    own = np.arange(HALF, HALF + x_cells)
    halo = np.concatenate([np.arange(HALF), np.arange(HALF + x_cells, n_x)])
    tables["slab_x"] = row_table(k_x, np.concatenate([own, halo]), n_x, -1.0, 1.0, True)
    high, low = two_parts(depth_table(np.arange(TEMPL) - HALF, n_z, 1.0, 1.0))
    tables["tmpl_z"] = np.concatenate([high, low], axis=1)
    ones = (high.astype(np.float64) + low.astype(np.float64)).sum(axis=0)
    tables["ones_z"] = np.broadcast_to(ones.astype(np.float32)[None], (8, LANES)).copy()
    tables["tmpl_y"] = row_table(k_y, np.arange(TEMPL) - HALF + mid_y, n_y, 1.0, 1.0, True)
    tmpl_rows = np.arange(TEMPL).reshape(BLOCKS, EACH).T.reshape(-1)
    tables["tmpl_x"] = row_table(k_x, tmpl_rows + mid_x, n_x, 1.0, 1.0, True)
    tables["back_x"] = row_table(half_odd(x_cells), both_x, n_x, 1.0, 1.0 / n_x, False)
    tables["back_y"] = row_table(half_odd(y_cells), both_y, n_y, 1.0, 1.0 / n_y, False)
    back = depth_table(np.arange(z_cells), n_z, -1.0, 2.0 / n_z).T
    high, low = two_parts(back)
    back_z = np.zeros((2 * LANES, 2 * LANES), ml_dtypes.bfloat16)
    for j in range(2):
        rows = slice(j * LANES, (j + 1) * LANES)
        back_z[rows, j * z_cells : (j + 1) * z_cells] = high
        back_z[rows, LANES + j * z_cells : LANES + (j + 1) * z_cells] = low
    tables["back_z"] = back_z
    return tables


def split_rows(value, wide):
    high = value.astype(BF16)
    if value.shape[0] % 16 == 0:
        low = (value - high.astype(F32)).astype(BF16)
        return jnp.concatenate([high, low, high] if wide else [high, low], axis=0)
    high = high.astype(F32)
    low = value - high
    return jnp.concatenate([high, low, high] if wide else [high, low], axis=0).astype(BF16)


def swap(value):
    parts = [
        pltpu.roll(value[:, s : s + LANES], SPLIT, 1) for s in range(0, value.shape[1], LANES)
    ]
    return jnp.concatenate(parts, axis=1)


def lane_sign(width):
    lane = lax.broadcasted_iota(jnp.int32, (8, width), 1) % LANES
    return jnp.where(lane < SPLIT, -1.0, 1.0)[:1]


def pair_rows(table, value, wide):
    return pair_dot(table, split_rows(value, wide), wide)


def pair_dot(table, parts, wide):
    out = jnp.dot(table, parts, preferred_element_type=F32)
    if not wide:
        half = out.shape[0] // 2
        out = out[:half] + out[half:]
    half = out.shape[0] // 2
    turned = swap(out[half:]) * lane_sign(out.shape[1])
    return out[:half] + turned, out[:half] - turned


def pick(ref, firsts, count, stride):
    return jnp.concatenate([ref[pl.ds(f, count, stride=stride), :] for f in firsts], axis=1)


def store(ref, start, value):
    ref[pl.ds(start, value.shape[0]), :] = value


def odd(rows):
    return rows + 1


def lane_block(value, i):
    return value[:, i * LANES : (i + 1) * LANES]


def loop(count, body):
    def one(i, carry):
        body(i)
        return carry

    lax.fori_loop(0, count, one, 0)


GROUP = 8


def pipeline(steps, stages, width):
    blocks = -(-steps // width)
    depth = len(stages)

    def turn(t, static):
        for s in reversed(range(depth)):
            if static and not 0 <= t - s < blocks:
                continue
            for slot in range(width):
                step = (t - s) * width + slot
                if not static or step < steps:
                    stages[s](step, slot)

    full = steps // width
    first, last = depth - 1, max(full, depth - 1)
    for t in range(first):
        turn(t, True)
    if last - first >= 2:
        loop(last - first, lambda i: turn(i + first, False))
    else:
        last = first
    for t in range(last, blocks + depth - 1):
        turn(t, True)


def slab_rows_kernel(dims, place_ref, *refs):
    sources, (table_ref, rows_ref, depth_buf, parts_buf) = refs[:-4], refs[-4:]
    x_cells, y_cells, z_cells = dims
    half = x_cells // 2
    count = depth_buf.shape[0] // y_cells - 1
    n_y = y_cells + HALF
    pad_y = n_y // 2 + -(n_y // 2) % 8
    many = 4

    def read(lanes):
        if len(sources) == 1:
            return sources[0][:, lanes].astype(F32)
        first = (place_ref[0] & 1) == 0
        mine, other = ([ref[i, :, lanes].astype(F32) for i in range(2)] for ref in sources)
        low, high = (
            jnp.concatenate([jnp.where(first, m, o), jnp.where(first, o, m)], axis=0)
            for m, o in zip(mine, other)
        )
        return jnp.concatenate([low[x_cells - HALF :], high[:HALF]], axis=0)

    def depth_step(i):
        lanes = [pl.ds(pl.multiple_of((many * i + u) * LANES, LANES), LANES) for u in range(many)]
        block = jnp.concatenate([read(l) for l in lanes], axis=0).astype(BF16)
        out = jnp.dot(block, table_ref[: 2 * z_cells], preferred_element_type=F32)
        for u in range(many):
            part = out[u * count : (u + 1) * count]
            for j in range(2):
                store(
                    depth_buf, (2 * many * i + 2 * u + j) * odd(count),
                    lane_block(part, 2 * j) + lane_block(part, 2 * j + 1),
                )

    loop(y_cells // (2 * many), depth_step)

    def gather_rows(i, slot):
        value = pick(depth_buf, [GROUP * i + u for u in range(GROUP)], y_cells, odd(count))
        parts_buf[slot] = split_rows(value, True)

    def y_step(i, slot):
        plus, minus = pair_dot(table_ref[2 * z_cells :, : 3 * y_cells], parts_buf[slot], True)
        for u in range(GROUP):
            start = (GROUP * i + u) * odd(2 * pad_y)
            store(rows_ref, start, lane_block(plus, u))
            store(rows_ref, start + pad_y, lane_block(minus, u))

    pipeline(count // GROUP, [gather_rows, y_step], 2)


def slab_rows(place, blocks, count, dims, tables, name):
    x_cells, y_cells, z_cells = dims
    n_y = y_cells + HALF
    pad_y = n_y // 2 + -(n_y // 2) % 8
    vmem = pl.BlockSpec(memory_space=pltpu.VMEM)
    return pl.pallas_call(
        functools.partial(slab_rows_kernel, dims),
        out_shape=jax.ShapeDtypeStruct((count * odd(2 * pad_y), LANES), F32),
        in_specs=[pl.BlockSpec(memory_space=pltpu.SMEM)] + [vmem] * (1 + len(blocks)),
        out_specs=vmem,
        scratch_shapes=[
            pltpu.VMEM((y_cells * odd(count), LANES), F32),
            pltpu.VMEM((2, 3 * y_cells, GROUP * LANES), BF16),
        ],
        compiler_params=pltpu.CompilerParams(vmem_limit_bytes=20 * 1024 * 1024),
        cost_estimate=pl.CostEstimate(flops=count * 10**8, bytes_accessed=10**6, transcendentals=0),
        name=name,
    )(place, *blocks, tables["slab_rows"])


def slab_x_kernel(
    dims, own_ref, halo_ref, x_ref, valid_ref, tz_ref, spec_ref, mask_ref, z_ref, parts_buf
):
    x_cells, y_cells, z_cells = dims
    n_y = y_cells + HALF
    pad_y = n_y // 2 + -(n_y // 2) % 8

    def gather_rows(i, slot):
        firsts = [GROUP // 2 * i + u // 2 + u % 2 * pad_y for u in range(GROUP)]
        value = jnp.concatenate(
            [
                pick(own_ref, firsts, x_cells, odd(2 * pad_y)),
                pick(halo_ref, firsts, TEMPL, odd(2 * pad_y)),
            ],
            axis=0,
        )
        parts_buf[slot] = split_rows(value, True)

    def x_step(i, slot):
        plus, minus = pair_dot(x_ref[...], parts_buf[slot], True)
        spec = jnp.concatenate([plus, minus], axis=0)
        turned = swap(spec)
        real_lane = lane_sign(GROUP * LANES) < 0
        spec_ref[i, 0] = jnp.where(real_lane, spec, turned)
        spec_ref[i, 1] = jnp.where(real_lane, -turned, spec)

    pipeline(n_y // GROUP, [gather_rows, x_step], 2)

    valid = valid_ref[...].astype(F32)
    low_lane = lax.broadcasted_iota(jnp.int32, (x_cells, LANES), 1) < z_cells
    for q in range(y_cells // 2):
        mask_ref[q] = jnp.where(low_lane, valid[:, 2 * q : 2 * q + 1], valid[:, 2 * q + 1 : 2 * q + 2])
    z_ref[...] = jnp.zeros(z_ref.shape, BF16)
    for j in range(8):
        start = TEMPL * j - (LANES if j >= 4 else 0)
        z_ref[j, start : start + TEMPL, :] = tz_ref[...]


def slab_x(own, halo, valid, dims, tables):
    x_cells, y_cells, z_cells = dims
    n_x, n_y = x_cells + TEMPL, y_cells + HALF
    steps = n_y // GROUP
    vmem = pl.BlockSpec(memory_space=pltpu.VMEM)
    shape = (steps, 2, n_x, GROUP * LANES)
    return pl.pallas_call(
        functools.partial(slab_x_kernel, dims),
        out_shape=(
            jax.ShapeDtypeStruct(shape, F32),
            jax.ShapeDtypeStruct((y_cells // 2, x_cells, LANES), F32),
            jax.ShapeDtypeStruct((8, 2 * LANES, 2 * LANES), BF16),
        ),
        in_specs=[vmem] * 5,
        out_specs=(vmem,) * 3,
        scratch_shapes=[pltpu.VMEM((2, 3 * n_x, GROUP * LANES), BF16)],
        compiler_params=pltpu.CompilerParams(vmem_limit_bytes=20 * 1024 * 1024),
        cost_estimate=pl.CostEstimate(flops=5 * 10**9, bytes_accessed=10**6, transcendentals=0),
        name="slab_x",
    )(own, halo, tables["slab_x"], valid, tables["tmpl_z"])


def corr_kernel(
    dims, rot, entry, place_ref, held_ref, last_ref, mask_ref, spec_ref,
    z_ref, ones_ref, y_ref, x_ref, bx_ref, by_ref, bz_ref,
    mine_ref, side_ref, far_ref, stat_ref,
    bank_buf, depth_buf, rows_buf, first_buf, second_buf, third_buf, back_buf, vol_buf,
):
    x_cells, y_cells, z_cells = dims
    n_x, n_y = x_cells + TEMPL, y_cells + HALF
    half_y = n_y // 2
    pad_y = half_y + -half_y % 8
    for i, block in enumerate(HELD):
        for ref, at, tile in ((held_ref, rot, block), (last_ref, entry, block ^ 1)):
            store(bank_buf, (place_ref[1] ^ tile) * odd(BLOCK_ROWS), ref[at, i].astype(F32))
    tmpl = jnp.concatenate(
        [
            pick(bank_buf, [a * CHUNKS + i for i in range(CHUNKS)], BLOCKS, odd(BLOCK_ROWS))
            for a in range(EACH)
        ],
        axis=0,
    )
    inv_size = 1.0 / TEMPL**3
    mean = jnp.sum(tmpl) * inv_size
    centred = tmpl - mean
    var = jnp.sum(centred * centred) * inv_size
    scale = 1.0 / (jnp.sqrt(jnp.full((1, LANES), var + EPSILON, F32)) * TEMPL**1.5)
    shift = ones_ref[:1] * mean

    wide = 8 * TEMPL
    narrow = tmpl.astype(BF16)
    block = jnp.concatenate(
        [narrow[:, g * wide : (g + 1) * wide] for g in range(TEMPL // 8)], axis=0
    )
    for j in range(8):
        window = block[:, : 2 * LANES] if j < 4 else block[:, LANES:]
        out = jnp.dot(window, z_ref[j], preferred_element_type=F32)
        part = out[:, :LANES] + out[:, LANES:] - shift
        for g in range(TEMPL // 8):
            start = (8 * g + j) * odd(TEMPL)
            store(depth_buf, start, part[g * TEMPL : (g + 1) * TEMPL])

    def gather_a(i, slot):
        value = pick(depth_buf, [GROUP * i + u for u in range(GROUP)], TEMPL, odd(TEMPL))
        first_buf[slot] = split_rows(value, True)

    def y_step(i, slot):
        plus, minus = pair_dot(y_ref[...], first_buf[slot], True)
        for u in range(GROUP):
            start = (GROUP * i + u) * odd(2 * pad_y)
            store(rows_buf, start, lane_block(plus, u))
            store(rows_buf, start + pad_y, lane_block(minus, u))

    pipeline(TEMPL // GROUP, [gather_a, y_step], 2)

    def gather_ky(i, slot):
        firsts = [GROUP // 2 * i + u // 2 + u % 2 * pad_y for u in range(GROUP)]
        first_buf[slot] = split_rows(pick(rows_buf, firsts, TEMPL, odd(2 * pad_y)), True)

    def multiply(i, slot):
        plus, minus = pair_dot(x_ref[...], first_buf[slot], True)
        spec = jnp.concatenate([plus, minus], axis=0)
        prod = spec * spec_ref[i, 0] + swap(spec) * spec_ref[i, 1]
        second_buf[slot] = split_rows(prod, False)

    def back_x(i, slot):
        plus, minus = pair_dot(bx_ref[...], second_buf[slot], False)
        for u in range(GROUP):
            start = (GROUP * i + u) * odd(x_cells)
            store(back_buf, start, lane_block(plus, u))
            store(back_buf, start + x_cells // 2, lane_block(minus, u))

    pipeline(n_y // GROUP, [gather_ky, multiply, back_x], 2)

    def gather_x(i, slot):
        value = pick(back_buf, [GROUP * i + u for u in range(GROUP)], n_y, odd(x_cells))
        third_buf[slot] = split_rows(value, False)

    def back_y(i, slot):
        plus, minus = pair_dot(by_ref[...], third_buf[slot], False)
        for u in range(GROUP):
            row = GROUP * i + u
            x = jnp.where(row < x_cells // 2, row + x_cells // 2, x_cells - 1 - row)
            store(vol_buf, x * odd(y_cells), lane_block(plus, u))
            store(vol_buf, x * odd(y_cells) + y_cells // 2, lane_block(minus, u))

    pipeline(x_cells // GROUP, [gather_x, back_y], 2)

    share = y_cells // 8
    me = place_ref[0]
    total = jnp.zeros((x_cells, LANES), F32)
    number = jnp.zeros((x_cells, LANES), F32)
    targets = [mine_ref, side_ref, far_ref.at[0], far_ref.at[1]]
    for p, target in enumerate(targets):
        first = (me ^ p) * share
        values = []
        for i in range(share):
            firsts = []
            for j in range(2):
                y = 2 * (first + i) + j
                firsts.append(jnp.where(y < y_cells // 2, y_cells - 1 - y, y - y_cells // 2))
            values.append(pick(vol_buf, firsts, x_cells, odd(y_cells)))
        value = jnp.concatenate(values, axis=0)
        out = jnp.dot(split_rows(value, False), bz_ref[...], preferred_element_type=F32)
        rows = value.shape[0]
        full = out[:rows, :LANES] + out[:rows, LANES:] + out[rows:, :LANES]
        for i in range(share):
            corr = full[i * x_cells : (i + 1) * x_cells] * scale
            target[:, i * LANES : (i + 1) * LANES] = corr
            mask = mask_ref[first + i]
            total = total + corr * mask
            number = number + mask
    number_sum = jnp.sum(number)
    total_sum = jnp.sum(total)
    local_mean = jnp.full((1, LANES), total_sum, F32) / jnp.maximum(number_sum, 1.0)
    square = jnp.zeros((x_cells, LANES), F32)
    for p, target in enumerate(targets):
        first = (me ^ p) * share
        for i in range(share):
            gap = target[:, i * LANES : (i + 1) * LANES] - local_mean
            square = square + gap * gap * mask_ref[first + i]
    row = lax.broadcasted_iota(jnp.int32, (8, LANES), 0)
    stat_ref[...] = jnp.where(row == 0, number_sum, jnp.where(row == 1, total_sum, jnp.sum(square)))


def correlate(place, held, rot, last, entry, mask, spec, tmpl_z, dims, tables):
    x_cells, y_cells, z_cells = dims
    n_x, n_y = x_cells + TEMPL, y_cells + HALF
    pad_y = n_y // 2 + -(n_y // 2) % 8
    width = y_cells * z_cells // 4
    vmem = pl.BlockSpec(memory_space=pltpu.VMEM)
    return pl.pallas_call(
        functools.partial(corr_kernel, dims, rot, entry),
        out_shape=(
            jax.ShapeDtypeStruct((x_cells, width), F32),
            jax.ShapeDtypeStruct((x_cells, width), F32),
            jax.ShapeDtypeStruct((2, x_cells, width), F32),
            jax.ShapeDtypeStruct((8, LANES), F32),
        ),
        in_specs=[pl.BlockSpec(memory_space=pltpu.SMEM)] + [vmem] * 11,
        out_specs=(vmem,) * 4,
        scratch_shapes=[
            pltpu.VMEM((BLOCKS * odd(BLOCK_ROWS), LANES), F32),
            pltpu.VMEM((TEMPL * odd(TEMPL), LANES), F32),
            pltpu.VMEM((TEMPL * odd(2 * pad_y), LANES), F32),
            pltpu.VMEM((2, 3 * TEMPL, GROUP * LANES), BF16),
            pltpu.VMEM((2, 2 * n_x, GROUP * LANES), BF16),
            pltpu.VMEM((2, 2 * n_y, GROUP * LANES), BF16),
            pltpu.VMEM((n_y * odd(x_cells), LANES), F32),
            pltpu.VMEM((x_cells * odd(y_cells), LANES), F32),
        ],
        compiler_params=pltpu.CompilerParams(vmem_limit_bytes=24 * 1024 * 1024),
        cost_estimate=pl.CostEstimate(flops=15 * 10**9, bytes_accessed=10**7, transcendentals=0),
        name="correlate",
    )(
        place, held, last, mask, spec,
        tmpl_z, tables["ones_z"], tables["tmpl_y"], tables["tmpl_x"],
        tables["back_x"], tables["back_y"], tables["back_z"],
    )


def score_kernel(pieces, place_ref, coef_ref, mask_ref, *refs):
    best_ref, evid_ref, mom_ref = refs[len(refs) - 3 :]

    blocks = best_ref.shape[1] // LANES

    def step(i):
        lanes = pl.ds(pl.multiple_of(i * LANES, LANES), LANES)
        for top in range(0, best_ref.shape[0], 8):
            rows = slice(top, top + 8)
            mask = mask_ref[place_ref[0] * blocks + i, rows]
            scores = []
            for k, (at, entry) in enumerate(pieces):
                corr = refs[at][rows, lanes] if entry is None else refs[at][entry, rows, lanes]
                scores.append((corr - coef_ref[k, 0]) * coef_ref[k, 1])
            high = functools.reduce(jnp.maximum, scores)
            total = jnp.zeros_like(high)
            moment = [jnp.zeros_like(high) for _ in range(4)]
            for k, score in enumerate(scores):
                weight = jnp.exp(score - high)
                total = total + weight
                for c in range(4):
                    moment[c] = moment[c] + weight * coef_ref[k, 2 + c]
            best_ref[rows, lanes] = mask * high
            evid_ref[rows, lanes] = mask * (high + jnp.log(total))
            share = mask / total
            for c in range(4):
                mom_ref[c, rows, lanes] = moment[c] * share

    loop(blocks, step)


def combine(place, coefs, mask, arrays, pieces):
    shape = arrays[0].shape
    vmem = pl.BlockSpec(memory_space=pltpu.VMEM)
    out = jax.ShapeDtypeStruct(shape, F32)
    return pl.pallas_call(
        functools.partial(score_kernel, pieces),
        out_shape=(out, out, jax.ShapeDtypeStruct((4,) + shape, F32)),
        in_specs=[pl.BlockSpec(memory_space=pltpu.SMEM)] * 2 + [vmem] * (1 + len(arrays)),
        out_specs=(vmem,) * 3,
        compiler_params=pltpu.CompilerParams(vmem_limit_bytes=16 * 1024 * 1024),
        name="combine",
    )(place, coefs, mask, *arrays)


def swap_blocks(block, axis, step):
    return lax.ppermute(block, axis, [(i, i ^ step) for i in range(lax.axis_size(axis))])


def general_gather(templates):
    rots = templates.shape[0]
    count = lax.axis_size("tile")
    block = templates[:, None]
    for step in [1 << i for i in reversed(range(count.bit_length() - 1))]:
        other = swap_blocks(block, "tile", step)
        upper = (lax.axis_index("tile") & step) != 0
        pair = [jnp.where(upper, other, block), jnp.where(upper, block, other)]
        block = jnp.stack(pair, axis=2).reshape((rots, -1) + block.shape[2:])
    block = block.reshape(rots, BLOCKS, EACH * CHUNKS, LANES)
    block = jnp.pad(block, ((0, 0), (0, 0), (0, BLOCK_ROWS - EACH * CHUNKS), (0, 0)))
    held = jnp.stack([block[:, i] for i in HELD], axis=1)
    return held, jnp.stack([block[:, i ^ 1] for i in HELD], axis=1)


def merge(first, other):
    number_a, number_b = first[:1], other[:1]
    mean_a = first[1:2] / jnp.maximum(number_a, 1.0)
    mean_b = other[1:2] / jnp.maximum(number_b, 1.0)
    gap = mean_b - mean_a
    between = gap * gap * (number_a * number_b / jnp.maximum(number_a + number_b, 1.0))
    return first + other + jnp.where(jnp.arange(3)[:, None] == 2, between, 0.0)


def exchange_all(block, axis, low, high):
    count = lax.axis_size(axis)
    parts = [block]
    for step in range(low, high, low):
        parts.append(lax.ppermute(block, axis, [(i, i ^ step) for i in range(count)]))
    return jnp.stack(parts)


def neighbours(block, axis):
    count = lax.axis_size(axis)
    forward = [(i, i + 1) for i in range(count - 1)]
    backward = [(target, source) for source, target in forward]
    return lax.ppermute(block, axis, forward), lax.ppermute(block, axis, backward)


def local(tomogram, templates, valid, quats, rot_index):
    x_cells, voxels = tomogram.shape
    y_cells = valid.shape[1]
    z_cells = voxels // y_cells
    dims = (x_cells, y_cells, z_cells)
    tables = {name: jnp.asarray(table) for name, table in make_tables(*dims).items()}
    groups = lax.axis_size("rot")
    tiles = lax.axis_size("tile")
    me = lax.axis_index("rot")
    rots = templates.shape[0]

    tile = lax.axis_index("tile")
    by_blocks = tiles == BLOCKS
    if by_blocks:
        held = templates.reshape(rots, 1, EACH * CHUNKS, LANES)
        held = jnp.pad(held, ((0, 0), (0, 0), (0, BLOCK_ROWS - EACH * CHUNKS), (0, 0)))
        held = jnp.concatenate([held, swap_blocks(held, "tile", 4)], axis=1)
    half = x_cells // 2
    piece = lax.dynamic_slice_in_dim(tomogram, (me & 1) * half, half, 0)
    mine = jnp.stack(neighbours(piece, "tile"))
    side_swap = [(i, i ^ 1) for i in range(groups)]
    other = lax.ppermute(mine, "rot", side_swap)
    if by_blocks:
        held = jnp.concatenate([held, swap_blocks(held, "tile", 2)], axis=1)
    else:
        held, last = general_gather(templates)
        tile = jnp.zeros_like(tile)
    one_hot = (rot_index[:, None] == jnp.arange(quats.shape[1], dtype=jnp.int32)[None, :]).astype(F32)
    orient = jnp.einsum("rq,kq->rk", one_hot, quats, precision=lax.Precision.HIGHEST)
    place = me_place = jnp.stack([me, tile]).astype(jnp.int32)
    own = slab_rows(place, [tomogram], x_cells, dims, tables, "slab_own")
    halo = slab_rows(place, [mine, other], TEMPL, dims, tables, "slab_halo")
    if by_blocks:
        held, halo = lax.optimization_barrier((held, halo))
        lasts = [swap_blocks(held[:1], "tile", 1), swap_blocks(held[1:], "tile", 1)]
    else:
        lasts = [last[:1], last[1:]]
    spec, mask, tmpl_z = slab_x(own, halo, valid, dims, tables)
    far_swap = [(i, i ^ 2) for i in range(groups)]
    mines, sides, fars, stats = [], [], [], []
    for r in range(rots):
        if r >= 2:
            place, fars[r - 2] = lax.optimization_barrier((place, fars[r - 2]))
        mine, side, far, stat = correlate(
            place, held, r, lasts[min(r, 1)], max(r - 1, 0), mask, spec, tmpl_z, dims, tables
        )
        if r >= 1:
            stat, fars[r - 1] = lax.optimization_barrier((stat, fars[r - 1]))
        mines.append(mine)
        sides.append(side)
        stats.append(stat[:3, 0])
        fars.append(lax.ppermute(far, "rot", far_swap))
        if r == rots - 2:
            early = jnp.stack(sides + [f[1] for f in fars[:-1]])
            early = lax.ppermute(early, "rot", side_swap)
    state = jnp.stack(stats, axis=1)
    state, early, fars[rots - 2] = lax.optimization_barrier((state, early, fars[rots - 2]))
    last = jnp.stack([sides[rots - 1], fars[rots - 2][1], fars[rots - 1][1]])
    step = 1
    while step < tiles:
        partner = lax.ppermute(state, "tile", [(i, i ^ step) for i in range(tiles)])
        step *= 2
        if step == tiles:
            partner, last = lax.optimization_barrier((partner, last))
        state = merge(state, partner)
    average = state[1] / state[0]
    inverse = 1.0 / jnp.sqrt(state[2] / state[0] + EPSILON)
    coefs = jnp.concatenate([average[:, None], inverse[:, None], orient], axis=1)
    coefs = exchange_all(coefs, "rot", 1, groups)
    last = lax.ppermute(last, "rot", side_swap)
    arrays = mines + fars + [early, last]
    at_far, at_early, at_last = rots, 2 * rots, 2 * rots + 1
    pieces = [(r, None) for r in range(rots)]
    pieces += [(at_early, r) for r in range(rots - 1)] + [(at_last, 0)]
    pieces += [(at_far + r, 0) for r in range(rots)]
    pieces += [(at_early, rots - 1 + r) for r in range(rots - 2)] + [(at_last, 1), (at_last, 2)]
    return combine(me_place, coefs.reshape(groups * rots, 6), mask, arrays, pieces)


def solution(mesh):
    placed = (P("tile", None), P("rot", "tile"), P("tile", None), P(), P("rot"))
    return jax.shard_map(
        local,
        mesh=mesh,
        in_specs=placed,
        out_specs=(P("tile", "rot"), P("tile", "rot"), P(None, "tile", "rot")),
        check_vma=False,
    )
```

```python
import functools
import math

import jax
import jax.numpy as jnp
import ml_dtypes
import numpy as np
from jax import lax
from jax.experimental import pallas as pl
from jax.experimental.pallas import tpu as pltpu
from jax.sharding import PartitionSpec as P

TEMPL = 48
HALF = 24
EPSILON = 1e-06
LANES = 128
SPLIT = 64
BLOCKS = 8
EACH = TEMPL // BLOCKS
CHUNKS = TEMPL * TEMPL // LANES
BLOCK_ROWS = EACH * CHUNKS + -EACH * CHUNKS % 16
HELD = (0, 4, 2, 6)
F32 = jnp.float32
BF16 = jnp.bfloat16


def two_parts(table):
    high = table.astype(ml_dtypes.bfloat16)
    low = (table - high.astype(np.float64)).astype(ml_dtypes.bfloat16)
    return high, low


def row_table(out_idx, in_idx, length, sign, factor, wide):
    theta = 2.0 * math.pi / length * np.outer(out_idx, in_idx)
    pad = np.zeros((-len(out_idx) % 8, len(in_idx)))
    full = np.concatenate([np.cos(theta), pad, sign * np.sin(theta), pad], axis=0) * factor
    high, low = two_parts(full)
    if wide:
        return np.concatenate([high, high, low], axis=1)
    zeros = np.zeros_like(low)
    return np.concatenate(
        [np.concatenate([high, high], axis=1), np.concatenate([low, zeros], axis=1)], axis=0
    )


def depth_table(in_idx, length, sign, factor):
    freq = np.arange(length // 2) + 0.5
    theta = 2.0 * math.pi / length * np.outer(in_idx, freq)
    out = np.zeros((len(in_idx), LANES))
    out[:, : length // 2] = np.cos(theta) * factor
    out[:, SPLIT : SPLIT + length // 2] = sign * np.sin(theta) * factor
    return out


def half_odd(count):
    return np.arange(count // 2) + 0.5


def make_tables(x_cells, y_cells, z_cells):
    n_x, n_y, n_z = x_cells + TEMPL, y_cells + HALF, z_cells + HALF
    k_x, k_y = half_odd(n_x), half_odd(n_y)
    both_x = np.concatenate([k_x, -k_x])
    both_y = np.stack([k_y, -k_y], axis=1).reshape(-1)
    mid_x, mid_y = (x_cells - 1) / 2, (y_cells - 1) / 2
    tables = {}
    slab = np.zeros((2 * z_cells, 4 * LANES), ml_dtypes.bfloat16)
    high, low = two_parts(depth_table(np.arange(z_cells), n_z, -1.0, 1.0))
    for j in range(2):
        rows = slice(j * z_cells, (j + 1) * z_cells)
        slab[rows, 2 * j * LANES : (2 * j + 1) * LANES] = high
        slab[rows, (2 * j + 1) * LANES : (2 * j + 2) * LANES] = low
    slab_y = row_table(k_y, np.arange(y_cells), n_y, -1.0, 1.0, True)
    slab_y = np.pad(slab_y, ((0, 0), (0, slab.shape[1] - slab_y.shape[1])))
    tables["slab_rows"] = np.concatenate([slab, slab_y], axis=0)
    own = np.arange(HALF, HALF + x_cells)
    halo = np.concatenate([np.arange(HALF), np.arange(HALF + x_cells, n_x)])
    tables["slab_x"] = row_table(k_x, np.concatenate([own, halo]), n_x, -1.0, 1.0, True)
    high, low = two_parts(depth_table(np.arange(TEMPL) - HALF, n_z, 1.0, 1.0))
    tables["tmpl_z"] = np.concatenate([high, low], axis=1)
    ones = (high.astype(np.float64) + low.astype(np.float64)).sum(axis=0)
    tables["ones_z"] = np.broadcast_to(ones.astype(np.float32)[None], (8, LANES)).copy()
    tables["tmpl_y"] = row_table(k_y, np.arange(TEMPL) - HALF + mid_y, n_y, 1.0, 1.0, True)
    tmpl_rows = np.arange(TEMPL).reshape(BLOCKS, EACH).T.reshape(-1)
    tables["tmpl_x"] = row_table(k_x, tmpl_rows + mid_x, n_x, 1.0, 1.0, True)
    tables["back_x"] = row_table(half_odd(x_cells), both_x, n_x, 1.0, 1.0 / n_x, False)
    tables["back_y"] = row_table(half_odd(y_cells), both_y, n_y, 1.0, 1.0 / n_y, False)
    back = depth_table(np.arange(z_cells), n_z, -1.0, 2.0 / n_z).T
    high, low = two_parts(back)
    back_z = np.zeros((2 * LANES, 2 * LANES), ml_dtypes.bfloat16)
    for j in range(2):
        rows = slice(j * LANES, (j + 1) * LANES)
        back_z[rows, j * z_cells : (j + 1) * z_cells] = high
        back_z[rows, LANES + j * z_cells : LANES + (j + 1) * z_cells] = low
    tables["back_z"] = back_z
    return tables


def split_rows(value, wide):
    high = value.astype(BF16)
    if value.shape[0] % 16 == 0:
        low = (value - high.astype(F32)).astype(BF16)
        return jnp.concatenate([high, low, high] if wide else [high, low], axis=0)
    high = high.astype(F32)
    low = value - high
    return jnp.concatenate([high, low, high] if wide else [high, low], axis=0).astype(BF16)


def swap(value):
    parts = [
        pltpu.roll(value[:, s : s + LANES], SPLIT, 1) for s in range(0, value.shape[1], LANES)
    ]
    return jnp.concatenate(parts, axis=1)


def lane_sign(width):
    lane = lax.broadcasted_iota(jnp.int32, (8, width), 1) % LANES
    return jnp.where(lane < SPLIT, -1.0, 1.0)[:1]


def pair_rows(table, value, wide):
    return pair_dot(table, split_rows(value, wide), wide)


def pair_dot(table, parts, wide):
    out = jnp.dot(table, parts, preferred_element_type=F32)
    if not wide:
        half = out.shape[0] // 2
        out = out[:half] + out[half:]
    half = out.shape[0] // 2
    turned = swap(out[half:]) * lane_sign(out.shape[1])
    return out[:half] + turned, out[:half] - turned


def pick(ref, firsts, count, stride):
    return jnp.concatenate([ref[pl.ds(f, count, stride=stride), :] for f in firsts], axis=1)


def store(ref, start, value):
    ref[pl.ds(start, value.shape[0]), :] = value


def odd(rows):
    return rows + 1


def lane_block(value, i):
    return value[:, i * LANES : (i + 1) * LANES]


def loop(count, body):
    def one(i, carry):
        body(i)
        return carry

    lax.fori_loop(0, count, one, 0)


GROUP = 8


def pipeline(steps, stages, width):
    blocks = -(-steps // width)
    depth = len(stages)

    def turn(t, static):
        for s in reversed(range(depth)):
            if static and not 0 <= t - s < blocks:
                continue
            for slot in range(width):
                step = (t - s) * width + slot
                if not static or step < steps:
                    stages[s](step, slot)

    full = steps // width
    first, last = depth - 1, max(full, depth - 1)
    for t in range(first):
        turn(t, True)
    if last - first >= 2:
        loop(last - first, lambda i: turn(i + first, False))
    else:
        last = first
    for t in range(last, blocks + depth - 1):
        turn(t, True)


def slab_rows_kernel(dims, place_ref, *refs):
    sources, (table_ref, rows_ref, depth_buf, parts_buf) = refs[:-4], refs[-4:]
    x_cells, y_cells, z_cells = dims
    half = x_cells // 2
    count = depth_buf.shape[0] // y_cells - 1
    n_y = y_cells + HALF
    pad_y = n_y // 2 + -(n_y // 2) % 8
    many = 4

    def read(lanes):
        if len(sources) == 1:
            return sources[0][:, lanes].astype(F32)
        first = (place_ref[0] & 1) == 0
        mine, other = ([ref[i, :, lanes].astype(F32) for i in range(2)] for ref in sources)
        low, high = (
            jnp.concatenate([jnp.where(first, m, o), jnp.where(first, o, m)], axis=0)
            for m, o in zip(mine, other)
        )
        return jnp.concatenate([low[x_cells - HALF :], high[:HALF]], axis=0)

    def depth_step(i):
        lanes = [pl.ds(pl.multiple_of((many * i + u) * LANES, LANES), LANES) for u in range(many)]
        block = jnp.concatenate([read(l) for l in lanes], axis=0).astype(BF16)
        out = jnp.dot(block, table_ref[: 2 * z_cells], preferred_element_type=F32)
        for u in range(many):
            part = out[u * count : (u + 1) * count]
            for j in range(2):
                store(
                    depth_buf, (2 * many * i + 2 * u + j) * odd(count),
                    lane_block(part, 2 * j) + lane_block(part, 2 * j + 1),
                )

    loop(y_cells // (2 * many), depth_step)

    def gather_rows(i, slot):
        value = pick(depth_buf, [GROUP * i + u for u in range(GROUP)], y_cells, odd(count))
        parts_buf[slot] = split_rows(value, True)

    def y_step(i, slot):
        plus, minus = pair_dot(table_ref[2 * z_cells :, : 3 * y_cells], parts_buf[slot], True)
        for u in range(GROUP):
            start = (GROUP * i + u) * odd(2 * pad_y)
            store(rows_ref, start, lane_block(plus, u))
            store(rows_ref, start + pad_y, lane_block(minus, u))

    pipeline(count // GROUP, [gather_rows, y_step], 2)


def slab_rows(place, blocks, count, dims, tables, name):
    x_cells, y_cells, z_cells = dims
    n_y = y_cells + HALF
    pad_y = n_y // 2 + -(n_y // 2) % 8
    vmem = pl.BlockSpec(memory_space=pltpu.VMEM)
    return pl.pallas_call(
        functools.partial(slab_rows_kernel, dims),
        out_shape=jax.ShapeDtypeStruct((count * odd(2 * pad_y), LANES), F32),
        in_specs=[pl.BlockSpec(memory_space=pltpu.SMEM)] + [vmem] * (1 + len(blocks)),
        out_specs=vmem,
        scratch_shapes=[
            pltpu.VMEM((y_cells * odd(count), LANES), F32),
            pltpu.VMEM((2, 3 * y_cells, GROUP * LANES), BF16),
        ],
        compiler_params=pltpu.CompilerParams(vmem_limit_bytes=9 * 1024 * 1024),
        cost_estimate=pl.CostEstimate(flops=count * 10**8, bytes_accessed=10**6, transcendentals=0),
        name=name,
    )(place, *blocks, tables["slab_rows"])


def slab_x_kernel(
    dims, own_ref, halo_ref, x_ref, valid_ref, tz_ref, spec_ref, mask_ref, z_ref, parts_buf
):
    x_cells, y_cells, z_cells = dims
    n_y = y_cells + HALF
    pad_y = n_y // 2 + -(n_y // 2) % 8

    def gather_rows(i, slot):
        firsts = [GROUP // 2 * i + u // 2 + u % 2 * pad_y for u in range(GROUP)]
        value = jnp.concatenate(
            [
                pick(own_ref, firsts, x_cells, odd(2 * pad_y)),
                pick(halo_ref, firsts, TEMPL, odd(2 * pad_y)),
            ],
            axis=0,
        )
        parts_buf[slot] = split_rows(value, True)

    def x_step(i, slot):
        plus, minus = pair_dot(x_ref[...], parts_buf[slot], True)
        spec = jnp.concatenate([plus, minus], axis=0)
        turned = swap(spec)
        real_lane = lane_sign(GROUP * LANES) < 0
        spec_ref[i, 0] = jnp.where(real_lane, spec, turned)
        spec_ref[i, 1] = jnp.where(real_lane, -turned, spec)

    pipeline(n_y // GROUP, [gather_rows, x_step], 2)

    valid = valid_ref[...].astype(F32)
    low_lane = lax.broadcasted_iota(jnp.int32, (x_cells, LANES), 1) < z_cells
    for q in range(y_cells // 2):
        mask_ref[q] = jnp.where(low_lane, valid[:, 2 * q : 2 * q + 1], valid[:, 2 * q + 1 : 2 * q + 2])
    z_ref[...] = jnp.zeros(z_ref.shape, BF16)
    for j in range(8):
        start = TEMPL * j - (LANES if j >= 4 else 0)
        z_ref[j, start : start + TEMPL, :] = tz_ref[...]


def slab_x(own, halo, valid, dims, tables):
    x_cells, y_cells, z_cells = dims
    n_x, n_y = x_cells + TEMPL, y_cells + HALF
    steps = n_y // GROUP
    vmem = pl.BlockSpec(memory_space=pltpu.VMEM)
    shape = (steps, 2, n_x, GROUP * LANES)
    return pl.pallas_call(
        functools.partial(slab_x_kernel, dims),
        out_shape=(
            jax.ShapeDtypeStruct(shape, F32),
            jax.ShapeDtypeStruct((y_cells // 2, x_cells, LANES), F32),
            jax.ShapeDtypeStruct((8, 2 * LANES, 2 * LANES), BF16),
        ),
        in_specs=[vmem] * 5,
        out_specs=(vmem,) * 3,
        scratch_shapes=[pltpu.VMEM((2, 3 * n_x, GROUP * LANES), BF16)],
        compiler_params=pltpu.CompilerParams(vmem_limit_bytes=6 * 1024 * 1024),
        cost_estimate=pl.CostEstimate(flops=5 * 10**9, bytes_accessed=10**6, transcendentals=0),
        name="slab_x",
    )(own, halo, tables["slab_x"], valid, tables["tmpl_z"])


def corr_kernel(
    dims, rot, entry, place_ref, held_ref, last_ref, mask_ref, spec_ref,
    z_ref, ones_ref, y_ref, x_ref, bx_ref, by_ref, bz_ref,
    mine_ref, side_ref, far_ref, stat_ref,
    bank_buf, depth_buf, rows_buf, first_buf, second_buf, third_buf, back_buf, vol_buf,
):
    x_cells, y_cells, z_cells = dims
    n_x, n_y = x_cells + TEMPL, y_cells + HALF
    half_y = n_y // 2
    pad_y = half_y + -half_y % 8
    for i, block in enumerate(HELD):
        for ref, at, tile in ((held_ref, rot, block), (last_ref, entry, block ^ 1)):
            store(bank_buf, (place_ref[1] ^ tile) * odd(BLOCK_ROWS), ref[at, i].astype(F32))
    tmpl = jnp.concatenate(
        [
            pick(bank_buf, [a * CHUNKS + i for i in range(CHUNKS)], BLOCKS, odd(BLOCK_ROWS))
            for a in range(EACH)
        ],
        axis=0,
    )
    inv_size = 1.0 / TEMPL**3
    mean = jnp.sum(tmpl) * inv_size
    centred = tmpl - mean
    var = jnp.sum(centred * centred) * inv_size
    scale = 1.0 / (jnp.sqrt(jnp.full((1, LANES), var + EPSILON, F32)) * TEMPL**1.5)
    shift = ones_ref[:1] * mean

    wide = 8 * TEMPL
    narrow = tmpl.astype(BF16)
    block = jnp.concatenate(
        [narrow[:, g * wide : (g + 1) * wide] for g in range(TEMPL // 8)], axis=0
    )
    for j in range(8):
        window = block[:, : 2 * LANES] if j < 4 else block[:, LANES:]
        out = jnp.dot(window, z_ref[j], preferred_element_type=F32)
        part = out[:, :LANES] + out[:, LANES:] - shift
        for g in range(TEMPL // 8):
            start = (8 * g + j) * odd(TEMPL)
            store(depth_buf, start, part[g * TEMPL : (g + 1) * TEMPL])

    def gather_a(i, slot):
        value = pick(depth_buf, [GROUP * i + u for u in range(GROUP)], TEMPL, odd(TEMPL))
        first_buf[slot] = split_rows(value, True)

    def y_step(i, slot):
        plus, minus = pair_dot(y_ref[...], first_buf[slot], True)
        for u in range(GROUP):
            start = (GROUP * i + u) * odd(2 * pad_y)
            store(rows_buf, start, lane_block(plus, u))
            store(rows_buf, start + pad_y, lane_block(minus, u))

    pipeline(TEMPL // GROUP, [gather_a, y_step], 2)

    def gather_ky(i, slot):
        firsts = [GROUP // 2 * i + u // 2 + u % 2 * pad_y for u in range(GROUP)]
        first_buf[slot] = split_rows(pick(rows_buf, firsts, TEMPL, odd(2 * pad_y)), True)

    def multiply(i, slot):
        plus, minus = pair_dot(x_ref[...], first_buf[slot], True)
        spec = jnp.concatenate([plus, minus], axis=0)
        prod = spec * spec_ref[i, 0] + swap(spec) * spec_ref[i, 1]
        second_buf[slot] = split_rows(prod, False)

    def back_x(i, slot):
        plus, minus = pair_dot(bx_ref[...], second_buf[slot], False)
        for u in range(GROUP):
            start = (GROUP * i + u) * odd(x_cells)
            store(back_buf, start, lane_block(plus, u))
            store(back_buf, start + x_cells // 2, lane_block(minus, u))

    pipeline(n_y // GROUP, [gather_ky, multiply, back_x], 2)

    def gather_x(i, slot):
        value = pick(back_buf, [GROUP * i + u for u in range(GROUP)], n_y, odd(x_cells))
        third_buf[slot] = split_rows(value, False)

    def back_y(i, slot):
        plus, minus = pair_dot(by_ref[...], third_buf[slot], False)
        for u in range(GROUP):
            row = GROUP * i + u
            x = jnp.where(row < x_cells // 2, row + x_cells // 2, x_cells - 1 - row)
            store(vol_buf, x * odd(y_cells), lane_block(plus, u))
            store(vol_buf, x * odd(y_cells) + y_cells // 2, lane_block(minus, u))

    pipeline(x_cells // GROUP, [gather_x, back_y], 2)

    share = y_cells // 8
    me = place_ref[0]
    total = jnp.zeros((x_cells, LANES), F32)
    number = jnp.zeros((x_cells, LANES), F32)
    targets = [mine_ref, side_ref, far_ref.at[0], far_ref.at[1]]
    for p, target in enumerate(targets):
        first = (me ^ p) * share
        values = []
        for i in range(share):
            firsts = []
            for j in range(2):
                y = 2 * (first + i) + j
                firsts.append(jnp.where(y < y_cells // 2, y_cells - 1 - y, y - y_cells // 2))
            values.append(pick(vol_buf, firsts, x_cells, odd(y_cells)))
        value = jnp.concatenate(values, axis=0)
        out = jnp.dot(split_rows(value, False), bz_ref[...], preferred_element_type=F32)
        rows = value.shape[0]
        full = out[:rows, :LANES] + out[:rows, LANES:] + out[rows:, :LANES]
        for i in range(share):
            corr = full[i * x_cells : (i + 1) * x_cells] * scale
            target[:, i * LANES : (i + 1) * LANES] = corr
            mask = mask_ref[first + i]
            total = total + corr * mask
            number = number + mask
    number_sum = jnp.sum(number)
    total_sum = jnp.sum(total)
    local_mean = jnp.full((1, LANES), total_sum, F32) / jnp.maximum(number_sum, 1.0)
    square = jnp.zeros((x_cells, LANES), F32)
    for p, target in enumerate(targets):
        first = (me ^ p) * share
        for i in range(share):
            gap = target[:, i * LANES : (i + 1) * LANES] - local_mean
            square = square + gap * gap * mask_ref[first + i]
    row = lax.broadcasted_iota(jnp.int32, (8, LANES), 0)
    stat_ref[...] = jnp.where(row == 0, number_sum, jnp.where(row == 1, total_sum, jnp.sum(square)))


def correlate(place, held, rot, last, entry, mask, spec, tmpl_z, dims, tables):
    x_cells, y_cells, z_cells = dims
    n_x, n_y = x_cells + TEMPL, y_cells + HALF
    pad_y = n_y // 2 + -(n_y // 2) % 8
    width = y_cells * z_cells // 4
    vmem = pl.BlockSpec(memory_space=pltpu.VMEM)
    return pl.pallas_call(
        functools.partial(corr_kernel, dims, rot, entry),
        out_shape=(
            jax.ShapeDtypeStruct((x_cells, width), F32),
            jax.ShapeDtypeStruct((x_cells, width), F32),
            jax.ShapeDtypeStruct((2, x_cells, width), F32),
            jax.ShapeDtypeStruct((8, LANES), F32),
        ),
        in_specs=[pl.BlockSpec(memory_space=pltpu.SMEM)] + [vmem] * 11,
        out_specs=(vmem,) * 4,
        scratch_shapes=[
            pltpu.VMEM((BLOCKS * odd(BLOCK_ROWS), LANES), F32),
            pltpu.VMEM((TEMPL * odd(TEMPL), LANES), F32),
            pltpu.VMEM((TEMPL * odd(2 * pad_y), LANES), F32),
            pltpu.VMEM((2, 3 * TEMPL, GROUP * LANES), BF16),
            pltpu.VMEM((2, 2 * n_x, GROUP * LANES), BF16),
            pltpu.VMEM((2, 2 * n_y, GROUP * LANES), BF16),
            pltpu.VMEM((n_y * odd(x_cells), LANES), F32),
            pltpu.VMEM((x_cells * odd(y_cells), LANES), F32),
        ],
        compiler_params=pltpu.CompilerParams(vmem_limit_bytes=14 * 1024 * 1024),
        cost_estimate=pl.CostEstimate(flops=15 * 10**9, bytes_accessed=10**7, transcendentals=0),
        name="correlate",
    )(
        place, held, last, mask, spec,
        tmpl_z, tables["ones_z"], tables["tmpl_y"], tables["tmpl_x"],
        tables["back_x"], tables["back_y"], tables["back_z"],
    )


def score_kernel(pieces, place_ref, coef_ref, mask_ref, *refs):
    best_ref, evid_ref, mom_ref = refs[len(refs) - 3 :]

    blocks = best_ref.shape[1] // LANES

    def step(i):
        lanes = pl.ds(pl.multiple_of(i * LANES, LANES), LANES)
        for top in range(0, best_ref.shape[0], 8):
            rows = slice(top, top + 8)
            mask = mask_ref[place_ref[0] * blocks + i, rows]
            scores = []
            for k, (at, entry) in enumerate(pieces):
                corr = refs[at][rows, lanes] if entry is None else refs[at][entry, rows, lanes]
                scores.append((corr - coef_ref[k, 0]) * coef_ref[k, 1])
            high = functools.reduce(jnp.maximum, scores)
            total = jnp.zeros_like(high)
            moment = [jnp.zeros_like(high) for _ in range(4)]
            for k, score in enumerate(scores):
                weight = jnp.exp(score - high)
                total = total + weight
                for c in range(4):
                    moment[c] = moment[c] + weight * coef_ref[k, 2 + c]
            best_ref[rows, lanes] = mask * high
            evid_ref[rows, lanes] = mask * (high + jnp.log(total))
            share = mask / total
            for c in range(4):
                mom_ref[c, rows, lanes] = moment[c] * share

    loop(blocks, step)


def combine(place, coefs, mask, arrays, pieces):
    shape = arrays[0].shape
    vmem = pl.BlockSpec(memory_space=pltpu.VMEM)
    out = jax.ShapeDtypeStruct(shape, F32)
    return pl.pallas_call(
        functools.partial(score_kernel, pieces),
        out_shape=(out, out, jax.ShapeDtypeStruct((4,) + shape, F32)),
        in_specs=[pl.BlockSpec(memory_space=pltpu.SMEM)] * 2 + [vmem] * (1 + len(arrays)),
        out_specs=(vmem,) * 3,
        compiler_params=pltpu.CompilerParams(vmem_limit_bytes=4 * 1024 * 1024),
        name="combine",
    )(place, coefs, mask, *arrays)


def swap_blocks(block, axis, step):
    return lax.ppermute(block, axis, [(i, i ^ step) for i in range(lax.axis_size(axis))])


def general_gather(templates):
    rots = templates.shape[0]
    count = lax.axis_size("tile")
    block = templates[:, None]
    for step in [1 << i for i in reversed(range(count.bit_length() - 1))]:
        other = swap_blocks(block, "tile", step)
        upper = (lax.axis_index("tile") & step) != 0
        pair = [jnp.where(upper, other, block), jnp.where(upper, block, other)]
        block = jnp.stack(pair, axis=2).reshape((rots, -1) + block.shape[2:])
    block = block.reshape(rots, BLOCKS, EACH * CHUNKS, LANES)
    block = jnp.pad(block, ((0, 0), (0, 0), (0, BLOCK_ROWS - EACH * CHUNKS), (0, 0)))
    held = jnp.stack([block[:, i] for i in HELD], axis=1)
    return held, jnp.stack([block[:, i ^ 1] for i in HELD], axis=1)


def merge(first, other):
    number_a, number_b = first[:1], other[:1]
    mean_a = first[1:2] / jnp.maximum(number_a, 1.0)
    mean_b = other[1:2] / jnp.maximum(number_b, 1.0)
    gap = mean_b - mean_a
    between = gap * gap * (number_a * number_b / jnp.maximum(number_a + number_b, 1.0))
    return first + other + jnp.where(jnp.arange(3)[:, None] == 2, between, 0.0)


def exchange_all(block, axis, low, high):
    count = lax.axis_size(axis)
    parts = [block]
    for step in range(low, high, low):
        parts.append(lax.ppermute(block, axis, [(i, i ^ step) for i in range(count)]))
    return jnp.stack(parts)


def neighbours(block, axis):
    count = lax.axis_size(axis)
    forward = [(i, i + 1) for i in range(count - 1)]
    backward = [(target, source) for source, target in forward]
    return lax.ppermute(block, axis, forward), lax.ppermute(block, axis, backward)


def local(tomogram, templates, valid, quats, rot_index):
    x_cells, voxels = tomogram.shape
    y_cells = valid.shape[1]
    z_cells = voxels // y_cells
    dims = (x_cells, y_cells, z_cells)
    tables = {name: jnp.asarray(table) for name, table in make_tables(*dims).items()}
    groups = lax.axis_size("rot")
    tiles = lax.axis_size("tile")
    me = lax.axis_index("rot")
    rots = templates.shape[0]

    tile = lax.axis_index("tile")
    by_blocks = tiles == BLOCKS
    if by_blocks:
        held = templates.reshape(rots, 1, EACH * CHUNKS, LANES)
        held = jnp.pad(held, ((0, 0), (0, 0), (0, BLOCK_ROWS - EACH * CHUNKS), (0, 0)))
        held = jnp.concatenate([held, swap_blocks(held, "tile", 4)], axis=1)
    half = x_cells // 2
    piece = lax.dynamic_slice_in_dim(tomogram, (me & 1) * half, half, 0)
    mine = jnp.stack(neighbours(piece, "tile"))
    side_swap = [(i, i ^ 1) for i in range(groups)]
    other = lax.ppermute(mine, "rot", side_swap)
    if by_blocks:
        held = jnp.concatenate([held, swap_blocks(held, "tile", 2)], axis=1)
    else:
        held, last = general_gather(templates)
        tile = jnp.zeros_like(tile)
    one_hot = (rot_index[:, None] == jnp.arange(quats.shape[1], dtype=jnp.int32)[None, :]).astype(F32)
    orient = jnp.einsum("rq,kq->rk", one_hot, quats, precision=lax.Precision.HIGHEST)
    place = me_place = jnp.stack([me, tile]).astype(jnp.int32)
    own = slab_rows(place, [tomogram], x_cells, dims, tables, "slab_own")
    halo = slab_rows(place, [mine, other], TEMPL, dims, tables, "slab_halo")
    if by_blocks:
        held, halo = lax.optimization_barrier((held, halo))
        lasts = [swap_blocks(held[:1], "tile", 1), swap_blocks(held[1:], "tile", 1)]
    else:
        lasts = [last[:1], last[1:]]
    spec, mask, tmpl_z = slab_x(own, halo, valid, dims, tables)
    far_swap = [(i, i ^ 2) for i in range(groups)]
    mines, sides, fars, stats = [], [], [], []
    for r in range(rots):
        if r >= 2:
            place, fars[r - 2] = lax.optimization_barrier((place, fars[r - 2]))
        mine, side, far, stat = correlate(
            place, held, r, lasts[min(r, 1)], max(r - 1, 0), mask, spec, tmpl_z, dims, tables
        )
        if r >= 1:
            stat, fars[r - 1] = lax.optimization_barrier((stat, fars[r - 1]))
        mines.append(mine)
        sides.append(side)
        stats.append(stat[:3, 0])
        fars.append(lax.ppermute(far, "rot", far_swap))
        if r == rots - 2:
            early = jnp.stack(sides + [f[1] for f in fars[:-1]])
            early = lax.ppermute(early, "rot", side_swap)
    state = jnp.stack(stats, axis=1)
    state, early, fars[rots - 2] = lax.optimization_barrier((state, early, fars[rots - 2]))
    step = 1
    while step < tiles:
        partner = lax.ppermute(state, "tile", [(i, i ^ step) for i in range(tiles)])
        if step * 4 == tiles:
            partner, fars[rots - 1] = lax.optimization_barrier((partner, fars[rots - 1]))
            last = jnp.stack([sides[rots - 1], fars[rots - 2][1], fars[rots - 1][1]])
        if step * 2 == tiles:
            partner, last = lax.optimization_barrier((partner, last))
        state = merge(state, partner)
        step *= 2
    average = state[1] / state[0]
    inverse = 1.0 / jnp.sqrt(state[2] / state[0] + EPSILON)
    coefs = jnp.concatenate([average[:, None], inverse[:, None], orient], axis=1)
    coefs = exchange_all(coefs, "rot", 1, groups)
    last = lax.ppermute(last, "rot", side_swap)
    arrays = mines + fars + [early, last]
    at_far, at_early, at_last = rots, 2 * rots, 2 * rots + 1
    pieces = [(r, None) for r in range(rots)]
    pieces += [(at_early, r) for r in range(rots - 1)] + [(at_last, 0)]
    pieces += [(at_far + r, 0) for r in range(rots)]
    pieces += [(at_early, rots - 1 + r) for r in range(rots - 2)] + [(at_last, 1), (at_last, 2)]
    return combine(me_place, coefs.reshape(groups * rots, 6), mask, arrays, pieces)


def solution(mesh):
    placed = (P("tile", None), P("rot", "tile"), P("tile", None), P(), P("rot"))
    return jax.shard_map(
        local,
        mesh=mesh,
        in_specs=placed,
        out_specs=(P("tile", "rot"), P("tile", "rot"), P(None, "tile", "rot")),
        check_vma=False,
    )
```

```python
import functools
import math

import jax
import jax.numpy as jnp
import ml_dtypes
import numpy as np
from jax import lax
from jax.experimental import pallas as pl
from jax.experimental.pallas import tpu as pltpu
from jax.sharding import PartitionSpec as P

TEMPL = 48
HALF = 24
EPSILON = 1e-06
LANES = 128
SPLIT = 64
BLOCKS = 8
EACH = TEMPL // BLOCKS
CHUNKS = TEMPL * TEMPL // LANES
BLOCK_ROWS = EACH * CHUNKS + -EACH * CHUNKS % 16
HELD = (0, 4, 2, 6)
F32 = jnp.float32
BF16 = jnp.bfloat16


def two_parts(table):
    high = table.astype(ml_dtypes.bfloat16)
    low = (table - high.astype(np.float64)).astype(ml_dtypes.bfloat16)
    return high, low


def row_table(out_idx, in_idx, length, sign, factor, wide):
    theta = 2.0 * math.pi / length * np.outer(out_idx, in_idx)
    pad = np.zeros((-len(out_idx) % 8, len(in_idx)))
    full = np.concatenate([np.cos(theta), pad, sign * np.sin(theta), pad], axis=0) * factor
    high, low = two_parts(full)
    if wide:
        return np.concatenate([high, high, low], axis=1)
    zeros = np.zeros_like(low)
    return np.concatenate(
        [np.concatenate([high, high], axis=1), np.concatenate([low, zeros], axis=1)], axis=0
    )


def depth_table(in_idx, length, sign, factor):
    freq = np.arange(length // 2) + 0.5
    theta = 2.0 * math.pi / length * np.outer(in_idx, freq)
    out = np.zeros((len(in_idx), LANES))
    out[:, : length // 2] = np.cos(theta) * factor
    out[:, SPLIT : SPLIT + length // 2] = sign * np.sin(theta) * factor
    return out


def half_odd(count):
    return np.arange(count // 2) + 0.5


def make_tables(x_cells, y_cells, z_cells):
    n_x, n_y, n_z = x_cells + TEMPL, y_cells + HALF, z_cells + HALF
    k_x, k_y = half_odd(n_x), half_odd(n_y)
    both_x = np.concatenate([k_x, -k_x])
    both_y = np.stack([k_y, -k_y], axis=1).reshape(-1)
    mid_x, mid_y = (x_cells - 1) / 2, (y_cells - 1) / 2
    tables = {}
    slab = np.zeros((2 * z_cells, 4 * LANES), ml_dtypes.bfloat16)
    high, low = two_parts(depth_table(np.arange(z_cells), n_z, -1.0, 1.0))
    for j in range(2):
        rows = slice(j * z_cells, (j + 1) * z_cells)
        slab[rows, 2 * j * LANES : (2 * j + 1) * LANES] = high
        slab[rows, (2 * j + 1) * LANES : (2 * j + 2) * LANES] = low
    slab_y = row_table(k_y, np.arange(y_cells), n_y, -1.0, 1.0, True)
    slab_y = np.pad(slab_y, ((0, 0), (0, slab.shape[1] - slab_y.shape[1])))
    tables["slab_rows"] = np.concatenate([slab, slab_y], axis=0)
    own = np.arange(HALF, HALF + x_cells)
    halo = np.concatenate([np.arange(HALF), np.arange(HALF + x_cells, n_x)])
    tables["slab_x"] = row_table(k_x, np.concatenate([own, halo]), n_x, -1.0, 1.0, True)
    high, low = two_parts(depth_table(np.arange(TEMPL) - HALF, n_z, 1.0, 1.0))
    tables["tmpl_z"] = np.concatenate([high, low], axis=1)
    ones = (high.astype(np.float64) + low.astype(np.float64)).sum(axis=0)
    tables["ones_z"] = np.broadcast_to(ones.astype(np.float32)[None], (8, LANES)).copy()
    tables["tmpl_y"] = row_table(k_y, np.arange(TEMPL) - HALF + mid_y, n_y, 1.0, 1.0, True)
    tmpl_rows = np.arange(TEMPL).reshape(BLOCKS, EACH).T.reshape(-1)
    tables["tmpl_x"] = row_table(k_x, tmpl_rows + mid_x, n_x, 1.0, 1.0, True)
    tables["back_x"] = row_table(half_odd(x_cells), both_x, n_x, 1.0, 1.0 / n_x, False)
    tables["back_y"] = row_table(half_odd(y_cells), both_y, n_y, 1.0, 1.0 / n_y, False)
    back = depth_table(np.arange(z_cells), n_z, -1.0, 2.0 / n_z).T
    high, low = two_parts(back)
    back_z = np.zeros((2 * LANES, 2 * LANES), ml_dtypes.bfloat16)
    for j in range(2):
        rows = slice(j * LANES, (j + 1) * LANES)
        back_z[rows, j * z_cells : (j + 1) * z_cells] = high
        back_z[rows, LANES + j * z_cells : LANES + (j + 1) * z_cells] = low
    tables["back_z"] = back_z
    return tables


def split_rows(value, wide):
    high = value.astype(BF16)
    if value.shape[0] % 16 == 0:
        low = (value - high.astype(F32)).astype(BF16)
        return jnp.concatenate([high, low, high] if wide else [high, low], axis=0)
    high = high.astype(F32)
    low = value - high
    return jnp.concatenate([high, low, high] if wide else [high, low], axis=0).astype(BF16)


def swap(value):
    parts = [
        pltpu.roll(value[:, s : s + LANES], SPLIT, 1) for s in range(0, value.shape[1], LANES)
    ]
    return jnp.concatenate(parts, axis=1)


def lane_sign(width):
    lane = lax.broadcasted_iota(jnp.int32, (8, width), 1) % LANES
    return jnp.where(lane < SPLIT, -1.0, 1.0)[:1]


def pair_rows(table, value, wide):
    return pair_dot(table, split_rows(value, wide), wide)


def pair_dot(table, parts, wide):
    out = jnp.dot(table, parts, preferred_element_type=F32)
    if not wide:
        half = out.shape[0] // 2
        out = out[:half] + out[half:]
    half = out.shape[0] // 2
    turned = swap(out[half:]) * lane_sign(out.shape[1])
    return out[:half] + turned, out[:half] - turned


def pick(ref, firsts, count, stride):
    return jnp.concatenate([ref[pl.ds(f, count, stride=stride), :] for f in firsts], axis=1)


def store(ref, start, value):
    ref[pl.ds(start, value.shape[0]), :] = value


def odd(rows):
    return rows + 1


def lane_block(value, i):
    return value[:, i * LANES : (i + 1) * LANES]


def loop(count, body):
    def one(i, carry):
        body(i)
        return carry

    lax.fori_loop(0, count, one, 0)


GROUP = 8


def pipeline(steps, stages, width):
    blocks = -(-steps // width)
    depth = len(stages)

    def turn(t, static):
        for s in reversed(range(depth)):
            if static and not 0 <= t - s < blocks:
                continue
            for slot in range(width):
                step = (t - s) * width + slot
                if not static or step < steps:
                    stages[s](step, slot)

    full = steps // width
    first, last = depth - 1, max(full, depth - 1)
    for t in range(first):
        turn(t, True)
    if last - first >= 2:
        loop(last - first, lambda i: turn(i + first, False))
    else:
        last = first
    for t in range(last, blocks + depth - 1):
        turn(t, True)


def slab_rows_kernel(dims, place_ref, *refs):
    sources, (table_ref, rows_ref, depth_buf, parts_buf) = refs[:-4], refs[-4:]
    x_cells, y_cells, z_cells = dims
    half = x_cells // 2
    count = depth_buf.shape[0] // y_cells - 1
    n_y = y_cells + HALF
    pad_y = n_y // 2 + -(n_y // 2) % 8
    many = 4

    def read(lanes):
        if len(sources) == 1:
            return sources[0][:, lanes].astype(F32)
        first = (place_ref[0] & 1) == 0
        mine, other = ([ref[i, :, lanes].astype(F32) for i in range(2)] for ref in sources)
        low, high = (
            jnp.concatenate([jnp.where(first, m, o), jnp.where(first, o, m)], axis=0)
            for m, o in zip(mine, other)
        )
        return jnp.concatenate([low[x_cells - HALF :], high[:HALF]], axis=0)

    def depth_step(i):
        lanes = [pl.ds(pl.multiple_of((many * i + u) * LANES, LANES), LANES) for u in range(many)]
        block = jnp.concatenate([read(l) for l in lanes], axis=0).astype(BF16)
        out = jnp.dot(block, table_ref[: 2 * z_cells], preferred_element_type=F32)
        for u in range(many):
            part = out[u * count : (u + 1) * count]
            for j in range(2):
                store(
                    depth_buf, (2 * many * i + 2 * u + j) * odd(count),
                    lane_block(part, 2 * j) + lane_block(part, 2 * j + 1),
                )

    loop(y_cells // (2 * many), depth_step)

    def gather_rows(i, slot):
        value = pick(depth_buf, [GROUP * i + u for u in range(GROUP)], y_cells, odd(count))
        parts_buf[slot] = split_rows(value, True)

    def y_step(i, slot):
        plus, minus = pair_dot(table_ref[2 * z_cells :, : 3 * y_cells], parts_buf[slot], True)
        for u in range(GROUP):
            start = (GROUP * i + u) * odd(2 * pad_y)
            store(rows_ref, start, lane_block(plus, u))
            store(rows_ref, start + pad_y, lane_block(minus, u))

    pipeline(count // GROUP, [gather_rows, y_step], 2)


def slab_rows(place, blocks, count, dims, tables, name):
    x_cells, y_cells, z_cells = dims
    n_y = y_cells + HALF
    pad_y = n_y // 2 + -(n_y // 2) % 8
    vmem = pl.BlockSpec(memory_space=pltpu.VMEM)
    return pl.pallas_call(
        functools.partial(slab_rows_kernel, dims),
        out_shape=jax.ShapeDtypeStruct((count * odd(2 * pad_y), LANES), F32),
        in_specs=[pl.BlockSpec(memory_space=pltpu.SMEM)] + [vmem] * (1 + len(blocks)),
        out_specs=vmem,
        scratch_shapes=[
            pltpu.VMEM((y_cells * odd(count), LANES), F32),
            pltpu.VMEM((2, 3 * y_cells, GROUP * LANES), BF16),
        ],
        compiler_params=pltpu.CompilerParams(vmem_limit_bytes=9 * 1024 * 1024),
        cost_estimate=pl.CostEstimate(flops=count * 10**8, bytes_accessed=10**6, transcendentals=0),
        name=name,
    )(place, *blocks, tables["slab_rows"])


def slab_x_kernel(
    dims, own_ref, halo_ref, x_ref, valid_ref, tz_ref, spec_ref, mask_ref, z_ref, parts_buf
):
    x_cells, y_cells, z_cells = dims
    n_y = y_cells + HALF
    pad_y = n_y // 2 + -(n_y // 2) % 8

    def gather_rows(i, slot):
        firsts = [GROUP // 2 * i + u // 2 + u % 2 * pad_y for u in range(GROUP)]
        value = jnp.concatenate(
            [
                pick(own_ref, firsts, x_cells, odd(2 * pad_y)),
                pick(halo_ref, firsts, TEMPL, odd(2 * pad_y)),
            ],
            axis=0,
        )
        parts_buf[slot] = split_rows(value, True)

    def x_step(i, slot):
        plus, minus = pair_dot(x_ref[...], parts_buf[slot], True)
        spec = jnp.concatenate([plus, minus], axis=0)
        turned = swap(spec)
        real_lane = lane_sign(GROUP * LANES) < 0
        spec_ref[i, 0] = jnp.where(real_lane, spec, turned)
        spec_ref[i, 1] = jnp.where(real_lane, -turned, spec)

    pipeline(n_y // GROUP, [gather_rows, x_step], 2)

    valid = valid_ref[...].astype(F32)
    low_lane = lax.broadcasted_iota(jnp.int32, (x_cells, LANES), 1) < z_cells
    for q in range(y_cells // 2):
        mask_ref[q] = jnp.where(low_lane, valid[:, 2 * q : 2 * q + 1], valid[:, 2 * q + 1 : 2 * q + 2])
    z_ref[...] = jnp.zeros(z_ref.shape, BF16)
    for j in range(8):
        start = TEMPL * j - (LANES if j >= 4 else 0)
        z_ref[j, start : start + TEMPL, :] = tz_ref[...]


def slab_x(own, halo, valid, dims, tables):
    x_cells, y_cells, z_cells = dims
    n_x, n_y = x_cells + TEMPL, y_cells + HALF
    steps = n_y // GROUP
    vmem = pl.BlockSpec(memory_space=pltpu.VMEM)
    shape = (steps, 2, n_x, GROUP * LANES)
    return pl.pallas_call(
        functools.partial(slab_x_kernel, dims),
        out_shape=(
            jax.ShapeDtypeStruct(shape, F32),
            jax.ShapeDtypeStruct((y_cells // 2, x_cells, LANES), F32),
            jax.ShapeDtypeStruct((8, 2 * LANES, 2 * LANES), BF16),
        ),
        in_specs=[vmem] * 5,
        out_specs=(vmem,) * 3,
        scratch_shapes=[pltpu.VMEM((2, 3 * n_x, GROUP * LANES), BF16)],
        compiler_params=pltpu.CompilerParams(vmem_limit_bytes=6 * 1024 * 1024),
        cost_estimate=pl.CostEstimate(flops=5 * 10**9, bytes_accessed=10**6, transcendentals=0),
        name="slab_x",
    )(own, halo, tables["slab_x"], valid, tables["tmpl_z"])


def corr_kernel(
    dims, rot, entry, place_ref, tile_ref, held_ref, last_ref, mask_ref, spec_ref,
    z_ref, ones_ref, y_ref, x_ref, bx_ref, by_ref, bz_ref,
    mine_ref, side_ref, far_ref, stat_ref,
    bank_buf, depth_buf, rows_buf, first_buf, second_buf, third_buf, back_buf, vol_buf,
):
    x_cells, y_cells, z_cells = dims
    n_x, n_y = x_cells + TEMPL, y_cells + HALF
    half_y = n_y // 2
    pad_y = half_y + -half_y % 8
    for i, block in enumerate(HELD):
        for ref, at, tile in ((held_ref, rot, block), (last_ref, entry, block ^ 1)):
            store(bank_buf, (tile_ref[0] ^ tile) * odd(BLOCK_ROWS), ref[at, i].astype(F32))
    tmpl = jnp.concatenate(
        [
            pick(bank_buf, [a * CHUNKS + i for i in range(CHUNKS)], BLOCKS, odd(BLOCK_ROWS))
            for a in range(EACH)
        ],
        axis=0,
    )
    inv_size = 1.0 / TEMPL**3
    mean = jnp.sum(tmpl) * inv_size
    centred = tmpl - mean
    var = jnp.sum(centred * centred) * inv_size
    scale = 1.0 / (jnp.sqrt(jnp.full((1, LANES), var + EPSILON, F32)) * TEMPL**1.5)
    shift = ones_ref[:1] * mean

    wide = 8 * TEMPL
    narrow = tmpl.astype(BF16)
    block = jnp.concatenate(
        [narrow[:, g * wide : (g + 1) * wide] for g in range(TEMPL // 8)], axis=0
    )
    for j in range(8):
        window = block[:, : 2 * LANES] if j < 4 else block[:, LANES:]
        out = jnp.dot(window, z_ref[j], preferred_element_type=F32)
        part = out[:, :LANES] + out[:, LANES:] - shift
        for g in range(TEMPL // 8):
            start = (8 * g + j) * odd(TEMPL)
            store(depth_buf, start, part[g * TEMPL : (g + 1) * TEMPL])

    def gather_a(i, slot):
        value = pick(depth_buf, [GROUP * i + u for u in range(GROUP)], TEMPL, odd(TEMPL))
        first_buf[slot] = split_rows(value, True)

    def y_step(i, slot):
        plus, minus = pair_dot(y_ref[...], first_buf[slot], True)
        for u in range(GROUP):
            start = (GROUP * i + u) * odd(2 * pad_y)
            store(rows_buf, start, lane_block(plus, u))
            store(rows_buf, start + pad_y, lane_block(minus, u))

    pipeline(TEMPL // GROUP, [gather_a, y_step], 2)

    def gather_ky(i, slot):
        firsts = [GROUP // 2 * i + u // 2 + u % 2 * pad_y for u in range(GROUP)]
        first_buf[slot] = split_rows(pick(rows_buf, firsts, TEMPL, odd(2 * pad_y)), True)

    def multiply(i, slot):
        plus, minus = pair_dot(x_ref[...], first_buf[slot], True)
        spec = jnp.concatenate([plus, minus], axis=0)
        prod = spec * spec_ref[i, 0] + swap(spec) * spec_ref[i, 1]
        second_buf[slot] = split_rows(prod, False)

    def back_x(i, slot):
        plus, minus = pair_dot(bx_ref[...], second_buf[slot], False)
        for u in range(GROUP):
            start = (GROUP * i + u) * odd(x_cells)
            store(back_buf, start, lane_block(plus, u))
            store(back_buf, start + x_cells // 2, lane_block(minus, u))

    pipeline(n_y // GROUP, [gather_ky, multiply, back_x], 2)

    def gather_x(i, slot):
        value = pick(back_buf, [GROUP * i + u for u in range(GROUP)], n_y, odd(x_cells))
        third_buf[slot] = split_rows(value, False)

    def back_y(i, slot):
        plus, minus = pair_dot(by_ref[...], third_buf[slot], False)
        for u in range(GROUP):
            row = GROUP * i + u
            x = jnp.where(row < x_cells // 2, row + x_cells // 2, x_cells - 1 - row)
            store(vol_buf, x * odd(y_cells), lane_block(plus, u))
            store(vol_buf, x * odd(y_cells) + y_cells // 2, lane_block(minus, u))

    pipeline(x_cells // GROUP, [gather_x, back_y], 2)

    share = y_cells // 8
    me = place_ref[0]
    total = jnp.zeros((x_cells, LANES), F32)
    number = jnp.zeros((x_cells, LANES), F32)
    targets = [mine_ref, side_ref, far_ref.at[0], far_ref.at[1]]
    for p, target in enumerate(targets):
        first = (me ^ p) * share
        values = []
        for i in range(share):
            firsts = []
            for j in range(2):
                y = 2 * (first + i) + j
                firsts.append(jnp.where(y < y_cells // 2, y_cells - 1 - y, y - y_cells // 2))
            values.append(pick(vol_buf, firsts, x_cells, odd(y_cells)))
        value = jnp.concatenate(values, axis=0)
        out = jnp.dot(split_rows(value, False), bz_ref[...], preferred_element_type=F32)
        rows = value.shape[0]
        full = out[:rows, :LANES] + out[:rows, LANES:] + out[rows:, :LANES]
        for i in range(share):
            corr = full[i * x_cells : (i + 1) * x_cells] * scale
            target[:, i * LANES : (i + 1) * LANES] = corr
            mask = mask_ref[first + i]
            total = total + corr * mask
            number = number + mask
    number_sum = jnp.sum(number)
    total_sum = jnp.sum(total)
    local_mean = jnp.full((1, LANES), total_sum, F32) / jnp.maximum(number_sum, 1.0)
    square = jnp.zeros((x_cells, LANES), F32)
    for p, target in enumerate(targets):
        first = (me ^ p) * share
        for i in range(share):
            gap = target[:, i * LANES : (i + 1) * LANES] - local_mean
            square = square + gap * gap * mask_ref[first + i]
    row = lax.broadcasted_iota(jnp.int32, (8, LANES), 0)
    stat_ref[...] = jnp.where(row == 0, number_sum, jnp.where(row == 1, total_sum, jnp.sum(square)))


def correlate(place, tile, held, rot, last, entry, mask, spec, tmpl_z, dims, tables):
    x_cells, y_cells, z_cells = dims
    n_x, n_y = x_cells + TEMPL, y_cells + HALF
    pad_y = n_y // 2 + -(n_y // 2) % 8
    width = y_cells * z_cells // 4
    vmem = pl.BlockSpec(memory_space=pltpu.VMEM)
    return pl.pallas_call(
        functools.partial(corr_kernel, dims, rot, entry),
        out_shape=(
            jax.ShapeDtypeStruct((x_cells, width), F32),
            jax.ShapeDtypeStruct((x_cells, width), F32),
            jax.ShapeDtypeStruct((2, x_cells, width), F32),
            jax.ShapeDtypeStruct((8, LANES), F32),
        ),
        in_specs=[pl.BlockSpec(memory_space=pltpu.SMEM)] * 2 + [vmem] * 11,
        out_specs=(vmem,) * 4,
        scratch_shapes=[
            pltpu.VMEM((BLOCKS * odd(BLOCK_ROWS), LANES), F32),
            pltpu.VMEM((TEMPL * odd(TEMPL), LANES), F32),
            pltpu.VMEM((TEMPL * odd(2 * pad_y), LANES), F32),
            pltpu.VMEM((2, 3 * TEMPL, GROUP * LANES), BF16),
            pltpu.VMEM((2, 2 * n_x, GROUP * LANES), BF16),
            pltpu.VMEM((2, 2 * n_y, GROUP * LANES), BF16),
            pltpu.VMEM((n_y * odd(x_cells), LANES), F32),
            pltpu.VMEM((x_cells * odd(y_cells), LANES), F32),
        ],
        compiler_params=pltpu.CompilerParams(vmem_limit_bytes=14 * 1024 * 1024),
        cost_estimate=pl.CostEstimate(flops=15 * 10**9, bytes_accessed=10**7, transcendentals=0),
        name="correlate",
    )(
        place, tile, held, last, mask, spec,
        tmpl_z, tables["ones_z"], tables["tmpl_y"], tables["tmpl_x"],
        tables["back_x"], tables["back_y"], tables["back_z"],
    )


def score_kernel(pieces, place_ref, coef_ref, mask_ref, *refs):
    best_ref, evid_ref, mom_ref = refs[len(refs) - 3 :]

    blocks = best_ref.shape[1] // LANES

    def step(i):
        lanes = pl.ds(pl.multiple_of(i * LANES, LANES), LANES)

        def score(k):
            at, entry = pieces[k]
            corr = refs[at][:, lanes] if entry is None else refs[at][entry, :, lanes]
            return (corr - coef_ref[k, 0]) * coef_ref[k, 1]

        mask = mask_ref[place_ref[0] * blocks + i]
        high = functools.reduce(jnp.maximum, [score(k) for k in range(len(pieces))])
        total = jnp.zeros_like(high)
        moment = [jnp.zeros_like(high) for _ in range(4)]
        for k in range(len(pieces)):
            weight = jnp.exp(score(k) - high)
            total = total + weight
            for c in range(4):
                moment[c] = moment[c] + weight * coef_ref[k, 2 + c]
        best_ref[:, lanes] = mask * high
        evid_ref[:, lanes] = mask * (high + jnp.log(total))
        share = mask / total
        for c in range(4):
            mom_ref[c, :, lanes] = moment[c] * share

    loop(blocks, step)


def combine(place, coefs, mask, arrays, pieces):
    shape = arrays[0].shape
    vmem = pl.BlockSpec(memory_space=pltpu.VMEM)
    out = jax.ShapeDtypeStruct(shape, F32)
    return pl.pallas_call(
        functools.partial(score_kernel, pieces),
        out_shape=(out, out, jax.ShapeDtypeStruct((4,) + shape, F32)),
        in_specs=[pl.BlockSpec(memory_space=pltpu.SMEM)] * 2 + [vmem] * (1 + len(arrays)),
        out_specs=(vmem,) * 3,
        compiler_params=pltpu.CompilerParams(vmem_limit_bytes=4 * 1024 * 1024),
        name="combine",
    )(place, coefs, mask, *arrays)


def swap_blocks(block, axis, step):
    return lax.ppermute(block, axis, [(i, i ^ step) for i in range(lax.axis_size(axis))])


def general_gather(templates):
    rots = templates.shape[0]
    count = lax.axis_size("tile")
    block = templates[:, None]
    for step in [1 << i for i in reversed(range(count.bit_length() - 1))]:
        other = swap_blocks(block, "tile", step)
        upper = (lax.axis_index("tile") & step) != 0
        pair = [jnp.where(upper, other, block), jnp.where(upper, block, other)]
        block = jnp.stack(pair, axis=2).reshape((rots, -1) + block.shape[2:])
    block = block.reshape(rots, BLOCKS, EACH * CHUNKS, LANES)
    block = jnp.pad(block, ((0, 0), (0, 0), (0, BLOCK_ROWS - EACH * CHUNKS), (0, 0)))
    held = jnp.stack([block[:, i] for i in HELD], axis=1)
    return held, jnp.stack([block[:, i ^ 1] for i in HELD], axis=1)


def merge(first, other):
    number_a, number_b = first[:1], other[:1]
    mean_a = first[1:2] / jnp.maximum(number_a, 1.0)
    mean_b = other[1:2] / jnp.maximum(number_b, 1.0)
    gap = mean_b - mean_a
    between = gap * gap * (number_a * number_b / jnp.maximum(number_a + number_b, 1.0))
    return first + other + jnp.where(jnp.arange(3)[:, None] == 2, between, 0.0)


def exchange_all(block, axis, low, high):
    count = lax.axis_size(axis)
    parts = [block]
    for step in range(low, high, low):
        parts.append(lax.ppermute(block, axis, [(i, i ^ step) for i in range(count)]))
    return jnp.stack(parts)


def neighbours(block, axis):
    count = lax.axis_size(axis)
    forward = [(i, i + 1) for i in range(count - 1)]
    backward = [(target, source) for source, target in forward]
    return lax.ppermute(block, axis, forward), lax.ppermute(block, axis, backward)


def local(tomogram, templates, valid, quats, rot_index):
    x_cells, voxels = tomogram.shape
    y_cells = valid.shape[1]
    z_cells = voxels // y_cells
    dims = (x_cells, y_cells, z_cells)
    tables = {name: jnp.asarray(table) for name, table in make_tables(*dims).items()}
    groups = lax.axis_size("rot")
    tiles = lax.axis_size("tile")
    me = lax.axis_index("rot")
    rots = templates.shape[0]

    tile = lax.axis_index("tile")
    by_blocks = tiles == BLOCKS
    if by_blocks:
        held = templates.reshape(rots, 1, EACH * CHUNKS, LANES)
        held = jnp.pad(held, ((0, 0), (0, 0), (0, BLOCK_ROWS - EACH * CHUNKS), (0, 0)))
        held, tomogram_after = lax.optimization_barrier((held, tomogram))
        held = jnp.concatenate([held, swap_blocks(held, "tile", 4)], axis=1)
    else:
        tomogram_after = tomogram
    half = x_cells // 2
    piece = lax.dynamic_slice_in_dim(tomogram_after, (me & 1) * half, half, 0)
    mine = jnp.stack(neighbours(piece, "tile"))
    side_swap = [(i, i ^ 1) for i in range(groups)]
    other = lax.ppermute(mine, "rot", side_swap)
    if by_blocks:
        held = jnp.concatenate([held, swap_blocks(held, "tile", 2)], axis=1)
    else:
        held, last = general_gather(templates)
        tile = jnp.zeros_like(tile)
    one_hot = (rot_index[:, None] == jnp.arange(quats.shape[1], dtype=jnp.int32)[None, :]).astype(F32)
    orient = jnp.einsum("rq,kq->rk", one_hot, quats, precision=lax.Precision.HIGHEST)
    place = me_place = jnp.reshape(me, (1,)).astype(jnp.int32)
    tile = jnp.reshape(tile, (1,)).astype(jnp.int32)
    own = slab_rows(place, [tomogram], x_cells, dims, tables, "slab_own")
    halo = slab_rows(place, [mine, other], TEMPL, dims, tables, "slab_halo")
    if by_blocks:
        held, halo = lax.optimization_barrier((held, halo))
        lasts = [swap_blocks(held[:1], "tile", 1), swap_blocks(held[1:], "tile", 1)]
    else:
        lasts = [last[:1], last[1:]]
    spec, mask, tmpl_z = slab_x(own, halo, valid, dims, tables)
    far_swap = [(i, i ^ 2) for i in range(groups)]
    mines, sides, fars, stats = [], [], [], []
    for r in range(rots):
        if r >= 2:
            place, fars[r - 2] = lax.optimization_barrier((place, fars[r - 2]))
        mine, side, far, stat = correlate(
            place, tile, held, r, lasts[min(r, 1)], max(r - 1, 0), mask, spec, tmpl_z, dims, tables
        )
        if r >= 1:
            stat, fars[r - 1] = lax.optimization_barrier((stat, fars[r - 1]))
        mines.append(mine)
        sides.append(side)
        stats.append(stat[:3, 0])
        fars.append(lax.ppermute(far, "rot", far_swap))
        if r == rots - 2:
            early = jnp.stack(sides[:-1] + [f[1] for f in fars[:-1]])
            early = lax.ppermute(early, "rot", side_swap)
    state = jnp.stack(stats, axis=1)
    state, early, fars[rots - 2] = lax.optimization_barrier((state, early, fars[rots - 2]))
    step = 1
    while step < tiles:
        partner = lax.ppermute(state, "tile", [(i, i ^ step) for i in range(tiles)])
        if step * 4 == tiles:
            late = jnp.where(partner[0, 0] >= 0.0, fars[rots - 1][1], 0.0)
            last = jnp.stack([sides[rots - 2], sides[rots - 1], fars[rots - 2][1], late])
        if step * 2 == tiles:
            partner, last = lax.optimization_barrier((partner, last))
        state = merge(state, partner)
        step *= 2
    average = state[1] / state[0]
    inverse = 1.0 / jnp.sqrt(state[2] / state[0] + EPSILON)
    coefs = jnp.concatenate([average[:, None], inverse[:, None], orient], axis=1)
    coefs = exchange_all(coefs, "rot", 1, groups)
    last = lax.ppermute(last, "rot", side_swap)
    arrays = mines + fars + [early, last]
    at_far, at_early, at_last = rots, 2 * rots, 2 * rots + 1
    pieces = [(r, None) for r in range(rots)]
    pieces += [(at_early, r) for r in range(rots - 2)] + [(at_last, 0), (at_last, 1)]
    pieces += [(at_far + r, 0) for r in range(rots)]
    pieces += [(at_early, rots - 2 + r) for r in range(rots - 2)] + [(at_last, 2), (at_last, 3)]
    return combine(me_place, coefs.reshape(groups * rots, 6), mask, arrays, pieces)


def solution(mesh):
    placed = (P("tile", None), P("rot", "tile"), P("tile", None), P(), P("rot"))
    return jax.shard_map(
        local,
        mesh=mesh,
        in_specs=placed,
        out_specs=(P("tile", "rot"), P("tile", "rot"), P(None, "tile", "rot")),
        check_vma=False,
    )
```

```python
import functools
import math

import jax
import jax.numpy as jnp
import ml_dtypes
import numpy as np
from jax import lax
from jax.experimental import pallas as pl
from jax.experimental.pallas import tpu as pltpu
from jax.sharding import PartitionSpec as P

TEMPL = 48
HALF = 24
EPSILON = 1e-06
LANES = 128
SPLIT = 64
BLOCKS = 8
EACH = TEMPL // BLOCKS
CHUNKS = TEMPL * TEMPL // LANES
BLOCK_ROWS = EACH * CHUNKS + -EACH * CHUNKS % 16
HELD = (0, 4, 2, 6)
F32 = jnp.float32
BF16 = jnp.bfloat16


def two_parts(table):
    high = table.astype(ml_dtypes.bfloat16)
    low = (table - high.astype(np.float64)).astype(ml_dtypes.bfloat16)
    return high, low


def row_table(out_idx, in_idx, length, sign, factor, wide):
    theta = 2.0 * math.pi / length * np.outer(out_idx, in_idx)
    pad = np.zeros((-len(out_idx) % 8, len(in_idx)))
    full = np.concatenate([np.cos(theta), pad, sign * np.sin(theta), pad], axis=0) * factor
    high, low = two_parts(full)
    if wide:
        return np.concatenate([high, high, low], axis=1)
    zeros = np.zeros_like(low)
    return np.concatenate(
        [np.concatenate([high, high], axis=1), np.concatenate([low, zeros], axis=1)], axis=0
    )


def depth_table(in_idx, length, sign, factor):
    freq = np.arange(length // 2) + 0.5
    theta = 2.0 * math.pi / length * np.outer(in_idx, freq)
    out = np.zeros((len(in_idx), LANES))
    out[:, : length // 2] = np.cos(theta) * factor
    out[:, SPLIT : SPLIT + length // 2] = sign * np.sin(theta) * factor
    return out


def half_odd(count):
    return np.arange(count // 2) + 0.5


def make_tables(x_cells, y_cells, z_cells):
    n_x, n_y, n_z = x_cells + TEMPL, y_cells + HALF, z_cells + HALF
    k_x, k_y = half_odd(n_x), half_odd(n_y)
    both_x = np.concatenate([k_x, -k_x])
    both_y = np.stack([k_y, -k_y], axis=1).reshape(-1)
    mid_x, mid_y = (x_cells - 1) / 2, (y_cells - 1) / 2
    tables = {}
    slab = np.zeros((2 * z_cells, 4 * LANES), ml_dtypes.bfloat16)
    high, low = two_parts(depth_table(np.arange(z_cells), n_z, -1.0, 1.0))
    for j in range(2):
        rows = slice(j * z_cells, (j + 1) * z_cells)
        slab[rows, 2 * j * LANES : (2 * j + 1) * LANES] = high
        slab[rows, (2 * j + 1) * LANES : (2 * j + 2) * LANES] = low
    slab_y = row_table(k_y, np.arange(y_cells), n_y, -1.0, 1.0, True)
    slab_y = np.pad(slab_y, ((0, 0), (0, slab.shape[1] - slab_y.shape[1])))
    tables["slab_rows"] = np.concatenate([slab, slab_y], axis=0)
    own = np.arange(HALF, HALF + x_cells)
    halo = np.concatenate([np.arange(HALF), np.arange(HALF + x_cells, n_x)])
    tables["slab_x"] = row_table(k_x, np.concatenate([own, halo]), n_x, -1.0, 1.0, True)
    high, low = two_parts(depth_table(np.arange(TEMPL) - HALF, n_z, 1.0, 1.0))
    tables["tmpl_z"] = np.concatenate([high, low], axis=1)
    ones = (high.astype(np.float64) + low.astype(np.float64)).sum(axis=0)
    tables["ones_z"] = np.broadcast_to(ones.astype(np.float32)[None], (8, LANES)).copy()
    tables["tmpl_y"] = row_table(k_y, np.arange(TEMPL) - HALF + mid_y, n_y, 1.0, 1.0, True)
    tmpl_rows = np.arange(TEMPL).reshape(BLOCKS, EACH).T.reshape(-1)
    tables["tmpl_x"] = row_table(k_x, tmpl_rows + mid_x, n_x, 1.0, 1.0, True)
    tables["back_x"] = row_table(half_odd(x_cells), both_x, n_x, 1.0, 1.0 / n_x, False)
    tables["back_y"] = row_table(half_odd(y_cells), both_y, n_y, 1.0, 1.0 / n_y, False)
    back = depth_table(np.arange(z_cells), n_z, -1.0, 2.0 / n_z).T
    high, low = two_parts(back)
    back_z = np.zeros((2 * LANES, 2 * LANES), ml_dtypes.bfloat16)
    for j in range(2):
        rows = slice(j * LANES, (j + 1) * LANES)
        back_z[rows, j * z_cells : (j + 1) * z_cells] = high
        back_z[rows, LANES + j * z_cells : LANES + (j + 1) * z_cells] = low
    tables["back_z"] = back_z
    return tables


def split_rows(value, wide):
    high = value.astype(BF16)
    if value.shape[0] % 16 == 0:
        low = (value - high.astype(F32)).astype(BF16)
        return jnp.concatenate([high, low, high] if wide else [high, low], axis=0)
    high = high.astype(F32)
    low = value - high
    return jnp.concatenate([high, low, high] if wide else [high, low], axis=0).astype(BF16)


def swap(value):
    parts = [
        pltpu.roll(value[:, s : s + LANES], SPLIT, 1) for s in range(0, value.shape[1], LANES)
    ]
    return jnp.concatenate(parts, axis=1)


def lane_sign(width):
    lane = lax.broadcasted_iota(jnp.int32, (8, width), 1) % LANES
    return jnp.where(lane < SPLIT, -1.0, 1.0)[:1]


def pair_rows(table, value, wide):
    return pair_dot(table, split_rows(value, wide), wide)


def pair_dot(table, parts, wide):
    out = jnp.dot(table, parts, preferred_element_type=F32)
    if not wide:
        half = out.shape[0] // 2
        out = out[:half] + out[half:]
    half = out.shape[0] // 2
    turned = swap(out[half:]) * lane_sign(out.shape[1])
    return out[:half] + turned, out[:half] - turned


def pick(ref, firsts, count, stride):
    return jnp.concatenate([ref[pl.ds(f, count, stride=stride), :] for f in firsts], axis=1)


def store(ref, start, value):
    ref[pl.ds(start, value.shape[0]), :] = value


def odd(rows):
    return rows + 1


def lane_block(value, i):
    return value[:, i * LANES : (i + 1) * LANES]


def loop(count, body):
    def one(i, carry):
        body(i)
        return carry

    lax.fori_loop(0, count, one, 0)


GROUP = 8


def pipeline(steps, stages, width):
    blocks = -(-steps // width)
    depth = len(stages)

    def turn(t, static):
        for s in reversed(range(depth)):
            if static and not 0 <= t - s < blocks:
                continue
            for slot in range(width):
                step = (t - s) * width + slot
                if not static or step < steps:
                    stages[s](step, slot)

    full = steps // width
    first, last = depth - 1, max(full, depth - 1)
    for t in range(first):
        turn(t, True)
    if last - first >= 2:
        loop(last - first, lambda i: turn(i + first, False))
    else:
        last = first
    for t in range(last, blocks + depth - 1):
        turn(t, True)


def slab_rows_kernel(dims, place_ref, *refs):
    sources, (table_ref, rows_ref, depth_buf, parts_buf) = refs[:-4], refs[-4:]
    x_cells, y_cells, z_cells = dims
    half = x_cells // 2
    count = depth_buf.shape[0] // y_cells - 1
    n_y = y_cells + HALF
    pad_y = n_y // 2 + -(n_y // 2) % 8
    many = 4

    def read(lanes):
        if len(sources) == 1:
            return sources[0][:, lanes].astype(F32)
        first = (place_ref[0] & 1) == 0
        mine, other = ([ref[i, :, lanes].astype(F32) for i in range(2)] for ref in sources)
        low, high = (
            jnp.concatenate([jnp.where(first, m, o), jnp.where(first, o, m)], axis=0)
            for m, o in zip(mine, other)
        )
        return jnp.concatenate([low[x_cells - HALF :], high[:HALF]], axis=0)

    def depth_step(i):
        lanes = [pl.ds(pl.multiple_of((many * i + u) * LANES, LANES), LANES) for u in range(many)]
        block = jnp.concatenate([read(l) for l in lanes], axis=0).astype(BF16)
        out = jnp.dot(block, table_ref[: 2 * z_cells], preferred_element_type=F32)
        for u in range(many):
            part = out[u * count : (u + 1) * count]
            for j in range(2):
                store(
                    depth_buf, (2 * many * i + 2 * u + j) * odd(count),
                    lane_block(part, 2 * j) + lane_block(part, 2 * j + 1),
                )

    loop(y_cells // (2 * many), depth_step)

    def gather_rows(i, slot):
        value = pick(depth_buf, [GROUP * i + u for u in range(GROUP)], y_cells, odd(count))
        parts_buf[slot] = split_rows(value, True)

    def y_step(i, slot):
        plus, minus = pair_dot(table_ref[2 * z_cells :, : 3 * y_cells], parts_buf[slot], True)
        for u in range(GROUP):
            start = (GROUP * i + u) * odd(2 * pad_y)
            store(rows_ref, start, lane_block(plus, u))
            store(rows_ref, start + pad_y, lane_block(minus, u))

    pipeline(count // GROUP, [gather_rows, y_step], 2)


def slab_rows(place, blocks, count, dims, tables, name):
    x_cells, y_cells, z_cells = dims
    n_y = y_cells + HALF
    pad_y = n_y // 2 + -(n_y // 2) % 8
    vmem = pl.BlockSpec(memory_space=pltpu.VMEM)
    return pl.pallas_call(
        functools.partial(slab_rows_kernel, dims),
        out_shape=jax.ShapeDtypeStruct((count * odd(2 * pad_y), LANES), F32),
        in_specs=[pl.BlockSpec(memory_space=pltpu.SMEM)] + [vmem] * (1 + len(blocks)),
        out_specs=vmem,
        scratch_shapes=[
            pltpu.VMEM((y_cells * odd(count), LANES), F32),
            pltpu.VMEM((2, 3 * y_cells, GROUP * LANES), BF16),
        ],
        compiler_params=pltpu.CompilerParams(vmem_limit_bytes=20 * 1024 * 1024),
        cost_estimate=pl.CostEstimate(flops=count * 10**8, bytes_accessed=10**6, transcendentals=0),
        name=name,
    )(place, *blocks, tables["slab_rows"])


def slab_x_kernel(
    dims, own_ref, halo_ref, x_ref, valid_ref, tz_ref, spec_ref, mask_ref, z_ref, parts_buf
):
    x_cells, y_cells, z_cells = dims
    n_y = y_cells + HALF
    pad_y = n_y // 2 + -(n_y // 2) % 8

    def gather_rows(i, slot):
        firsts = [GROUP // 2 * i + u // 2 + u % 2 * pad_y for u in range(GROUP)]
        value = jnp.concatenate(
            [
                pick(own_ref, firsts, x_cells, odd(2 * pad_y)),
                pick(halo_ref, firsts, TEMPL, odd(2 * pad_y)),
            ],
            axis=0,
        )
        parts_buf[slot] = split_rows(value, True)

    def x_step(i, slot):
        plus, minus = pair_dot(x_ref[...], parts_buf[slot], True)
        spec = jnp.concatenate([plus, minus], axis=0)
        turned = swap(spec)
        real_lane = lane_sign(GROUP * LANES) < 0
        spec_ref[i, 0] = jnp.where(real_lane, spec, turned)
        spec_ref[i, 1] = jnp.where(real_lane, -turned, spec)

    pipeline(n_y // GROUP, [gather_rows, x_step], 2)

    valid = valid_ref[...].astype(F32)
    low_lane = lax.broadcasted_iota(jnp.int32, (x_cells, LANES), 1) < z_cells
    for q in range(y_cells // 2):
        mask_ref[q] = jnp.where(low_lane, valid[:, 2 * q : 2 * q + 1], valid[:, 2 * q + 1 : 2 * q + 2])
    z_ref[...] = jnp.zeros(z_ref.shape, BF16)
    for j in range(8):
        start = TEMPL * j - (LANES if j >= 4 else 0)
        z_ref[j, start : start + TEMPL, :] = tz_ref[...]


def slab_x(own, halo, valid, dims, tables):
    x_cells, y_cells, z_cells = dims
    n_x, n_y = x_cells + TEMPL, y_cells + HALF
    steps = n_y // GROUP
    vmem = pl.BlockSpec(memory_space=pltpu.VMEM)
    shape = (steps, 2, n_x, GROUP * LANES)
    return pl.pallas_call(
        functools.partial(slab_x_kernel, dims),
        out_shape=(
            jax.ShapeDtypeStruct(shape, F32),
            jax.ShapeDtypeStruct((y_cells // 2, x_cells, LANES), F32),
            jax.ShapeDtypeStruct((8, 2 * LANES, 2 * LANES), BF16),
        ),
        in_specs=[vmem] * 5,
        out_specs=(vmem,) * 3,
        scratch_shapes=[pltpu.VMEM((2, 3 * n_x, GROUP * LANES), BF16)],
        compiler_params=pltpu.CompilerParams(vmem_limit_bytes=20 * 1024 * 1024),
        cost_estimate=pl.CostEstimate(flops=5 * 10**9, bytes_accessed=10**6, transcendentals=0),
        name="slab_x",
    )(own, halo, tables["slab_x"], valid, tables["tmpl_z"])


def corr_kernel(
    dims, rot, entry, place_ref, tile_ref, held_ref, last_ref, mask_ref, spec_ref,
    z_ref, ones_ref, y_ref, x_ref, bx_ref, by_ref, bz_ref,
    mine_ref, side_ref, far_ref, stat_ref,
    bank_buf, depth_buf, rows_buf, first_buf, second_buf, third_buf, back_buf, vol_buf,
):
    x_cells, y_cells, z_cells = dims
    n_x, n_y = x_cells + TEMPL, y_cells + HALF
    half_y = n_y // 2
    pad_y = half_y + -half_y % 8
    for i, block in enumerate(HELD):
        for ref, at, tile in ((held_ref, rot, block), (last_ref, entry, block ^ 1)):
            store(bank_buf, (tile_ref[0] ^ tile) * odd(BLOCK_ROWS), ref[at, i].astype(F32))
    tmpl = jnp.concatenate(
        [
            pick(bank_buf, [a * CHUNKS + i for i in range(CHUNKS)], BLOCKS, odd(BLOCK_ROWS))
            for a in range(EACH)
        ],
        axis=0,
    )
    inv_size = 1.0 / TEMPL**3
    mean = jnp.sum(tmpl) * inv_size
    centred = tmpl - mean
    var = jnp.sum(centred * centred) * inv_size
    scale = 1.0 / (jnp.sqrt(jnp.full((1, LANES), var + EPSILON, F32)) * TEMPL**1.5)
    shift = ones_ref[:1] * mean

    wide = 8 * TEMPL
    narrow = tmpl.astype(BF16)
    block = jnp.concatenate(
        [narrow[:, g * wide : (g + 1) * wide] for g in range(TEMPL // 8)], axis=0
    )
    for j in range(8):
        window = block[:, : 2 * LANES] if j < 4 else block[:, LANES:]
        out = jnp.dot(window, z_ref[j], preferred_element_type=F32)
        part = out[:, :LANES] + out[:, LANES:] - shift
        for g in range(TEMPL // 8):
            start = (8 * g + j) * odd(TEMPL)
            store(depth_buf, start, part[g * TEMPL : (g + 1) * TEMPL])

    def gather_a(i, slot):
        value = pick(depth_buf, [GROUP * i + u for u in range(GROUP)], TEMPL, odd(TEMPL))
        first_buf[slot] = split_rows(value, True)

    def y_step(i, slot):
        plus, minus = pair_dot(y_ref[...], first_buf[slot], True)
        for u in range(GROUP):
            start = (GROUP * i + u) * odd(2 * pad_y)
            store(rows_buf, start, lane_block(plus, u))
            store(rows_buf, start + pad_y, lane_block(minus, u))

    pipeline(TEMPL // GROUP, [gather_a, y_step], 2)

    def gather_ky(i, slot):
        firsts = [GROUP // 2 * i + u // 2 + u % 2 * pad_y for u in range(GROUP)]
        first_buf[slot] = split_rows(pick(rows_buf, firsts, TEMPL, odd(2 * pad_y)), True)

    def multiply(i, slot):
        plus, minus = pair_dot(x_ref[...], first_buf[slot], True)
        spec = jnp.concatenate([plus, minus], axis=0)
        prod = spec * spec_ref[i, 0] + swap(spec) * spec_ref[i, 1]
        second_buf[slot] = split_rows(prod, False)

    def back_x(i, slot):
        plus, minus = pair_dot(bx_ref[...], second_buf[slot], False)
        for u in range(GROUP):
            start = (GROUP * i + u) * odd(x_cells)
            store(back_buf, start, lane_block(plus, u))
            store(back_buf, start + x_cells // 2, lane_block(minus, u))

    pipeline(n_y // GROUP, [gather_ky, multiply, back_x], 2)

    def gather_x(i, slot):
        value = pick(back_buf, [GROUP * i + u for u in range(GROUP)], n_y, odd(x_cells))
        third_buf[slot] = split_rows(value, False)

    def back_y(i, slot):
        plus, minus = pair_dot(by_ref[...], third_buf[slot], False)
        for u in range(GROUP):
            row = GROUP * i + u
            x = jnp.where(row < x_cells // 2, row + x_cells // 2, x_cells - 1 - row)
            store(vol_buf, x * odd(y_cells), lane_block(plus, u))
            store(vol_buf, x * odd(y_cells) + y_cells // 2, lane_block(minus, u))

    pipeline(x_cells // GROUP, [gather_x, back_y], 2)

    share = y_cells // 8
    me = place_ref[0]
    total = jnp.zeros((x_cells, LANES), F32)
    number = jnp.zeros((x_cells, LANES), F32)
    targets = [mine_ref, side_ref, far_ref.at[0], far_ref.at[1]]
    for p, target in enumerate(targets):
        first = (me ^ p) * share
        values = []
        for i in range(share):
            firsts = []
            for j in range(2):
                y = 2 * (first + i) + j
                firsts.append(jnp.where(y < y_cells // 2, y_cells - 1 - y, y - y_cells // 2))
            values.append(pick(vol_buf, firsts, x_cells, odd(y_cells)))
        value = jnp.concatenate(values, axis=0)
        out = jnp.dot(split_rows(value, False), bz_ref[...], preferred_element_type=F32)
        rows = value.shape[0]
        full = out[:rows, :LANES] + out[:rows, LANES:] + out[rows:, :LANES]
        for i in range(share):
            corr = full[i * x_cells : (i + 1) * x_cells] * scale
            target[:, i * LANES : (i + 1) * LANES] = corr
            mask = mask_ref[first + i]
            total = total + corr * mask
            number = number + mask
    number_sum = jnp.sum(number)
    total_sum = jnp.sum(total)
    local_mean = jnp.full((1, LANES), total_sum, F32) / jnp.maximum(number_sum, 1.0)
    square = jnp.zeros((x_cells, LANES), F32)
    for p, target in enumerate(targets):
        first = (me ^ p) * share
        for i in range(share):
            gap = target[:, i * LANES : (i + 1) * LANES] - local_mean
            square = square + gap * gap * mask_ref[first + i]
    row = lax.broadcasted_iota(jnp.int32, (8, LANES), 0)
    stat_ref[...] = jnp.where(row == 0, number_sum, jnp.where(row == 1, total_sum, jnp.sum(square)))


def correlate(place, tile, held, rot, last, entry, mask, spec, tmpl_z, dims, tables):
    x_cells, y_cells, z_cells = dims
    n_x, n_y = x_cells + TEMPL, y_cells + HALF
    pad_y = n_y // 2 + -(n_y // 2) % 8
    width = y_cells * z_cells // 4
    vmem = pl.BlockSpec(memory_space=pltpu.VMEM)
    return pl.pallas_call(
        functools.partial(corr_kernel, dims, rot, entry),
        out_shape=(
            jax.ShapeDtypeStruct((x_cells, width), F32),
            jax.ShapeDtypeStruct((x_cells, width), F32),
            jax.ShapeDtypeStruct((2, x_cells, width), F32),
            jax.ShapeDtypeStruct((8, LANES), F32),
        ),
        in_specs=[pl.BlockSpec(memory_space=pltpu.SMEM)] * 2 + [vmem] * 11,
        out_specs=(vmem,) * 4,
        scratch_shapes=[
            pltpu.VMEM((BLOCKS * odd(BLOCK_ROWS), LANES), F32),
            pltpu.VMEM((TEMPL * odd(TEMPL), LANES), F32),
            pltpu.VMEM((TEMPL * odd(2 * pad_y), LANES), F32),
            pltpu.VMEM((2, 3 * TEMPL, GROUP * LANES), BF16),
            pltpu.VMEM((2, 2 * n_x, GROUP * LANES), BF16),
            pltpu.VMEM((2, 2 * n_y, GROUP * LANES), BF16),
            pltpu.VMEM((n_y * odd(x_cells), LANES), F32),
            pltpu.VMEM((x_cells * odd(y_cells), LANES), F32),
        ],
        compiler_params=pltpu.CompilerParams(vmem_limit_bytes=24 * 1024 * 1024),
        cost_estimate=pl.CostEstimate(flops=15 * 10**9, bytes_accessed=10**7, transcendentals=0),
        name="correlate",
    )(
        place, tile, held, last, mask, spec,
        tmpl_z, tables["ones_z"], tables["tmpl_y"], tables["tmpl_x"],
        tables["back_x"], tables["back_y"], tables["back_z"],
    )


def score_kernel(pieces, place_ref, coef_ref, mask_ref, *refs):
    best_ref, evid_ref, mom_ref = refs[len(refs) - 3 :]

    blocks = best_ref.shape[1] // LANES

    def step(i):
        lanes = pl.ds(pl.multiple_of(i * LANES, LANES), LANES)

        def score(k):
            at, entry = pieces[k]
            corr = refs[at][:, lanes] if entry is None else refs[at][entry, :, lanes]
            return (corr - coef_ref[k, 0]) * coef_ref[k, 1]

        mask = mask_ref[place_ref[0] * blocks + i]
        high = functools.reduce(jnp.maximum, [score(k) for k in range(len(pieces))])
        total = jnp.zeros_like(high)
        moment = [jnp.zeros_like(high) for _ in range(4)]
        for k in range(len(pieces)):
            weight = jnp.exp(score(k) - high)
            total = total + weight
            for c in range(4):
                moment[c] = moment[c] + weight * coef_ref[k, 2 + c]
        best_ref[:, lanes] = mask * high
        evid_ref[:, lanes] = mask * (high + jnp.log(total))
        share = mask / total
        for c in range(4):
            mom_ref[c, :, lanes] = moment[c] * share

    loop(blocks, step)


def combine(place, coefs, mask, arrays, pieces):
    shape = arrays[0].shape
    vmem = pl.BlockSpec(memory_space=pltpu.VMEM)
    out = jax.ShapeDtypeStruct(shape, F32)
    return pl.pallas_call(
        functools.partial(score_kernel, pieces),
        out_shape=(out, out, jax.ShapeDtypeStruct((4,) + shape, F32)),
        in_specs=[pl.BlockSpec(memory_space=pltpu.SMEM)] * 2 + [vmem] * (1 + len(arrays)),
        out_specs=(vmem,) * 3,
        compiler_params=pltpu.CompilerParams(vmem_limit_bytes=16 * 1024 * 1024),
        name="combine",
    )(place, coefs, mask, *arrays)


def swap_blocks(block, axis, step):
    return lax.ppermute(block, axis, [(i, i ^ step) for i in range(lax.axis_size(axis))])


def general_gather(templates):
    rots = templates.shape[0]
    count = lax.axis_size("tile")
    block = templates[:, None]
    for step in [1 << i for i in reversed(range(count.bit_length() - 1))]:
        other = swap_blocks(block, "tile", step)
        upper = (lax.axis_index("tile") & step) != 0
        pair = [jnp.where(upper, other, block), jnp.where(upper, block, other)]
        block = jnp.stack(pair, axis=2).reshape((rots, -1) + block.shape[2:])
    block = block.reshape(rots, BLOCKS, EACH * CHUNKS, LANES)
    block = jnp.pad(block, ((0, 0), (0, 0), (0, BLOCK_ROWS - EACH * CHUNKS), (0, 0)))
    held = jnp.stack([block[:, i] for i in HELD], axis=1)
    return held, jnp.stack([block[:, i ^ 1] for i in HELD], axis=1)


def merge(first, other):
    number_a, number_b = first[:1], other[:1]
    mean_a = first[1:2] / jnp.maximum(number_a, 1.0)
    mean_b = other[1:2] / jnp.maximum(number_b, 1.0)
    gap = mean_b - mean_a
    between = gap * gap * (number_a * number_b / jnp.maximum(number_a + number_b, 1.0))
    return first + other + jnp.where(jnp.arange(3)[:, None] == 2, between, 0.0)


def exchange_all(block, axis, low, high):
    count = lax.axis_size(axis)
    parts = [block]
    for step in range(low, high, low):
        parts.append(lax.ppermute(block, axis, [(i, i ^ step) for i in range(count)]))
    return jnp.stack(parts)


def neighbours(block, axis):
    count = lax.axis_size(axis)
    forward = [(i, i + 1) for i in range(count - 1)]
    backward = [(target, source) for source, target in forward]
    return lax.ppermute(block, axis, forward), lax.ppermute(block, axis, backward)


def local(tomogram, templates, valid, quats, rot_index):
    x_cells, voxels = tomogram.shape
    y_cells = valid.shape[1]
    z_cells = voxels // y_cells
    dims = (x_cells, y_cells, z_cells)
    tables = {name: jnp.asarray(table) for name, table in make_tables(*dims).items()}
    groups = lax.axis_size("rot")
    tiles = lax.axis_size("tile")
    me = lax.axis_index("rot")
    rots = templates.shape[0]

    tile = lax.axis_index("tile")
    by_blocks = tiles == BLOCKS
    if by_blocks:
        held = templates.reshape(rots, 1, EACH * CHUNKS, LANES)
        held = jnp.pad(held, ((0, 0), (0, 0), (0, BLOCK_ROWS - EACH * CHUNKS), (0, 0)))
        first = swap_blocks(held, "tile", 4)
        held = jnp.concatenate([held, first], axis=1)
    half = x_cells // 2
    piece = lax.dynamic_slice_in_dim(tomogram, (me & 1) * half, half, 0)
    if by_blocks:
        piece = jnp.where(first[0, 0, 0, 0].astype(F32) < 100.0, piece, jnp.zeros_like(piece))
    mine = jnp.stack(neighbours(piece, "tile"))
    side_swap = [(i, i ^ 1) for i in range(groups)]
    other = lax.ppermute(mine, "rot", side_swap)
    if by_blocks:
        held = jnp.concatenate([held, swap_blocks(held, "tile", 2)], axis=1)
    else:
        held, last = general_gather(templates)
        tile = jnp.zeros_like(tile)
    one_hot = (rot_index[:, None] == jnp.arange(quats.shape[1], dtype=jnp.int32)[None, :]).astype(F32)
    orient = jnp.einsum("rq,kq->rk", one_hot, quats, precision=lax.Precision.HIGHEST)
    place = me_place = jnp.reshape(me, (1,)).astype(jnp.int32)
    tile = jnp.reshape(tile, (1,)).astype(jnp.int32)
    own = slab_rows(place, [tomogram], x_cells, dims, tables, "slab_own")
    halo = slab_rows(place, [mine, other], TEMPL, dims, tables, "slab_halo")
    if by_blocks:
        lasts = [swap_blocks(held[:1], "tile", 1), swap_blocks(held[1:], "tile", 1)]
    else:
        lasts = [last[:1], last[1:]]
    spec, mask, tmpl_z = slab_x(own, halo, valid, dims, tables)
    far_swap = [(i, i ^ 2) for i in range(groups)]
    mines, sides, fars, stats = [], [], [], []
    for r in range(rots):
        if r >= 2:
            place, fars[r - 2] = lax.optimization_barrier((place, fars[r - 2]))
        mine, side, far, stat = correlate(
            place, tile, held, r, lasts[min(r, 1)], max(r - 1, 0), mask, spec, tmpl_z, dims, tables
        )
        if r >= 1:
            stat, fars[r - 1] = lax.optimization_barrier((stat, fars[r - 1]))
        mines.append(mine)
        sides.append(side)
        stats.append(stat[:3, 0])
        fars.append(lax.ppermute(far, "rot", far_swap))
        if r == rots - 2:
            early = jnp.stack(sides[:-1] + [f[1] for f in fars[:-1]])
            early = lax.ppermute(early, "rot", side_swap)
    state = jnp.stack(stats, axis=1)
    state, early, fars[rots - 2] = lax.optimization_barrier((state, early, fars[rots - 2]))
    step = 1
    while step < tiles:
        partner = lax.ppermute(state, "tile", [(i, i ^ step) for i in range(tiles)])
        if step * 4 == tiles:
            late = jnp.where(partner[0, 0] >= 0.0, fars[rots - 1][1], 0.0)
            last = jnp.stack([sides[rots - 2], sides[rots - 1], fars[rots - 2][1], late])
        if step * 2 == tiles:
            partner, last = lax.optimization_barrier((partner, last))
        state = merge(state, partner)
        step *= 2
    average = state[1] / state[0]
    inverse = 1.0 / jnp.sqrt(state[2] / state[0] + EPSILON)
    coefs = jnp.concatenate([average[:, None], inverse[:, None], orient], axis=1)
    coefs = exchange_all(coefs, "rot", 1, groups)
    last = lax.ppermute(last, "rot", side_swap)
    arrays = mines + fars + [early, last]
    at_far, at_early, at_last = rots, 2 * rots, 2 * rots + 1
    pieces = [(r, None) for r in range(rots)]
    pieces += [(at_early, r) for r in range(rots - 2)] + [(at_last, 0), (at_last, 1)]
    pieces += [(at_far + r, 0) for r in range(rots)]
    pieces += [(at_early, rots - 2 + r) for r in range(rots - 2)] + [(at_last, 2), (at_last, 3)]
    return combine(me_place, coefs.reshape(groups * rots, 6), mask, arrays, pieces)


def solution(mesh):
    placed = (P("tile", None), P("rot", "tile"), P("tile", None), P(), P("rot"))
    return jax.shard_map(
        local,
        mesh=mesh,
        in_specs=placed,
        out_specs=(P("tile", "rot"), P("tile", "rot"), P(None, "tile", "rot")),
        check_vma=False,
    )
```

```python
import functools
import math

import jax
import jax.numpy as jnp
import ml_dtypes
import numpy as np
from jax import lax
from jax.experimental import pallas as pl
from jax.experimental.pallas import tpu as pltpu
from jax.sharding import PartitionSpec as P

TEMPL = 48
HALF = 24
EPSILON = 1e-06
LANES = 128
SPLIT = 64
BLOCKS = 8
EACH = TEMPL // BLOCKS
CHUNKS = TEMPL * TEMPL // LANES
BLOCK_ROWS = EACH * CHUNKS + -EACH * CHUNKS % 16
HELD = (0, 4, 2, 6)
F32 = jnp.float32
BF16 = jnp.bfloat16


def two_parts(table):
    high = table.astype(ml_dtypes.bfloat16)
    low = (table - high.astype(np.float64)).astype(ml_dtypes.bfloat16)
    return high, low


def row_table(out_idx, in_idx, length, sign, factor, wide):
    theta = 2.0 * math.pi / length * np.outer(out_idx, in_idx)
    pad = np.zeros((-len(out_idx) % 8, len(in_idx)))
    full = np.concatenate([np.cos(theta), pad, sign * np.sin(theta), pad], axis=0) * factor
    high, low = two_parts(full)
    if wide:
        return np.concatenate([high, high, low], axis=1)
    zeros = np.zeros_like(low)
    return np.concatenate(
        [np.concatenate([high, high], axis=1), np.concatenate([low, zeros], axis=1)], axis=0
    )


def depth_table(in_idx, length, sign, factor):
    freq = np.arange(length // 2) + 0.5
    theta = 2.0 * math.pi / length * np.outer(in_idx, freq)
    out = np.zeros((len(in_idx), LANES))
    out[:, : length // 2] = np.cos(theta) * factor
    out[:, SPLIT : SPLIT + length // 2] = sign * np.sin(theta) * factor
    return out


def half_odd(count):
    return np.arange(count // 2) + 0.5


def make_tables(x_cells, y_cells, z_cells):
    n_x, n_y, n_z = x_cells + TEMPL, y_cells + HALF, z_cells + HALF
    k_x, k_y = half_odd(n_x), half_odd(n_y)
    both_x = np.concatenate([k_x, -k_x])
    both_y = np.stack([k_y, -k_y], axis=1).reshape(-1)
    mid_x, mid_y = (x_cells - 1) / 2, (y_cells - 1) / 2
    tables = {}
    slab = np.zeros((2 * z_cells, 4 * LANES), ml_dtypes.bfloat16)
    high, low = two_parts(depth_table(np.arange(z_cells), n_z, -1.0, 1.0))
    for j in range(2):
        rows = slice(j * z_cells, (j + 1) * z_cells)
        slab[rows, 2 * j * LANES : (2 * j + 1) * LANES] = high
        slab[rows, (2 * j + 1) * LANES : (2 * j + 2) * LANES] = low
    slab_y = row_table(k_y, np.arange(y_cells), n_y, -1.0, 1.0, True)
    slab_y = np.pad(slab_y, ((0, 0), (0, slab.shape[1] - slab_y.shape[1])))
    tables["slab_rows"] = np.concatenate([slab, slab_y], axis=0)
    own = np.arange(HALF, HALF + x_cells)
    halo = np.concatenate([np.arange(HALF), np.arange(HALF + x_cells, n_x)])
    tables["slab_x"] = row_table(k_x, np.concatenate([own, halo]), n_x, -1.0, 1.0, True)
    high, low = two_parts(depth_table(np.arange(TEMPL) - HALF, n_z, 1.0, 1.0))
    tables["tmpl_z"] = np.concatenate([high, low], axis=1)
    ones = (high.astype(np.float64) + low.astype(np.float64)).sum(axis=0)
    tables["ones_z"] = np.broadcast_to(ones.astype(np.float32)[None], (8, LANES)).copy()
    tables["tmpl_y"] = row_table(k_y, np.arange(TEMPL) - HALF + mid_y, n_y, 1.0, 1.0, True)
    tmpl_rows = np.arange(TEMPL).reshape(BLOCKS, EACH).T.reshape(-1)
    tables["tmpl_x"] = row_table(k_x, tmpl_rows + mid_x, n_x, 1.0, 1.0, True)
    tables["back_x"] = row_table(half_odd(x_cells), both_x, n_x, 1.0, 1.0 / n_x, False)
    tables["back_y"] = row_table(half_odd(y_cells), both_y, n_y, 1.0, 1.0 / n_y, False)
    back = depth_table(np.arange(z_cells), n_z, -1.0, 2.0 / n_z).T
    high, low = two_parts(back)
    back_z = np.zeros((2 * LANES, 2 * LANES), ml_dtypes.bfloat16)
    for j in range(2):
        rows = slice(j * LANES, (j + 1) * LANES)
        back_z[rows, j * z_cells : (j + 1) * z_cells] = high
        back_z[rows, LANES + j * z_cells : LANES + (j + 1) * z_cells] = low
    tables["back_z"] = back_z
    return tables


def split_rows(value, wide):
    high = value.astype(BF16)
    if value.shape[0] % 16 == 0:
        low = (value - high.astype(F32)).astype(BF16)
        return jnp.concatenate([high, low, high] if wide else [high, low], axis=0)
    high = high.astype(F32)
    low = value - high
    return jnp.concatenate([high, low, high] if wide else [high, low], axis=0).astype(BF16)


def swap(value):
    parts = [
        pltpu.roll(value[:, s : s + LANES], SPLIT, 1) for s in range(0, value.shape[1], LANES)
    ]
    return jnp.concatenate(parts, axis=1)


def lane_sign(width):
    lane = lax.broadcasted_iota(jnp.int32, (8, width), 1) % LANES
    return jnp.where(lane < SPLIT, -1.0, 1.0)[:1]


def pair_rows(table, value, wide):
    return pair_dot(table, split_rows(value, wide), wide)


def pair_dot(table, parts, wide):
    out = jnp.dot(table, parts, preferred_element_type=F32)
    if not wide:
        half = out.shape[0] // 2
        out = out[:half] + out[half:]
    half = out.shape[0] // 2
    turned = swap(out[half:]) * lane_sign(out.shape[1])
    return out[:half] + turned, out[:half] - turned


def pick(ref, firsts, count, stride):
    return jnp.concatenate([ref[pl.ds(f, count, stride=stride), :] for f in firsts], axis=1)


def store(ref, start, value):
    ref[pl.ds(start, value.shape[0]), :] = value


def odd(rows):
    return rows + 1


def lane_block(value, i):
    return value[:, i * LANES : (i + 1) * LANES]


def loop(count, body):
    def one(i, carry):
        body(i)
        return carry

    lax.fori_loop(0, count, one, 0)


GROUP = 8


def pipeline(steps, stages, width):
    blocks = -(-steps // width)
    depth = len(stages)

    def turn(t, static):
        for s in reversed(range(depth)):
            if static and not 0 <= t - s < blocks:
                continue
            for slot in range(width):
                step = (t - s) * width + slot
                if not static or step < steps:
                    stages[s](step, slot)

    full = steps // width
    first, last = depth - 1, max(full, depth - 1)
    for t in range(first):
        turn(t, True)
    if last - first >= 2:
        loop(last - first, lambda i: turn(i + first, False))
    else:
        last = first
    for t in range(last, blocks + depth - 1):
        turn(t, True)


def slab_rows_kernel(dims, place_ref, *refs):
    sources, (table_ref, rows_ref, depth_buf, parts_buf) = refs[:-4], refs[-4:]
    x_cells, y_cells, z_cells = dims
    half = x_cells // 2
    count = depth_buf.shape[0] // y_cells - 1
    n_y = y_cells + HALF
    pad_y = n_y // 2 + -(n_y // 2) % 8
    many = 4

    def read(lanes):
        if len(sources) == 1:
            return sources[0][:, lanes].astype(F32)
        first = (place_ref[0] & 1) == 0
        mine, other = ([ref[i, :, lanes].astype(F32) for i in range(2)] for ref in sources)
        low, high = (
            jnp.concatenate([jnp.where(first, m, o), jnp.where(first, o, m)], axis=0)
            for m, o in zip(mine, other)
        )
        return jnp.concatenate([low[x_cells - HALF :], high[:HALF]], axis=0)

    def depth_step(i):
        lanes = [pl.ds(pl.multiple_of((many * i + u) * LANES, LANES), LANES) for u in range(many)]
        block = jnp.concatenate([read(l) for l in lanes], axis=0).astype(BF16)
        out = jnp.dot(block, table_ref[: 2 * z_cells], preferred_element_type=F32)
        for u in range(many):
            part = out[u * count : (u + 1) * count]
            for j in range(2):
                store(
                    depth_buf, (2 * many * i + 2 * u + j) * odd(count),
                    lane_block(part, 2 * j) + lane_block(part, 2 * j + 1),
                )

    loop(y_cells // (2 * many), depth_step)

    def gather_rows(i, slot):
        value = pick(depth_buf, [GROUP * i + u for u in range(GROUP)], y_cells, odd(count))
        parts_buf[slot] = split_rows(value, True)

    def y_step(i, slot):
        plus, minus = pair_dot(table_ref[2 * z_cells :, : 3 * y_cells], parts_buf[slot], True)
        for u in range(GROUP):
            start = (GROUP * i + u) * odd(2 * pad_y)
            store(rows_ref, start, lane_block(plus, u))
            store(rows_ref, start + pad_y, lane_block(minus, u))

    pipeline(count // GROUP, [gather_rows, y_step], 2)


def slab_rows(place, blocks, count, dims, tables, name):
    x_cells, y_cells, z_cells = dims
    n_y = y_cells + HALF
    pad_y = n_y // 2 + -(n_y // 2) % 8
    vmem = pl.BlockSpec(memory_space=pltpu.VMEM)
    return pl.pallas_call(
        functools.partial(slab_rows_kernel, dims),
        out_shape=jax.ShapeDtypeStruct((count * odd(2 * pad_y), LANES), F32),
        in_specs=[pl.BlockSpec(memory_space=pltpu.SMEM)] + [vmem] * (1 + len(blocks)),
        out_specs=vmem,
        scratch_shapes=[
            pltpu.VMEM((y_cells * odd(count), LANES), F32),
            pltpu.VMEM((2, 3 * y_cells, GROUP * LANES), BF16),
        ],
        compiler_params=pltpu.CompilerParams(vmem_limit_bytes=9 * 1024 * 1024),
        cost_estimate=pl.CostEstimate(flops=count * 10**8, bytes_accessed=10**6, transcendentals=0),
        name=name,
    )(place, *blocks, tables["slab_rows"])


def slab_x_kernel(
    dims, own_ref, halo_ref, x_ref, valid_ref, tz_ref, spec_ref, mask_ref, z_ref, parts_buf
):
    x_cells, y_cells, z_cells = dims
    n_y = y_cells + HALF
    pad_y = n_y // 2 + -(n_y // 2) % 8

    def gather_rows(i, slot):
        firsts = [GROUP // 2 * i + u // 2 + u % 2 * pad_y for u in range(GROUP)]
        value = jnp.concatenate(
            [
                pick(own_ref, firsts, x_cells, odd(2 * pad_y)),
                pick(halo_ref, firsts, TEMPL, odd(2 * pad_y)),
            ],
            axis=0,
        )
        parts_buf[slot] = split_rows(value, True)

    def x_step(i, slot):
        plus, minus = pair_dot(x_ref[...], parts_buf[slot], True)
        spec = jnp.concatenate([plus, minus], axis=0)
        turned = swap(spec)
        real_lane = lane_sign(GROUP * LANES) < 0
        spec_ref[i, 0] = jnp.where(real_lane, spec, turned)
        spec_ref[i, 1] = jnp.where(real_lane, -turned, spec)

    pipeline(n_y // GROUP, [gather_rows, x_step], 2)

    valid = valid_ref[...].astype(F32)
    low_lane = lax.broadcasted_iota(jnp.int32, (x_cells, LANES), 1) < z_cells
    for q in range(y_cells // 2):
        mask_ref[q] = jnp.where(low_lane, valid[:, 2 * q : 2 * q + 1], valid[:, 2 * q + 1 : 2 * q + 2])
    z_ref[...] = jnp.zeros(z_ref.shape, BF16)
    for j in range(8):
        start = TEMPL * j - (LANES if j >= 4 else 0)
        z_ref[j, start : start + TEMPL, :] = tz_ref[...]


def slab_x(own, halo, valid, dims, tables):
    x_cells, y_cells, z_cells = dims
    n_x, n_y = x_cells + TEMPL, y_cells + HALF
    steps = n_y // GROUP
    vmem = pl.BlockSpec(memory_space=pltpu.VMEM)
    shape = (steps, 2, n_x, GROUP * LANES)
    return pl.pallas_call(
        functools.partial(slab_x_kernel, dims),
        out_shape=(
            jax.ShapeDtypeStruct(shape, F32),
            jax.ShapeDtypeStruct((y_cells // 2, x_cells, LANES), F32),
            jax.ShapeDtypeStruct((8, 2 * LANES, 2 * LANES), BF16),
        ),
        in_specs=[vmem] * 5,
        out_specs=(vmem,) * 3,
        scratch_shapes=[pltpu.VMEM((2, 3 * n_x, GROUP * LANES), BF16)],
        compiler_params=pltpu.CompilerParams(vmem_limit_bytes=6 * 1024 * 1024),
        cost_estimate=pl.CostEstimate(flops=5 * 10**9, bytes_accessed=10**6, transcendentals=0),
        name="slab_x",
    )(own, halo, tables["slab_x"], valid, tables["tmpl_z"])


def corr_kernel(
    dims, rot, entry, place_ref, tile_ref, held_ref, last_ref, mask_ref, spec_ref,
    z_ref, ones_ref, y_ref, x_ref, bx_ref, by_ref, bz_ref,
    mine_ref, side_ref, far_ref, stat_ref,
    bank_buf, depth_buf, rows_buf, first_buf, second_buf, third_buf, back_buf, vol_buf,
):
    x_cells, y_cells, z_cells = dims
    n_x, n_y = x_cells + TEMPL, y_cells + HALF
    half_y = n_y // 2
    pad_y = half_y + -half_y % 8
    for i, block in enumerate(HELD):
        for ref, at, tile in ((held_ref, rot, block), (last_ref, entry, block ^ 1)):
            store(bank_buf, (tile_ref[0] ^ tile) * odd(BLOCK_ROWS), ref[at, i].astype(F32))
    tmpl = jnp.concatenate(
        [
            pick(bank_buf, [a * CHUNKS + i for i in range(CHUNKS)], BLOCKS, odd(BLOCK_ROWS))
            for a in range(EACH)
        ],
        axis=0,
    )
    inv_size = 1.0 / TEMPL**3
    mean = jnp.sum(tmpl) * inv_size
    centred = tmpl - mean
    var = jnp.sum(centred * centred) * inv_size
    scale = 1.0 / (jnp.sqrt(jnp.full((1, LANES), var + EPSILON, F32)) * TEMPL**1.5)
    shift = ones_ref[:1] * mean

    wide = 8 * TEMPL
    narrow = tmpl.astype(BF16)
    block = jnp.concatenate(
        [narrow[:, g * wide : (g + 1) * wide] for g in range(TEMPL // 8)], axis=0
    )
    for j in range(8):
        window = block[:, : 2 * LANES] if j < 4 else block[:, LANES:]
        out = jnp.dot(window, z_ref[j], preferred_element_type=F32)
        part = out[:, :LANES] + out[:, LANES:] - shift
        for g in range(TEMPL // 8):
            start = (8 * g + j) * odd(TEMPL)
            store(depth_buf, start, part[g * TEMPL : (g + 1) * TEMPL])

    def gather_a(i, slot):
        value = pick(depth_buf, [GROUP * i + u for u in range(GROUP)], TEMPL, odd(TEMPL))
        first_buf[slot] = split_rows(value, True)

    def y_step(i, slot):
        plus, minus = pair_dot(y_ref[...], first_buf[slot], True)
        for u in range(GROUP):
            start = (GROUP * i + u) * odd(2 * pad_y)
            store(rows_buf, start, lane_block(plus, u))
            store(rows_buf, start + pad_y, lane_block(minus, u))

    pipeline(TEMPL // GROUP, [gather_a, y_step], 3)

    def gather_ky(i, slot):
        firsts = [GROUP // 2 * i + u // 2 + u % 2 * pad_y for u in range(GROUP)]
        first_buf[slot] = split_rows(pick(rows_buf, firsts, TEMPL, odd(2 * pad_y)), True)

    def multiply(i, slot):
        plus, minus = pair_dot(x_ref[...], first_buf[slot], True)
        spec = jnp.concatenate([plus, minus], axis=0)
        prod = spec * spec_ref[i, 0] + swap(spec) * spec_ref[i, 1]
        second_buf[slot] = split_rows(prod, False)

    def back_x(i, slot):
        plus, minus = pair_dot(bx_ref[...], second_buf[slot], False)
        for u in range(GROUP):
            start = (GROUP * i + u) * odd(x_cells)
            store(back_buf, start, lane_block(plus, u))
            store(back_buf, start + x_cells // 2, lane_block(minus, u))

    pipeline(n_y // GROUP, [gather_ky, multiply, back_x], 4)

    def gather_x(i, slot):
        value = pick(back_buf, [GROUP * i + u for u in range(GROUP)], n_y, odd(x_cells))
        third_buf[slot] = split_rows(value, False)

    def back_y(i, slot):
        plus, minus = pair_dot(by_ref[...], third_buf[slot], False)
        for u in range(GROUP):
            row = GROUP * i + u
            x = jnp.where(row < x_cells // 2, row + x_cells // 2, x_cells - 1 - row)
            store(vol_buf, x * odd(y_cells), lane_block(plus, u))
            store(vol_buf, x * odd(y_cells) + y_cells // 2, lane_block(minus, u))

    pipeline(x_cells // GROUP, [gather_x, back_y], 2)

    share = y_cells // 8
    me = place_ref[0]
    total = jnp.zeros((x_cells, LANES), F32)
    number = jnp.zeros((x_cells, LANES), F32)
    targets = [mine_ref, side_ref, far_ref.at[0], far_ref.at[1]]
    for p, target in enumerate(targets):
        first = (me ^ p) * share
        values = []
        for i in range(share):
            firsts = []
            for j in range(2):
                y = 2 * (first + i) + j
                firsts.append(jnp.where(y < y_cells // 2, y_cells - 1 - y, y - y_cells // 2))
            values.append(pick(vol_buf, firsts, x_cells, odd(y_cells)))
        value = jnp.concatenate(values, axis=0)
        out = jnp.dot(split_rows(value, False), bz_ref[...], preferred_element_type=F32)
        rows = value.shape[0]
        full = out[:rows, :LANES] + out[:rows, LANES:] + out[rows:, :LANES]
        for i in range(share):
            corr = full[i * x_cells : (i + 1) * x_cells] * scale
            target[:, i * LANES : (i + 1) * LANES] = corr
            mask = mask_ref[first + i]
            total = total + corr * mask
            number = number + mask
    number_sum = jnp.sum(number)
    total_sum = jnp.sum(total)
    local_mean = jnp.full((1, LANES), total_sum, F32) / jnp.maximum(number_sum, 1.0)
    square = jnp.zeros((x_cells, LANES), F32)
    for p, target in enumerate(targets):
        first = (me ^ p) * share
        for i in range(share):
            gap = target[:, i * LANES : (i + 1) * LANES] - local_mean
            square = square + gap * gap * mask_ref[first + i]
    row = lax.broadcasted_iota(jnp.int32, (8, LANES), 0)
    stat_ref[...] = jnp.where(row == 0, number_sum, jnp.where(row == 1, total_sum, jnp.sum(square)))


def correlate(place, tile, held, rot, last, entry, mask, spec, tmpl_z, dims, tables):
    x_cells, y_cells, z_cells = dims
    n_x, n_y = x_cells + TEMPL, y_cells + HALF
    pad_y = n_y // 2 + -(n_y // 2) % 8
    width = y_cells * z_cells // 4
    vmem = pl.BlockSpec(memory_space=pltpu.VMEM)
    return pl.pallas_call(
        functools.partial(corr_kernel, dims, rot, entry),
        out_shape=(
            jax.ShapeDtypeStruct((x_cells, width), F32),
            jax.ShapeDtypeStruct((x_cells, width), F32),
            jax.ShapeDtypeStruct((2, x_cells, width), F32),
            jax.ShapeDtypeStruct((8, LANES), F32),
        ),
        in_specs=[pl.BlockSpec(memory_space=pltpu.SMEM)] * 2 + [vmem] * 11,
        out_specs=(vmem,) * 4,
        scratch_shapes=[
            pltpu.VMEM((BLOCKS * odd(BLOCK_ROWS), LANES), F32),
            pltpu.VMEM((TEMPL * odd(TEMPL), LANES), F32),
            pltpu.VMEM((TEMPL * odd(2 * pad_y), LANES), F32),
            pltpu.VMEM((4, 3 * TEMPL, GROUP * LANES), BF16),
            pltpu.VMEM((4, 2 * n_x, GROUP * LANES), BF16),
            pltpu.VMEM((2, 2 * n_y, GROUP * LANES), BF16),
            pltpu.VMEM((n_y * odd(x_cells), LANES), F32),
            pltpu.VMEM((x_cells * odd(y_cells), LANES), F32),
        ],
        compiler_params=pltpu.CompilerParams(vmem_limit_bytes=16 * 1024 * 1024),
        cost_estimate=pl.CostEstimate(flops=15 * 10**9, bytes_accessed=10**7, transcendentals=0),
        name="correlate",
    )(
        place, tile, held, last, mask, spec,
        tmpl_z, tables["ones_z"], tables["tmpl_y"], tables["tmpl_x"],
        tables["back_x"], tables["back_y"], tables["back_z"],
    )


def score_kernel(pieces, own, place_ref, coef_ref, mask_ref, *refs):
    refs, (best_ref, evid_ref, mom_ref, own_buf, sems) = list(refs[:-5]), refs[-5:]
    copies = [pltpu.make_async_copy(refs[i], own_buf.at[i], sems.at[i]) for i in range(own)]
    for copy in copies:
        copy.start()
    for copy in copies:
        copy.wait()
    refs[:own] = [own_buf.at[i] for i in range(own)]
    blocks = best_ref.shape[1] // LANES

    def step(i):
        lanes = pl.ds(pl.multiple_of(i * LANES, LANES), LANES)

        def score(k):
            at, entry = pieces[k]
            corr = refs[at][:, lanes] if entry is None else refs[at][entry, :, lanes]
            return (corr - coef_ref[k, 0]) * coef_ref[k, 1]

        mask = mask_ref[place_ref[0] * blocks + i]
        high = functools.reduce(jnp.maximum, [score(k) for k in range(len(pieces))])
        total = jnp.zeros_like(high)
        moment = [jnp.zeros_like(high) for _ in range(4)]
        for k in range(len(pieces)):
            weight = jnp.exp(score(k) - high)
            total = total + weight
            for c in range(4):
                moment[c] = moment[c] + weight * coef_ref[k, 2 + c]
        best_ref[:, lanes] = mask * high
        evid_ref[:, lanes] = mask * (high + jnp.log(total))
        share = mask / total
        for c in range(4):
            mom_ref[c, :, lanes] = moment[c] * share

    loop(blocks, step)


def combine(place, coefs, mask, arrays, pieces, own):
    shape = arrays[0].shape
    vmem = pl.BlockSpec(memory_space=pltpu.VMEM)
    out = jax.ShapeDtypeStruct(shape, F32)
    return pl.pallas_call(
        functools.partial(score_kernel, pieces, own),
        out_shape=(out, out, jax.ShapeDtypeStruct((4,) + shape, F32)),
        in_specs=[pl.BlockSpec(memory_space=pltpu.SMEM)] * 2
        + [vmem] + [pl.BlockSpec(memory_space=pl.ANY)] * own + [vmem] * (len(arrays) - own),
        out_specs=(vmem,) * 3,
        scratch_shapes=[pltpu.VMEM((own,) + shape, F32), pltpu.SemaphoreType.DMA((own,))],
        compiler_params=pltpu.CompilerParams(vmem_limit_bytes=4 * 1024 * 1024),
        name="combine",
    )(place, coefs, mask, *arrays)


def swap_blocks(block, axis, step):
    return lax.ppermute(block, axis, [(i, i ^ step) for i in range(lax.axis_size(axis))])


def general_gather(templates):
    rots = templates.shape[0]
    count = lax.axis_size("tile")
    block = templates[:, None]
    for step in [1 << i for i in reversed(range(count.bit_length() - 1))]:
        other = swap_blocks(block, "tile", step)
        upper = (lax.axis_index("tile") & step) != 0
        pair = [jnp.where(upper, other, block), jnp.where(upper, block, other)]
        block = jnp.stack(pair, axis=2).reshape((rots, -1) + block.shape[2:])
    block = block.reshape(rots, BLOCKS, EACH * CHUNKS, LANES)
    block = jnp.pad(block, ((0, 0), (0, 0), (0, BLOCK_ROWS - EACH * CHUNKS), (0, 0)))
    held = jnp.stack([block[:, i] for i in HELD], axis=1)
    return held, jnp.stack([block[:, i ^ 1] for i in HELD], axis=1)


def merge(first, other):
    number_a, number_b = first[:1], other[:1]
    mean_a = first[1:2] / jnp.maximum(number_a, 1.0)
    mean_b = other[1:2] / jnp.maximum(number_b, 1.0)
    gap = mean_b - mean_a
    between = gap * gap * (number_a * number_b / jnp.maximum(number_a + number_b, 1.0))
    return first + other + jnp.where(jnp.arange(3)[:, None] == 2, between, 0.0)


def exchange_all(block, axis, low, high):
    count = lax.axis_size(axis)
    parts = [block]
    for step in range(low, high, low):
        parts.append(lax.ppermute(block, axis, [(i, i ^ step) for i in range(count)]))
    return jnp.stack(parts)


def neighbours(block, axis):
    count = lax.axis_size(axis)
    forward = [(i, i + 1) for i in range(count - 1)]
    backward = [(target, source) for source, target in forward]
    return lax.ppermute(block, axis, forward), lax.ppermute(block, axis, backward)


def local(tomogram, templates, valid, quats, rot_index):
    x_cells, voxels = tomogram.shape
    y_cells = valid.shape[1]
    z_cells = voxels // y_cells
    dims = (x_cells, y_cells, z_cells)
    tables = {name: jnp.asarray(table) for name, table in make_tables(*dims).items()}
    groups = lax.axis_size("rot")
    tiles = lax.axis_size("tile")
    me = lax.axis_index("rot")
    rots = templates.shape[0]

    tile = lax.axis_index("tile")
    by_blocks = tiles == BLOCKS
    if by_blocks:
        held = templates.reshape(rots, 1, EACH * CHUNKS, LANES)
        held = jnp.pad(held, ((0, 0), (0, 0), (0, BLOCK_ROWS - EACH * CHUNKS), (0, 0)))
        held, tomogram_after = lax.optimization_barrier((held, tomogram))
        held = jnp.concatenate([held, swap_blocks(held, "tile", 4)], axis=1)
    else:
        tomogram_after = tomogram
    half = x_cells // 2
    piece = lax.dynamic_slice_in_dim(tomogram_after, (me & 1) * half, half, 0)
    mine = jnp.stack(neighbours(piece, "tile"))
    side_swap = [(i, i ^ 1) for i in range(groups)]
    other = lax.ppermute(mine, "rot", side_swap)
    if by_blocks:
        second = swap_blocks(held, "tile", 2)
    else:
        held, last = general_gather(templates)
        tile = jnp.zeros_like(tile)
    one_hot = (rot_index[:, None] == jnp.arange(quats.shape[1], dtype=jnp.int32)[None, :]).astype(F32)
    orient = jnp.einsum("rq,kq->rk", one_hot, quats, precision=lax.Precision.HIGHEST)
    place = me_place = jnp.reshape(me, (1,)).astype(jnp.int32)
    tile = jnp.reshape(tile, (1,)).astype(jnp.int32)
    own = slab_rows(place, [tomogram], x_cells, dims, tables, "slab_own")
    halo = slab_rows(place, [mine, other], TEMPL, dims, tables, "slab_halo")
    if by_blocks:
        second = jnp.where(halo[0, 0] < 1e9, second, jnp.zeros_like(second))
        held = jnp.concatenate([held, second], axis=1)
        lasts = [swap_blocks(held[:1], "tile", 1), swap_blocks(held[1:], "tile", 1)]
    else:
        lasts = [last[:1], last[1:]]
    spec, mask, tmpl_z = slab_x(own, halo, valid, dims, tables)
    far_swap = [(i, i ^ 2) for i in range(groups)]
    mines, sides, fars, stats = [], [], [], []
    for r in range(rots):
        if r >= 2:
            place, fars[r - 2] = lax.optimization_barrier((place, fars[r - 2]))
        mine, side, far, stat = correlate(
            place, tile, held, r, lasts[min(r, 1)], max(r - 1, 0), mask, spec, tmpl_z, dims, tables
        )
        if r >= 1:
            stat, fars[r - 1] = lax.optimization_barrier((stat, fars[r - 1]))
        mines.append(mine)
        sides.append(side)
        stats.append(stat[:3, 0])
        fars.append(lax.ppermute(far, "rot", far_swap))
        if r == rots - 2:
            early = jnp.stack(sides[:-1] + [f[1] for f in fars[:-1]])
            early = lax.ppermute(early, "rot", side_swap)
    state = jnp.stack(stats, axis=1)
    state, early, fars[rots - 2] = lax.optimization_barrier((state, early, fars[rots - 2]))
    step = 1
    while step < tiles:
        partner = lax.ppermute(state, "tile", [(i, i ^ step) for i in range(tiles)])
        if step * 4 == tiles:
            late = jnp.where(partner[0, 0] >= 0.0, fars[rots - 1][1], 0.0)
            last = jnp.stack([sides[rots - 2], sides[rots - 1], fars[rots - 2][1], late])
        if step * 2 == tiles:
            partner, last = lax.optimization_barrier((partner, last))
        state = merge(state, partner)
        step *= 2
    average = state[1] / state[0]
    inverse = 1.0 / jnp.sqrt(state[2] / state[0] + EPSILON)
    coefs = jnp.concatenate([average[:, None], inverse[:, None], orient], axis=1)
    coefs = exchange_all(coefs, "rot", 1, groups)
    last = lax.ppermute(last, "rot", side_swap)
    arrays = mines + fars + [early, last]
    at_far, at_early, at_last = rots, 2 * rots, 2 * rots + 1
    pieces = [(r, None) for r in range(rots)]
    pieces += [(at_early, r) for r in range(rots - 2)] + [(at_last, 0), (at_last, 1)]
    pieces += [(at_far + r, 0) for r in range(rots)]
    pieces += [(at_early, rots - 2 + r) for r in range(rots - 2)] + [(at_last, 2), (at_last, 3)]
    return combine(me_place, coefs.reshape(groups * rots, 6), mask, arrays, pieces, rots)


def solution(mesh):
    placed = (P("tile", None), P("rot", "tile"), P("tile", None), P(), P("rot"))
    return jax.shard_map(
        local,
        mesh=mesh,
        in_specs=placed,
        out_specs=(P("tile", "rot"), P("tile", "rot"), P(None, "tile", "rot")),
        check_vma=False,
    )
```

```python
import functools
import math

import jax
import jax.numpy as jnp
import ml_dtypes
import numpy as np
from jax import lax
from jax.experimental import pallas as pl
from jax.experimental.pallas import tpu as pltpu
from jax.sharding import PartitionSpec as P

TEMPL = 48
HALF = 24
EPSILON = 1e-06
LANES = 128
SPLIT = 64
BLOCKS = 8
EACH = TEMPL // BLOCKS
CHUNKS = TEMPL * TEMPL // LANES
BLOCK_ROWS = EACH * CHUNKS + -EACH * CHUNKS % 16
HELD = (0, 4, 2, 6)
F32 = jnp.float32
BF16 = jnp.bfloat16


def two_parts(table):
    high = table.astype(ml_dtypes.bfloat16)
    low = (table - high.astype(np.float64)).astype(ml_dtypes.bfloat16)
    return high, low


def row_table(out_idx, in_idx, length, sign, factor, wide):
    theta = 2.0 * math.pi / length * np.outer(out_idx, in_idx)
    pad = np.zeros((-len(out_idx) % 8, len(in_idx)))
    full = np.concatenate([np.cos(theta), pad, sign * np.sin(theta), pad], axis=0) * factor
    high, low = two_parts(full)
    if wide:
        return np.concatenate([high, high, low], axis=1)
    zeros = np.zeros_like(low)
    return np.concatenate(
        [np.concatenate([high, high], axis=1), np.concatenate([low, zeros], axis=1)], axis=0
    )


def depth_table(in_idx, length, sign, factor):
    freq = np.arange(length // 2) + 0.5
    theta = 2.0 * math.pi / length * np.outer(in_idx, freq)
    out = np.zeros((len(in_idx), LANES))
    out[:, : length // 2] = np.cos(theta) * factor
    out[:, SPLIT : SPLIT + length // 2] = sign * np.sin(theta) * factor
    return out


def half_odd(count):
    return np.arange(count // 2) + 0.5


def make_tables(x_cells, y_cells, z_cells):
    n_x, n_y, n_z = x_cells + TEMPL, y_cells + HALF, z_cells + HALF
    k_x, k_y = half_odd(n_x), half_odd(n_y)
    both_x = np.concatenate([k_x, -k_x])
    both_y = np.stack([k_y, -k_y], axis=1).reshape(-1)
    mid_x, mid_y = (x_cells - 1) / 2, (y_cells - 1) / 2
    tables = {}
    slab = np.zeros((2 * z_cells, 4 * LANES), ml_dtypes.bfloat16)
    high, low = two_parts(depth_table(np.arange(z_cells), n_z, -1.0, 1.0))
    for j in range(2):
        rows = slice(j * z_cells, (j + 1) * z_cells)
        slab[rows, 2 * j * LANES : (2 * j + 1) * LANES] = high
        slab[rows, (2 * j + 1) * LANES : (2 * j + 2) * LANES] = low
    slab_y = row_table(k_y, np.arange(y_cells), n_y, -1.0, 1.0, True)
    slab_y = np.pad(slab_y, ((0, 0), (0, slab.shape[1] - slab_y.shape[1])))
    tables["slab_rows"] = np.concatenate([slab, slab_y], axis=0)
    own = np.arange(HALF, HALF + x_cells)
    halo = np.concatenate([np.arange(HALF), np.arange(HALF + x_cells, n_x)])
    tables["slab_x"] = row_table(k_x, np.concatenate([own, halo]), n_x, -1.0, 1.0, True)
    high, low = two_parts(depth_table(np.arange(TEMPL) - HALF, n_z, 1.0, 1.0))
    tables["tmpl_z"] = np.concatenate([high, low], axis=1)
    ones = (high.astype(np.float64) + low.astype(np.float64)).sum(axis=0)
    tables["ones_z"] = np.broadcast_to(ones.astype(np.float32)[None], (8, LANES)).copy()
    tables["tmpl_y"] = row_table(k_y, np.arange(TEMPL) - HALF + mid_y, n_y, 1.0, 1.0, True)
    tmpl_rows = np.arange(TEMPL).reshape(BLOCKS, EACH).T.reshape(-1)
    tables["tmpl_x"] = row_table(k_x, tmpl_rows + mid_x, n_x, 1.0, 1.0, True)
    tables["back_x"] = row_table(half_odd(x_cells), both_x, n_x, 1.0, 1.0 / n_x, False)
    tables["back_y"] = row_table(half_odd(y_cells), both_y, n_y, 1.0, 1.0 / n_y, False)
    back = depth_table(np.arange(z_cells), n_z, -1.0, 2.0 / n_z).T
    high, low = two_parts(back)
    back_z = np.zeros((2 * LANES, 2 * LANES), ml_dtypes.bfloat16)
    for j in range(2):
        rows = slice(j * LANES, (j + 1) * LANES)
        back_z[rows, j * z_cells : (j + 1) * z_cells] = high
        back_z[rows, LANES + j * z_cells : LANES + (j + 1) * z_cells] = low
    tables["back_z"] = back_z
    return tables


def split_rows(value, wide):
    high = value.astype(BF16)
    if value.shape[0] % 16 == 0:
        low = (value - high.astype(F32)).astype(BF16)
        return jnp.concatenate([high, low, high] if wide else [high, low], axis=0)
    high = high.astype(F32)
    low = value - high
    return jnp.concatenate([high, low, high] if wide else [high, low], axis=0).astype(BF16)


def swap(value):
    parts = [
        pltpu.roll(value[:, s : s + LANES], SPLIT, 1) for s in range(0, value.shape[1], LANES)
    ]
    return jnp.concatenate(parts, axis=1)


def lane_sign(width):
    lane = lax.broadcasted_iota(jnp.int32, (8, width), 1) % LANES
    return jnp.where(lane < SPLIT, -1.0, 1.0)[:1]


def pair_rows(table, value, wide):
    return pair_dot(table, split_rows(value, wide), wide)


def pair_dot(table, parts, wide):
    out = jnp.dot(table, parts, preferred_element_type=F32)
    if not wide:
        half = out.shape[0] // 2
        out = out[:half] + out[half:]
    half = out.shape[0] // 2
    turned = swap(out[half:]) * lane_sign(out.shape[1])
    return out[:half] + turned, out[:half] - turned


def pick(ref, firsts, count, stride):
    return jnp.concatenate([ref[pl.ds(f, count, stride=stride), :] for f in firsts], axis=1)


def store(ref, start, value):
    ref[pl.ds(start, value.shape[0]), :] = value


def odd(rows):
    return rows + 1


def lane_block(value, i):
    return value[:, i * LANES : (i + 1) * LANES]


def loop(count, body):
    def one(i, carry):
        body(i)
        return carry

    lax.fori_loop(0, count, one, 0)


GROUP = 8


def pipeline(steps, stages, width):
    blocks = -(-steps // width)
    depth = len(stages)

    def turn(t, static):
        for s in reversed(range(depth)):
            if static and not 0 <= t - s < blocks:
                continue
            for slot in range(width):
                step = (t - s) * width + slot
                if not static or step < steps:
                    stages[s](step, slot)

    full = steps // width
    first, last = depth - 1, max(full, depth - 1)
    for t in range(first):
        turn(t, True)
    if last - first >= 2:
        loop(last - first, lambda i: turn(i + first, False))
    else:
        last = first
    for t in range(last, blocks + depth - 1):
        turn(t, True)


def slab_rows_kernel(dims, place_ref, *refs):
    *sources, table_ref, rows_ref, depth_buf, parts_buf = refs
    x_cells, y_cells, z_cells = dims
    base = 0
    if len(sources) > 1:
        own_ref, *sources = sources
        base = own_ref.shape[0]
        rows_ref[:base, :] = own_ref[...]
    half = x_cells // 2
    count = depth_buf.shape[0] // y_cells - 1
    n_y = y_cells + HALF
    pad_y = n_y // 2 + -(n_y // 2) % 8
    many = 4

    def read(lanes):
        if len(sources) == 1:
            return sources[0][:, lanes].astype(F32)
        first = (place_ref[0] & 1) == 0
        mine, other = ([ref[i, :, lanes].astype(F32) for i in range(2)] for ref in sources)
        low, high = (
            jnp.concatenate([jnp.where(first, m, o), jnp.where(first, o, m)], axis=0)
            for m, o in zip(mine, other)
        )
        return jnp.concatenate([low[x_cells - HALF :], high[:HALF]], axis=0)

    def depth_step(i):
        lanes = [pl.ds(pl.multiple_of((many * i + u) * LANES, LANES), LANES) for u in range(many)]
        block = jnp.concatenate([read(l) for l in lanes], axis=0).astype(BF16)
        out = jnp.dot(block, table_ref[: 2 * z_cells], preferred_element_type=F32)
        for u in range(many):
            part = out[u * count : (u + 1) * count]
            for j in range(2):
                store(
                    depth_buf, (2 * many * i + 2 * u + j) * odd(count),
                    lane_block(part, 2 * j) + lane_block(part, 2 * j + 1),
                )

    loop(y_cells // (2 * many), depth_step)

    def gather_rows(i, slot):
        value = pick(depth_buf, [GROUP * i + u for u in range(GROUP)], y_cells, odd(count))
        parts_buf[slot] = split_rows(value, True)

    def y_step(i, slot):
        plus, minus = pair_dot(table_ref[2 * z_cells :, : 3 * y_cells], parts_buf[slot], True)
        for u in range(GROUP):
            start = base + (GROUP * i + u) * odd(2 * pad_y)
            store(rows_ref, start, lane_block(plus, u))
            store(rows_ref, start + pad_y, lane_block(minus, u))

    pipeline(count // GROUP, [gather_rows, y_step], 3)


def slab_rows(place, blocks, count, passed, dims, tables, name):
    x_cells, y_cells, z_cells = dims
    n_y = y_cells + HALF
    pad_y = n_y // 2 + -(n_y // 2) % 8
    vmem = pl.BlockSpec(memory_space=pltpu.VMEM)
    return pl.pallas_call(
        functools.partial(slab_rows_kernel, dims),
        out_shape=jax.ShapeDtypeStruct(((passed + count) * odd(2 * pad_y), LANES), F32),
        in_specs=[pl.BlockSpec(memory_space=pltpu.SMEM)] + [vmem] * (1 + len(blocks)),
        out_specs=vmem,
        scratch_shapes=[
            pltpu.VMEM((y_cells * odd(count), LANES), F32),
            pltpu.VMEM((3, 3 * y_cells, GROUP * LANES), BF16),
        ],
        compiler_params=pltpu.CompilerParams(vmem_limit_bytes=12 * 1024 * 1024),
        cost_estimate=pl.CostEstimate(flops=count * 10**8, bytes_accessed=10**6, transcendentals=0),
        name=name,
    )(place, *blocks, tables["slab_rows"])


def slab_x_kernel(
    dims, rows_ref, x_ref, valid_ref, tz_ref, spec_ref, mask_ref, z_ref, parts_buf
):
    x_cells, y_cells, z_cells = dims
    n_y = y_cells + HALF
    pad_y = n_y // 2 + -(n_y // 2) % 8

    def gather_rows(i, slot):
        firsts = [GROUP // 2 * i + u // 2 + u % 2 * pad_y for u in range(GROUP)]
        value = pick(rows_ref, firsts, x_cells + TEMPL, odd(2 * pad_y))
        parts_buf[slot] = split_rows(value, True)

    def x_step(i, slot):
        plus, minus = pair_dot(x_ref[...], parts_buf[slot], True)
        spec = jnp.concatenate([plus, minus], axis=0)
        turned = swap(spec)
        real_lane = lane_sign(GROUP * LANES) < 0
        spec_ref[i, 0] = jnp.where(real_lane, spec, turned)
        spec_ref[i, 1] = jnp.where(real_lane, -turned, spec)

    pipeline(n_y // GROUP, [gather_rows, x_step], 4)

    valid = valid_ref[...].astype(F32)
    low_lane = lax.broadcasted_iota(jnp.int32, (x_cells, LANES), 1) < z_cells
    for q in range(y_cells // 2):
        mask_ref[q] = jnp.where(low_lane, valid[:, 2 * q : 2 * q + 1], valid[:, 2 * q + 1 : 2 * q + 2])
    z_ref[...] = jnp.zeros(z_ref.shape, BF16)
    for j in range(8):
        start = TEMPL * j - (LANES if j >= 4 else 0)
        z_ref[j, start : start + TEMPL, :] = tz_ref[...]


def slab_x(rows, valid, dims, tables):
    x_cells, y_cells, z_cells = dims
    n_x, n_y = x_cells + TEMPL, y_cells + HALF
    steps = n_y // GROUP
    vmem = pl.BlockSpec(memory_space=pltpu.VMEM)
    shape = (steps, 2, n_x, GROUP * LANES)
    return pl.pallas_call(
        functools.partial(slab_x_kernel, dims),
        out_shape=(
            jax.ShapeDtypeStruct(shape, F32),
            jax.ShapeDtypeStruct((y_cells // 2, x_cells, LANES), F32),
            jax.ShapeDtypeStruct((8, 2 * LANES, 2 * LANES), BF16),
        ),
        in_specs=[vmem] * 4,
        out_specs=(vmem,) * 3,
        scratch_shapes=[pltpu.VMEM((4, 3 * n_x, GROUP * LANES), BF16)],
        compiler_params=pltpu.CompilerParams(vmem_limit_bytes=9 * 1024 * 1024),
        cost_estimate=pl.CostEstimate(flops=5 * 10**9, bytes_accessed=10**6, transcendentals=0),
        name="slab_x",
    )(rows, tables["slab_x"], valid, tables["tmpl_z"])


def corr_kernel(
    dims, rot, entry, place_ref, tile_ref, *refs
):
    if rot > 0:
        before_ref, *refs = refs
    held_ref, last_ref, mask_ref, spec_ref, z_ref, ones_ref, y_ref, x_ref, bx_ref, by_ref, bz_ref, *refs = refs
    mines_ref, side_ref, far_ref, stat_ref, *refs = refs
    bank_buf, depth_buf, rows_buf, first_buf, second_buf, third_buf, back_buf, vol_buf = refs
    if rot > 0:
        mines_ref[:rot] = before_ref[...]
    x_cells, y_cells, z_cells = dims
    n_x, n_y = x_cells + TEMPL, y_cells + HALF
    half_y = n_y // 2
    pad_y = half_y + -half_y % 8
    for i, block in enumerate(HELD):
        for ref, at, tile in ((held_ref, rot, block), (last_ref, entry, block ^ 1)):
            store(bank_buf, (tile_ref[0] ^ tile) * odd(BLOCK_ROWS), ref[at, i].astype(F32))
    tmpl = jnp.concatenate(
        [
            pick(bank_buf, [a * CHUNKS + i for i in range(CHUNKS)], BLOCKS, odd(BLOCK_ROWS))
            for a in range(EACH)
        ],
        axis=0,
    )
    inv_size = 1.0 / TEMPL**3
    mean = jnp.sum(tmpl) * inv_size
    centred = tmpl - mean
    var = jnp.sum(centred * centred) * inv_size
    scale = 1.0 / (jnp.sqrt(jnp.full((1, LANES), var + EPSILON, F32)) * TEMPL**1.5)
    shift = ones_ref[:1] * mean

    wide = 8 * TEMPL
    narrow = tmpl.astype(BF16)
    block = jnp.concatenate(
        [narrow[:, g * wide : (g + 1) * wide] for g in range(TEMPL // 8)], axis=0
    )
    for j in range(8):
        window = block[:, : 2 * LANES] if j < 4 else block[:, LANES:]
        out = jnp.dot(window, z_ref[j], preferred_element_type=F32)
        part = out[:, :LANES] + out[:, LANES:] - shift
        for g in range(TEMPL // 8):
            start = (8 * g + j) * odd(TEMPL)
            store(depth_buf, start, part[g * TEMPL : (g + 1) * TEMPL])

    def gather_a(i, slot):
        value = pick(depth_buf, [GROUP * i + u for u in range(GROUP)], TEMPL, odd(TEMPL))
        first_buf[slot] = split_rows(value, True)

    def y_step(i, slot):
        plus, minus = pair_dot(y_ref[...], first_buf[slot], True)
        for u in range(GROUP):
            start = (GROUP * i + u) * odd(2 * pad_y)
            store(rows_buf, start, lane_block(plus, u))
            store(rows_buf, start + pad_y, lane_block(minus, u))

    pipeline(TEMPL // GROUP, [gather_a, y_step], 6)

    def gather_ky(i, slot):
        firsts = [GROUP // 2 * i + u // 2 + u % 2 * pad_y for u in range(GROUP)]
        first_buf[slot] = split_rows(pick(rows_buf, firsts, TEMPL, odd(2 * pad_y)), True)

    def multiply(i, slot):
        plus, minus = pair_dot(x_ref[...], first_buf[slot], True)
        spec = jnp.concatenate([plus, minus], axis=0)
        prod = spec * spec_ref[i, 0] + swap(spec) * spec_ref[i, 1]
        second_buf[slot] = split_rows(prod, False)

    def back_x(i, slot):
        plus, minus = pair_dot(bx_ref[...], second_buf[slot], False)
        for u in range(GROUP):
            start = (GROUP * i + u) * odd(x_cells)
            store(back_buf, start, lane_block(plus, u))
            store(back_buf, start + x_cells // 2, lane_block(minus, u))

    pipeline(n_y // GROUP, [gather_ky, multiply, back_x], 4)

    def gather_x(i, slot):
        value = pick(back_buf, [GROUP * i + u for u in range(GROUP)], n_y, odd(x_cells))
        third_buf[slot] = split_rows(value, False)

    def back_y(i, slot):
        plus, minus = pair_dot(by_ref[...], third_buf[slot], False)
        for u in range(GROUP):
            row = GROUP * i + u
            x = jnp.where(row < x_cells // 2, row + x_cells // 2, x_cells - 1 - row)
            store(vol_buf, x * odd(y_cells), lane_block(plus, u))
            store(vol_buf, x * odd(y_cells) + y_cells // 2, lane_block(minus, u))

    pipeline(x_cells // GROUP, [gather_x, back_y], 4)

    share = y_cells // 8
    me = place_ref[0]
    total = jnp.zeros((x_cells, LANES), F32)
    number = jnp.zeros((x_cells, LANES), F32)
    targets = [mines_ref.at[rot], side_ref, far_ref.at[0], far_ref.at[1]]
    for p, target in enumerate(targets):
        first = (me ^ p) * share
        values = []
        for i in range(share):
            firsts = []
            for j in range(2):
                y = 2 * (first + i) + j
                firsts.append(jnp.where(y < y_cells // 2, y_cells - 1 - y, y - y_cells // 2))
            values.append(pick(vol_buf, firsts, x_cells, odd(y_cells)))
        value = jnp.concatenate(values, axis=0)
        out = jnp.dot(split_rows(value, False), bz_ref[...], preferred_element_type=F32)
        rows = value.shape[0]
        full = out[:rows, :LANES] + out[:rows, LANES:] + out[rows:, :LANES]
        for i in range(share):
            corr = full[i * x_cells : (i + 1) * x_cells] * scale
            target[:, i * LANES : (i + 1) * LANES] = corr
            mask = mask_ref[first + i]
            total = total + corr * mask
            number = number + mask
    number_sum = jnp.sum(number)
    total_sum = jnp.sum(total)
    local_mean = jnp.full((1, LANES), total_sum, F32) / jnp.maximum(number_sum, 1.0)
    square = jnp.zeros((x_cells, LANES), F32)
    for p, target in enumerate(targets):
        first = (me ^ p) * share
        for i in range(share):
            gap = target[:, i * LANES : (i + 1) * LANES] - local_mean
            square = square + gap * gap * mask_ref[first + i]
    row = lax.broadcasted_iota(jnp.int32, (8, LANES), 0)
    stat_ref[...] = jnp.where(row == 0, number_sum, jnp.where(row == 1, total_sum, jnp.sum(square)))


def correlate(mines, place, tile, held, rot, last, entry, mask, spec, tmpl_z, dims, tables):
    x_cells, y_cells, z_cells = dims
    n_x, n_y = x_cells + TEMPL, y_cells + HALF
    pad_y = n_y // 2 + -(n_y // 2) % 8
    width = y_cells * z_cells // 4
    before = [] if mines is None else [mines]
    vmem = pl.BlockSpec(memory_space=pltpu.VMEM)
    return pl.pallas_call(
        functools.partial(corr_kernel, dims, rot, entry),
        out_shape=(
            jax.ShapeDtypeStruct((rot + 1, x_cells, width), F32),
            jax.ShapeDtypeStruct((x_cells, width), F32),
            jax.ShapeDtypeStruct((2, x_cells, width), F32),
            jax.ShapeDtypeStruct((8, LANES), F32),
        ),
        in_specs=[pl.BlockSpec(memory_space=pltpu.SMEM)] * 2 + [vmem] * (11 + len(before)),
        out_specs=(vmem,) * 4,
        scratch_shapes=[
            pltpu.VMEM((BLOCKS * odd(BLOCK_ROWS), LANES), F32),
            pltpu.VMEM((TEMPL * odd(TEMPL), LANES), F32),
            pltpu.VMEM((TEMPL * odd(2 * pad_y), LANES), F32),
            pltpu.VMEM((6, 3 * TEMPL, GROUP * LANES), BF16),
            pltpu.VMEM((4, 2 * n_x, GROUP * LANES), BF16),
            pltpu.VMEM((4, 2 * n_y, GROUP * LANES), BF16),
            pltpu.VMEM((n_y * odd(x_cells), LANES), F32),
            pltpu.VMEM((x_cells * odd(y_cells), LANES), F32),
        ],
        compiler_params=pltpu.CompilerParams(vmem_limit_bytes=20 * 1024 * 1024),
        cost_estimate=pl.CostEstimate(flops=15 * 10**9, bytes_accessed=10**7, transcendentals=0),
        name="correlate",
    )(
        place, tile, *before, held, last, mask, spec,
        tmpl_z, tables["ones_z"], tables["tmpl_y"], tables["tmpl_x"],
        tables["back_x"], tables["back_y"], tables["back_z"],
    )


def score_kernel(pieces, place_ref, coef_ref, mask_ref, *refs):
    best_ref, evid_ref, mom_ref = refs[-3:]
    blocks = best_ref.shape[1] // LANES

    def step(i):
        lanes = pl.ds(pl.multiple_of(i * LANES, LANES), LANES)

        def score(k):
            at, entry = pieces[k]
            return (refs[at][entry, :, lanes] - coef_ref[k, 0]) * coef_ref[k, 1]

        mask = mask_ref[place_ref[0] * blocks + i]
        high = functools.reduce(jnp.maximum, [score(k) for k in range(len(pieces))])
        total = jnp.zeros_like(high)
        moment = [jnp.zeros_like(high) for _ in range(4)]
        for k in range(len(pieces)):
            weight = jnp.exp(score(k) - high)
            total = total + weight
            for c in range(4):
                moment[c] = moment[c] + weight * coef_ref[k, 2 + c]
        best_ref[:, lanes] = mask * high
        evid_ref[:, lanes] = mask * (high + jnp.log(total))
        share = mask / total
        for c in range(4):
            mom_ref[c, :, lanes] = moment[c] * share

    loop(blocks, step)


def combine(place, coefs, mask, arrays, pieces):
    shape = arrays[0].shape[1:]
    vmem = pl.BlockSpec(memory_space=pltpu.VMEM)
    out = jax.ShapeDtypeStruct(shape, F32)
    return pl.pallas_call(
        functools.partial(score_kernel, pieces),
        out_shape=(out, out, jax.ShapeDtypeStruct((4,) + shape, F32)),
        in_specs=[pl.BlockSpec(memory_space=pltpu.SMEM)] * 2 + [vmem] * (1 + len(arrays)),
        out_specs=(vmem,) * 3,
        compiler_params=pltpu.CompilerParams(vmem_limit_bytes=4 * 1024 * 1024),
        name="combine",
    )(place, coefs, mask, *arrays)


def swap_blocks(block, axis, step):
    return lax.ppermute(block, axis, [(i, i ^ step) for i in range(lax.axis_size(axis))])


def general_gather(templates):
    rots = templates.shape[0]
    count = lax.axis_size("tile")
    block = templates[:, None]
    for step in [1 << i for i in reversed(range(count.bit_length() - 1))]:
        other = swap_blocks(block, "tile", step)
        upper = (lax.axis_index("tile") & step) != 0
        pair = [jnp.where(upper, other, block), jnp.where(upper, block, other)]
        block = jnp.stack(pair, axis=2).reshape((rots, -1) + block.shape[2:])
    block = block.reshape(rots, BLOCKS, EACH * CHUNKS, LANES)
    block = jnp.pad(block, ((0, 0), (0, 0), (0, BLOCK_ROWS - EACH * CHUNKS), (0, 0)))
    held = jnp.stack([block[:, i] for i in HELD], axis=1)
    return held, jnp.stack([block[:, i ^ 1] for i in HELD], axis=1)


def merge(first, other):
    number_a, number_b = first[:1], other[:1]
    mean_a = first[1:2] / jnp.maximum(number_a, 1.0)
    mean_b = other[1:2] / jnp.maximum(number_b, 1.0)
    gap = mean_b - mean_a
    between = gap * gap * (number_a * number_b / jnp.maximum(number_a + number_b, 1.0))
    return first + other + jnp.where(jnp.arange(3)[:, None] == 2, between, 0.0)


def exchange_all(block, axis, low, high):
    count = lax.axis_size(axis)
    parts = [block]
    for step in range(low, high, low):
        parts.append(lax.ppermute(block, axis, [(i, i ^ step) for i in range(count)]))
    return jnp.stack(parts)


def neighbours(block, axis):
    count = lax.axis_size(axis)
    forward = [(i, i + 1) for i in range(count - 1)]
    backward = [(target, source) for source, target in forward]
    return lax.ppermute(block, axis, forward), lax.ppermute(block, axis, backward)


def local(tomogram, templates, valid, quats, rot_index):
    x_cells, voxels = tomogram.shape
    y_cells = valid.shape[1]
    z_cells = voxels // y_cells
    dims = (x_cells, y_cells, z_cells)
    tables = {name: jnp.asarray(table) for name, table in make_tables(*dims).items()}
    groups = lax.axis_size("rot")
    tiles = lax.axis_size("tile")
    me = lax.axis_index("rot")
    rots = templates.shape[0]

    tile = lax.axis_index("tile")
    by_blocks = tiles == BLOCKS
    if by_blocks:
        held = templates.reshape(rots, 1, EACH * CHUNKS, LANES)
        held = jnp.pad(held, ((0, 0), (0, 0), (0, BLOCK_ROWS - EACH * CHUNKS), (0, 0)))
        held, tomogram_after = lax.optimization_barrier((held, tomogram))
        held = jnp.concatenate([held, swap_blocks(held, "tile", 4)], axis=1)
    else:
        tomogram_after = tomogram
    half = x_cells // 2
    piece = lax.dynamic_slice_in_dim(tomogram_after, (me & 1) * half, half, 0)
    mine = jnp.stack(neighbours(piece, "tile"))
    side_swap = [(i, i ^ 1) for i in range(groups)]
    other = lax.ppermute(mine, "rot", side_swap)
    if by_blocks:
        second = swap_blocks(held, "tile", 2)
    else:
        held, last = general_gather(templates)
        tile = jnp.zeros_like(tile)
    one_hot = (rot_index[:, None] == jnp.arange(quats.shape[1], dtype=jnp.int32)[None, :]).astype(F32)
    orient = jnp.einsum("rq,kq->rk", one_hot, quats, precision=lax.Precision.HIGHEST)
    place = me_place = jnp.reshape(me, (1,)).astype(jnp.int32)
    tile = jnp.reshape(tile, (1,)).astype(jnp.int32)
    own = slab_rows(place, [tomogram], x_cells, 0, dims, tables, "slab_own")
    rows = slab_rows(place, [own, mine, other], TEMPL, x_cells, dims, tables, "slab_halo")
    if by_blocks:
        second = jnp.where(rows[0, 0] < 1e9, second, jnp.zeros_like(second))
        held = jnp.concatenate([held, second], axis=1)
        lasts = [swap_blocks(held[:1], "tile", 1), swap_blocks(held[1:], "tile", 1)]
    else:
        lasts = [last[:1], last[1:]]
    spec, mask, tmpl_z = slab_x(rows, valid, dims, tables)
    far_swap = [(i, i ^ 2) for i in range(groups)]
    mines, sides, fars, stats = None, [], [], []
    for r in range(rots):
        if r >= 2:
            place, fars[r - 2] = lax.optimization_barrier((place, fars[r - 2]))
        mines, side, far, stat = correlate(
            mines, place, tile, held, r, lasts[min(r, 1)], max(r - 1, 0), mask, spec, tmpl_z, dims, tables
        )
        if r >= 1:
            stat, fars[r - 1] = lax.optimization_barrier((stat, fars[r - 1]))
        sides.append(side)
        stats.append(stat[:3, 0])
        fars.append(lax.ppermute(far, "rot", far_swap))
        if r == rots - 2:
            early = jnp.stack(sides[:-1] + [f[1] for f in fars[:-1]])
            early = lax.ppermute(early, "rot", side_swap)
    state = jnp.stack(stats, axis=1)
    state, early, fars[rots - 2] = lax.optimization_barrier((state, early, fars[rots - 2]))
    step = 1
    while step < tiles:
        partner = lax.ppermute(state, "tile", [(i, i ^ step) for i in range(tiles)])
        if step * 4 == tiles:
            late = jnp.where(partner[0, 0] >= 0.0, fars[rots - 1][1], 0.0)
            last = jnp.stack([sides[rots - 2], sides[rots - 1], fars[rots - 2][1], late])
        if step * 2 == tiles:
            partner, last = lax.optimization_barrier((partner, last))
        state = merge(state, partner)
        step *= 2
    average = state[1] / state[0]
    inverse = 1.0 / jnp.sqrt(state[2] / state[0] + EPSILON)
    coefs = jnp.concatenate([average[:, None], inverse[:, None], orient], axis=1)
    coefs = exchange_all(coefs, "rot", 1, groups)
    last = lax.ppermute(last, "rot", side_swap)
    arrays = [mines] + fars + [early, last]
    at_far, at_early, at_last = 1, 1 + rots, 2 + rots
    pieces = [(0, r) for r in range(rots)]
    pieces += [(at_early, r) for r in range(rots - 2)] + [(at_last, 0), (at_last, 1)]
    pieces += [(at_far + r, 0) for r in range(rots)]
    pieces += [(at_early, rots - 2 + r) for r in range(rots - 2)] + [(at_last, 2), (at_last, 3)]
    return combine(me_place, coefs.reshape(groups * rots, 6), mask, arrays, pieces)


def solution(mesh):
    placed = (P("tile", None), P("rot", "tile"), P("tile", None), P(), P("rot"))
    return jax.shard_map(
        local,
        mesh=mesh,
        in_specs=placed,
        out_specs=(P("tile", "rot"), P("tile", "rot"), P(None, "tile", "rot")),
        check_vma=False,
    )
```

```python
import functools
import math

import jax
import jax.numpy as jnp
import ml_dtypes
import numpy as np
from jax import lax
from jax.experimental import pallas as pl
from jax.experimental.pallas import tpu as pltpu
from jax.sharding import PartitionSpec as P

TEMPL = 48
HALF = 24
EPSILON = 1e-06
LANES = 128
SPLIT = 64
BLOCKS = 8
EACH = TEMPL // BLOCKS
CHUNKS = TEMPL * TEMPL // LANES
BLOCK_ROWS = EACH * CHUNKS + -EACH * CHUNKS % 16
HELD = (0, 4, 2, 6)
F32 = jnp.float32
BF16 = jnp.bfloat16


def two_parts(table):
    high = table.astype(ml_dtypes.bfloat16)
    low = (table - high.astype(np.float64)).astype(ml_dtypes.bfloat16)
    return high, low


def row_table(out_idx, in_idx, length, sign, factor, wide):
    theta = 2.0 * math.pi / length * np.outer(out_idx, in_idx)
    pad = np.zeros((-len(out_idx) % 8, len(in_idx)))
    full = np.concatenate([np.cos(theta), pad, sign * np.sin(theta), pad], axis=0) * factor
    high, low = two_parts(full)
    if wide:
        return np.concatenate([high, high, low], axis=1)
    zeros = np.zeros_like(low)
    return np.concatenate(
        [np.concatenate([high, high], axis=1), np.concatenate([low, zeros], axis=1)], axis=0
    )


def depth_table(in_idx, length, sign, factor):
    freq = np.arange(length // 2) + 0.5
    theta = 2.0 * math.pi / length * np.outer(in_idx, freq)
    out = np.zeros((len(in_idx), LANES))
    out[:, : length // 2] = np.cos(theta) * factor
    out[:, SPLIT : SPLIT + length // 2] = sign * np.sin(theta) * factor
    return out


def half_odd(count):
    return np.arange(count // 2) + 0.5


def make_tables(x_cells, y_cells, z_cells):
    n_x, n_y, n_z = x_cells + TEMPL, y_cells + HALF, z_cells + HALF
    k_x, k_y = half_odd(n_x), half_odd(n_y)
    both_x = np.concatenate([k_x, -k_x])
    both_y = np.stack([k_y, -k_y], axis=1).reshape(-1)
    mid_x, mid_y = (x_cells - 1) / 2, (y_cells - 1) / 2
    tables = {}
    slab = np.zeros((2 * z_cells, 4 * LANES), ml_dtypes.bfloat16)
    high, low = two_parts(depth_table(np.arange(z_cells), n_z, -1.0, 1.0))
    for j in range(2):
        rows = slice(j * z_cells, (j + 1) * z_cells)
        slab[rows, 2 * j * LANES : (2 * j + 1) * LANES] = high
        slab[rows, (2 * j + 1) * LANES : (2 * j + 2) * LANES] = low
    slab_y = row_table(k_y, np.arange(y_cells), n_y, -1.0, 1.0, True)
    slab_y = np.pad(slab_y, ((0, 0), (0, slab.shape[1] - slab_y.shape[1])))
    tables["slab_rows"] = np.concatenate([slab, slab_y], axis=0)
    own = np.arange(HALF, HALF + x_cells)
    halo = np.concatenate([np.arange(HALF), np.arange(HALF + x_cells, n_x)])
    tables["slab_x"] = row_table(k_x, np.concatenate([own, halo]), n_x, -1.0, 1.0, True)
    high, low = two_parts(depth_table(np.arange(TEMPL) - HALF, n_z, 1.0, 1.0))
    tables["tmpl_z"] = np.concatenate([high, low], axis=1)
    ones = (high.astype(np.float64) + low.astype(np.float64)).sum(axis=0)
    tables["ones_z"] = np.broadcast_to(ones.astype(np.float32)[None], (8, LANES)).copy()
    tables["tmpl_y"] = row_table(k_y, np.arange(TEMPL) - HALF + mid_y, n_y, 1.0, 1.0, True)
    tmpl_rows = np.arange(TEMPL).reshape(BLOCKS, EACH).T.reshape(-1)
    tables["tmpl_x"] = row_table(k_x, tmpl_rows + mid_x, n_x, 1.0, 1.0, True)
    tables["back_x"] = row_table(half_odd(x_cells), both_x, n_x, 1.0, 1.0 / n_x, False)
    tables["back_y"] = row_table(half_odd(y_cells), both_y, n_y, 1.0, 1.0 / n_y, False)
    back = depth_table(np.arange(z_cells), n_z, -1.0, 2.0 / n_z).T
    high, low = two_parts(back)
    back_z = np.zeros((2 * LANES, 2 * LANES), ml_dtypes.bfloat16)
    for j in range(2):
        rows = slice(j * LANES, (j + 1) * LANES)
        back_z[rows, j * z_cells : (j + 1) * z_cells] = high
        back_z[rows, LANES + j * z_cells : LANES + (j + 1) * z_cells] = low
    tables["back_z"] = back_z
    return tables


def split_rows(value, wide):
    high = value.astype(BF16)
    if value.shape[0] % 16 == 0:
        low = (value - high.astype(F32)).astype(BF16)
        return jnp.concatenate([high, low, high] if wide else [high, low], axis=0)
    high = high.astype(F32)
    low = value - high
    return jnp.concatenate([high, low, high] if wide else [high, low], axis=0).astype(BF16)


def swap(value):
    parts = [
        pltpu.roll(value[:, s : s + LANES], SPLIT, 1) for s in range(0, value.shape[1], LANES)
    ]
    return jnp.concatenate(parts, axis=1)


def lane_sign(width):
    lane = lax.broadcasted_iota(jnp.int32, (8, width), 1) % LANES
    return jnp.where(lane < SPLIT, -1.0, 1.0)[:1]


def pair_rows(table, value, wide):
    return pair_dot(table, split_rows(value, wide), wide)


def pair_dot(table, parts, wide):
    out = jnp.dot(table, parts, preferred_element_type=F32)
    if not wide:
        half = out.shape[0] // 2
        out = out[:half] + out[half:]
    half = out.shape[0] // 2
    turned = swap(out[half:]) * lane_sign(out.shape[1])
    return out[:half] + turned, out[:half] - turned


def pick(ref, firsts, count, stride):
    return jnp.concatenate([ref[pl.ds(f, count, stride=stride), :] for f in firsts], axis=1)


def store(ref, start, value):
    ref[pl.ds(start, value.shape[0]), :] = value


def odd(rows):
    return rows + 1


def lane_block(value, i):
    return value[:, i * LANES : (i + 1) * LANES]


def loop(count, body):
    def one(i, carry):
        body(i)
        return carry

    lax.fori_loop(0, count, one, 0)


GROUP = 8


def pipeline(steps, stages, width):
    blocks = -(-steps // width)
    depth = len(stages)

    def turn(t, static):
        for s in reversed(range(depth)):
            if static and not 0 <= t - s < blocks:
                continue
            for slot in range(width):
                step = (t - s) * width + slot
                if not static or step < steps:
                    stages[s](step, slot)

    full = steps // width
    first, last = depth - 1, max(full, depth - 1)
    for t in range(first):
        turn(t, True)
    if last - first >= 2:
        loop(last - first, lambda i: turn(i + first, False))
    else:
        last = first
    for t in range(last, blocks + depth - 1):
        turn(t, True)


def slab_rows_kernel(dims, place_ref, *refs):
    *sources, table_ref, rows_ref, depth_buf, parts_buf = refs
    x_cells, y_cells, z_cells = dims
    base = 0
    if len(sources) > 1:
        own_ref, *sources = sources
        base = own_ref.shape[0]
        rows_ref[:base, :] = own_ref[...]
    half = x_cells // 2
    count = depth_buf.shape[0] // y_cells - 1
    n_y = y_cells + HALF
    pad_y = n_y // 2 + -(n_y // 2) % 8
    many = 4

    def read(lanes):
        if len(sources) == 1:
            return sources[0][:, lanes].astype(F32)
        first = (place_ref[0] & 1) == 0
        mine, other = ([ref[i, :, lanes].astype(F32) for i in range(2)] for ref in sources)
        low, high = (
            jnp.concatenate([jnp.where(first, m, o), jnp.where(first, o, m)], axis=0)
            for m, o in zip(mine, other)
        )
        return jnp.concatenate([low[x_cells - HALF :], high[:HALF]], axis=0)

    def depth_step(i):
        lanes = [pl.ds(pl.multiple_of((many * i + u) * LANES, LANES), LANES) for u in range(many)]
        block = jnp.concatenate([read(l) for l in lanes], axis=0).astype(BF16)
        out = jnp.dot(block, table_ref[: 2 * z_cells], preferred_element_type=F32)
        for u in range(many):
            part = out[u * count : (u + 1) * count]
            for j in range(2):
                store(
                    depth_buf, (2 * many * i + 2 * u + j) * odd(count),
                    lane_block(part, 2 * j) + lane_block(part, 2 * j + 1),
                )

    loop(y_cells // (2 * many), depth_step)

    def gather_rows(i, slot):
        value = pick(depth_buf, [GROUP * i + u for u in range(GROUP)], y_cells, odd(count))
        parts_buf[slot] = split_rows(value, True)

    def y_step(i, slot):
        plus, minus = pair_dot(table_ref[2 * z_cells :, : 3 * y_cells], parts_buf[slot], True)
        for u in range(GROUP):
            start = base + (GROUP * i + u) * odd(2 * pad_y)
            store(rows_ref, start, lane_block(plus, u))
            store(rows_ref, start + pad_y, lane_block(minus, u))

    pipeline(count // GROUP, [gather_rows, y_step], 3)


def slab_rows(place, blocks, count, passed, dims, tables, name):
    x_cells, y_cells, z_cells = dims
    n_y = y_cells + HALF
    pad_y = n_y // 2 + -(n_y // 2) % 8
    vmem = pl.BlockSpec(memory_space=pltpu.VMEM)
    return pl.pallas_call(
        functools.partial(slab_rows_kernel, dims),
        out_shape=jax.ShapeDtypeStruct(((passed + count) * odd(2 * pad_y), LANES), F32),
        in_specs=[pl.BlockSpec(memory_space=pltpu.SMEM)] + [vmem] * (1 + len(blocks)),
        out_specs=vmem,
        scratch_shapes=[
            pltpu.VMEM((y_cells * odd(count), LANES), F32),
            pltpu.VMEM((3, 3 * y_cells, GROUP * LANES), BF16),
        ],
        compiler_params=pltpu.CompilerParams(vmem_limit_bytes=12 * 1024 * 1024),
        cost_estimate=pl.CostEstimate(flops=count * 10**8, bytes_accessed=10**6, transcendentals=0),
        name=name,
    )(place, *blocks, tables["slab_rows"])


def slab_x_kernel(
    dims, rows_ref, x_ref, valid_ref, tz_ref, spec_ref, mask_ref, z_ref, parts_buf
):
    x_cells, y_cells, z_cells = dims
    n_y = y_cells + HALF
    pad_y = n_y // 2 + -(n_y // 2) % 8

    def gather_rows(i, slot):
        firsts = [GROUP // 2 * i + u // 2 + u % 2 * pad_y for u in range(GROUP)]
        value = pick(rows_ref, firsts, x_cells + TEMPL, odd(2 * pad_y))
        parts_buf[slot] = split_rows(value, True)

    def x_step(i, slot):
        plus, minus = pair_dot(x_ref[...], parts_buf[slot], True)
        spec = jnp.concatenate([plus, minus], axis=0)
        turned = swap(spec)
        real_lane = lane_sign(GROUP * LANES) < 0
        spec_ref[i, 0] = jnp.where(real_lane, spec, turned)
        spec_ref[i, 1] = jnp.where(real_lane, -turned, spec)

    pipeline(n_y // GROUP, [gather_rows, x_step], 4)

    valid = valid_ref[...].astype(F32)
    low_lane = lax.broadcasted_iota(jnp.int32, (x_cells, LANES), 1) < z_cells
    for q in range(y_cells // 2):
        mask_ref[q] = jnp.where(low_lane, valid[:, 2 * q : 2 * q + 1], valid[:, 2 * q + 1 : 2 * q + 2])
    z_ref[...] = jnp.zeros(z_ref.shape, BF16)
    for j in range(8):
        start = TEMPL * j - (LANES if j >= 4 else 0)
        z_ref[j, start : start + TEMPL, :] = tz_ref[...]


def slab_x(rows, valid, dims, tables):
    x_cells, y_cells, z_cells = dims
    n_x, n_y = x_cells + TEMPL, y_cells + HALF
    steps = n_y // GROUP
    vmem = pl.BlockSpec(memory_space=pltpu.VMEM)
    shape = (steps, 2, n_x, GROUP * LANES)
    return pl.pallas_call(
        functools.partial(slab_x_kernel, dims),
        out_shape=(
            jax.ShapeDtypeStruct(shape, F32),
            jax.ShapeDtypeStruct((y_cells // 2, x_cells, LANES), F32),
            jax.ShapeDtypeStruct((8, 2 * LANES, 2 * LANES), BF16),
        ),
        in_specs=[vmem] * 4,
        out_specs=(vmem,) * 3,
        scratch_shapes=[pltpu.VMEM((4, 3 * n_x, GROUP * LANES), BF16)],
        compiler_params=pltpu.CompilerParams(vmem_limit_bytes=9 * 1024 * 1024),
        cost_estimate=pl.CostEstimate(flops=5 * 10**9, bytes_accessed=10**6, transcendentals=0),
        name="slab_x",
    )(rows, tables["slab_x"], valid, tables["tmpl_z"])


def corr_kernel(
    dims, rot, entry, place_ref, tile_ref, *refs
):
    if rot > 0:
        before_ref, *refs = refs
    held_ref, last_ref, mask_ref, spec_ref, z_ref, ones_ref, y_ref, x_ref, bx_ref, by_ref, bz_ref, *refs = refs
    mines_ref, side_ref, far_ref, stat_ref, *refs = refs
    bank_buf, depth_buf, rows_buf, first_buf, second_buf, third_buf, back_buf, vol_buf = refs
    if rot > 0:
        mines_ref[:rot] = before_ref[...]
    x_cells, y_cells, z_cells = dims
    n_x, n_y = x_cells + TEMPL, y_cells + HALF
    half_y = n_y // 2
    pad_y = half_y + -half_y % 8
    for i, block in enumerate(HELD):
        for ref, at, tile in ((held_ref, rot, block), (last_ref, entry, block ^ 1)):
            store(bank_buf, (tile_ref[0] ^ tile) * odd(BLOCK_ROWS), ref[at, i].astype(F32))
    tmpl = jnp.concatenate(
        [
            pick(bank_buf, [a * CHUNKS + i for i in range(CHUNKS)], BLOCKS, odd(BLOCK_ROWS))
            for a in range(EACH)
        ],
        axis=0,
    )
    inv_size = 1.0 / TEMPL**3
    mean = jnp.sum(tmpl) * inv_size
    centred = tmpl - mean
    var = jnp.sum(centred * centred) * inv_size
    scale = 1.0 / (jnp.sqrt(jnp.full((1, LANES), var + EPSILON, F32)) * TEMPL**1.5)
    shift = ones_ref[:1] * mean

    wide = 8 * TEMPL
    narrow = tmpl.astype(BF16)
    block = jnp.concatenate(
        [narrow[:, g * wide : (g + 1) * wide] for g in range(TEMPL // 8)], axis=0
    )
    for j in range(8):
        window = block[:, : 2 * LANES] if j < 4 else block[:, LANES:]
        out = jnp.dot(window, z_ref[j], preferred_element_type=F32)
        part = out[:, :LANES] + out[:, LANES:] - shift
        for g in range(TEMPL // 8):
            start = (8 * g + j) * odd(TEMPL)
            store(depth_buf, start, part[g * TEMPL : (g + 1) * TEMPL])

    def gather_a(i, slot):
        value = pick(depth_buf, [GROUP * i + u for u in range(GROUP)], TEMPL, odd(TEMPL))
        first_buf[slot] = split_rows(value, True)

    def y_step(i, slot):
        plus, minus = pair_dot(y_ref[...], first_buf[slot], True)
        for u in range(GROUP):
            start = (GROUP * i + u) * odd(2 * pad_y)
            store(rows_buf, start, lane_block(plus, u))
            store(rows_buf, start + pad_y, lane_block(minus, u))

    pipeline(TEMPL // GROUP, [gather_a, y_step], 6)

    def gather_ky(i, slot):
        firsts = [GROUP // 2 * i + u // 2 + u % 2 * pad_y for u in range(GROUP)]
        first_buf[slot] = split_rows(pick(rows_buf, firsts, TEMPL, odd(2 * pad_y)), True)

    def multiply(i, slot):
        plus, minus = pair_dot(x_ref[...], first_buf[slot], True)
        spec = jnp.concatenate([plus, minus], axis=0)
        prod = spec * spec_ref[i, 0] + swap(spec) * spec_ref[i, 1]
        second_buf[slot] = split_rows(prod, False)

    def back_x(i, slot):
        plus, minus = pair_dot(bx_ref[...], second_buf[slot], False)
        for u in range(GROUP):
            start = (GROUP * i + u) * odd(x_cells)
            store(back_buf, start, lane_block(plus, u))
            store(back_buf, start + x_cells // 2, lane_block(minus, u))

    pipeline(n_y // GROUP, [gather_ky, multiply, back_x], 4)

    def gather_x(i, slot):
        value = pick(back_buf, [GROUP * i + u for u in range(GROUP)], n_y, odd(x_cells))
        third_buf[slot] = split_rows(value, False)

    def back_y(i, slot):
        plus, minus = pair_dot(by_ref[...], third_buf[slot], False)
        for u in range(GROUP):
            row = GROUP * i + u
            x = jnp.where(row < x_cells // 2, row + x_cells // 2, x_cells - 1 - row)
            store(vol_buf, x * odd(y_cells), lane_block(plus, u))
            store(vol_buf, x * odd(y_cells) + y_cells // 2, lane_block(minus, u))

    pipeline(x_cells // GROUP, [gather_x, back_y], 4)

    share = y_cells // 8
    me = place_ref[0]
    total = jnp.zeros((x_cells, LANES), F32)
    number = jnp.zeros((x_cells, LANES), F32)
    targets = [mines_ref.at[rot], side_ref, far_ref.at[0], far_ref.at[1]]
    for p, target in enumerate(targets):
        first = (me ^ p) * share
        values = []
        for i in range(share):
            firsts = []
            for j in range(2):
                y = 2 * (first + i) + j
                firsts.append(jnp.where(y < y_cells // 2, y_cells - 1 - y, y - y_cells // 2))
            values.append(pick(vol_buf, firsts, x_cells, odd(y_cells)))
        value = jnp.concatenate(values, axis=0)
        out = jnp.dot(split_rows(value, False), bz_ref[...], preferred_element_type=F32)
        rows = value.shape[0]
        full = out[:rows, :LANES] + out[:rows, LANES:] + out[rows:, :LANES]
        for i in range(share):
            corr = full[i * x_cells : (i + 1) * x_cells] * scale
            target[:, i * LANES : (i + 1) * LANES] = corr
            mask = mask_ref[first + i]
            total = total + corr * mask
            number = number + mask
    number_sum = jnp.sum(number)
    total_sum = jnp.sum(total)
    local_mean = jnp.full((1, LANES), total_sum, F32) / jnp.maximum(number_sum, 1.0)
    square = jnp.zeros((x_cells, LANES), F32)
    for p, target in enumerate(targets):
        first = (me ^ p) * share
        for i in range(share):
            gap = target[:, i * LANES : (i + 1) * LANES] - local_mean
            square = square + gap * gap * mask_ref[first + i]
    row = lax.broadcasted_iota(jnp.int32, (8, LANES), 0)
    stat_ref[...] = jnp.where(row == 0, number_sum, jnp.where(row == 1, total_sum, jnp.sum(square)))


def correlate(mines, place, tile, held, rot, last, entry, mask, spec, tmpl_z, dims, tables):
    x_cells, y_cells, z_cells = dims
    n_x, n_y = x_cells + TEMPL, y_cells + HALF
    pad_y = n_y // 2 + -(n_y // 2) % 8
    width = y_cells * z_cells // 4
    before = [] if mines is None else [mines]
    vmem = pl.BlockSpec(memory_space=pltpu.VMEM)
    return pl.pallas_call(
        functools.partial(corr_kernel, dims, rot, entry),
        out_shape=(
            jax.ShapeDtypeStruct((rot + 1, x_cells, width), F32),
            jax.ShapeDtypeStruct((x_cells, width), F32),
            jax.ShapeDtypeStruct((2, x_cells, width), F32),
            jax.ShapeDtypeStruct((8, LANES), F32),
        ),
        in_specs=[pl.BlockSpec(memory_space=pltpu.SMEM)] * 2 + [vmem] * (11 + len(before)),
        out_specs=(vmem,) * 4,
        scratch_shapes=[
            pltpu.VMEM((BLOCKS * odd(BLOCK_ROWS), LANES), F32),
            pltpu.VMEM((TEMPL * odd(TEMPL), LANES), F32),
            pltpu.VMEM((TEMPL * odd(2 * pad_y), LANES), F32),
            pltpu.VMEM((6, 3 * TEMPL, GROUP * LANES), BF16),
            pltpu.VMEM((4, 2 * n_x, GROUP * LANES), BF16),
            pltpu.VMEM((4, 2 * n_y, GROUP * LANES), BF16),
            pltpu.VMEM((n_y * odd(x_cells), LANES), F32),
            pltpu.VMEM((x_cells * odd(y_cells), LANES), F32),
        ],
        compiler_params=pltpu.CompilerParams(vmem_limit_bytes=20 * 1024 * 1024),
        cost_estimate=pl.CostEstimate(flops=15 * 10**9, bytes_accessed=10**7, transcendentals=0),
        name="correlate",
    )(
        place, tile, *before, held, last, mask, spec,
        tmpl_z, tables["ones_z"], tables["tmpl_y"], tables["tmpl_x"],
        tables["back_x"], tables["back_y"], tables["back_z"],
    )


def score_kernel(pieces, place_ref, coef_ref, mask_ref, *refs):
    best_ref, evid_ref, mom_ref = refs[-3:]
    blocks = best_ref.shape[1] // LANES

    def step(i):
        lanes = pl.ds(pl.multiple_of(i * LANES, LANES), LANES)

        def score(k):
            at, entry = pieces[k]
            return (refs[at][entry, :, lanes] - coef_ref[k, 0]) * coef_ref[k, 1]

        mask = mask_ref[place_ref[0] * blocks + i]
        high = functools.reduce(jnp.maximum, [score(k) for k in range(len(pieces))])
        total = jnp.zeros_like(high)
        moment = [jnp.zeros_like(high) for _ in range(4)]
        for k in range(len(pieces)):
            weight = jnp.exp(score(k) - high)
            total = total + weight
            for c in range(4):
                moment[c] = moment[c] + weight * coef_ref[k, 2 + c]
        best_ref[:, lanes] = mask * high
        evid_ref[:, lanes] = mask * (high + jnp.log(total))
        share = mask / total
        for c in range(4):
            mom_ref[c, :, lanes] = moment[c] * share

    def two_steps(i):
        step(2 * i)
        step(2 * i + 1)

    loop(blocks // 2, two_steps)


def combine(place, coefs, mask, arrays, pieces):
    shape = arrays[0].shape[1:]
    vmem = pl.BlockSpec(memory_space=pltpu.VMEM)
    out = jax.ShapeDtypeStruct(shape, F32)
    return pl.pallas_call(
        functools.partial(score_kernel, pieces),
        out_shape=(out, out, jax.ShapeDtypeStruct((4,) + shape, F32)),
        in_specs=[pl.BlockSpec(memory_space=pltpu.SMEM)] * 2 + [vmem] * (1 + len(arrays)),
        out_specs=(vmem,) * 3,
        compiler_params=pltpu.CompilerParams(vmem_limit_bytes=4 * 1024 * 1024),
        name="combine",
    )(place, coefs, mask, *arrays)


def pack_kernel(after_ref, *refs):
    *sources, out_ref = refs
    for i, source in enumerate(sources):
        out_ref[i] = source[...] if len(source.shape) == 2 else source[1]


def pack(after, sides, fars):
    vmem = pl.BlockSpec(memory_space=pltpu.VMEM)
    count = len(sides) + len(fars)
    return pl.pallas_call(
        pack_kernel,
        out_shape=jax.ShapeDtypeStruct((count,) + sides[0].shape, F32),
        in_specs=[pl.BlockSpec(memory_space=pl.ANY)] + [vmem] * count,
        out_specs=vmem,
        compiler_params=pltpu.CompilerParams(vmem_limit_bytes=8 * 1024 * 1024),
        name="pack",
    )(after, *sides, *fars)


def swap_blocks(block, axis, step):
    return lax.ppermute(block, axis, [(i, i ^ step) for i in range(lax.axis_size(axis))])


def general_gather(templates):
    rots = templates.shape[0]
    count = lax.axis_size("tile")
    block = templates[:, None]
    for step in [1 << i for i in reversed(range(count.bit_length() - 1))]:
        other = swap_blocks(block, "tile", step)
        upper = (lax.axis_index("tile") & step) != 0
        pair = [jnp.where(upper, other, block), jnp.where(upper, block, other)]
        block = jnp.stack(pair, axis=2).reshape((rots, -1) + block.shape[2:])
    block = block.reshape(rots, BLOCKS, EACH * CHUNKS, LANES)
    block = jnp.pad(block, ((0, 0), (0, 0), (0, BLOCK_ROWS - EACH * CHUNKS), (0, 0)))
    held = jnp.stack([block[:, i] for i in HELD], axis=1)
    return held, jnp.stack([block[:, i ^ 1] for i in HELD], axis=1)


def merge(first, other):
    number_a, number_b = first[:1], other[:1]
    mean_a = first[1:2] / jnp.maximum(number_a, 1.0)
    mean_b = other[1:2] / jnp.maximum(number_b, 1.0)
    gap = mean_b - mean_a
    between = gap * gap * (number_a * number_b / jnp.maximum(number_a + number_b, 1.0))
    return first + other + jnp.where(jnp.arange(3)[:, None] == 2, between, 0.0)


def exchange_all(block, axis, low, high):
    count = lax.axis_size(axis)
    parts = [block]
    for step in range(low, high, low):
        parts.append(lax.ppermute(block, axis, [(i, i ^ step) for i in range(count)]))
    return jnp.stack(parts)


def neighbours(block, axis):
    count = lax.axis_size(axis)
    forward = [(i, i + 1) for i in range(count - 1)]
    backward = [(target, source) for source, target in forward]
    return lax.ppermute(block, axis, forward), lax.ppermute(block, axis, backward)


def local(tomogram, templates, valid, quats, rot_index):
    x_cells, voxels = tomogram.shape
    y_cells = valid.shape[1]
    z_cells = voxels // y_cells
    dims = (x_cells, y_cells, z_cells)
    tables = {name: jnp.asarray(table) for name, table in make_tables(*dims).items()}
    groups = lax.axis_size("rot")
    tiles = lax.axis_size("tile")
    me = lax.axis_index("rot")
    rots = templates.shape[0]

    tile = lax.axis_index("tile")
    by_blocks = tiles == BLOCKS
    if by_blocks:
        first = swap_blocks(templates, "tile", 4)
        held = [part.reshape(rots, 1, EACH * CHUNKS, LANES) for part in (templates, first)]
        held = jnp.concatenate(held, axis=1)
        held = jnp.pad(held, ((0, 0), (0, 0), (0, BLOCK_ROWS - EACH * CHUNKS), (0, 0)))
    half = x_cells // 2
    piece = lax.dynamic_slice_in_dim(tomogram, (me & 1) * half, half, 0)
    mine = jnp.stack(neighbours(piece, "tile"))
    side_swap = [(i, i ^ 1) for i in range(groups)]
    other = lax.ppermute(mine, "rot", side_swap)
    if by_blocks:
        second = swap_blocks(held, "tile", 2)
    else:
        held, last = general_gather(templates)
        tile = jnp.zeros_like(tile)
    one_hot = (rot_index[:, None] == jnp.arange(quats.shape[1], dtype=jnp.int32)[None, :]).astype(F32)
    orient = jnp.einsum("rq,kq->rk", one_hot, quats, precision=lax.Precision.HIGHEST)
    place = me_place = jnp.reshape(me, (1,)).astype(jnp.int32)
    tile = jnp.reshape(tile, (1,)).astype(jnp.int32)
    own = slab_rows(place, [tomogram], x_cells, 0, dims, tables, "slab_own")
    rows = slab_rows(place, [own, mine, other], TEMPL, x_cells, dims, tables, "slab_halo")
    if by_blocks:
        second = jnp.where(rows[0, 0] < 1e9, second, jnp.zeros_like(second))
        held = jnp.concatenate([held, second], axis=1)
        lasts = [swap_blocks(held[:1], "tile", 1), swap_blocks(held[1:], "tile", 1)]
    else:
        lasts = [last[:1], last[1:]]
    spec, mask, tmpl_z = slab_x(rows, valid, dims, tables)
    far_swap = [(i, i ^ 2) for i in range(groups)]
    mines, sides, fars, stats = None, [], [], []
    for r in range(rots):
        if r >= 2:
            place, fars[r - 2] = lax.optimization_barrier((place, fars[r - 2]))
        mines, side, far, stat = correlate(
            mines, place, tile, held, r, lasts[min(r, 1)], max(r - 1, 0), mask, spec, tmpl_z, dims, tables
        )
        if r >= 1:
            stat, fars[r - 1] = lax.optimization_barrier((stat, fars[r - 1]))
        sides.append(side)
        stats.append(stat[:3, 0])
        fars.append(lax.ppermute(far, "rot", far_swap))
    state = jnp.stack(stats, axis=1)
    state, fars[rots - 2] = lax.optimization_barrier((state, fars[rots - 2]))
    step = 1
    while step < tiles:
        partner = lax.ppermute(state, "tile", [(i, i ^ step) for i in range(tiles)])
        if step * 4 == tiles:
            last = pack(partner, sides, fars)
        if step * 2 == tiles:
            partner, last = lax.optimization_barrier((partner, last))
        state = merge(state, partner)
        step *= 2
    average = state[1] / state[0]
    inverse = 1.0 / jnp.sqrt(state[2] / state[0] + EPSILON)
    coefs = jnp.concatenate([average[:, None], inverse[:, None], orient], axis=1)
    coefs = exchange_all(coefs, "rot", 1, groups)
    last = lax.ppermute(last, "rot", side_swap)
    arrays = [mines] + fars + [last]
    pieces = [(0, r) for r in range(rots)]
    pieces += [(1 + rots, r) for r in range(rots)]
    pieces += [(1 + r, 0) for r in range(rots)]
    pieces += [(1 + rots, rots + r) for r in range(rots)]
    return combine(me_place, coefs.reshape(groups * rots, 6), mask, arrays, pieces)


def solution(mesh):
    placed = (P("tile", None), P("rot", "tile"), P("tile", None), P(), P("rot"))
    return jax.shard_map(
        local,
        mesh=mesh,
        in_specs=placed,
        out_specs=(P("tile", "rot"), P("tile", "rot"), P(None, "tile", "rot")),
        check_vma=False,
    )
```

```python
import functools
import math

import jax
import jax.numpy as jnp
import ml_dtypes
import numpy as np
from jax import lax
from jax.experimental import pallas as pl
from jax.experimental.pallas import tpu as pltpu
from jax.sharding import PartitionSpec as P

TEMPL = 48
HALF = 24
EPSILON = 1e-06
LANES = 128
SPLIT = 64
BLOCKS = 8
EACH = TEMPL // BLOCKS
CHUNKS = TEMPL * TEMPL // LANES
BLOCK_ROWS = EACH * CHUNKS + -EACH * CHUNKS % 16
HELD = (0, 4, 2, 6)
F32 = jnp.float32
BF16 = jnp.bfloat16


def two_parts(table):
    high = table.astype(ml_dtypes.bfloat16)
    low = (table - high.astype(np.float64)).astype(ml_dtypes.bfloat16)
    return high, low


def row_table(out_idx, in_idx, length, sign, factor, wide):
    theta = 2.0 * math.pi / length * np.outer(out_idx, in_idx)
    pad = np.zeros((-len(out_idx) % 8, len(in_idx)))
    full = np.concatenate([np.cos(theta), pad, sign * np.sin(theta), pad], axis=0) * factor
    high, low = two_parts(full)
    if wide:
        return np.concatenate([high, high, low], axis=1)
    zeros = np.zeros_like(low)
    return np.concatenate(
        [np.concatenate([high, high], axis=1), np.concatenate([low, zeros], axis=1)], axis=0
    )


def depth_table(in_idx, length, sign, factor):
    freq = np.arange(length // 2) + 0.5
    theta = 2.0 * math.pi / length * np.outer(in_idx, freq)
    out = np.zeros((len(in_idx), LANES))
    out[:, : length // 2] = np.cos(theta) * factor
    out[:, SPLIT : SPLIT + length // 2] = sign * np.sin(theta) * factor
    return out


def half_odd(count):
    return np.arange(count // 2) + 0.5


def make_tables(x_cells, y_cells, z_cells):
    n_x, n_y, n_z = x_cells + TEMPL, y_cells + HALF, z_cells + HALF
    k_x, k_y = half_odd(n_x), half_odd(n_y)
    both_x = np.concatenate([k_x, -k_x])
    both_y = np.stack([k_y, -k_y], axis=1).reshape(-1)
    mid_x, mid_y = (x_cells - 1) / 2, (y_cells - 1) / 2
    tables = {}
    slab = np.zeros((2 * z_cells, 4 * LANES), ml_dtypes.bfloat16)
    high, low = two_parts(depth_table(np.arange(z_cells), n_z, -1.0, 1.0))
    for j in range(2):
        rows = slice(j * z_cells, (j + 1) * z_cells)
        slab[rows, 2 * j * LANES : (2 * j + 1) * LANES] = high
        slab[rows, (2 * j + 1) * LANES : (2 * j + 2) * LANES] = low
    slab_y = row_table(k_y, np.arange(y_cells), n_y, -1.0, 1.0, True)
    slab_y = np.pad(slab_y, ((0, 0), (0, slab.shape[1] - slab_y.shape[1])))
    tables["slab_rows"] = np.concatenate([slab, slab_y], axis=0)
    own = np.arange(HALF, HALF + x_cells)
    halo = np.concatenate([np.arange(HALF), np.arange(HALF + x_cells, n_x)])
    tables["slab_x"] = row_table(k_x, np.concatenate([own, halo]), n_x, -1.0, 1.0, True)
    high, low = two_parts(depth_table(np.arange(TEMPL) - HALF, n_z, 1.0, 1.0))
    tables["tmpl_z"] = np.concatenate([high, low], axis=1)
    ones = (high.astype(np.float64) + low.astype(np.float64)).sum(axis=0)
    tables["ones_z"] = np.broadcast_to(ones.astype(np.float32)[None], (8, LANES)).copy()
    tables["tmpl_y"] = row_table(k_y, np.arange(TEMPL) - HALF + mid_y, n_y, 1.0, 1.0, True)
    tmpl_rows = np.arange(TEMPL).reshape(BLOCKS, EACH).T.reshape(-1)
    tables["tmpl_x"] = row_table(k_x, tmpl_rows + mid_x, n_x, 1.0, 1.0, True)
    tables["back_x"] = row_table(half_odd(x_cells), both_x, n_x, 1.0, 1.0 / n_x, False)
    tables["back_y"] = row_table(half_odd(y_cells), both_y, n_y, 1.0, 1.0 / n_y, False)
    back = depth_table(np.arange(z_cells), n_z, -1.0, 2.0 / n_z).T
    high, low = two_parts(back)
    back_z = np.zeros((2 * LANES, 2 * LANES), ml_dtypes.bfloat16)
    for j in range(2):
        rows = slice(j * LANES, (j + 1) * LANES)
        back_z[rows, j * z_cells : (j + 1) * z_cells] = high
        back_z[rows, LANES + j * z_cells : LANES + (j + 1) * z_cells] = low
    tables["back_z"] = back_z
    return tables


def split_rows(value, wide):
    high = value.astype(BF16)
    if value.shape[0] % 16 == 0:
        low = (value - high.astype(F32)).astype(BF16)
        return jnp.concatenate([high, low, high] if wide else [high, low], axis=0)
    high = high.astype(F32)
    low = value - high
    return jnp.concatenate([high, low, high] if wide else [high, low], axis=0).astype(BF16)


def swap(value):
    parts = [
        pltpu.roll(value[:, s : s + LANES], SPLIT, 1) for s in range(0, value.shape[1], LANES)
    ]
    return jnp.concatenate(parts, axis=1)


def lane_sign(width):
    lane = lax.broadcasted_iota(jnp.int32, (8, width), 1) % LANES
    return jnp.where(lane < SPLIT, -1.0, 1.0)[:1]


def pair_rows(table, value, wide):
    return pair_dot(table, split_rows(value, wide), wide)


def pair_dot(table, parts, wide):
    out = jnp.dot(table, parts, preferred_element_type=F32)
    if not wide:
        half = out.shape[0] // 2
        out = out[:half] + out[half:]
    half = out.shape[0] // 2
    turned = swap(out[half:]) * lane_sign(out.shape[1])
    return out[:half] + turned, out[:half] - turned


def pick(ref, firsts, count, stride):
    return jnp.concatenate([ref[pl.ds(f, count, stride=stride), :] for f in firsts], axis=1)


def store(ref, start, value):
    ref[pl.ds(start, value.shape[0]), :] = value


def odd(rows):
    return rows + 1


def lane_block(value, i):
    return value[:, i * LANES : (i + 1) * LANES]


def loop(count, body):
    def one(i, carry):
        body(i)
        return carry

    lax.fori_loop(0, count, one, 0)


GROUP = 8


def pipeline(steps, stages, width):
    blocks = -(-steps // width)
    depth = len(stages)

    def turn(t, static):
        for s in reversed(range(depth)):
            if static and not 0 <= t - s < blocks:
                continue
            for slot in range(width):
                step = (t - s) * width + slot
                if not static or step < steps:
                    stages[s](step, slot)

    full = steps // width
    first, last = depth - 1, max(full, depth - 1)
    for t in range(first):
        turn(t, True)
    if last - first >= 2:
        loop(last - first, lambda i: turn(i + first, False))
    else:
        last = first
    for t in range(last, blocks + depth - 1):
        turn(t, True)


def slab_rows_kernel(dims, place_ref, *refs):
    *sources, table_ref, rows_ref, depth_buf, parts_buf = refs
    x_cells, y_cells, z_cells = dims
    base = 0
    if len(sources) > 1:
        own_ref, *sources = sources
        base = own_ref.shape[0]
        rows_ref[:base, :] = own_ref[...]
    half = x_cells // 2
    count = depth_buf.shape[0] // y_cells - 1
    n_y = y_cells + HALF
    pad_y = n_y // 2 + -(n_y // 2) % 8
    many = 4

    def read(lanes):
        if len(sources) == 1:
            return sources[0][:, lanes].astype(F32)
        first = (place_ref[0] & 1) == 0
        mine, other = ([ref[i, :, lanes].astype(F32) for i in range(2)] for ref in sources)
        low, high = (
            jnp.concatenate([jnp.where(first, m, o), jnp.where(first, o, m)], axis=0)
            for m, o in zip(mine, other)
        )
        return jnp.concatenate([low[x_cells - HALF :], high[:HALF]], axis=0)

    def depth_step(i):
        lanes = [pl.ds(pl.multiple_of((many * i + u) * LANES, LANES), LANES) for u in range(many)]
        block = jnp.concatenate([read(l) for l in lanes], axis=0).astype(BF16)
        out = jnp.dot(block, table_ref[: 2 * z_cells], preferred_element_type=F32)
        for u in range(many):
            part = out[u * count : (u + 1) * count]
            for j in range(2):
                store(
                    depth_buf, (2 * many * i + 2 * u + j) * odd(count),
                    lane_block(part, 2 * j) + lane_block(part, 2 * j + 1),
                )

    def two_depth_steps(i):
        depth_step(2 * i)
        depth_step(2 * i + 1)

    loop(y_cells // (4 * many), two_depth_steps)

    def gather_rows(i, slot):
        value = pick(depth_buf, [GROUP * i + u for u in range(GROUP)], y_cells, odd(count))
        parts_buf[slot] = split_rows(value, True)

    def y_step(i, slot):
        plus, minus = pair_dot(table_ref[2 * z_cells :, : 3 * y_cells], parts_buf[slot], True)
        for u in range(GROUP):
            start = base + (GROUP * i + u) * odd(2 * pad_y)
            store(rows_ref, start, lane_block(plus, u))
            store(rows_ref, start + pad_y, lane_block(minus, u))

    pipeline(count // GROUP, [gather_rows, y_step], 3)


def slab_rows(place, blocks, count, passed, dims, tables, name):
    x_cells, y_cells, z_cells = dims
    n_y = y_cells + HALF
    pad_y = n_y // 2 + -(n_y // 2) % 8
    vmem = pl.BlockSpec(memory_space=pltpu.VMEM)
    return pl.pallas_call(
        functools.partial(slab_rows_kernel, dims),
        out_shape=jax.ShapeDtypeStruct(((passed + count) * odd(2 * pad_y), LANES), F32),
        in_specs=[pl.BlockSpec(memory_space=pltpu.SMEM)] + [vmem] * (1 + len(blocks)),
        out_specs=vmem,
        scratch_shapes=[
            pltpu.VMEM((y_cells * odd(count), LANES), F32),
            pltpu.VMEM((3, 3 * y_cells, GROUP * LANES), BF16),
        ],
        compiler_params=pltpu.CompilerParams(vmem_limit_bytes=12 * 1024 * 1024),
        cost_estimate=pl.CostEstimate(flops=count * 10**8, bytes_accessed=10**6, transcendentals=0),
        name=name,
    )(place, *blocks, tables["slab_rows"])


def slab_x_kernel(
    dims, rows_ref, x_ref, valid_ref, tz_ref, spec_ref, mask_ref, z_ref, parts_buf
):
    x_cells, y_cells, z_cells = dims
    n_y = y_cells + HALF
    pad_y = n_y // 2 + -(n_y // 2) % 8

    def gather_rows(i, slot):
        firsts = [GROUP // 2 * i + u // 2 + u % 2 * pad_y for u in range(GROUP)]
        value = pick(rows_ref, firsts, x_cells + TEMPL, odd(2 * pad_y))
        parts_buf[slot] = split_rows(value, True)

    def x_step(i, slot):
        plus, minus = pair_dot(x_ref[...], parts_buf[slot], True)
        spec = jnp.concatenate([plus, minus], axis=0)
        turned = swap(spec)
        real_lane = lane_sign(GROUP * LANES) < 0
        spec_ref[i, 0] = jnp.where(real_lane, spec, turned)
        spec_ref[i, 1] = jnp.where(real_lane, -turned, spec)

    pipeline(n_y // GROUP, [gather_rows, x_step], 4)

    valid = valid_ref[...].astype(F32)
    low_lane = lax.broadcasted_iota(jnp.int32, (x_cells, LANES), 1) < z_cells
    for q in range(y_cells // 2):
        mask_ref[q] = jnp.where(low_lane, valid[:, 2 * q : 2 * q + 1], valid[:, 2 * q + 1 : 2 * q + 2])
    z_ref[...] = jnp.zeros(z_ref.shape, BF16)
    for j in range(8):
        start = TEMPL * j - (LANES if j >= 4 else 0)
        z_ref[j, start : start + TEMPL, :] = tz_ref[...]


def slab_x(rows, valid, dims, tables):
    x_cells, y_cells, z_cells = dims
    n_x, n_y = x_cells + TEMPL, y_cells + HALF
    steps = n_y // GROUP
    vmem = pl.BlockSpec(memory_space=pltpu.VMEM)
    shape = (steps, 2, n_x, GROUP * LANES)
    return pl.pallas_call(
        functools.partial(slab_x_kernel, dims),
        out_shape=(
            jax.ShapeDtypeStruct(shape, F32),
            jax.ShapeDtypeStruct((y_cells // 2, x_cells, LANES), F32),
            jax.ShapeDtypeStruct((8, 2 * LANES, 2 * LANES), BF16),
        ),
        in_specs=[vmem] * 4,
        out_specs=(vmem,) * 3,
        scratch_shapes=[pltpu.VMEM((4, 3 * n_x, GROUP * LANES), BF16)],
        compiler_params=pltpu.CompilerParams(vmem_limit_bytes=9 * 1024 * 1024),
        cost_estimate=pl.CostEstimate(flops=5 * 10**9, bytes_accessed=10**6, transcendentals=0),
        name="slab_x",
    )(rows, tables["slab_x"], valid, tables["tmpl_z"])


def corr_kernel(
    dims, rot, entry, place_ref, tile_ref, *refs
):
    if rot > 0:
        before_ref, *refs = refs
    held_ref, last_ref, mask_ref, spec_ref, z_ref, ones_ref, y_ref, x_ref, bx_ref, by_ref, bz_ref, *refs = refs
    mines_ref, side_ref, far_ref, stat_ref, *refs = refs
    bank_buf, depth_buf, rows_buf, first_buf, second_buf, third_buf, back_buf, vol_buf = refs
    if rot > 0:
        mines_ref[:rot] = before_ref[...]
    x_cells, y_cells, z_cells = dims
    n_x, n_y = x_cells + TEMPL, y_cells + HALF
    half_y = n_y // 2
    pad_y = half_y + -half_y % 8
    for i, block in enumerate(HELD):
        for ref, at, tile in ((held_ref, rot, block), (last_ref, entry, block ^ 1)):
            store(bank_buf, (tile_ref[0] ^ tile) * odd(BLOCK_ROWS), ref[at, i].astype(F32))
    tmpl = jnp.concatenate(
        [
            pick(bank_buf, [a * CHUNKS + i for i in range(CHUNKS)], BLOCKS, odd(BLOCK_ROWS))
            for a in range(EACH)
        ],
        axis=0,
    )
    inv_size = 1.0 / TEMPL**3
    mean = jnp.sum(tmpl) * inv_size
    centred = tmpl - mean
    var = jnp.sum(centred * centred) * inv_size
    scale = 1.0 / (jnp.sqrt(jnp.full((1, LANES), var + EPSILON, F32)) * TEMPL**1.5)
    shift = ones_ref[:1] * mean

    wide = 8 * TEMPL
    narrow = tmpl.astype(BF16)
    block = jnp.concatenate(
        [narrow[:, g * wide : (g + 1) * wide] for g in range(TEMPL // 8)], axis=0
    )
    for j in range(8):
        window = block[:, : 2 * LANES] if j < 4 else block[:, LANES:]
        out = jnp.dot(window, z_ref[j], preferred_element_type=F32)
        part = out[:, :LANES] + out[:, LANES:] - shift
        for g in range(TEMPL // 8):
            start = (8 * g + j) * odd(TEMPL)
            store(depth_buf, start, part[g * TEMPL : (g + 1) * TEMPL])

    def gather_a(i, slot):
        value = pick(depth_buf, [GROUP * i + u for u in range(GROUP)], TEMPL, odd(TEMPL))
        first_buf[slot] = split_rows(value, True)

    def y_step(i, slot):
        plus, minus = pair_dot(y_ref[...], first_buf[slot], True)
        for u in range(GROUP):
            start = (GROUP * i + u) * odd(2 * pad_y)
            store(rows_buf, start, lane_block(plus, u))
            store(rows_buf, start + pad_y, lane_block(minus, u))

    pipeline(TEMPL // GROUP, [gather_a, y_step], 6)

    def gather_ky(i, slot):
        firsts = [GROUP // 2 * i + u // 2 + u % 2 * pad_y for u in range(GROUP)]
        first_buf[slot] = split_rows(pick(rows_buf, firsts, TEMPL, odd(2 * pad_y)), True)

    def multiply(i, slot):
        plus, minus = pair_dot(x_ref[...], first_buf[slot], True)
        spec = jnp.concatenate([plus, minus], axis=0)
        prod = spec * spec_ref[i, 0] + swap(spec) * spec_ref[i, 1]
        second_buf[slot] = split_rows(prod, False)

    def back_x(i, slot):
        plus, minus = pair_dot(bx_ref[...], second_buf[slot], False)
        for u in range(GROUP):
            start = (GROUP * i + u) * odd(x_cells)
            store(back_buf, start, lane_block(plus, u))
            store(back_buf, start + x_cells // 2, lane_block(minus, u))

    pipeline(n_y // GROUP, [gather_ky, multiply, back_x], 4)

    def gather_x(i, slot):
        value = pick(back_buf, [GROUP * i + u for u in range(GROUP)], n_y, odd(x_cells))
        third_buf[slot] = split_rows(value, False)

    def back_y(i, slot):
        plus, minus = pair_dot(by_ref[...], third_buf[slot], False)
        for u in range(GROUP):
            row = GROUP * i + u
            x = jnp.where(row < x_cells // 2, row + x_cells // 2, x_cells - 1 - row)
            store(vol_buf, x * odd(y_cells), lane_block(plus, u))
            store(vol_buf, x * odd(y_cells) + y_cells // 2, lane_block(minus, u))

    pipeline(x_cells // GROUP, [gather_x, back_y], 4)

    share = y_cells // 8
    me = place_ref[0]
    total = jnp.zeros((x_cells, LANES), F32)
    number = jnp.zeros((x_cells, LANES), F32)
    targets = [mines_ref.at[rot], side_ref, far_ref.at[0], far_ref.at[1]]
    for p, target in enumerate(targets):
        first = (me ^ p) * share
        values = []
        for i in range(share):
            firsts = []
            for j in range(2):
                y = 2 * (first + i) + j
                firsts.append(jnp.where(y < y_cells // 2, y_cells - 1 - y, y - y_cells // 2))
            values.append(pick(vol_buf, firsts, x_cells, odd(y_cells)))
        value = jnp.concatenate(values, axis=0)
        out = jnp.dot(split_rows(value, False), bz_ref[...], preferred_element_type=F32)
        rows = value.shape[0]
        full = out[:rows, :LANES] + out[:rows, LANES:] + out[rows:, :LANES]
        for i in range(share):
            corr = full[i * x_cells : (i + 1) * x_cells] * scale
            target[:, i * LANES : (i + 1) * LANES] = corr
            mask = mask_ref[first + i]
            total = total + corr * mask
            number = number + mask
    number_sum = jnp.sum(number)
    total_sum = jnp.sum(total)
    local_mean = jnp.full((1, LANES), total_sum, F32) / jnp.maximum(number_sum, 1.0)
    square = jnp.zeros((x_cells, LANES), F32)
    for p, target in enumerate(targets):
        first = (me ^ p) * share
        for i in range(share):
            gap = target[:, i * LANES : (i + 1) * LANES] - local_mean
            square = square + gap * gap * mask_ref[first + i]
    row = lax.broadcasted_iota(jnp.int32, (8, LANES), 0)
    stat_ref[...] = jnp.where(row == 0, number_sum, jnp.where(row == 1, total_sum, jnp.sum(square)))


def correlate(mines, place, tile, held, rot, last, entry, mask, spec, tmpl_z, dims, tables):
    x_cells, y_cells, z_cells = dims
    n_x, n_y = x_cells + TEMPL, y_cells + HALF
    pad_y = n_y // 2 + -(n_y // 2) % 8
    width = y_cells * z_cells // 4
    before = [] if mines is None else [mines]
    vmem = pl.BlockSpec(memory_space=pltpu.VMEM)
    return pl.pallas_call(
        functools.partial(corr_kernel, dims, rot, entry),
        out_shape=(
            jax.ShapeDtypeStruct((rot + 1, x_cells, width), F32),
            jax.ShapeDtypeStruct((x_cells, width), F32),
            jax.ShapeDtypeStruct((2, x_cells, width), F32),
            jax.ShapeDtypeStruct((8, LANES), F32),
        ),
        in_specs=[pl.BlockSpec(memory_space=pltpu.SMEM)] * 2 + [vmem] * (11 + len(before)),
        out_specs=(vmem,) * 4,
        scratch_shapes=[
            pltpu.VMEM((BLOCKS * odd(BLOCK_ROWS), LANES), F32),
            pltpu.VMEM((TEMPL * odd(TEMPL), LANES), F32),
            pltpu.VMEM((TEMPL * odd(2 * pad_y), LANES), F32),
            pltpu.VMEM((6, 3 * TEMPL, GROUP * LANES), BF16),
            pltpu.VMEM((4, 2 * n_x, GROUP * LANES), BF16),
            pltpu.VMEM((4, 2 * n_y, GROUP * LANES), BF16),
            pltpu.VMEM((n_y * odd(x_cells), LANES), F32),
            pltpu.VMEM((x_cells * odd(y_cells), LANES), F32),
        ],
        compiler_params=pltpu.CompilerParams(vmem_limit_bytes=20 * 1024 * 1024),
        cost_estimate=pl.CostEstimate(flops=15 * 10**9, bytes_accessed=10**7, transcendentals=0),
        name="correlate",
    )(
        place, tile, *before, held, last, mask, spec,
        tmpl_z, tables["ones_z"], tables["tmpl_y"], tables["tmpl_x"],
        tables["back_x"], tables["back_y"], tables["back_z"],
    )


def score_kernel(pieces, place_ref, coef_ref, mask_ref, *refs):
    best_ref, evid_ref, mom_ref = refs[-3:]
    blocks = best_ref.shape[1] // LANES

    def step(i):
        lanes = pl.ds(pl.multiple_of(i * LANES, LANES), LANES)

        def score(k):
            at, entry = pieces[k]
            return (refs[at][entry, :, lanes] - coef_ref[k, 0]) * coef_ref[k, 1]

        mask = mask_ref[place_ref[0] * blocks + i]
        high = functools.reduce(jnp.maximum, [score(k) for k in range(len(pieces))])
        total = jnp.zeros_like(high)
        moment = [jnp.zeros_like(high) for _ in range(4)]
        for k in range(len(pieces)):
            weight = jnp.exp(score(k) - high)
            total = total + weight
            for c in range(4):
                moment[c] = moment[c] + weight * coef_ref[k, 2 + c]
        best_ref[:, lanes] = mask * high
        evid_ref[:, lanes] = mask * (high + jnp.log(total))
        share = mask / total
        for c in range(4):
            mom_ref[c, :, lanes] = moment[c] * share

    def two_steps(i):
        step(2 * i)
        step(2 * i + 1)

    loop(blocks // 2, two_steps)


def combine(place, coefs, mask, arrays, pieces):
    shape = arrays[0].shape[1:]
    vmem = pl.BlockSpec(memory_space=pltpu.VMEM)
    out = jax.ShapeDtypeStruct(shape, F32)
    return pl.pallas_call(
        functools.partial(score_kernel, pieces),
        out_shape=(out, out, jax.ShapeDtypeStruct((4,) + shape, F32)),
        in_specs=[pl.BlockSpec(memory_space=pltpu.SMEM)] * 2 + [vmem] * (1 + len(arrays)),
        out_specs=(vmem,) * 3,
        compiler_params=pltpu.CompilerParams(vmem_limit_bytes=4 * 1024 * 1024),
        name="combine",
    )(place, coefs, mask, *arrays)


def swap_blocks(block, axis, step):
    return lax.ppermute(block, axis, [(i, i ^ step) for i in range(lax.axis_size(axis))])


def general_gather(templates):
    rots = templates.shape[0]
    count = lax.axis_size("tile")
    block = templates[:, None]
    for step in [1 << i for i in reversed(range(count.bit_length() - 1))]:
        other = swap_blocks(block, "tile", step)
        upper = (lax.axis_index("tile") & step) != 0
        pair = [jnp.where(upper, other, block), jnp.where(upper, block, other)]
        block = jnp.stack(pair, axis=2).reshape((rots, -1) + block.shape[2:])
    block = block.reshape(rots, BLOCKS, EACH * CHUNKS, LANES)
    block = jnp.pad(block, ((0, 0), (0, 0), (0, BLOCK_ROWS - EACH * CHUNKS), (0, 0)))
    held = jnp.stack([block[:, i] for i in HELD], axis=1)
    return held, jnp.stack([block[:, i ^ 1] for i in HELD], axis=1)


def merge(first, other):
    number_a, number_b = first[:1], other[:1]
    mean_a = first[1:2] / jnp.maximum(number_a, 1.0)
    mean_b = other[1:2] / jnp.maximum(number_b, 1.0)
    gap = mean_b - mean_a
    between = gap * gap * (number_a * number_b / jnp.maximum(number_a + number_b, 1.0))
    return first + other + jnp.where(jnp.arange(3)[:, None] == 2, between, 0.0)


def exchange_all(block, axis, low, high):
    count = lax.axis_size(axis)
    parts = [block]
    for step in range(low, high, low):
        parts.append(lax.ppermute(block, axis, [(i, i ^ step) for i in range(count)]))
    return jnp.stack(parts)


def neighbours(block, axis):
    count = lax.axis_size(axis)
    forward = [(i, i + 1) for i in range(count - 1)]
    backward = [(target, source) for source, target in forward]
    return lax.ppermute(block, axis, forward), lax.ppermute(block, axis, backward)


def local(tomogram, templates, valid, quats, rot_index):
    x_cells, voxels = tomogram.shape
    y_cells = valid.shape[1]
    z_cells = voxels // y_cells
    dims = (x_cells, y_cells, z_cells)
    tables = {name: jnp.asarray(table) for name, table in make_tables(*dims).items()}
    groups = lax.axis_size("rot")
    tiles = lax.axis_size("tile")
    me = lax.axis_index("rot")
    rots = templates.shape[0]

    tile = lax.axis_index("tile")
    by_blocks = tiles == BLOCKS
    if by_blocks:
        held = templates.reshape(rots, 1, EACH * CHUNKS, LANES)
        held = jnp.pad(held, ((0, 0), (0, 0), (0, BLOCK_ROWS - EACH * CHUNKS), (0, 0)))
        held, tomogram_after = lax.optimization_barrier((held, tomogram))
        held = jnp.concatenate([held, swap_blocks(held, "tile", 4)], axis=1)
    else:
        tomogram_after = tomogram
    half = x_cells // 2
    piece = lax.dynamic_slice_in_dim(tomogram_after, (me & 1) * half, half, 0)
    mine = jnp.stack(neighbours(piece, "tile"))
    side_swap = [(i, i ^ 1) for i in range(groups)]
    other = lax.ppermute(mine, "rot", side_swap)
    if by_blocks:
        second = swap_blocks(held, "tile", 2)
    else:
        held, last = general_gather(templates)
        tile = jnp.zeros_like(tile)
    one_hot = (rot_index[:, None] == jnp.arange(quats.shape[1], dtype=jnp.int32)[None, :]).astype(F32)
    orient = jnp.einsum("rq,kq->rk", one_hot, quats, precision=lax.Precision.HIGHEST)
    place = me_place = jnp.reshape(me, (1,)).astype(jnp.int32)
    tile = jnp.reshape(tile, (1,)).astype(jnp.int32)
    own = slab_rows(place, [tomogram], x_cells, 0, dims, tables, "slab_own")
    rows = slab_rows(place, [own, mine, other], TEMPL, x_cells, dims, tables, "slab_halo")
    if by_blocks:
        second = jnp.where(rows[0, 0] < 1e9, second, jnp.zeros_like(second))
        held = jnp.concatenate([held, second], axis=1)
        lasts = [swap_blocks(held[:1], "tile", 1), swap_blocks(held[1:], "tile", 1)]
    else:
        lasts = [last[:1], last[1:]]
    spec, mask, tmpl_z = slab_x(rows, valid, dims, tables)
    far_swap = [(i, i ^ 2) for i in range(groups)]
    mines, sides, fars, stats = None, [], [], []
    for r in range(rots):
        if r >= 2:
            place, fars[r - 2] = lax.optimization_barrier((place, fars[r - 2]))
        mines, side, far, stat = correlate(
            mines, place, tile, held, r, lasts[min(r, 1)], max(r - 1, 0), mask, spec, tmpl_z, dims, tables
        )
        if r >= 1:
            stat, fars[r - 1] = lax.optimization_barrier((stat, fars[r - 1]))
        sides.append(side)
        stats.append(stat[:3, 0])
        fars.append(lax.ppermute(far, "rot", far_swap))
        if r == rots - 2:
            early = jnp.stack(sides[:-1] + [f[1] for f in fars[:-1]])
            early = lax.ppermute(early, "rot", side_swap)
    state = jnp.stack(stats, axis=1)
    state, early, fars[rots - 2] = lax.optimization_barrier((state, early, fars[rots - 2]))
    step = 1
    while step < tiles:
        partner = lax.ppermute(state, "tile", [(i, i ^ step) for i in range(tiles)])
        if step * 4 == tiles:
            late = jnp.where(partner[0, 0] >= 0.0, fars[rots - 1][1], 0.0)
            last = jnp.stack([sides[rots - 2], sides[rots - 1], fars[rots - 2][1], late])
        if step * 2 == tiles:
            partner, last = lax.optimization_barrier((partner, last))
        state = merge(state, partner)
        step *= 2
    average = state[1] / state[0]
    inverse = 1.0 / jnp.sqrt(state[2] / state[0] + EPSILON)
    coefs = jnp.concatenate([average[:, None], inverse[:, None], orient], axis=1)
    coefs = exchange_all(coefs, "rot", 1, groups)
    last = lax.ppermute(last, "rot", side_swap)
    arrays = [mines] + fars + [early, last]
    at_far, at_early, at_last = 1, 1 + rots, 2 + rots
    pieces = [(0, r) for r in range(rots)]
    pieces += [(at_early, r) for r in range(rots - 2)] + [(at_last, 0), (at_last, 1)]
    pieces += [(at_far + r, 0) for r in range(rots)]
    pieces += [(at_early, rots - 2 + r) for r in range(rots - 2)] + [(at_last, 2), (at_last, 3)]
    return combine(me_place, coefs.reshape(groups * rots, 6), mask, arrays, pieces)


def solution(mesh):
    placed = (P("tile", None), P("rot", "tile"), P("tile", None), P(), P("rot"))
    return jax.shard_map(
        local,
        mesh=mesh,
        in_specs=placed,
        out_specs=(P("tile", "rot"), P("tile", "rot"), P(None, "tile", "rot")),
        check_vma=False,
    )
```

```python
import functools
import math

import jax
import jax.numpy as jnp
import ml_dtypes
import numpy as np
from jax import lax
from jax.experimental import pallas as pl
from jax.experimental.pallas import tpu as pltpu
from jax.sharding import PartitionSpec as P

TEMPL = 48
HALF = 24
EPSILON = 1e-06
LANES = 128
SPLIT = 64
BLOCKS = 8
EACH = TEMPL // BLOCKS
CHUNKS = TEMPL * TEMPL // LANES
BLOCK_ROWS = EACH * CHUNKS + -EACH * CHUNKS % 16
HELD = (0, 4, 2, 6)
F32 = jnp.float32
BF16 = jnp.bfloat16


def two_parts(table):
    high = table.astype(ml_dtypes.bfloat16)
    low = (table - high.astype(np.float64)).astype(ml_dtypes.bfloat16)
    return high, low


def row_table(out_idx, in_idx, length, sign, factor, wide):
    theta = 2.0 * math.pi / length * np.outer(out_idx, in_idx)
    pad = np.zeros((-len(out_idx) % 8, len(in_idx)))
    full = np.concatenate([np.cos(theta), pad, sign * np.sin(theta), pad], axis=0) * factor
    high, low = two_parts(full)
    if wide:
        return np.concatenate([high, high, low], axis=1)
    zeros = np.zeros_like(low)
    return np.concatenate(
        [np.concatenate([high, high], axis=1), np.concatenate([low, zeros], axis=1)], axis=0
    )


def depth_table(in_idx, length, sign, factor):
    freq = np.arange(length // 2) + 0.5
    theta = 2.0 * math.pi / length * np.outer(in_idx, freq)
    out = np.zeros((len(in_idx), LANES))
    out[:, : length // 2] = np.cos(theta) * factor
    out[:, SPLIT : SPLIT + length // 2] = sign * np.sin(theta) * factor
    return out


def half_odd(count):
    return np.arange(count // 2) + 0.5


def make_tables(x_cells, y_cells, z_cells):
    n_x, n_y, n_z = x_cells + TEMPL, y_cells + HALF, z_cells + HALF
    k_x, k_y = half_odd(n_x), half_odd(n_y)
    both_x = np.concatenate([k_x, -k_x])
    both_y = np.stack([k_y, -k_y], axis=1).reshape(-1)
    mid_x, mid_y = (x_cells - 1) / 2, (y_cells - 1) / 2
    tables = {}
    slab = np.zeros((2 * z_cells, 4 * LANES), ml_dtypes.bfloat16)
    high, low = two_parts(depth_table(np.arange(z_cells), n_z, -1.0, 1.0))
    for j in range(2):
        rows = slice(j * z_cells, (j + 1) * z_cells)
        slab[rows, 2 * j * LANES : (2 * j + 1) * LANES] = high
        slab[rows, (2 * j + 1) * LANES : (2 * j + 2) * LANES] = low
    slab_y = row_table(k_y, np.arange(y_cells), n_y, -1.0, 1.0, True)
    slab_y = np.pad(slab_y, ((0, 0), (0, slab.shape[1] - slab_y.shape[1])))
    tables["slab_rows"] = np.concatenate([slab, slab_y], axis=0)
    own = np.arange(HALF, HALF + x_cells)
    halo = np.concatenate([np.arange(HALF), np.arange(HALF + x_cells, n_x)])
    tables["slab_x"] = row_table(k_x, np.concatenate([own, halo]), n_x, -1.0, 1.0, True)
    high, low = two_parts(depth_table(np.arange(TEMPL) - HALF, n_z, 1.0, 1.0))
    tables["tmpl_z"] = np.concatenate([high, low], axis=1)
    ones = (high.astype(np.float64) + low.astype(np.float64)).sum(axis=0)
    tables["ones_z"] = np.broadcast_to(ones.astype(np.float32)[None], (8, LANES)).copy()
    tables["tmpl_y"] = row_table(k_y, np.arange(TEMPL) - HALF + mid_y, n_y, 1.0, 1.0, True)
    tmpl_rows = np.arange(TEMPL).reshape(BLOCKS, EACH).T.reshape(-1)
    tables["tmpl_x"] = row_table(k_x, tmpl_rows + mid_x, n_x, 1.0, 1.0, True)
    tables["back_x"] = row_table(half_odd(x_cells), both_x, n_x, 1.0, 1.0 / n_x, False)
    tables["back_y"] = row_table(half_odd(y_cells), both_y, n_y, 1.0, 1.0 / n_y, False)
    back = depth_table(np.arange(z_cells), n_z, -1.0, 2.0 / n_z).T
    high, low = two_parts(back)
    back_z = np.zeros((2 * LANES, 2 * LANES), ml_dtypes.bfloat16)
    for j in range(2):
        rows = slice(j * LANES, (j + 1) * LANES)
        back_z[rows, j * z_cells : (j + 1) * z_cells] = high
        back_z[rows, LANES + j * z_cells : LANES + (j + 1) * z_cells] = low
    tables["back_z"] = back_z
    return tables


def split_rows(value, wide):
    high = value.astype(BF16)
    if value.shape[0] % 16 == 0:
        low = (value - high.astype(F32)).astype(BF16)
        return jnp.concatenate([high, low, high] if wide else [high, low], axis=0)
    high = high.astype(F32)
    low = value - high
    return jnp.concatenate([high, low, high] if wide else [high, low], axis=0).astype(BF16)


def swap(value):
    parts = [
        pltpu.roll(value[:, s : s + LANES], SPLIT, 1) for s in range(0, value.shape[1], LANES)
    ]
    return jnp.concatenate(parts, axis=1)


def lane_sign(width):
    lane = lax.broadcasted_iota(jnp.int32, (8, width), 1) % LANES
    return jnp.where(lane < SPLIT, -1.0, 1.0)[:1]


def pair_rows(table, value, wide):
    return pair_dot(table, split_rows(value, wide), wide)


def pair_dot(table, parts, wide):
    out = jnp.dot(table, parts, preferred_element_type=F32)
    if not wide:
        half = out.shape[0] // 2
        out = out[:half] + out[half:]
    half = out.shape[0] // 2
    turned = swap(out[half:]) * lane_sign(out.shape[1])
    return out[:half] + turned, out[:half] - turned


def pick(ref, firsts, count, stride):
    return jnp.concatenate([ref[pl.ds(f, count, stride=stride), :] for f in firsts], axis=1)


def store(ref, start, value):
    ref[pl.ds(start, value.shape[0]), :] = value


def odd(rows):
    return rows + 1


def lane_block(value, i):
    return value[:, i * LANES : (i + 1) * LANES]


def loop(count, body):
    def one(i, carry):
        body(i)
        return carry

    lax.fori_loop(0, count, one, 0)


GROUP = 8


def pipeline(steps, stages, width):
    blocks = -(-steps // width)
    depth = len(stages)

    def turn(t, static):
        for s in reversed(range(depth)):
            if static and not 0 <= t - s < blocks:
                continue
            for slot in range(width):
                step = (t - s) * width + slot
                if not static or step < steps:
                    stages[s](step, slot)

    full = steps // width
    first, last = depth - 1, max(full, depth - 1)
    for t in range(first):
        turn(t, True)
    if last - first >= 2:
        loop(last - first, lambda i: turn(i + first, False))
    else:
        last = first
    for t in range(last, blocks + depth - 1):
        turn(t, True)


def slab_rows_kernel(dims, place_ref, *refs):
    *sources, table_ref, rows_ref, depth_buf, parts_buf = refs
    x_cells, y_cells, z_cells = dims
    base = 0
    if len(sources) > 1:
        own_ref, *sources = sources
        base = own_ref.shape[0]
        rows_ref[:base, :] = own_ref[...]
    half = x_cells // 2
    count = depth_buf.shape[0] // y_cells - 1
    n_y = y_cells + HALF
    pad_y = n_y // 2 + -(n_y // 2) % 8
    many = 4

    def read(lanes):
        if len(sources) == 1:
            return sources[0][:, lanes].astype(F32)
        first = (place_ref[0] & 1) == 0
        mine, other = ([ref[i, :, lanes].astype(F32) for i in range(2)] for ref in sources)
        low, high = (
            jnp.concatenate([jnp.where(first, m, o), jnp.where(first, o, m)], axis=0)
            for m, o in zip(mine, other)
        )
        return jnp.concatenate([low[x_cells - HALF :], high[:HALF]], axis=0)

    def depth_step(i):
        lanes = [pl.ds(pl.multiple_of((many * i + u) * LANES, LANES), LANES) for u in range(many)]
        block = jnp.concatenate([read(l) for l in lanes], axis=0).astype(BF16)
        out = jnp.dot(block, table_ref[: 2 * z_cells], preferred_element_type=F32)
        for u in range(many):
            part = out[u * count : (u + 1) * count]
            for j in range(2):
                store(
                    depth_buf, (2 * many * i + 2 * u + j) * odd(count),
                    lane_block(part, 2 * j) + lane_block(part, 2 * j + 1),
                )

    def two_depth_steps(i):
        depth_step(2 * i)
        depth_step(2 * i + 1)

    loop(y_cells // (4 * many), two_depth_steps)

    def gather_rows(i, slot):
        value = pick(depth_buf, [GROUP * i + u for u in range(GROUP)], y_cells, odd(count))
        parts_buf[slot] = split_rows(value, True)

    def y_step(i, slot):
        plus, minus = pair_dot(table_ref[2 * z_cells :, : 3 * y_cells], parts_buf[slot], True)
        for u in range(GROUP):
            start = base + (GROUP * i + u) * odd(2 * pad_y)
            store(rows_ref, start, lane_block(plus, u))
            store(rows_ref, start + pad_y, lane_block(minus, u))

    pipeline(count // GROUP, [gather_rows, y_step], 3)


def slab_rows(place, blocks, count, passed, dims, tables, name):
    x_cells, y_cells, z_cells = dims
    n_y = y_cells + HALF
    pad_y = n_y // 2 + -(n_y // 2) % 8
    vmem = pl.BlockSpec(memory_space=pltpu.VMEM)
    return pl.pallas_call(
        functools.partial(slab_rows_kernel, dims),
        out_shape=jax.ShapeDtypeStruct(((passed + count) * odd(2 * pad_y), LANES), F32),
        in_specs=[pl.BlockSpec(memory_space=pltpu.SMEM)] + [vmem] * (1 + len(blocks)),
        out_specs=vmem,
        scratch_shapes=[
            pltpu.VMEM((y_cells * odd(count), LANES), F32),
            pltpu.VMEM((3, 3 * y_cells, GROUP * LANES), BF16),
        ],
        compiler_params=pltpu.CompilerParams(vmem_limit_bytes=12 * 1024 * 1024),
        cost_estimate=pl.CostEstimate(flops=count * 10**8, bytes_accessed=10**6, transcendentals=0),
        name=name,
    )(place, *blocks, tables["slab_rows"])


def slab_x_kernel(
    dims, rows_ref, x_ref, valid_ref, tz_ref, spec_ref, mask_ref, z_ref, parts_buf
):
    x_cells, y_cells, z_cells = dims
    n_y = y_cells + HALF
    pad_y = n_y // 2 + -(n_y // 2) % 8

    def gather_rows(i, slot):
        firsts = [GROUP // 2 * i + u // 2 + u % 2 * pad_y for u in range(GROUP)]
        value = pick(rows_ref, firsts, x_cells + TEMPL, odd(2 * pad_y))
        parts_buf[slot] = split_rows(value, True)

    def x_step(i, slot):
        plus, minus = pair_dot(x_ref[...], parts_buf[slot], True)
        spec = jnp.concatenate([plus, minus], axis=0)
        turned = swap(spec)
        real_lane = lane_sign(GROUP * LANES) < 0
        spec_ref[i, 0] = jnp.where(real_lane, spec, turned)
        spec_ref[i, 1] = jnp.where(real_lane, -turned, spec)

    pipeline(n_y // GROUP, [gather_rows, x_step], 4)

    valid = valid_ref[...].astype(F32)
    low_lane = lax.broadcasted_iota(jnp.int32, (x_cells, LANES), 1) < z_cells
    for q in range(y_cells // 2):
        mask_ref[q] = jnp.where(low_lane, valid[:, 2 * q : 2 * q + 1], valid[:, 2 * q + 1 : 2 * q + 2])
    z_ref[...] = jnp.zeros(z_ref.shape, BF16)
    for j in range(8):
        start = TEMPL * j - (LANES if j >= 4 else 0)
        z_ref[j, start : start + TEMPL, :] = tz_ref[...]


def slab_x(rows, valid, dims, tables):
    x_cells, y_cells, z_cells = dims
    n_x, n_y = x_cells + TEMPL, y_cells + HALF
    steps = n_y // GROUP
    vmem = pl.BlockSpec(memory_space=pltpu.VMEM)
    shape = (steps, 2, n_x, GROUP * LANES)
    return pl.pallas_call(
        functools.partial(slab_x_kernel, dims),
        out_shape=(
            jax.ShapeDtypeStruct(shape, F32),
            jax.ShapeDtypeStruct((y_cells // 2, x_cells, LANES), F32),
            jax.ShapeDtypeStruct((8, 2 * LANES, 2 * LANES), BF16),
        ),
        in_specs=[vmem] * 4,
        out_specs=(vmem,) * 3,
        scratch_shapes=[pltpu.VMEM((4, 3 * n_x, GROUP * LANES), BF16)],
        compiler_params=pltpu.CompilerParams(vmem_limit_bytes=9 * 1024 * 1024),
        cost_estimate=pl.CostEstimate(flops=5 * 10**9, bytes_accessed=10**6, transcendentals=0),
        name="slab_x",
    )(rows, tables["slab_x"], valid, tables["tmpl_z"])


def corr_kernel(
    dims, rot, entry, place_ref, tile_ref, *refs
):
    if rot > 0:
        before_ref, *refs = refs
    held_ref, last_ref, mask_ref, spec_ref, z_ref, ones_ref, y_ref, x_ref, bx_ref, by_ref, bz_ref, *refs = refs
    mines_ref, side_ref, far_ref, stat_ref, *refs = refs
    bank_buf, depth_buf, rows_buf, first_buf, second_buf, third_buf, back_buf, vol_buf = refs
    if rot > 0:
        mines_ref[:rot] = before_ref[...]
    x_cells, y_cells, z_cells = dims
    n_x, n_y = x_cells + TEMPL, y_cells + HALF
    half_y = n_y // 2
    pad_y = half_y + -half_y % 8
    for i, block in enumerate(HELD):
        for ref, at, tile in ((held_ref, rot, block), (last_ref, entry, block ^ 1)):
            store(bank_buf, (tile_ref[0] ^ tile) * odd(BLOCK_ROWS), ref[at, i].astype(F32))
    tmpl = jnp.concatenate(
        [
            pick(bank_buf, [a * CHUNKS + i for i in range(CHUNKS)], BLOCKS, odd(BLOCK_ROWS))
            for a in range(EACH)
        ],
        axis=0,
    )
    inv_size = 1.0 / TEMPL**3
    mean = jnp.sum(tmpl) * inv_size
    centred = tmpl - mean
    var = jnp.sum(centred * centred) * inv_size
    scale = 1.0 / (jnp.sqrt(jnp.full((1, LANES), var + EPSILON, F32)) * TEMPL**1.5)
    shift = ones_ref[:1] * mean

    wide = 8 * TEMPL
    narrow = tmpl.astype(BF16)
    block = jnp.concatenate(
        [narrow[:, g * wide : (g + 1) * wide] for g in range(TEMPL // 8)], axis=0
    )
    for j in range(8):
        window = block[:, : 2 * LANES] if j < 4 else block[:, LANES:]
        out = jnp.dot(window, z_ref[j], preferred_element_type=F32)
        part = out[:, :LANES] + out[:, LANES:] - shift
        for g in range(TEMPL // 8):
            start = (8 * g + j) * odd(TEMPL)
            store(depth_buf, start, part[g * TEMPL : (g + 1) * TEMPL])

    def gather_a(i, slot):
        value = pick(depth_buf, [GROUP * i + u for u in range(GROUP)], TEMPL, odd(TEMPL))
        first_buf[slot] = split_rows(value, True)

    def y_step(i, slot):
        plus, minus = pair_dot(y_ref[...], first_buf[slot], True)
        for u in range(GROUP):
            start = (GROUP * i + u) * odd(2 * pad_y)
            store(rows_buf, start, lane_block(plus, u))
            store(rows_buf, start + pad_y, lane_block(minus, u))

    pipeline(TEMPL // GROUP, [gather_a, y_step], 6)

    def gather_ky(i, slot):
        firsts = [GROUP // 2 * i + u // 2 + u % 2 * pad_y for u in range(GROUP)]
        first_buf[slot] = split_rows(pick(rows_buf, firsts, TEMPL, odd(2 * pad_y)), True)

    def multiply(i, slot):
        plus, minus = pair_dot(x_ref[...], first_buf[slot], True)
        spec = jnp.concatenate([plus, minus], axis=0)
        prod = spec * spec_ref[i, 0] + swap(spec) * spec_ref[i, 1]
        second_buf[slot] = split_rows(prod, False)

    def back_x(i, slot):
        plus, minus = pair_dot(bx_ref[...], second_buf[slot], False)
        for u in range(GROUP):
            start = (GROUP * i + u) * odd(x_cells)
            store(back_buf, start, lane_block(plus, u))
            store(back_buf, start + x_cells // 2, lane_block(minus, u))

    pipeline(n_y // GROUP, [gather_ky, multiply, back_x], 4)

    def gather_x(i, slot):
        value = pick(back_buf, [GROUP * i + u for u in range(GROUP)], n_y, odd(x_cells))
        third_buf[slot] = split_rows(value, False)

    def back_y(i, slot):
        plus, minus = pair_dot(by_ref[...], third_buf[slot], False)
        for u in range(GROUP):
            row = GROUP * i + u
            x = jnp.where(row < x_cells // 2, row + x_cells // 2, x_cells - 1 - row)
            store(vol_buf, x * odd(y_cells), lane_block(plus, u))
            store(vol_buf, x * odd(y_cells) + y_cells // 2, lane_block(minus, u))

    pipeline(x_cells // GROUP, [gather_x, back_y], 4)

    share = y_cells // 8
    me = place_ref[0]
    total = jnp.zeros((x_cells, LANES), F32)
    number = jnp.zeros((x_cells, LANES), F32)
    targets = [mines_ref.at[rot], side_ref, far_ref.at[0], far_ref.at[1]]
    for p, target in enumerate(targets):
        first = (me ^ p) * share
        values = []
        for i in range(share):
            firsts = []
            for j in range(2):
                y = 2 * (first + i) + j
                firsts.append(jnp.where(y < y_cells // 2, y_cells - 1 - y, y - y_cells // 2))
            values.append(pick(vol_buf, firsts, x_cells, odd(y_cells)))
        value = jnp.concatenate(values, axis=0)
        out = jnp.dot(split_rows(value, False), bz_ref[...], preferred_element_type=F32)
        rows = value.shape[0]
        full = out[:rows, :LANES] + out[:rows, LANES:] + out[rows:, :LANES]
        for i in range(share):
            corr = full[i * x_cells : (i + 1) * x_cells] * scale
            target[:, i * LANES : (i + 1) * LANES] = corr
            mask = mask_ref[first + i]
            total = total + corr * mask
            number = number + mask
    number_sum = jnp.sum(number)
    total_sum = jnp.sum(total)
    local_mean = jnp.full((1, LANES), total_sum, F32) / jnp.maximum(number_sum, 1.0)
    square = jnp.zeros((x_cells, LANES), F32)
    for p, target in enumerate(targets):
        first = (me ^ p) * share
        for i in range(share):
            gap = target[:, i * LANES : (i + 1) * LANES] - local_mean
            square = square + gap * gap * mask_ref[first + i]
    row = lax.broadcasted_iota(jnp.int32, (8, LANES), 0)
    stat_ref[...] = jnp.where(row == 0, number_sum, jnp.where(row == 1, total_sum, jnp.sum(square)))


def correlate(mines, place, tile, held, rot, last, entry, mask, spec, tmpl_z, dims, tables):
    x_cells, y_cells, z_cells = dims
    n_x, n_y = x_cells + TEMPL, y_cells + HALF
    pad_y = n_y // 2 + -(n_y // 2) % 8
    width = y_cells * z_cells // 4
    before = [] if mines is None else [mines]
    vmem = pl.BlockSpec(memory_space=pltpu.VMEM)
    return pl.pallas_call(
        functools.partial(corr_kernel, dims, rot, entry),
        out_shape=(
            jax.ShapeDtypeStruct((rot + 1, x_cells, width), F32),
            jax.ShapeDtypeStruct((x_cells, width), F32),
            jax.ShapeDtypeStruct((2, x_cells, width), F32),
            jax.ShapeDtypeStruct((8, LANES), F32),
        ),
        in_specs=[pl.BlockSpec(memory_space=pltpu.SMEM)] * 2 + [vmem] * (11 + len(before)),
        out_specs=(vmem,) * 4,
        scratch_shapes=[
            pltpu.VMEM((BLOCKS * odd(BLOCK_ROWS), LANES), F32),
            pltpu.VMEM((TEMPL * odd(TEMPL), LANES), F32),
            pltpu.VMEM((TEMPL * odd(2 * pad_y), LANES), F32),
            pltpu.VMEM((6, 3 * TEMPL, GROUP * LANES), BF16),
            pltpu.VMEM((4, 2 * n_x, GROUP * LANES), BF16),
            pltpu.VMEM((4, 2 * n_y, GROUP * LANES), BF16),
            pltpu.VMEM((n_y * odd(x_cells), LANES), F32),
            pltpu.VMEM((x_cells * odd(y_cells), LANES), F32),
        ],
        compiler_params=pltpu.CompilerParams(vmem_limit_bytes=20 * 1024 * 1024),
        cost_estimate=pl.CostEstimate(flops=15 * 10**9, bytes_accessed=10**7, transcendentals=0),
        name="correlate",
    )(
        place, tile, *before, held, last, mask, spec,
        tmpl_z, tables["ones_z"], tables["tmpl_y"], tables["tmpl_x"],
        tables["back_x"], tables["back_y"], tables["back_z"],
    )


def score_kernel(pieces, place_ref, coef_ref, mask_ref, *refs):
    best_ref, evid_ref, mom_ref = refs[-3:]
    blocks = best_ref.shape[1] // LANES

    def step(i):
        lanes = pl.ds(pl.multiple_of(i * LANES, LANES), LANES)

        def score(k):
            at, entry = pieces[k]
            return (refs[at][entry, :, lanes] - coef_ref[k, 0]) * coef_ref[k, 1]

        mask = mask_ref[place_ref[0] * blocks + i]
        high = functools.reduce(jnp.maximum, [score(k) for k in range(len(pieces))])
        total = jnp.zeros_like(high)
        moment = [jnp.zeros_like(high) for _ in range(4)]
        for k in range(len(pieces)):
            weight = jnp.exp(score(k) - high)
            total = total + weight
            for c in range(4):
                moment[c] = moment[c] + weight * coef_ref[k, 2 + c]
        best_ref[:, lanes] = mask * high
        evid_ref[:, lanes] = mask * (high + jnp.log(total))
        share = mask / total
        for c in range(4):
            mom_ref[c, :, lanes] = moment[c] * share

    def two_steps(i):
        step(2 * i)
        step(2 * i + 1)

    loop(blocks // 2, two_steps)


def combine(place, coefs, mask, arrays, pieces):
    shape = arrays[0].shape[1:]
    vmem = pl.BlockSpec(memory_space=pltpu.VMEM)
    out = jax.ShapeDtypeStruct(shape, F32)
    return pl.pallas_call(
        functools.partial(score_kernel, pieces),
        out_shape=(out, out, jax.ShapeDtypeStruct((4,) + shape, F32)),
        in_specs=[pl.BlockSpec(memory_space=pltpu.SMEM)] * 2 + [vmem] * (1 + len(arrays)),
        out_specs=(vmem,) * 3,
        compiler_params=pltpu.CompilerParams(vmem_limit_bytes=4 * 1024 * 1024),
        name="combine",
    )(place, coefs, mask, *arrays)


def pack_kernel(after_ref, *refs):
    *sources, out_ref = refs
    for i, source in enumerate(sources):
        out_ref[i] = source[...] if len(source.shape) == 2 else source[1]


def pack(after, sides, fars):
    vmem = pl.BlockSpec(memory_space=pltpu.VMEM)
    count = len(sides) + len(fars)
    return pl.pallas_call(
        pack_kernel,
        out_shape=jax.ShapeDtypeStruct((count,) + sides[0].shape, F32),
        in_specs=[pl.BlockSpec(memory_space=pl.ANY)] + [vmem] * count,
        out_specs=vmem,
        compiler_params=pltpu.CompilerParams(vmem_limit_bytes=8 * 1024 * 1024),
        name="pack",
    )(after, *sides, *fars)


def swap_blocks(block, axis, step):
    return lax.ppermute(block, axis, [(i, i ^ step) for i in range(lax.axis_size(axis))])


def general_gather(templates):
    rots = templates.shape[0]
    count = lax.axis_size("tile")
    block = templates[:, None]
    for step in [1 << i for i in reversed(range(count.bit_length() - 1))]:
        other = swap_blocks(block, "tile", step)
        upper = (lax.axis_index("tile") & step) != 0
        pair = [jnp.where(upper, other, block), jnp.where(upper, block, other)]
        block = jnp.stack(pair, axis=2).reshape((rots, -1) + block.shape[2:])
    block = block.reshape(rots, BLOCKS, EACH * CHUNKS, LANES)
    block = jnp.pad(block, ((0, 0), (0, 0), (0, BLOCK_ROWS - EACH * CHUNKS), (0, 0)))
    held = jnp.stack([block[:, i] for i in HELD], axis=1)
    return held, jnp.stack([block[:, i ^ 1] for i in HELD], axis=1)


def merge(first, other):
    number_a, number_b = first[:1], other[:1]
    mean_a = first[1:2] / jnp.maximum(number_a, 1.0)
    mean_b = other[1:2] / jnp.maximum(number_b, 1.0)
    gap = mean_b - mean_a
    between = gap * gap * (number_a * number_b / jnp.maximum(number_a + number_b, 1.0))
    return first + other + jnp.where(jnp.arange(3)[:, None] == 2, between, 0.0)


def exchange_all(block, axis, low, high):
    count = lax.axis_size(axis)
    parts = [block]
    for step in range(low, high, low):
        parts.append(lax.ppermute(block, axis, [(i, i ^ step) for i in range(count)]))
    return jnp.stack(parts)


def neighbours(block, axis):
    count = lax.axis_size(axis)
    forward = [(i, i + 1) for i in range(count - 1)]
    backward = [(target, source) for source, target in forward]
    return lax.ppermute(block, axis, forward), lax.ppermute(block, axis, backward)


def local(tomogram, templates, valid, quats, rot_index):
    x_cells, voxels = tomogram.shape
    y_cells = valid.shape[1]
    z_cells = voxels // y_cells
    dims = (x_cells, y_cells, z_cells)
    tables = {name: jnp.asarray(table) for name, table in make_tables(*dims).items()}
    groups = lax.axis_size("rot")
    tiles = lax.axis_size("tile")
    me = lax.axis_index("rot")
    rots = templates.shape[0]

    tile = lax.axis_index("tile")
    by_blocks = tiles == BLOCKS
    if by_blocks:
        held = templates.reshape(rots, 1, EACH * CHUNKS, LANES)
        held = jnp.pad(held, ((0, 0), (0, 0), (0, BLOCK_ROWS - EACH * CHUNKS), (0, 0)))
        held, tomogram_after = lax.optimization_barrier((held, tomogram))
        held = jnp.concatenate([held, swap_blocks(held, "tile", 4)], axis=1)
    else:
        tomogram_after = tomogram
    half = x_cells // 2
    piece = lax.dynamic_slice_in_dim(tomogram_after, (me & 1) * half, half, 0)
    mine = jnp.stack(neighbours(piece, "tile"))
    side_swap = [(i, i ^ 1) for i in range(groups)]
    other = lax.ppermute(mine, "rot", side_swap)
    if by_blocks:
        second = swap_blocks(held, "tile", 2)
    else:
        held, last = general_gather(templates)
        tile = jnp.zeros_like(tile)
    one_hot = (rot_index[:, None] == jnp.arange(quats.shape[1], dtype=jnp.int32)[None, :]).astype(F32)
    orient = jnp.einsum("rq,kq->rk", one_hot, quats, precision=lax.Precision.HIGHEST)
    place = me_place = jnp.reshape(me, (1,)).astype(jnp.int32)
    tile = jnp.reshape(tile, (1,)).astype(jnp.int32)
    own = slab_rows(place, [tomogram], x_cells, 0, dims, tables, "slab_own")
    rows = slab_rows(place, [own, mine, other], TEMPL, x_cells, dims, tables, "slab_halo")
    if by_blocks:
        second = jnp.where(rows[0, 0] < 1e9, second, jnp.zeros_like(second))
        held = jnp.concatenate([held, second], axis=1)
        lasts = [swap_blocks(held[:1], "tile", 1), swap_blocks(held[1:], "tile", 1)]
    else:
        lasts = [last[:1], last[1:]]
    spec, mask, tmpl_z = slab_x(rows, valid, dims, tables)
    far_swap = [(i, i ^ 2) for i in range(groups)]
    mines, sides, fars, stats = None, [], [], []
    for r in range(rots):
        if r >= 2:
            place, fars[r - 2] = lax.optimization_barrier((place, fars[r - 2]))
        mines, side, far, stat = correlate(
            mines, place, tile, held, r, lasts[min(r, 1)], max(r - 1, 0), mask, spec, tmpl_z, dims, tables
        )
        if r >= 1:
            stat, fars[r - 1] = lax.optimization_barrier((stat, fars[r - 1]))
        sides.append(side)
        stats.append(stat[:3, 0])
        fars.append(lax.ppermute(far, "rot", far_swap))
        if r == rots - 2:
            early = jnp.stack(sides[:-1] + [f[1] for f in fars[:-1]])
            early = lax.ppermute(early, "rot", side_swap)
    state = jnp.stack(stats, axis=1)
    state, early, fars[rots - 2] = lax.optimization_barrier((state, early, fars[rots - 2]))
    step = 1
    while step < tiles:
        partner = lax.ppermute(state, "tile", [(i, i ^ step) for i in range(tiles)])
        if step * 4 == tiles:
            last = pack(partner, sides[rots - 2 :], fars[rots - 2 :])
        if step * 2 == tiles:
            partner, last = lax.optimization_barrier((partner, last))
        state = merge(state, partner)
        step *= 2
    average = state[1] / state[0]
    inverse = 1.0 / jnp.sqrt(state[2] / state[0] + EPSILON)
    coefs = jnp.concatenate([average[:, None], inverse[:, None], orient], axis=1)
    coefs = exchange_all(coefs, "rot", 1, groups)
    last = lax.ppermute(last, "rot", side_swap)
    arrays = [mines] + fars + [early, last]
    at_far, at_early, at_last = 1, 1 + rots, 2 + rots
    pieces = [(0, r) for r in range(rots)]
    pieces += [(at_early, r) for r in range(rots - 2)] + [(at_last, 0), (at_last, 1)]
    pieces += [(at_far + r, 0) for r in range(rots)]
    pieces += [(at_early, rots - 2 + r) for r in range(rots - 2)] + [(at_last, 2), (at_last, 3)]
    return combine(me_place, coefs.reshape(groups * rots, 6), mask, arrays, pieces)


def solution(mesh):
    placed = (P("tile", None), P("rot", "tile"), P("tile", None), P(), P("rot"))
    return jax.shard_map(
        local,
        mesh=mesh,
        in_specs=placed,
        out_specs=(P("tile", "rot"), P("tile", "rot"), P(None, "tile", "rot")),
        check_vma=False,
    )
```

```python
import functools
import math

import jax
import jax.numpy as jnp
import ml_dtypes
import numpy as np
from jax import lax
from jax.experimental import pallas as pl
from jax.experimental.pallas import tpu as pltpu
from jax.sharding import PartitionSpec as P

TEMPL = 48
HALF = 24
EPSILON = 1e-06
LANES = 128
SPLIT = 64
BLOCKS = 8
EACH = TEMPL // BLOCKS
CHUNKS = TEMPL * TEMPL // LANES
BLOCK_ROWS = EACH * CHUNKS + -EACH * CHUNKS % 16
HELD = (0, 4, 2, 6)
F32 = jnp.float32
BF16 = jnp.bfloat16


def two_parts(table):
    high = table.astype(ml_dtypes.bfloat16)
    low = (table - high.astype(np.float64)).astype(ml_dtypes.bfloat16)
    return high, low


def row_table(out_idx, in_idx, length, sign, factor, wide):
    theta = 2.0 * math.pi / length * np.outer(out_idx, in_idx)
    pad = np.zeros((-len(out_idx) % 8, len(in_idx)))
    full = np.concatenate([np.cos(theta), pad, sign * np.sin(theta), pad], axis=0) * factor
    high, low = two_parts(full)
    if wide:
        return np.concatenate([high, high, low], axis=1)
    zeros = np.zeros_like(low)
    return np.concatenate(
        [np.concatenate([high, high], axis=1), np.concatenate([low, zeros], axis=1)], axis=0
    )


def depth_table(in_idx, length, sign, factor):
    freq = np.arange(length // 2) + 0.5
    theta = 2.0 * math.pi / length * np.outer(in_idx, freq)
    out = np.zeros((len(in_idx), LANES))
    out[:, : length // 2] = np.cos(theta) * factor
    out[:, SPLIT : SPLIT + length // 2] = sign * np.sin(theta) * factor
    return out


def half_odd(count):
    return np.arange(count // 2) + 0.5


def make_tables(x_cells, y_cells, z_cells):
    n_x, n_y, n_z = x_cells + TEMPL, y_cells + HALF, z_cells + HALF
    k_x, k_y = half_odd(n_x), half_odd(n_y)
    both_x = np.concatenate([k_x, -k_x])
    both_y = np.stack([k_y, -k_y], axis=1).reshape(-1)
    mid_x, mid_y = (x_cells - 1) / 2, (y_cells - 1) / 2
    tables = {}
    slab = np.zeros((2 * z_cells, 4 * LANES), ml_dtypes.bfloat16)
    high, low = two_parts(depth_table(np.arange(z_cells), n_z, -1.0, 1.0))
    for j in range(2):
        rows = slice(j * z_cells, (j + 1) * z_cells)
        slab[rows, 2 * j * LANES : (2 * j + 1) * LANES] = high
        slab[rows, (2 * j + 1) * LANES : (2 * j + 2) * LANES] = low
    slab_y = row_table(k_y, np.arange(y_cells), n_y, -1.0, 1.0, True)
    slab_y = np.pad(slab_y, ((0, 0), (0, slab.shape[1] - slab_y.shape[1])))
    tables["slab_rows"] = np.concatenate([slab, slab_y], axis=0)
    own = np.arange(HALF, HALF + x_cells)
    halo = np.concatenate([np.arange(HALF), np.arange(HALF + x_cells, n_x)])
    tables["slab_x"] = row_table(k_x, np.concatenate([own, halo]), n_x, -1.0, 1.0, True)
    high, low = two_parts(depth_table(np.arange(TEMPL) - HALF, n_z, 1.0, 1.0))
    tables["tmpl_z"] = np.concatenate([high, low], axis=1)
    ones = (high.astype(np.float64) + low.astype(np.float64)).sum(axis=0)
    tables["ones_z"] = np.broadcast_to(ones.astype(np.float32)[None], (8, LANES)).copy()
    tables["tmpl_y"] = row_table(k_y, np.arange(TEMPL) - HALF + mid_y, n_y, 1.0, 1.0, True)
    tmpl_rows = np.arange(TEMPL).reshape(BLOCKS, EACH).T.reshape(-1)
    tables["tmpl_x"] = row_table(k_x, tmpl_rows + mid_x, n_x, 1.0, 1.0, True)
    tables["back_x"] = row_table(half_odd(x_cells), both_x, n_x, 1.0, 1.0 / n_x, False)
    tables["back_y"] = row_table(half_odd(y_cells), both_y, n_y, 1.0, 1.0 / n_y, False)
    back = depth_table(np.arange(z_cells), n_z, -1.0, 2.0 / n_z).T
    high, low = two_parts(back)
    back_z = np.zeros((2 * LANES, 2 * LANES), ml_dtypes.bfloat16)
    for j in range(2):
        rows = slice(j * LANES, (j + 1) * LANES)
        back_z[rows, j * z_cells : (j + 1) * z_cells] = high
        back_z[rows, LANES + j * z_cells : LANES + (j + 1) * z_cells] = low
    tables["back_z"] = back_z
    return tables


def split_rows(value, wide):
    high = value.astype(BF16)
    if value.shape[0] % 16 == 0:
        low = (value - high.astype(F32)).astype(BF16)
        return jnp.concatenate([high, low, high] if wide else [high, low], axis=0)
    high = high.astype(F32)
    low = value - high
    return jnp.concatenate([high, low, high] if wide else [high, low], axis=0).astype(BF16)


def swap(value):
    parts = [
        pltpu.roll(value[:, s : s + LANES], SPLIT, 1) for s in range(0, value.shape[1], LANES)
    ]
    return jnp.concatenate(parts, axis=1)


def lane_sign(width):
    lane = lax.broadcasted_iota(jnp.int32, (8, width), 1) % LANES
    return jnp.where(lane < SPLIT, -1.0, 1.0)[:1]


def pair_rows(table, value, wide):
    return pair_dot(table, split_rows(value, wide), wide)


def pair_dot(table, parts, wide):
    out = jnp.dot(table, parts, preferred_element_type=F32)
    if not wide:
        half = out.shape[0] // 2
        out = out[:half] + out[half:]
    half = out.shape[0] // 2
    turned = swap(out[half:]) * lane_sign(out.shape[1])
    return out[:half] + turned, out[:half] - turned


def pick(ref, firsts, count, stride):
    return jnp.concatenate([ref[pl.ds(f, count, stride=stride), :] for f in firsts], axis=1)


def store(ref, start, value):
    ref[pl.ds(start, value.shape[0]), :] = value


def odd(rows):
    return rows + 1


def lane_block(value, i):
    return value[:, i * LANES : (i + 1) * LANES]


def loop(count, body):
    def one(i, carry):
        body(i)
        return carry

    lax.fori_loop(0, count, one, 0)


GROUP = 8


def pipeline(steps, stages, width):
    blocks = -(-steps // width)
    depth = len(stages)

    def turn(t, static):
        for s in reversed(range(depth)):
            if static and not 0 <= t - s < blocks:
                continue
            for slot in range(width):
                step = (t - s) * width + slot
                if not static or step < steps:
                    stages[s](step, slot)

    full = steps // width
    first, last = depth - 1, max(full, depth - 1)
    for t in range(first):
        turn(t, True)
    if last - first >= 2:
        loop(last - first, lambda i: turn(i + first, False))
    else:
        last = first
    for t in range(last, blocks + depth - 1):
        turn(t, True)


def slab_rows_kernel(dims, place_ref, *refs):
    *sources, table_ref, rows_ref, depth_buf, parts_buf = refs
    x_cells, y_cells, z_cells = dims
    base = 0
    if len(sources) > 1:
        own_ref, *sources = sources
        base = own_ref.shape[0]
        rows_ref[:base, :] = own_ref[...]
    half = x_cells // 2
    count = depth_buf.shape[0] // y_cells - 1
    n_y = y_cells + HALF
    pad_y = n_y // 2 + -(n_y // 2) % 8
    many = 4

    def read(lanes):
        if len(sources) == 1:
            return sources[0][:, lanes].astype(F32)
        first = (place_ref[0] & 1) == 0
        mine, other = ([ref[i, :, lanes].astype(F32) for i in range(2)] for ref in sources)
        low, high = (
            jnp.concatenate([jnp.where(first, m, o), jnp.where(first, o, m)], axis=0)
            for m, o in zip(mine, other)
        )
        return jnp.concatenate([low[x_cells - HALF :], high[:HALF]], axis=0)

    def depth_step(i):
        lanes = [pl.ds(pl.multiple_of((many * i + u) * LANES, LANES), LANES) for u in range(many)]
        block = jnp.concatenate([read(l) for l in lanes], axis=0).astype(BF16)
        out = jnp.dot(block, table_ref[: 2 * z_cells], preferred_element_type=F32)
        for u in range(many):
            part = out[u * count : (u + 1) * count]
            for j in range(2):
                store(
                    depth_buf, (2 * many * i + 2 * u + j) * odd(count),
                    lane_block(part, 2 * j) + lane_block(part, 2 * j + 1),
                )

    def two_depth_steps(i):
        depth_step(2 * i)
        depth_step(2 * i + 1)

    loop(y_cells // (4 * many), two_depth_steps)

    def gather_rows(i, slot):
        value = pick(depth_buf, [GROUP * i + u for u in range(GROUP)], y_cells, odd(count))
        parts_buf[slot] = split_rows(value, True)

    def y_step(i, slot):
        plus, minus = pair_dot(table_ref[2 * z_cells :, : 3 * y_cells], parts_buf[slot], True)
        for u in range(GROUP):
            start = base + (GROUP * i + u) * odd(2 * pad_y)
            store(rows_ref, start, lane_block(plus, u))
            store(rows_ref, start + pad_y, lane_block(minus, u))

    pipeline(count // GROUP, [gather_rows, y_step], 3)


def slab_rows(place, blocks, count, passed, dims, tables, name):
    x_cells, y_cells, z_cells = dims
    n_y = y_cells + HALF
    pad_y = n_y // 2 + -(n_y // 2) % 8
    vmem = pl.BlockSpec(memory_space=pltpu.VMEM)
    return pl.pallas_call(
        functools.partial(slab_rows_kernel, dims),
        out_shape=jax.ShapeDtypeStruct(((passed + count) * odd(2 * pad_y), LANES), F32),
        in_specs=[pl.BlockSpec(memory_space=pltpu.SMEM)] + [vmem] * (1 + len(blocks)),
        out_specs=vmem,
        scratch_shapes=[
            pltpu.VMEM((y_cells * odd(count), LANES), F32),
            pltpu.VMEM((3, 3 * y_cells, GROUP * LANES), BF16),
        ],
        compiler_params=pltpu.CompilerParams(vmem_limit_bytes=12 * 1024 * 1024),
        cost_estimate=pl.CostEstimate(flops=count * 10**8, bytes_accessed=10**6, transcendentals=0),
        name=name,
    )(place, *blocks, tables["slab_rows"])


def slab_x_kernel(
    dims, rows_ref, x_ref, valid_ref, tz_ref, spec_ref, mask_ref, z_ref, parts_buf
):
    x_cells, y_cells, z_cells = dims
    n_y = y_cells + HALF
    pad_y = n_y // 2 + -(n_y // 2) % 8

    def gather_rows(i, slot):
        firsts = [GROUP // 2 * i + u // 2 + u % 2 * pad_y for u in range(GROUP)]
        value = pick(rows_ref, firsts, x_cells + TEMPL, odd(2 * pad_y))
        parts_buf[slot] = split_rows(value, True)

    def x_step(i, slot):
        plus, minus = pair_dot(x_ref[...], parts_buf[slot], True)
        spec = jnp.concatenate([plus, minus], axis=0)
        turned = swap(spec)
        real_lane = lane_sign(GROUP * LANES) < 0
        spec_ref[i, 0] = jnp.where(real_lane, spec, turned)
        spec_ref[i, 1] = jnp.where(real_lane, -turned, spec)

    pipeline(n_y // GROUP, [gather_rows, x_step], 4)

    valid = valid_ref[...].astype(F32)
    low_lane = lax.broadcasted_iota(jnp.int32, (x_cells, LANES), 1) < z_cells
    for q in range(y_cells // 2):
        mask_ref[q] = jnp.where(low_lane, valid[:, 2 * q : 2 * q + 1], valid[:, 2 * q + 1 : 2 * q + 2])
    z_ref[...] = jnp.zeros(z_ref.shape, BF16)
    for j in range(8):
        start = TEMPL * j - (LANES if j >= 4 else 0)
        z_ref[j, start : start + TEMPL, :] = tz_ref[...]


def slab_x(rows, valid, dims, tables):
    x_cells, y_cells, z_cells = dims
    n_x, n_y = x_cells + TEMPL, y_cells + HALF
    steps = n_y // GROUP
    vmem = pl.BlockSpec(memory_space=pltpu.VMEM)
    shape = (steps, 2, n_x, GROUP * LANES)
    return pl.pallas_call(
        functools.partial(slab_x_kernel, dims),
        out_shape=(
            jax.ShapeDtypeStruct(shape, F32),
            jax.ShapeDtypeStruct((y_cells // 2, x_cells, LANES), F32),
            jax.ShapeDtypeStruct((8, 2 * LANES, 2 * LANES), BF16),
        ),
        in_specs=[vmem] * 4,
        out_specs=(vmem,) * 3,
        scratch_shapes=[pltpu.VMEM((4, 3 * n_x, GROUP * LANES), BF16)],
        compiler_params=pltpu.CompilerParams(vmem_limit_bytes=9 * 1024 * 1024),
        cost_estimate=pl.CostEstimate(flops=5 * 10**9, bytes_accessed=10**6, transcendentals=0),
        name="slab_x",
    )(rows, tables["slab_x"], valid, tables["tmpl_z"])


def corr_kernel(
    dims, rot, entry, place_ref, tile_ref, *refs
):
    if rot > 0:
        before_ref, *refs = refs
    held_ref, last_ref, mask_ref, spec_ref, z_ref, ones_ref, y_ref, x_ref, bx_ref, by_ref, bz_ref, *refs = refs
    mines_ref, side_ref, far_ref, stat_ref, *refs = refs
    bank_buf, depth_buf, rows_buf, first_buf, second_buf, third_buf, back_buf, vol_buf = refs
    if rot > 0:
        mines_ref[:rot] = before_ref[...]
    x_cells, y_cells, z_cells = dims
    n_x, n_y = x_cells + TEMPL, y_cells + HALF
    half_y = n_y // 2
    pad_y = half_y + -half_y % 8
    for i, block in enumerate(HELD):
        for ref, at, tile in ((held_ref, rot, block), (last_ref, entry, block ^ 1)):
            store(bank_buf, (tile_ref[0] ^ tile) * odd(BLOCK_ROWS), ref[at, i].astype(F32))
    tmpl = jnp.concatenate(
        [
            pick(bank_buf, [a * CHUNKS + i for i in range(CHUNKS)], BLOCKS, odd(BLOCK_ROWS))
            for a in range(EACH)
        ],
        axis=0,
    )
    inv_size = 1.0 / TEMPL**3
    mean = jnp.sum(tmpl) * inv_size
    centred = tmpl - mean
    var = jnp.sum(centred * centred) * inv_size
    scale = 1.0 / (jnp.sqrt(jnp.full((1, LANES), var + EPSILON, F32)) * TEMPL**1.5)
    shift = ones_ref[:1] * mean

    wide = 8 * TEMPL
    narrow = tmpl.astype(BF16)
    block = jnp.concatenate(
        [narrow[:, g * wide : (g + 1) * wide] for g in range(TEMPL // 8)], axis=0
    )
    for j in range(8):
        window = block[:, : 2 * LANES] if j < 4 else block[:, LANES:]
        out = jnp.dot(window, z_ref[j], preferred_element_type=F32)
        part = out[:, :LANES] + out[:, LANES:] - shift
        for g in range(TEMPL // 8):
            start = (8 * g + j) * odd(TEMPL)
            store(depth_buf, start, part[g * TEMPL : (g + 1) * TEMPL])

    def gather_a(i, slot):
        value = pick(depth_buf, [GROUP * i + u for u in range(GROUP)], TEMPL, odd(TEMPL))
        first_buf[slot] = split_rows(value, True)

    def y_step(i, slot):
        plus, minus = pair_dot(y_ref[...], first_buf[slot], True)
        for u in range(GROUP):
            start = (GROUP * i + u) * odd(2 * pad_y)
            store(rows_buf, start, lane_block(plus, u))
            store(rows_buf, start + pad_y, lane_block(minus, u))

    pipeline(TEMPL // GROUP, [gather_a, y_step], 6)

    def gather_ky(i, slot):
        firsts = [GROUP // 2 * i + u // 2 + u % 2 * pad_y for u in range(GROUP)]
        first_buf[slot] = split_rows(pick(rows_buf, firsts, TEMPL, odd(2 * pad_y)), True)

    def multiply(i, slot):
        plus, minus = pair_dot(x_ref[...], first_buf[slot], True)
        spec = jnp.concatenate([plus, minus], axis=0)
        prod = spec * spec_ref[i, 0] + swap(spec) * spec_ref[i, 1]
        second_buf[slot] = split_rows(prod, False)

    def back_x(i, slot):
        plus, minus = pair_dot(bx_ref[...], second_buf[slot], False)
        for u in range(GROUP):
            start = (GROUP * i + u) * odd(x_cells)
            store(back_buf, start, lane_block(plus, u))
            store(back_buf, start + x_cells // 2, lane_block(minus, u))

    pipeline(n_y // GROUP, [gather_ky, multiply, back_x], 4)

    def gather_x(i, slot):
        value = pick(back_buf, [GROUP * i + u for u in range(GROUP)], n_y, odd(x_cells))
        third_buf[slot] = split_rows(value, False)

    def back_y(i, slot):
        plus, minus = pair_dot(by_ref[...], third_buf[slot], False)
        for u in range(GROUP):
            row = GROUP * i + u
            x = jnp.where(row < x_cells // 2, row + x_cells // 2, x_cells - 1 - row)
            store(vol_buf, x * odd(y_cells), lane_block(plus, u))
            store(vol_buf, x * odd(y_cells) + y_cells // 2, lane_block(minus, u))

    pipeline(x_cells // GROUP, [gather_x, back_y], 4)

    share = y_cells // 8
    me = place_ref[0]
    total = jnp.zeros((x_cells, LANES), F32)
    number = jnp.zeros((x_cells, LANES), F32)
    targets = [mines_ref.at[rot], side_ref, far_ref.at[0], far_ref.at[1]]
    for p, target in enumerate(targets):
        first = (me ^ p) * share
        values = []
        for i in range(share):
            firsts = []
            for j in range(2):
                y = 2 * (first + i) + j
                firsts.append(jnp.where(y < y_cells // 2, y_cells - 1 - y, y - y_cells // 2))
            values.append(pick(vol_buf, firsts, x_cells, odd(y_cells)))
        value = jnp.concatenate(values, axis=0)
        out = jnp.dot(split_rows(value, False), bz_ref[...], preferred_element_type=F32)
        rows = value.shape[0]
        full = out[:rows, :LANES] + out[:rows, LANES:] + out[rows:, :LANES]
        for i in range(share):
            corr = full[i * x_cells : (i + 1) * x_cells] * scale
            target[:, i * LANES : (i + 1) * LANES] = corr
            mask = mask_ref[first + i]
            total = total + corr * mask
            number = number + mask
    number_sum = jnp.sum(number)
    total_sum = jnp.sum(total)
    local_mean = jnp.full((1, LANES), total_sum, F32) / jnp.maximum(number_sum, 1.0)
    square = jnp.zeros((x_cells, LANES), F32)
    for p, target in enumerate(targets):
        first = (me ^ p) * share
        for i in range(share):
            gap = target[:, i * LANES : (i + 1) * LANES] - local_mean
            square = square + gap * gap * mask_ref[first + i]
    row = lax.broadcasted_iota(jnp.int32, (8, LANES), 0)
    stat_ref[...] = jnp.where(row == 0, number_sum, jnp.where(row == 1, total_sum, jnp.sum(square)))


def correlate(mines, place, tile, held, rot, last, entry, mask, spec, tmpl_z, dims, tables):
    x_cells, y_cells, z_cells = dims
    n_x, n_y = x_cells + TEMPL, y_cells + HALF
    pad_y = n_y // 2 + -(n_y // 2) % 8
    width = y_cells * z_cells // 4
    before = [] if mines is None else [mines]
    vmem = pl.BlockSpec(memory_space=pltpu.VMEM)
    return pl.pallas_call(
        functools.partial(corr_kernel, dims, rot, entry),
        out_shape=(
            jax.ShapeDtypeStruct((rot + 1, x_cells, width), F32),
            jax.ShapeDtypeStruct((x_cells, width), F32),
            jax.ShapeDtypeStruct((2, x_cells, width), F32),
            jax.ShapeDtypeStruct((8, LANES), F32),
        ),
        in_specs=[pl.BlockSpec(memory_space=pltpu.SMEM)] * 2 + [vmem] * (11 + len(before)),
        out_specs=(vmem,) * 4,
        scratch_shapes=[
            pltpu.VMEM((BLOCKS * odd(BLOCK_ROWS), LANES), F32),
            pltpu.VMEM((TEMPL * odd(TEMPL), LANES), F32),
            pltpu.VMEM((TEMPL * odd(2 * pad_y), LANES), F32),
            pltpu.VMEM((6, 3 * TEMPL, GROUP * LANES), BF16),
            pltpu.VMEM((4, 2 * n_x, GROUP * LANES), BF16),
            pltpu.VMEM((4, 2 * n_y, GROUP * LANES), BF16),
            pltpu.VMEM((n_y * odd(x_cells), LANES), F32),
            pltpu.VMEM((x_cells * odd(y_cells), LANES), F32),
        ],
        compiler_params=pltpu.CompilerParams(vmem_limit_bytes=20 * 1024 * 1024),
        cost_estimate=pl.CostEstimate(flops=15 * 10**9, bytes_accessed=10**7, transcendentals=0),
        name="correlate",
    )(
        place, tile, *before, held, last, mask, spec,
        tmpl_z, tables["ones_z"], tables["tmpl_y"], tables["tmpl_x"],
        tables["back_x"], tables["back_y"], tables["back_z"],
    )


def score_kernel(pieces, place_ref, coef_ref, mask_ref, *refs):
    best_ref, evid_ref, mom_ref = refs[-3:]
    blocks = best_ref.shape[1] // LANES

    def step(i):
        lanes = pl.ds(pl.multiple_of(i * LANES, LANES), LANES)

        def score(k):
            at, entry = pieces[k]
            return (refs[at][entry, :, lanes] - coef_ref[k, 0]) * coef_ref[k, 1]

        mask = mask_ref[place_ref[0] * blocks + i]
        high = functools.reduce(jnp.maximum, [score(k) for k in range(len(pieces))])
        total = jnp.zeros_like(high)
        moment = [jnp.zeros_like(high) for _ in range(4)]
        for k in range(len(pieces)):
            weight = jnp.exp(score(k) - high)
            total = total + weight
            for c in range(4):
                moment[c] = moment[c] + weight * coef_ref[k, 2 + c]
        best_ref[:, lanes] = mask * high
        evid_ref[:, lanes] = mask * (high + jnp.log(total))
        share = mask / total
        for c in range(4):
            mom_ref[c, :, lanes] = moment[c] * share

    def two_steps(i):
        step(2 * i)
        step(2 * i + 1)

    loop(blocks // 2, two_steps)


def combine(place, coefs, mask, arrays, pieces):
    shape = arrays[0].shape[1:]
    vmem = pl.BlockSpec(memory_space=pltpu.VMEM)
    out = jax.ShapeDtypeStruct(shape, F32)
    return pl.pallas_call(
        functools.partial(score_kernel, pieces),
        out_shape=(out, out, jax.ShapeDtypeStruct((4,) + shape, F32)),
        in_specs=[pl.BlockSpec(memory_space=pltpu.SMEM)] * 2 + [vmem] * (1 + len(arrays)),
        out_specs=(vmem,) * 3,
        compiler_params=pltpu.CompilerParams(vmem_limit_bytes=4 * 1024 * 1024),
        name="combine",
    )(place, coefs, mask, *arrays)


def swap_blocks(block, axis, step):
    return lax.ppermute(block, axis, [(i, i ^ step) for i in range(lax.axis_size(axis))])


def general_gather(templates):
    rots = templates.shape[0]
    count = lax.axis_size("tile")
    block = templates[:, None]
    for step in [1 << i for i in reversed(range(count.bit_length() - 1))]:
        other = swap_blocks(block, "tile", step)
        upper = (lax.axis_index("tile") & step) != 0
        pair = [jnp.where(upper, other, block), jnp.where(upper, block, other)]
        block = jnp.stack(pair, axis=2).reshape((rots, -1) + block.shape[2:])
    block = block.reshape(rots, BLOCKS, EACH * CHUNKS, LANES)
    block = jnp.pad(block, ((0, 0), (0, 0), (0, BLOCK_ROWS - EACH * CHUNKS), (0, 0)))
    held = jnp.stack([block[:, i] for i in HELD], axis=1)
    return held, jnp.stack([block[:, i ^ 1] for i in HELD], axis=1)


def merge(first, other):
    number_a, number_b = first[:1], other[:1]
    mean_a = first[1:2] / jnp.maximum(number_a, 1.0)
    mean_b = other[1:2] / jnp.maximum(number_b, 1.0)
    gap = mean_b - mean_a
    between = gap * gap * (number_a * number_b / jnp.maximum(number_a + number_b, 1.0))
    return first + other + jnp.where(jnp.arange(3)[:, None] == 2, between, 0.0)


def exchange_all(block, axis, low, high):
    count = lax.axis_size(axis)
    parts = [block]
    for step in range(low, high, low):
        parts.append(lax.ppermute(block, axis, [(i, i ^ step) for i in range(count)]))
    return jnp.stack(parts)


def neighbours(block, axis):
    count = lax.axis_size(axis)
    forward = [(i, i + 1) for i in range(count - 1)]
    backward = [(target, source) for source, target in forward]
    return lax.ppermute(block, axis, forward), lax.ppermute(block, axis, backward)


def local(tomogram, templates, valid, quats, rot_index):
    x_cells, voxels = tomogram.shape
    y_cells = valid.shape[1]
    z_cells = voxels // y_cells
    dims = (x_cells, y_cells, z_cells)
    tables = {name: jnp.asarray(table) for name, table in make_tables(*dims).items()}
    groups = lax.axis_size("rot")
    tiles = lax.axis_size("tile")
    me = lax.axis_index("rot")
    rots = templates.shape[0]

    tile = lax.axis_index("tile")
    by_blocks = tiles == BLOCKS
    if by_blocks:
        held = templates.reshape(rots, 1, EACH * CHUNKS, LANES)
        held = jnp.pad(held, ((0, 0), (0, 0), (0, BLOCK_ROWS - EACH * CHUNKS), (0, 0)))
        held, tomogram_after = lax.optimization_barrier((held, tomogram))
        held = jnp.concatenate([held, swap_blocks(held, "tile", 4)], axis=1)
    else:
        tomogram_after = tomogram
    half = x_cells // 2
    piece = lax.dynamic_slice_in_dim(tomogram_after, (me & 1) * half, half, 0)
    mine = jnp.stack(neighbours(piece, "tile"))
    side_swap = [(i, i ^ 1) for i in range(groups)]
    other = lax.ppermute(mine, "rot", side_swap)
    if by_blocks:
        second = swap_blocks(held, "tile", 2)
    else:
        held, last = general_gather(templates)
        tile = jnp.zeros_like(tile)
    one_hot = (rot_index[:, None] == jnp.arange(quats.shape[1], dtype=jnp.int32)[None, :]).astype(F32)
    orient = jnp.einsum("rq,kq->rk", one_hot, quats, precision=lax.Precision.HIGHEST)
    place = me_place = jnp.reshape(me, (1,)).astype(jnp.int32)
    tile = jnp.reshape(tile, (1,)).astype(jnp.int32)
    own = slab_rows(place, [tomogram], x_cells, 0, dims, tables, "slab_own")
    rows = slab_rows(place, [own, mine, other], TEMPL, x_cells, dims, tables, "slab_halo")
    if by_blocks:
        second = jnp.where(rows[0, 0] < 1e9, second, jnp.zeros_like(second))
        held = jnp.concatenate([held, second], axis=1)
        lasts = [swap_blocks(held[:1], "tile", 1), swap_blocks(held[1:], "tile", 1)]
    else:
        lasts = [last[:1], last[1:]]
    spec, mask, tmpl_z = slab_x(rows, valid, dims, tables)
    far_swap = [(i, i ^ 2) for i in range(groups)]
    mines, sides, fars, stats = None, [], [], []
    for r in range(rots):
        if r >= 3:
            place, fars[r - 3] = lax.optimization_barrier((place, fars[r - 3]))
        mines, side, far, stat = correlate(
            mines, place, tile, held, r, lasts[min(r, 1)], max(r - 1, 0), mask, spec, tmpl_z, dims, tables
        )
        if r >= 1:
            stat, fars[r - 1] = lax.optimization_barrier((stat, fars[r - 1]))
        sides.append(side)
        stats.append(stat[:3, 0])
        fars.append(lax.ppermute(far, "rot", far_swap))
        if r == rots - 2:
            early = jnp.stack(sides[:-1] + [f[1] for f in fars[:-1]])
            early = lax.ppermute(early, "rot", side_swap)
    state = jnp.stack(stats, axis=1)
    state, early, fars[rots - 2] = lax.optimization_barrier((state, early, fars[rots - 2]))
    step = 1
    while step < tiles:
        partner = lax.ppermute(state, "tile", [(i, i ^ step) for i in range(tiles)])
        if step * 4 == tiles:
            late = jnp.where(partner[0, 0] >= 0.0, fars[rots - 1][1], 0.0)
            last = jnp.stack([sides[rots - 2], sides[rots - 1], fars[rots - 2][1], late])
        if step * 2 == tiles:
            partner, last = lax.optimization_barrier((partner, last))
        state = merge(state, partner)
        step *= 2
    average = state[1] / state[0]
    inverse = 1.0 / jnp.sqrt(state[2] / state[0] + EPSILON)
    coefs = jnp.concatenate([average[:, None], inverse[:, None], orient], axis=1)
    coefs = exchange_all(coefs, "rot", 1, groups)
    last = lax.ppermute(last, "rot", side_swap)
    arrays = [mines] + fars + [early, last]
    at_far, at_early, at_last = 1, 1 + rots, 2 + rots
    pieces = [(0, r) for r in range(rots)]
    pieces += [(at_early, r) for r in range(rots - 2)] + [(at_last, 0), (at_last, 1)]
    pieces += [(at_far + r, 0) for r in range(rots)]
    pieces += [(at_early, rots - 2 + r) for r in range(rots - 2)] + [(at_last, 2), (at_last, 3)]
    return combine(me_place, coefs.reshape(groups * rots, 6), mask, arrays, pieces)


def solution(mesh):
    placed = (P("tile", None), P("rot", "tile"), P("tile", None), P(), P("rot"))
    return jax.shard_map(
        local,
        mesh=mesh,
        in_specs=placed,
        out_specs=(P("tile", "rot"), P("tile", "rot"), P(None, "tile", "rot")),
        check_vma=False,
    )
```
